32 devices in a mesh: parts: 2 (over y), row: 4 (over z), col: 4 (over x, core).
Axes of the slice: x: 2, y: 2, z: 4, core: 2. Of those that a mesh axis runs over, the one named last changes fastest.
Arguments:
- pair_act: bfloat16 [64, 32, 128], P(('parts', 'row'), 'col'), parts along dimension 0, may hold values from -6 to 6
- pair_mask: int32 [64, 32], P(('parts', 'row'), 'col'), parts along dimension 0, may hold values 0 or 1
- crop_length: int32 [2], P('parts'), parts along dimension 0, may hold values from 16 to 32
- weights: bfloat16 [6, 128, 128], replicated, may hold values from -0.5 to 0.5
- in_gain: float32 [128], replicated, may hold values from 0.25 to 1.75
- out_gain: float32 [128], replicated, may hold values from 0.25 to 1.75
- cotangent: bfloat16 [64, 32, 128], P(('parts', 'row'), 'col'), parts along dimension 0, may hold values from -6 to 6
Outputs:
- update: bfloat16 [64, 32, 128], P(('parts', 'row'), 'col'), parts along dimension 0
- pair_grad: bfloat16 [64, 32, 128], P(('parts', 'row'), 'col'), parts along dimension 0
- weight_grad: float32 [12, 128, 128], P('parts'), parts along dimension 0
The draws below stay inside these ranges and needn't reach their ends.
There are 2 independent parts, one for each index of `parts`. The reference program is written for one: setup_inputs(seed, part) draws one part's arguments, and reference() takes and returns one part's arrays. A program takes and returns all parts, laid end to end along the dimension named above; an argument that names none is the same for every part. Nothing has to cross between parts.
All inputs are finite; a program needn't handle non-finite values. No bound on the sum of `pair_mask` on one device may be relied on, other than what follows from the above.
Results may differ from the reference program's by a relative error of at most 0.014.
Values may be sent and summed in bfloat16 or wider, within the bound.
No kernel may reach another device: no remote copies, remote signals or barrier semaphores. Data moves between devices by JAX's collectives and lax.ppermute only.
A program may use at most 64 MiB of HBM per device.

```python
import jax
import jax.numpy as jnp
from jax import lax

CH = 128
ROW_TILE = 8
RESIDUES = 32
N_ROW = 4


def touch_ends(result, rng, smallest, high):
    index_at = [jax.random.randint(jax.random.fold_in(rng, axis), (), 0, length) for axis, length in enumerate(result.shape)]
    widest = result.shape.index(max(result.shape))
    beside = index_at[:widest] + [(index_at[widest] + 1) % result.shape[widest]] + index_at[widest + 1:]
    return result.at[tuple(index_at)].set(smallest).at[tuple(beside)].set(high)


def shard_levels(stream_key, extent, split, low, top_value):
    gain = 1.0
    for position, blocks in split:
        steps = jax.random.uniform(jax.random.fold_in(jax.random.fold_in(stream_key, 6), position), (blocks,), jnp.float32, low / len(split), top_value / len(split))
        gain = gain * jnp.repeat(jnp.exp(steps), extent[position] // blocks).reshape((-1,) + (1,) * (len(extent) - 1 - position))
    return gain


def bell_draw(key, shape, width, reach, shards=(), held_as=jnp.bfloat16):
    drawn = jax.random.normal(key, shape, jnp.float32) * width
    if len(shards) > 0:
        drawn = shard_levels(key, shape, shards, -0.22, 0.18) * drawn
    return jnp.clip(drawn, min=-reach, max=reach).astype(held_as)


def setup_inputs(seed: int = 0, part: int = 0) -> dict:
    streams_of = jax.random.split(jax.random.key(seed), 8)
    part_splits = jax.random.split(jax.random.fold_in(streams_of[7], part), 8)
    pair_act = bell_draw(part_splits[0], (RESIDUES, RESIDUES, CH), 1.0, 6.0, ((0, 4), (1, 4)))
    pair_mask = touch_ends((jax.random.randint(part_splits[1], (RESIDUES, RESIDUES), 0, 8) < 7).astype(jnp.int32), jax.random.fold_in(part_splits[1], 1), 0, 1)
    crop_length = jax.random.randint(part_splits[2], (1,), RESIDUES // 2, RESIDUES + 1).astype(jnp.int32)
    weights = bell_draw(streams_of[3], (6, CH, CH), CH ** -0.5, 0.5)
    in_gain = jnp.clip(1.0 + 0.15 * jax.random.normal(streams_of[4], (CH,), jnp.float32), 0.25, 1.75)
    out_gain = jnp.clip(1.0 + 0.15 * jax.random.normal(streams_of[5], (CH,), jnp.float32), 0.25, 1.75)
    cotangent = bell_draw(part_splits[6], (RESIDUES, RESIDUES, CH), 1.0, 6.0, ((0, 4), (1, 4)))
    return {"pair_act": pair_act, "pair_mask": pair_mask, "crop_length": crop_length, "weights": weights, "in_gain": in_gain, "out_gain": out_gain, "cotangent": cotangent}


def normalize(values):
    average = lax.optimization_barrier(jnp.mean(values, axis=-1, keepdims=True))
    centered = values - average
    inverse = lax.rsqrt(lax.optimization_barrier(jnp.mean(centered * centered, axis=-1, keepdims=True)) + 1e-05)
    return (centered * inverse, inverse)

def norm_back(grad_hat, values_hat, inverse):
    first = lax.optimization_barrier(jnp.mean(grad_hat, axis=-1, keepdims=True))
    second = lax.optimization_barrier(jnp.mean(grad_hat * values_hat, axis=-1, keepdims=True))
    return (grad_hat - first - values_hat * second) * inverse

def project(flat_in, matrix):
    return jnp.dot(flat_in, matrix, preferred_element_type=jnp.float32)

def gate_back(grad_act, proj_value, proj_gate, keep_mask):
    gate_sig = jax.nn.sigmoid(proj_gate)
    masked = grad_act * keep_mask
    grad_value = (masked * gate_sig).astype(jnp.bfloat16)
    grad_gate = (masked * proj_value * gate_sig * (1.0 - gate_sig)).astype(jnp.bfloat16)
    return (grad_value, grad_gate)

def reference(pair_act, pair_mask, crop_length, weights, in_gain, out_gain, cotangent):
    positions = jnp.arange(RESIDUES, dtype=jnp.int32)
    inside = (positions < crop_length[0]).astype(jnp.float32)
    keep_mask = pair_mask.astype(jnp.float32) * inside[:, None] * inside[None, :]
    keep_mask = keep_mask[:, :, None]
    z_hat, z_inverse = normalize(pair_act.astype(jnp.float32))
    normed = (z_hat * in_gain).astype(jnp.bfloat16)
    flat_norm = normed.reshape(RESIDUES * RESIDUES, CH)
    projections = [project(flat_norm, weights[select]).reshape(RESIDUES, RESIDUES, CH) for select in range(5)]
    left_act = (jax.nn.sigmoid(projections[1]) * projections[0] * keep_mask).astype(jnp.bfloat16)
    right_act = (jax.nn.sigmoid(projections[3]) * projections[2] * keep_mask).astype(jnp.bfloat16)
    tri_sum = jnp.einsum('ikh,jkh->ijh', left_act.astype(jnp.float32), right_act.astype(jnp.float32))
    x_hat, x_inverse = normalize(tri_sum)
    normed_out = (x_hat * out_gain).astype(jnp.bfloat16)
    flat_out = normed_out.reshape(RESIDUES * RESIDUES, CH)
    update_lin = project(flat_out, weights[5]).reshape(RESIDUES, RESIDUES, CH)
    out_gate = jax.nn.sigmoid(projections[4])
    update = (out_gate * update_lin).astype(jnp.bfloat16)
    cot_value = cotangent.astype(jnp.float32)
    grad_lin = (cot_value * out_gate).astype(jnp.bfloat16)
    grad_gate_out = (cot_value * update_lin * out_gate * (1.0 - out_gate)).astype(jnp.bfloat16)
    flat_lin = grad_lin.reshape(RESIDUES * RESIDUES, CH)
    grad_norm_out = project(flat_lin, weights[5].T).reshape(RESIDUES, RESIDUES, CH)
    grad_tri = norm_back(grad_norm_out * out_gain, x_hat, x_inverse).astype(jnp.bfloat16)
    grad_left = jnp.einsum('ijh,jkh->ikh', grad_tri.astype(jnp.float32), right_act.astype(jnp.float32))
    grouped_tri = grad_tri.reshape(N_ROW, ROW_TILE, RESIDUES, CH)
    grouped_left = left_act.reshape(N_ROW, ROW_TILE, RESIDUES, CH)

    def accumulate(running, grouped):
        partial_sum = jnp.einsum('ijh,ikh->jkh', grouped[0].astype(jnp.float32), grouped[1].astype(jnp.float32))
        rounded = lax.optimization_barrier(partial_sum.astype(jnp.bfloat16))
        return (running + rounded.astype(jnp.float32), None)
    grad_right, _ = lax.scan(accumulate, jnp.zeros((RESIDUES, RESIDUES, CH), jnp.float32), (grouped_tri, grouped_left))
    grad_pa, grad_ga = gate_back(grad_left, projections[0], projections[1], keep_mask)
    grad_pb, grad_gb = gate_back(grad_right, projections[2], projections[3], keep_mask)
    grads = [grad_pa, grad_ga, grad_pb, grad_gb, grad_gate_out]
    grad_normed = jnp.zeros((RESIDUES * RESIDUES, CH), jnp.float32)
    for select in range(5):
        grad_normed = grad_normed + project(grads[select].reshape(RESIDUES * RESIDUES, CH), weights[select].T)
    grad_normed = grad_normed.reshape(RESIDUES, RESIDUES, CH)
    pair_grad = norm_back(grad_normed * in_gain, z_hat, z_inverse).astype(jnp.bfloat16)
    stacked = [project(flat_norm.T, grads[select].reshape(RESIDUES * RESIDUES, CH)) for select in range(5)]
    stacked.append(project(flat_out.T, flat_lin))
    weight_grad = jnp.stack(stacked) / RESIDUES
    return (update, pair_grad, weight_grad)
```

```python
import functools

import jax
import jax.numpy as jnp
from jax import lax
from jax.experimental import pallas as pl
from jax.experimental.pallas import tpu as pltpu
from jax.sharding import PartitionSpec as P

SUB = 8
EPS = 1e-05


def normalize(values):
    average = jnp.mean(values, axis=-1, keepdims=True)
    centered = values - average
    inverse = lax.rsqrt(jnp.mean(centered * centered, axis=-1, keepdims=True) + 1e-05)
    return (centered * inverse, inverse)


def norm_back(grad_hat, values_hat, inverse):
    first = jnp.mean(grad_hat, axis=-1, keepdims=True)
    second = jnp.mean(grad_hat * values_hat, axis=-1, keepdims=True)
    return (grad_hat - first - values_hat * second) * inverse


def gate_back(grad_act, proj_value, proj_gate, keep_mask):
    gate_sig = jax.nn.sigmoid(proj_gate)
    masked = grad_act * keep_mask
    grad_value = (masked * gate_sig).astype(jnp.bfloat16)
    grad_gate = (masked * proj_value * gate_sig * (1.0 - gate_sig)).astype(jnp.bfloat16)
    return (grad_value, grad_gate)


def spread_body(pair_act, pair_mask, crop_length, weights, in_gain, out_gain, cotangent):
    tile_rows, tile_cols, channels = pair_act.shape
    residues = tile_rows * lax.axis_size("row")
    row_pos = lax.axis_index("row") * tile_rows + jnp.arange(tile_rows, dtype=jnp.int32)
    col_pos = lax.axis_index("col") * tile_cols + jnp.arange(tile_cols, dtype=jnp.int32)
    row_in = (row_pos < crop_length[0]).astype(jnp.float32)
    col_in = (col_pos < crop_length[0]).astype(jnp.float32)
    keep_mask = (pair_mask.astype(jnp.float32) * row_in[:, None] * col_in[None, :])[:, :, None]
    z_hat, z_inverse = normalize(pair_act.astype(jnp.float32))
    normed = (z_hat * in_gain).astype(jnp.bfloat16)
    flat_norm = normed.reshape(tile_rows * tile_cols, channels)
    projections = jnp.einsum(
        "pc,scd->spd", flat_norm, weights[:5], preferred_element_type=jnp.float32
    )
    projections = projections.reshape(5, tile_rows, tile_cols, channels)
    left_act = (jax.nn.sigmoid(projections[1]) * projections[0] * keep_mask).astype(jnp.bfloat16)
    right_act = (jax.nn.sigmoid(projections[3]) * projections[2] * keep_mask).astype(jnp.bfloat16)
    partial_value = jnp.einsum(
        "ikh,jkh->ijh",
        left_act,
        lax.all_gather(right_act, "row", axis=0, tiled=True),
        preferred_element_type=jnp.float32,
    )
    tri_sum = lax.psum_scatter(
        partial_value.astype(jnp.bfloat16), "col", scatter_dimension=1, tiled=True
    ).astype(jnp.float32)
    x_hat, x_inverse = normalize(tri_sum)
    normed_out = (x_hat * out_gain).astype(jnp.bfloat16)
    flat_out = normed_out.reshape(tile_rows * tile_cols, channels)
    update_lin = jnp.dot(flat_out, weights[5], preferred_element_type=jnp.float32)
    update_lin = update_lin.reshape(tile_rows, tile_cols, channels)
    out_gate = jax.nn.sigmoid(projections[4])
    update = (out_gate * update_lin).astype(jnp.bfloat16)
    cot_value = cotangent.astype(jnp.float32)
    grad_lin = (cot_value * out_gate).astype(jnp.bfloat16)
    grad_gate_out = (cot_value * update_lin * out_gate * (1.0 - out_gate)).astype(jnp.bfloat16)
    flat_lin = grad_lin.reshape(tile_rows * tile_cols, channels)
    grad_norm_out = jnp.einsum(
        "pd,cd->pc", flat_lin, weights[5], preferred_element_type=jnp.float32
    )
    grad_norm_out = grad_norm_out.reshape(tile_rows, tile_cols, channels)
    grad_tri = norm_back(grad_norm_out * out_gain, x_hat, x_inverse).astype(jnp.bfloat16)
    grad_full = lax.all_gather(grad_tri, "col", axis=1, tiled=True)
    grad_slab = grad_full
    grad_left = jnp.einsum(
        "ijh,jkh->ikh",
        grad_slab,
        lax.all_gather(right_act, "row", axis=0, tiled=True),
        preferred_element_type=jnp.float32,
    )
    grad_slab = grad_full
    grad_right = lax.psum_scatter(
        jnp.einsum("ijh,ikh->jkh", grad_slab, left_act, preferred_element_type=jnp.float32).astype(
            jnp.bfloat16
        ),
        "row",
        scatter_dimension=0,
        tiled=True,
    ).astype(jnp.float32)
    grad_pa, grad_ga = gate_back(grad_left, projections[0], projections[1], keep_mask)
    grad_pb, grad_gb = gate_back(grad_right, projections[2], projections[3], keep_mask)
    grads = jnp.stack([grad_pa, grad_ga, grad_pb, grad_gb, grad_gate_out]).reshape(
        5, tile_rows * tile_cols, channels
    )
    grad_normed = jnp.einsum("spd,scd->pc", grads, weights[:5], preferred_element_type=jnp.float32)
    grad_normed = grad_normed.reshape(tile_rows, tile_cols, channels)
    pair_grad = norm_back(grad_normed * in_gain, z_hat, z_inverse).astype(jnp.bfloat16)
    local_in = jnp.einsum("pc,spd->scd", flat_norm, grads, preferred_element_type=jnp.float32)
    local_out = jnp.dot(flat_out.T, flat_lin, preferred_element_type=jnp.float32)
    local_grads = jnp.concatenate([local_in, local_out[None]], axis=0) / residues
    weight_grad = lax.psum(local_grads, ("row", "col"))
    return (update, pair_grad, weight_grad)


def pack_kernel(crop_ref, act_ref, mask_ref, cot_ref, gain_ref, out_ref):
    tile_rows, tile_cols, channels = act_ref.shape
    pairs = tile_rows * tile_cols
    z_hat, _ = normalize(act_ref[...].astype(jnp.float32).reshape(pairs, channels))
    out_ref[0:pairs] = (z_hat * gain_ref[...]).astype(jnp.bfloat16)
    out_ref[pairs : 2 * pairs] = cot_ref[...].reshape(pairs, channels)
    row_at = lax.axis_index("row") * tile_rows
    col_at = lax.axis_index("col") * tile_cols
    rows = row_at + lax.broadcasted_iota(jnp.int32, (tile_rows, tile_cols), 0)
    cols = col_at + lax.broadcasted_iota(jnp.int32, (tile_rows, tile_cols), 1)
    inside = (rows < crop_ref[0]) & (cols < crop_ref[0])
    keep = jnp.where(inside, mask_ref[...], 0).astype(jnp.float32)
    wide = jnp.concatenate([keep, jnp.zeros((tile_rows, channels - tile_cols), jnp.float32)], axis=1)
    tall = jnp.concatenate([wide, jnp.zeros((channels - tile_rows, channels), jnp.float32)], axis=0)
    flipped = tall.T
    extra = out_ref.shape[0] - 2 * pairs
    out_ref[2 * pairs :] = flipped[0:extra].astype(jnp.bfloat16)


def triangle(residues, vector_at, scalar_at, store_at):
    groups = residues // SUB

    def block(a, _):
        def step(q, totals):
            totals = list(totals)
            for inner in range(SUB):
                m = q * SUB + inner
                vectors = [vector_at(m, g) for g in range(groups)]
                for lane in range(SUB):
                    factor = scalar_at(a * SUB + lane, m)
                    for g in range(groups):
                        at = lane * groups + g
                        totals[at] = totals[at] + factor * vectors[g]
            return tuple(totals)

        zero = jnp.zeros((SUB, 128), jnp.float32)
        totals = lax.fori_loop(0, groups, step, (zero,) * (SUB * groups))
        for lane in range(SUB):
            for g in range(groups):
                store_at(a * SUB + lane, g, totals[lane * groups + g])
        return 0

    lax.fori_loop(0, groups, block, 0)


def part_kernel(
    n_row, n_col, all_ref, act_ref, weights_ref, in_gain_ref, out_gain_ref,
    update_ref, pair_grad_ref, weight_grad_ref,
    proj_ref, left_ref, right_ref, keep_ref, tri_ref, lin_ref, gate_ref, hat_ref, upd_ref, d_ref,
):
    tile_rows, tile_cols, channels = act_ref.shape
    tile = tile_rows * tile_cols
    residues = n_row * tile_rows
    pairs = residues * residues
    blocks = n_row * n_col
    chunk = 4 * tile
    bf16, f32 = jnp.bfloat16, jnp.float32

    def row_of(i, k):
        return ((i // tile_rows * n_col + k // tile_cols) * tile_rows + i % tile_rows) * tile_cols + k % tile_cols

    def vector(ref, i, k):
        return ref[pl.ds(pl.multiple_of(row_of(i, k), SUB), SUB), :]

    def spread(ref, i, k):
        return jnp.broadcast_to(ref[pl.ds(row_of(i, k), 1), :], (SUB, channels))

    def chunks():
        return [(at, slice(at, at + chunk)) for at in range(0, pairs, chunk)]

    def normed_rows(at):
        first = at // tile
        return all_ref[first : first + chunk // tile, 0:tile, :].reshape(chunk, channels)

    def cot_rows(at):
        first = at // tile
        return all_ref[first : first + chunk // tile, tile : 2 * tile, :].reshape(chunk, channels)

    for at, rows in chunks():
        normed = normed_rows(at)
        for s in range(5):
            proj_ref[s, rows, :] = jnp.dot(normed, weights_ref[s], preferred_element_type=f32)
        for b in range(at // tile, (at + chunk) // tile):
            keep = all_ref[b, 2 * tile : 2 * tile + 16, :].astype(f32)[0:tile_cols]
            for ii in range(tile_rows):
                spot = (b * tile_rows + ii) * tile_cols
                keep_ref[spot : spot + tile_cols, :] = jnp.broadcast_to(keep[:, ii : ii + 1], (tile_cols, channels))
        kept = keep_ref[rows, :]
        left = jax.nn.sigmoid(proj_ref[1, rows, :]) * proj_ref[0, rows, :] * kept
        right = jax.nn.sigmoid(proj_ref[3, rows, :]) * proj_ref[2, rows, :] * kept
        left_ref[rows, :] = left.astype(bf16).astype(f32)
        right_ref[rows, :] = right.astype(bf16).astype(f32)

    def right_flipped(k, g):
        return right_ref[pl.ds(row_of(g * SUB, k), SUB, stride=tile_cols), :]

    def keep_tri(i, g, total):
        tri_ref[pl.ds(pl.multiple_of(row_of(i, g * SUB), SUB), SUB), :] = total

    triangle(residues, right_flipped, lambda i, k: spread(left_ref, i, k), keep_tri)

    out_gain = out_gain_ref[...]
    for at, rows in chunks():
        x_hat, inverse = normalize(tri_ref[rows, :])
        normed_out = (x_hat * out_gain).astype(bf16)
        hat_ref[rows, :] = normed_out
        lin = jnp.dot(normed_out, weights_ref[5], preferred_element_type=f32)
        out_gate = jax.nn.sigmoid(proj_ref[4, rows, :])
        cot = cot_rows(at).astype(f32)
        upd_ref[rows, :] = out_gate * lin
        grad_lin = (cot * out_gate).astype(bf16)
        lin_ref[rows, :] = grad_lin
        d_ref[4, rows, :] = (cot * lin * out_gate * (1.0 - out_gate)).astype(bf16)
        back = lax.dot_general(grad_lin, weights_ref[5], (((1,), (1,)), ((), ())), preferred_element_type=f32)
        tri_ref[rows, :] = norm_back(back * out_gain, x_hat, inverse).astype(bf16).astype(f32)

    def keep_left(i, g, total):
        gate_ref[0, pl.ds(pl.multiple_of(row_of(i, g * SUB), SUB), SUB), :] = total

    def keep_right(j, g, total):
        gate_ref[1, pl.ds(pl.multiple_of(row_of(j, g * SUB), SUB), SUB), :] = total

    triangle(residues, lambda j, g: vector(right_ref, j, g * SUB), lambda i, j: spread(tri_ref, i, j), keep_left)
    triangle(residues, lambda i, g: vector(left_ref, i, g * SUB), lambda j, i: spread(tri_ref, i, j), keep_right)

    for at, rows in chunks():
        kept = keep_ref[rows, :]
        for side in range(2):
            value, gate = gate_back(gate_ref[side, rows, :], proj_ref[2 * side, rows, :], proj_ref[2 * side + 1, rows, :], kept)
            d_ref[2 * side, rows, :] = value
            d_ref[2 * side + 1, rows, :] = gate

    normed_all = all_ref[:, 0:tile, :].reshape(pairs, channels)
    for s in range(5):
        weight_grad_ref[s] = lax.dot_general(
            normed_all, d_ref[s], (((0,), (0,)), ((), ())), preferred_element_type=f32
        ) / residues
    weight_grad_ref[5] = lax.dot_general(
        hat_ref[...], lin_ref[...], (((0,), (0,)), ((), ())), preferred_element_type=f32
    ) / residues

    mine = pl.multiple_of((lax.axis_index("row") * n_col + lax.axis_index("col")) * tile, tile)
    own = pl.ds(mine, tile)
    update_ref[...] = upd_ref[own, :].astype(bf16).reshape(update_ref.shape)
    total = jnp.zeros((tile, channels), f32)
    for s in range(5):
        total = total + lax.dot_general(d_ref[s, own, :], weights_ref[s], (((1,), (1,)), ((), ())), preferred_element_type=f32)
    z_hat, z_inverse = normalize(act_ref[...].astype(f32).reshape(tile, channels))
    grad = norm_back(total * in_gain_ref[...], z_hat, z_inverse)
    pair_grad_ref[...] = grad.astype(bf16).reshape(pair_grad_ref.shape)


def gathered_body(n_row, n_col, pair_act, pair_mask, crop_length, weights, in_gain, out_gain, cotangent):
    tile_rows, tile_cols, channels = pair_act.shape
    tile = tile_rows * tile_cols
    pairs = tile * n_row * n_col
    vmem = pl.BlockSpec(memory_space=pltpu.VMEM)
    smem = pl.BlockSpec(memory_space=pltpu.SMEM)
    packed = pl.pallas_call(
        pack_kernel,
        name="pack",
        out_shape=jax.ShapeDtypeStruct((2 * tile + 16, channels), jnp.bfloat16),
        in_specs=[smem, vmem, vmem, vmem, vmem],
        out_specs=vmem,
    )(crop_length, pair_act, pair_mask, cotangent, in_gain.reshape(1, channels))
    everyone = lax.all_gather(packed, ("row", "col"), axis=0)
    f32, bf16 = jnp.float32, jnp.bfloat16
    return pl.pallas_call(
        functools.partial(part_kernel, n_row, n_col),
        name="part",
        out_shape=(
            jax.ShapeDtypeStruct(pair_act.shape, bf16),
            jax.ShapeDtypeStruct(pair_act.shape, bf16),
            jax.ShapeDtypeStruct(weights.shape, f32),
        ),
        in_specs=[vmem] * 5,
        out_specs=(vmem, vmem, vmem),
        scratch_shapes=[
            pltpu.VMEM((5, pairs, channels), f32),
            pltpu.VMEM((pairs, channels), f32),
            pltpu.VMEM((pairs, channels), f32),
            pltpu.VMEM((pairs, channels), f32),
            pltpu.VMEM((pairs, channels), f32),
            pltpu.VMEM((pairs, channels), bf16),
            pltpu.VMEM((2, pairs, channels), f32),
            pltpu.VMEM((pairs, channels), bf16),
            pltpu.VMEM((pairs, channels), f32),
            pltpu.VMEM((5, pairs, channels), bf16),
        ],
        compiler_params=pltpu.CompilerParams(vmem_limit_bytes=32 * 1024 * 1024),
    )(everyone, pair_act, weights, in_gain.reshape(1, channels), out_gain.reshape(1, channels))


def body(n_row, n_col, pair_act, *others):
    tile_rows, tile_cols, channels = pair_act.shape
    pairs = tile_rows * n_row * tile_cols * n_col
    small = pairs * channels * 4 <= 1024 * 1024
    if small and channels == 128 and tile_rows % SUB == 0 and tile_cols % SUB == 0 and tile_cols <= 16:
        return gathered_body(n_row, n_col, pair_act, *others)
    return spread_body(pair_act, *others)


def solution(mesh):
    return jax.shard_map(
        functools.partial(body, mesh.shape["row"], mesh.shape["col"]),
        mesh=mesh,
        in_specs=(
            P(("parts", "row"), "col", None),
            P(("parts", "row"), "col"),
            P("parts"),
            P(),
            P(),
            P(),
            P(("parts", "row"), "col", None),
        ),
        out_specs=(
            P(("parts", "row"), "col", None),
            P(("parts", "row"), "col", None),
            P("parts", None, None),
        ),
        check_vma=False,
    )
```

```python
import functools

import jax
import jax.numpy as jnp
from jax import lax
from jax.experimental import pallas as pl
from jax.experimental.pallas import tpu as pltpu
from jax.sharding import PartitionSpec as P

SUB = 8
EPS = 1e-05


def normalize(values):
    average = jnp.mean(values, axis=-1, keepdims=True)
    centered = values - average
    inverse = lax.rsqrt(jnp.mean(centered * centered, axis=-1, keepdims=True) + 1e-05)
    return (centered * inverse, inverse)


def norm_back(grad_hat, values_hat, inverse):
    first = jnp.mean(grad_hat, axis=-1, keepdims=True)
    second = jnp.mean(grad_hat * values_hat, axis=-1, keepdims=True)
    return (grad_hat - first - values_hat * second) * inverse


def gate_back(grad_act, proj_value, proj_gate, keep_mask):
    gate_sig = jax.nn.sigmoid(proj_gate)
    masked = grad_act * keep_mask
    grad_value = (masked * gate_sig).astype(jnp.bfloat16)
    grad_gate = (masked * proj_value * gate_sig * (1.0 - gate_sig)).astype(jnp.bfloat16)
    return (grad_value, grad_gate)


def spread_body(pair_act, pair_mask, crop_length, weights, in_gain, out_gain, cotangent):
    tile_rows, tile_cols, channels = pair_act.shape
    residues = tile_rows * lax.axis_size("row")
    row_pos = lax.axis_index("row") * tile_rows + jnp.arange(tile_rows, dtype=jnp.int32)
    col_pos = lax.axis_index("col") * tile_cols + jnp.arange(tile_cols, dtype=jnp.int32)
    row_in = (row_pos < crop_length[0]).astype(jnp.float32)
    col_in = (col_pos < crop_length[0]).astype(jnp.float32)
    keep_mask = (pair_mask.astype(jnp.float32) * row_in[:, None] * col_in[None, :])[:, :, None]
    z_hat, z_inverse = normalize(pair_act.astype(jnp.float32))
    normed = (z_hat * in_gain).astype(jnp.bfloat16)
    flat_norm = normed.reshape(tile_rows * tile_cols, channels)
    projections = jnp.einsum(
        "pc,scd->spd", flat_norm, weights[:5], preferred_element_type=jnp.float32
    )
    projections = projections.reshape(5, tile_rows, tile_cols, channels)
    left_act = (jax.nn.sigmoid(projections[1]) * projections[0] * keep_mask).astype(jnp.bfloat16)
    right_act = (jax.nn.sigmoid(projections[3]) * projections[2] * keep_mask).astype(jnp.bfloat16)
    partial_value = jnp.einsum(
        "ikh,jkh->ijh",
        left_act,
        lax.all_gather(right_act, "row", axis=0, tiled=True),
        preferred_element_type=jnp.float32,
    )
    tri_sum = lax.psum_scatter(
        partial_value.astype(jnp.bfloat16), "col", scatter_dimension=1, tiled=True
    ).astype(jnp.float32)
    x_hat, x_inverse = normalize(tri_sum)
    normed_out = (x_hat * out_gain).astype(jnp.bfloat16)
    flat_out = normed_out.reshape(tile_rows * tile_cols, channels)
    update_lin = jnp.dot(flat_out, weights[5], preferred_element_type=jnp.float32)
    update_lin = update_lin.reshape(tile_rows, tile_cols, channels)
    out_gate = jax.nn.sigmoid(projections[4])
    update = (out_gate * update_lin).astype(jnp.bfloat16)
    cot_value = cotangent.astype(jnp.float32)
    grad_lin = (cot_value * out_gate).astype(jnp.bfloat16)
    grad_gate_out = (cot_value * update_lin * out_gate * (1.0 - out_gate)).astype(jnp.bfloat16)
    flat_lin = grad_lin.reshape(tile_rows * tile_cols, channels)
    grad_norm_out = jnp.einsum(
        "pd,cd->pc", flat_lin, weights[5], preferred_element_type=jnp.float32
    )
    grad_norm_out = grad_norm_out.reshape(tile_rows, tile_cols, channels)
    grad_tri = norm_back(grad_norm_out * out_gain, x_hat, x_inverse).astype(jnp.bfloat16)
    grad_full = lax.all_gather(grad_tri, "col", axis=1, tiled=True)
    grad_slab = grad_full
    grad_left = jnp.einsum(
        "ijh,jkh->ikh",
        grad_slab,
        lax.all_gather(right_act, "row", axis=0, tiled=True),
        preferred_element_type=jnp.float32,
    )
    grad_slab = grad_full
    grad_right = lax.psum_scatter(
        jnp.einsum("ijh,ikh->jkh", grad_slab, left_act, preferred_element_type=jnp.float32).astype(
            jnp.bfloat16
        ),
        "row",
        scatter_dimension=0,
        tiled=True,
    ).astype(jnp.float32)
    grad_pa, grad_ga = gate_back(grad_left, projections[0], projections[1], keep_mask)
    grad_pb, grad_gb = gate_back(grad_right, projections[2], projections[3], keep_mask)
    grads = jnp.stack([grad_pa, grad_ga, grad_pb, grad_gb, grad_gate_out]).reshape(
        5, tile_rows * tile_cols, channels
    )
    grad_normed = jnp.einsum("spd,scd->pc", grads, weights[:5], preferred_element_type=jnp.float32)
    grad_normed = grad_normed.reshape(tile_rows, tile_cols, channels)
    pair_grad = norm_back(grad_normed * in_gain, z_hat, z_inverse).astype(jnp.bfloat16)
    local_in = jnp.einsum("pc,spd->scd", flat_norm, grads, preferred_element_type=jnp.float32)
    local_out = jnp.dot(flat_out.T, flat_lin, preferred_element_type=jnp.float32)
    local_grads = jnp.concatenate([local_in, local_out[None]], axis=0) / residues
    weight_grad = lax.psum(local_grads, ("row", "col"))
    return (update, pair_grad, weight_grad)


def pack_kernel(crop_ref, act_ref, mask_ref, cot_ref, gain_ref, out_ref):
    tile_rows, tile_cols, channels = act_ref.shape
    pairs = tile_rows * tile_cols
    z_hat, _ = normalize(act_ref[...].astype(jnp.float32).reshape(pairs, channels))
    out_ref[0:pairs] = (z_hat * gain_ref[...]).astype(jnp.bfloat16)
    out_ref[pairs : 2 * pairs] = cot_ref[...].reshape(pairs, channels)
    row_at = lax.axis_index("row") * tile_rows
    col_at = lax.axis_index("col") * tile_cols
    rows = row_at + lax.broadcasted_iota(jnp.int32, (tile_rows, tile_cols), 0)
    cols = col_at + lax.broadcasted_iota(jnp.int32, (tile_rows, tile_cols), 1)
    inside = (rows < crop_ref[0]) & (cols < crop_ref[0])
    keep = jnp.where(inside, mask_ref[...], 0).astype(jnp.float32)
    wide = jnp.concatenate([keep, jnp.zeros((tile_rows, channels - tile_cols), jnp.float32)], axis=1)
    tall = jnp.concatenate([wide, jnp.zeros((channels - tile_rows, channels), jnp.float32)], axis=0)
    flipped = tall.T
    extra = out_ref.shape[0] - 2 * pairs
    out_ref[2 * pairs :] = flipped[0:extra].astype(jnp.bfloat16)


def triangle(groups, vectors_at, factors_at, store_at):
    def block(a, _):
        def step(q, totals):
            totals = list(totals)
            vectors = vectors_at(q)
            factors = factors_at(a, q)
            for inner in range(SUB):
                rows = [vectors(g, inner) for g in range(groups)]
                for lane in range(SUB):
                    factor = factors(lane, inner)
                    for g in range(groups):
                        at = lane * groups + g
                        totals[at] = totals[at] + factor * rows[g]
            return tuple(totals)

        zero = jnp.zeros((SUB, 128), jnp.float32)
        totals = lax.fori_loop(0, groups, step, (zero,) * (SUB * groups))
        for g in range(groups):
            store_at(a, g, [totals[lane * groups + g] for lane in range(SUB)])
        return 0

    lax.fori_loop(0, groups, block, 0)


def part_kernel(
    n_row, n_col, act_ref, weights_ref, in_gain_ref, out_gain_ref, *refs,
):
    blocks = n_row * n_col
    part_refs(n_row, n_col, act_ref, weights_ref, in_gain_ref, out_gain_ref, refs[:blocks], *refs[blocks:])


def part_refs(
    n_row, n_col, act_ref, weights_ref, in_gain_ref, out_gain_ref, all_refs,
    update_ref, pair_grad_ref, weight_grad_ref,
    proj_ref, left_ref, right_ref, keep_ref, tri_ref, lin_ref, gate_ref, hat_ref, upd_ref, d_ref,
):
    tile_rows, tile_cols, channels = act_ref.shape
    tile = tile_rows * tile_cols
    residues = n_row * tile_rows
    pairs = residues * residues
    chunk = 4 * tile
    bf16, f32 = jnp.bfloat16, jnp.float32

    row_me, col_me = lax.axis_index("row"), lax.axis_index("col")

    def base(row, col):
        slot = lax.rem(row_me + n_row - row, n_row) * n_col + (col ^ col_me)
        return pl.multiple_of(slot * tile, tile)

    def spread(ref, row):
        return jnp.broadcast_to(ref[pl.ds(row, 1), :], (SUB, channels))

    def line(ref, row):
        return ref[pl.ds(pl.multiple_of(row, SUB), SUB), :]

    def lines(ref):
        def store(row, col, values):
            first = base(row, col)
            for lane in range(SUB):
                ref[pl.ds(pl.multiple_of(first + lane * SUB, SUB), SUB), :] = values[lane]
        return store

    def across(ref):
        def at(q):
            firsts = [base(q, g) for g in range(n_col)]
            return lambda g, inner: line(ref, firsts[g] + inner * SUB)
        return at

    def chunks():
        return [(at, slice(at, at + chunk)) for at in range(0, pairs, chunk)]

    def normed_rows(at):
        return jnp.concatenate([all_refs[b][0:tile] for b in range(at // tile, (at + chunk) // tile)], axis=0)

    def cot_rows(at):
        return jnp.concatenate([all_refs[b][tile : 2 * tile] for b in range(at // tile, (at + chunk) // tile)], axis=0)

    for at, rows in chunks():
        normed = normed_rows(at)
        for s in range(5):
            proj_ref[s, rows, :] = jnp.dot(normed, weights_ref[s], preferred_element_type=f32)
        for b in range(at // tile, (at + chunk) // tile):
            keep = all_refs[b][2 * tile : 2 * tile + 16, :].astype(f32)[0:tile_cols]
            for ii in range(tile_rows):
                spot = (b * tile_rows + ii) * tile_cols
                keep_ref[spot : spot + tile_cols, :] = jnp.broadcast_to(keep[:, ii : ii + 1], (tile_cols, channels))
        kept = keep_ref[rows, :]
        left = jax.nn.sigmoid(proj_ref[1, rows, :]) * proj_ref[0, rows, :] * kept
        right = jax.nn.sigmoid(proj_ref[3, rows, :]) * proj_ref[2, rows, :] * kept
        left_ref[rows, :] = left.astype(bf16).astype(f32)
        right_ref[rows, :] = right.astype(bf16).astype(f32)

    def flipped(q):
        firsts = [base(g, q) for g in range(n_row)]
        return lambda g, inner: right_ref[pl.ds(firsts[g] + inner, SUB, stride=SUB), :]

    def along(ref):
        def at(a, q):
            first = base(a, q)
            return lambda lane, inner: spread(ref, first + lane * SUB + inner)
        return at

    def down(ref):
        def at(a, q):
            first = base(q, a)
            return lambda lane, inner: spread(ref, first + inner * SUB + lane)
        return at

    triangle(n_row, flipped, along(left_ref), lines(tri_ref))

    out_gain = out_gain_ref[...]
    for at, rows in chunks():
        x_hat, inverse = normalize(tri_ref[rows, :])
        normed_out = (x_hat * out_gain).astype(bf16)
        hat_ref[rows, :] = normed_out
        lin = jnp.dot(normed_out, weights_ref[5], preferred_element_type=f32)
        out_gate = jax.nn.sigmoid(proj_ref[4, rows, :])
        cot = cot_rows(at).astype(f32)
        upd_ref[rows, :] = out_gate * lin
        grad_lin = (cot * out_gate).astype(bf16)
        lin_ref[rows, :] = grad_lin
        d_ref[4, rows, :] = (cot * lin * out_gate * (1.0 - out_gate)).astype(bf16)
        back = lax.dot_general(grad_lin, weights_ref[5], (((1,), (1,)), ((), ())), preferred_element_type=f32)
        tri_ref[rows, :] = norm_back(back * out_gain, x_hat, inverse).astype(bf16).astype(f32)

    triangle(n_row, across(right_ref), along(tri_ref), lines(gate_ref.at[0]))
    triangle(n_row, across(left_ref), down(tri_ref), lines(gate_ref.at[1]))

    for at, rows in chunks():
        kept = keep_ref[rows, :]
        for side in range(2):
            value, gate = gate_back(gate_ref[side, rows, :], proj_ref[2 * side, rows, :], proj_ref[2 * side + 1, rows, :], kept)
            d_ref[2 * side, rows, :] = value
            d_ref[2 * side + 1, rows, :] = gate

    normed_all = jnp.concatenate([ref[0:tile] for ref in all_refs], axis=0)
    for s in range(5):
        weight_grad_ref[s] = lax.dot_general(
            normed_all, d_ref[s], (((0,), (0,)), ((), ())), preferred_element_type=f32
        ) / residues
    weight_grad_ref[5] = lax.dot_general(
        hat_ref[...], lin_ref[...], (((0,), (0,)), ((), ())), preferred_element_type=f32
    ) / residues

    own = slice(0, tile)
    update_ref[...] = upd_ref[own, :].astype(bf16).reshape(update_ref.shape)
    total = jnp.zeros((tile, channels), f32)
    for s in range(5):
        total = total + lax.dot_general(d_ref[s, own, :], weights_ref[s], (((1,), (1,)), ((), ())), preferred_element_type=f32)
    z_hat, z_inverse = normalize(act_ref[...].astype(f32).reshape(tile, channels))
    grad = norm_back(total * in_gain_ref[...], z_hat, z_inverse)
    pair_grad_ref[...] = grad.astype(bf16).reshape(pair_grad_ref.shape)


def gather_tree(own, n_row, n_col):
    blocks = {(0, 0): own}
    for shift in range(1, n_row):
        blocks[shift, 0] = lax.ppermute(own, "row", [(r, (r + shift) % n_row) for r in range(n_row)])
    bit = n_col // 2
    while bit > 0:
        for (shift, flip), piece in list(blocks.items()):
            blocks[shift, flip ^ bit] = lax.ppermute(piece, "col", [(c, c ^ bit) for c in range(n_col)])
        bit //= 2
    return [blocks[shift, flip] for shift in range(n_row) for flip in range(n_col)]


def gathered_body(n_row, n_col, pair_act, pair_mask, crop_length, weights, in_gain, out_gain, cotangent):
    tile_rows, tile_cols, channels = pair_act.shape
    tile = tile_rows * tile_cols
    pairs = tile * n_row * n_col
    vmem = pl.BlockSpec(memory_space=pltpu.VMEM)
    smem = pl.BlockSpec(memory_space=pltpu.SMEM)
    packed = pl.pallas_call(
        pack_kernel,
        name="pack",
        out_shape=jax.ShapeDtypeStruct((2 * tile + 16, channels), jnp.bfloat16),
        in_specs=[smem, vmem, vmem, vmem, vmem],
        out_specs=vmem,
    )(crop_length, pair_act, pair_mask, cotangent, in_gain.reshape(1, channels))
    everyone = gather_tree(packed, n_row, n_col)
    f32, bf16 = jnp.float32, jnp.bfloat16
    return pl.pallas_call(
        functools.partial(part_kernel, n_row, n_col),
        name="part",
        out_shape=(
            jax.ShapeDtypeStruct(pair_act.shape, bf16),
            jax.ShapeDtypeStruct(pair_act.shape, bf16),
            jax.ShapeDtypeStruct(weights.shape, f32),
        ),
        in_specs=[vmem] * (4 + n_row * n_col),
        out_specs=(vmem, vmem, vmem),
        scratch_shapes=[
            pltpu.VMEM((5, pairs, channels), f32),
            pltpu.VMEM((pairs, channels), f32),
            pltpu.VMEM((pairs, channels), f32),
            pltpu.VMEM((pairs, channels), f32),
            pltpu.VMEM((pairs, channels), f32),
            pltpu.VMEM((pairs, channels), bf16),
            pltpu.VMEM((2, pairs, channels), f32),
            pltpu.VMEM((pairs, channels), bf16),
            pltpu.VMEM((pairs, channels), f32),
            pltpu.VMEM((5, pairs, channels), bf16),
        ],
        compiler_params=pltpu.CompilerParams(vmem_limit_bytes=32 * 1024 * 1024),
    )(pair_act, weights, in_gain.reshape(1, channels), out_gain.reshape(1, channels), *everyone)


def body(n_row, n_col, pair_act, *others):
    tile_rows, tile_cols, channels = pair_act.shape
    pairs = tile_rows * n_row * tile_cols * n_col
    small = pairs * channels * 4 <= 1024 * 1024 and channels == 128
    square = n_row == n_col and tile_rows == SUB and tile_cols == SUB and n_col & (n_col - 1) == 0
    if small and square:
        return gathered_body(n_row, n_col, pair_act, *others)
    return spread_body(pair_act, *others)


def solution(mesh):
    return jax.shard_map(
        functools.partial(body, mesh.shape["row"], mesh.shape["col"]),
        mesh=mesh,
        in_specs=(
            P(("parts", "row"), "col", None),
            P(("parts", "row"), "col"),
            P("parts"),
            P(),
            P(),
            P(),
            P(("parts", "row"), "col", None),
        ),
        out_specs=(
            P(("parts", "row"), "col", None),
            P(("parts", "row"), "col", None),
            P("parts", None, None),
        ),
        check_vma=False,
    )
```

```python
import functools

import jax
import jax.numpy as jnp
from jax import lax
from jax.experimental import pallas as pl
from jax.experimental.pallas import tpu as pltpu
from jax.sharding import PartitionSpec as P

SUB = 8
EPS = 1e-05


def normalize(values):
    average = jnp.mean(values, axis=-1, keepdims=True)
    centered = values - average
    inverse = lax.rsqrt(jnp.mean(centered * centered, axis=-1, keepdims=True) + 1e-05)
    return (centered * inverse, inverse)


def norm_back(grad_hat, values_hat, inverse):
    first = jnp.mean(grad_hat, axis=-1, keepdims=True)
    second = jnp.mean(grad_hat * values_hat, axis=-1, keepdims=True)
    return (grad_hat - first - values_hat * second) * inverse


def gate_back(grad_act, proj_value, proj_gate, keep_mask):
    gate_sig = jax.nn.sigmoid(proj_gate)
    masked = grad_act * keep_mask
    grad_value = (masked * gate_sig).astype(jnp.bfloat16)
    grad_gate = (masked * proj_value * gate_sig * (1.0 - gate_sig)).astype(jnp.bfloat16)
    return (grad_value, grad_gate)


def spread_body(pair_act, pair_mask, crop_length, weights, in_gain, out_gain, cotangent):
    tile_rows, tile_cols, channels = pair_act.shape
    residues = tile_rows * lax.axis_size("row")
    row_pos = lax.axis_index("row") * tile_rows + jnp.arange(tile_rows, dtype=jnp.int32)
    col_pos = lax.axis_index("col") * tile_cols + jnp.arange(tile_cols, dtype=jnp.int32)
    row_in = (row_pos < crop_length[0]).astype(jnp.float32)
    col_in = (col_pos < crop_length[0]).astype(jnp.float32)
    keep_mask = (pair_mask.astype(jnp.float32) * row_in[:, None] * col_in[None, :])[:, :, None]
    z_hat, z_inverse = normalize(pair_act.astype(jnp.float32))
    normed = (z_hat * in_gain).astype(jnp.bfloat16)
    flat_norm = normed.reshape(tile_rows * tile_cols, channels)
    projections = jnp.einsum(
        "pc,scd->spd", flat_norm, weights[:5], preferred_element_type=jnp.float32
    )
    projections = projections.reshape(5, tile_rows, tile_cols, channels)
    left_act = (jax.nn.sigmoid(projections[1]) * projections[0] * keep_mask).astype(jnp.bfloat16)
    right_act = (jax.nn.sigmoid(projections[3]) * projections[2] * keep_mask).astype(jnp.bfloat16)
    partial_value = jnp.einsum(
        "ikh,jkh->ijh",
        left_act,
        lax.all_gather(right_act, "row", axis=0, tiled=True),
        preferred_element_type=jnp.float32,
    )
    tri_sum = lax.psum_scatter(
        partial_value.astype(jnp.bfloat16), "col", scatter_dimension=1, tiled=True
    ).astype(jnp.float32)
    x_hat, x_inverse = normalize(tri_sum)
    normed_out = (x_hat * out_gain).astype(jnp.bfloat16)
    flat_out = normed_out.reshape(tile_rows * tile_cols, channels)
    update_lin = jnp.dot(flat_out, weights[5], preferred_element_type=jnp.float32)
    update_lin = update_lin.reshape(tile_rows, tile_cols, channels)
    out_gate = jax.nn.sigmoid(projections[4])
    update = (out_gate * update_lin).astype(jnp.bfloat16)
    cot_value = cotangent.astype(jnp.float32)
    grad_lin = (cot_value * out_gate).astype(jnp.bfloat16)
    grad_gate_out = (cot_value * update_lin * out_gate * (1.0 - out_gate)).astype(jnp.bfloat16)
    flat_lin = grad_lin.reshape(tile_rows * tile_cols, channels)
    grad_norm_out = jnp.einsum(
        "pd,cd->pc", flat_lin, weights[5], preferred_element_type=jnp.float32
    )
    grad_norm_out = grad_norm_out.reshape(tile_rows, tile_cols, channels)
    grad_tri = norm_back(grad_norm_out * out_gain, x_hat, x_inverse).astype(jnp.bfloat16)
    grad_full = lax.all_gather(grad_tri, "col", axis=1, tiled=True)
    grad_slab = grad_full
    grad_left = jnp.einsum(
        "ijh,jkh->ikh",
        grad_slab,
        lax.all_gather(right_act, "row", axis=0, tiled=True),
        preferred_element_type=jnp.float32,
    )
    grad_slab = grad_full
    grad_right = lax.psum_scatter(
        jnp.einsum("ijh,ikh->jkh", grad_slab, left_act, preferred_element_type=jnp.float32).astype(
            jnp.bfloat16
        ),
        "row",
        scatter_dimension=0,
        tiled=True,
    ).astype(jnp.float32)
    grad_pa, grad_ga = gate_back(grad_left, projections[0], projections[1], keep_mask)
    grad_pb, grad_gb = gate_back(grad_right, projections[2], projections[3], keep_mask)
    grads = jnp.stack([grad_pa, grad_ga, grad_pb, grad_gb, grad_gate_out]).reshape(
        5, tile_rows * tile_cols, channels
    )
    grad_normed = jnp.einsum("spd,scd->pc", grads, weights[:5], preferred_element_type=jnp.float32)
    grad_normed = grad_normed.reshape(tile_rows, tile_cols, channels)
    pair_grad = norm_back(grad_normed * in_gain, z_hat, z_inverse).astype(jnp.bfloat16)
    local_in = jnp.einsum("pc,spd->scd", flat_norm, grads, preferred_element_type=jnp.float32)
    local_out = jnp.dot(flat_out.T, flat_lin, preferred_element_type=jnp.float32)
    local_grads = jnp.concatenate([local_in, local_out[None]], axis=0) / residues
    weight_grad = lax.psum(local_grads, ("row", "col"))
    return (update, pair_grad, weight_grad)


def pack_kernel(crop_ref, act_ref, mask_ref, cot_ref, gain_ref, out_ref):
    tile_rows, tile_cols, channels = act_ref.shape
    pairs = tile_rows * tile_cols
    z_hat, _ = normalize(act_ref[...].astype(jnp.float32).reshape(pairs, channels))
    out_ref[0:pairs] = (z_hat * gain_ref[...]).astype(jnp.bfloat16)
    out_ref[pairs : 2 * pairs] = cot_ref[...].reshape(pairs, channels)
    row_at = lax.axis_index("row") * tile_rows
    col_at = lax.axis_index("col") * tile_cols
    rows = row_at + lax.broadcasted_iota(jnp.int32, (tile_rows, tile_cols), 0)
    cols = col_at + lax.broadcasted_iota(jnp.int32, (tile_rows, tile_cols), 1)
    inside = (rows < crop_ref[0]) & (cols < crop_ref[0])
    keep = jnp.where(inside, mask_ref[...], 0).astype(jnp.float32)
    wide = jnp.concatenate([keep, jnp.zeros((tile_rows, channels - tile_cols), jnp.float32)], axis=1)
    tall = jnp.concatenate([wide, jnp.zeros((channels - tile_rows, channels), jnp.float32)], axis=0)
    flipped = tall.T
    extra = out_ref.shape[0] - 2 * pairs
    out_ref[2 * pairs :] = flipped[0:extra].astype(jnp.bfloat16)


def triangle(groups, vectors_at, factors_at, store_at):
    def block(a, _):
        def step(q, totals):
            totals = list(totals)
            vectors = vectors_at(q)
            factors = factors_at(a, q)
            for inner in range(SUB):
                rows = [vectors(g, inner) for g in range(groups)]
                for lane in range(SUB):
                    factor = factors(lane, inner)
                    for g in range(groups):
                        at = lane * groups + g
                        totals[at] = totals[at] + factor * rows[g]
            return tuple(totals)

        zero = jnp.zeros((SUB, 128), jnp.float32)
        totals = lax.fori_loop(0, groups, step, (zero,) * (SUB * groups))
        for g in range(groups):
            store_at(a, g, [totals[lane * groups + g] for lane in range(SUB)])
        return 0

    lax.fori_loop(0, groups, block, 0)


def part_kernel(
    n_row, n_col, counts, slot_of, act_ref, weights_ref, in_gain_ref, out_gain_ref, *refs,
):
    pieces = [ref.at[b] for ref, count in zip(refs, counts) for b in range(count)]
    part_refs(n_row, n_col, slot_of, act_ref, weights_ref, in_gain_ref, out_gain_ref, pieces, *refs[len(counts) :])


def part_refs(
    n_row, n_col, slot_of, act_ref, weights_ref, in_gain_ref, out_gain_ref, all_refs,
    update_ref, pair_grad_ref, weight_grad_ref,
    proj_ref, left_ref, right_ref, keep_ref, tri_ref, lin_ref, gate_ref, hat_ref, upd_ref, d_ref,
):
    tile_rows, tile_cols, channels = act_ref.shape
    tile = tile_rows * tile_cols
    residues = n_row * tile_rows
    pairs = residues * residues
    chunk = 4 * tile
    bf16, f32 = jnp.bfloat16, jnp.float32

    row_me, col_me = lax.axis_index("row"), lax.axis_index("col")

    def base(row, col):
        return pl.multiple_of(slot_of(row, col, row_me, col_me) * tile, tile)

    def spread(ref, row):
        return jnp.broadcast_to(ref[pl.ds(row, 1), :], (SUB, channels))

    def line(ref, row):
        return ref[pl.ds(pl.multiple_of(row, SUB), SUB), :]

    def lines(ref):
        def store(row, col, values):
            first = base(row, col)
            for lane in range(SUB):
                ref[pl.ds(pl.multiple_of(first + lane * SUB, SUB), SUB), :] = values[lane]
        return store

    def across(ref):
        def at(q):
            firsts = [base(q, g) for g in range(n_col)]
            return lambda g, inner: line(ref, firsts[g] + inner * SUB)
        return at

    def chunks():
        return [(at, slice(at, at + chunk)) for at in range(0, pairs, chunk)]

    def normed_rows(at):
        return jnp.concatenate([all_refs[b][0:tile] for b in range(at // tile, (at + chunk) // tile)], axis=0)

    def cot_rows(at):
        return jnp.concatenate([all_refs[b][tile : 2 * tile] for b in range(at // tile, (at + chunk) // tile)], axis=0)

    for at, rows in chunks():
        normed = normed_rows(at)
        for s in range(5):
            proj_ref[s, rows, :] = jnp.dot(normed, weights_ref[s], preferred_element_type=f32)
        for b in range(at // tile, (at + chunk) // tile):
            keep = all_refs[b][2 * tile : 2 * tile + 16, :].astype(f32)[0:tile_cols]
            for ii in range(tile_rows):
                spot = (b * tile_rows + ii) * tile_cols
                keep_ref[spot : spot + tile_cols, :] = jnp.broadcast_to(keep[:, ii : ii + 1], (tile_cols, channels))
        kept = keep_ref[rows, :]
        left = jax.nn.sigmoid(proj_ref[1, rows, :]) * proj_ref[0, rows, :] * kept
        right = jax.nn.sigmoid(proj_ref[3, rows, :]) * proj_ref[2, rows, :] * kept
        left_ref[rows, :] = left.astype(bf16).astype(f32)
        right_ref[rows, :] = right.astype(bf16).astype(f32)

    def flipped(q):
        firsts = [base(g, q) for g in range(n_row)]
        return lambda g, inner: right_ref[pl.ds(firsts[g] + inner, SUB, stride=SUB), :]

    def along(ref):
        def at(a, q):
            first = base(a, q)
            return lambda lane, inner: spread(ref, first + lane * SUB + inner)
        return at

    def down(ref):
        def at(a, q):
            first = base(q, a)
            return lambda lane, inner: spread(ref, first + inner * SUB + lane)
        return at

    triangle(n_row, flipped, along(left_ref), lines(tri_ref))

    out_gain = out_gain_ref[...]
    for at, rows in chunks():
        x_hat, inverse = normalize(tri_ref[rows, :])
        normed_out = (x_hat * out_gain).astype(bf16)
        hat_ref[rows, :] = normed_out
        lin = jnp.dot(normed_out, weights_ref[5], preferred_element_type=f32)
        out_gate = jax.nn.sigmoid(proj_ref[4, rows, :])
        cot = cot_rows(at).astype(f32)
        upd_ref[rows, :] = out_gate * lin
        grad_lin = (cot * out_gate).astype(bf16)
        lin_ref[rows, :] = grad_lin
        d_ref[4, rows, :] = (cot * lin * out_gate * (1.0 - out_gate)).astype(bf16)
        back = lax.dot_general(grad_lin, weights_ref[5], (((1,), (1,)), ((), ())), preferred_element_type=f32)
        tri_ref[rows, :] = norm_back(back * out_gain, x_hat, inverse).astype(bf16).astype(f32)

    triangle(n_row, across(right_ref), along(tri_ref), lines(gate_ref.at[0]))
    triangle(n_row, across(left_ref), down(tri_ref), lines(gate_ref.at[1]))

    for at, rows in chunks():
        kept = keep_ref[rows, :]
        for side in range(2):
            value, gate = gate_back(gate_ref[side, rows, :], proj_ref[2 * side, rows, :], proj_ref[2 * side + 1, rows, :], kept)
            d_ref[2 * side, rows, :] = value
            d_ref[2 * side + 1, rows, :] = gate

    normed_all = jnp.concatenate([ref[0:tile] for ref in all_refs], axis=0)
    for s in range(5):
        weight_grad_ref[s] = lax.dot_general(
            normed_all, d_ref[s], (((0,), (0,)), ((), ())), preferred_element_type=f32
        ) / residues
    weight_grad_ref[5] = lax.dot_general(
        hat_ref[...], lin_ref[...], (((0,), (0,)), ((), ())), preferred_element_type=f32
    ) / residues

    own = pl.ds(base(row_me, col_me), tile)
    update_ref[...] = upd_ref[own, :].astype(bf16).reshape(update_ref.shape)
    total = jnp.zeros((tile, channels), f32)
    for s in range(5):
        total = total + lax.dot_general(d_ref[s, own, :], weights_ref[s], (((1,), (1,)), ((), ())), preferred_element_type=f32)
    z_hat, z_inverse = normalize(act_ref[...].astype(f32).reshape(tile, channels))
    grad = norm_back(total * in_gain_ref[...], z_hat, z_inverse)
    pair_grad_ref[...] = grad.astype(bf16).reshape(pair_grad_ref.shape)


def gather(own, n_row, n_col):
    along = lax.all_gather(own, "row", axis=0)
    everyone = lax.all_gather(along, "col", axis=0, tiled=True)

    def slot_of(row, col, row_me, col_me):
        return col * n_row + row

    return [everyone], slot_of


def gathered_body(n_row, n_col, pair_act, pair_mask, crop_length, weights, in_gain, out_gain, cotangent):
    tile_rows, tile_cols, channels = pair_act.shape
    tile = tile_rows * tile_cols
    pairs = tile * n_row * n_col
    vmem = pl.BlockSpec(memory_space=pltpu.VMEM)
    smem = pl.BlockSpec(memory_space=pltpu.SMEM)
    packed = pl.pallas_call(
        pack_kernel,
        name="pack",
        out_shape=jax.ShapeDtypeStruct((2 * tile + 16, channels), jnp.bfloat16),
        in_specs=[smem, vmem, vmem, vmem, vmem],
        out_specs=vmem,
    )(crop_length, pair_act, pair_mask, cotangent, in_gain.reshape(1, channels))
    everyone, slot_of = gather(packed, n_row, n_col)
    counts = tuple(piece.shape[0] for piece in everyone)
    f32, bf16 = jnp.float32, jnp.bfloat16
    return pl.pallas_call(
        functools.partial(part_kernel, n_row, n_col, counts, slot_of),
        name="part",
        out_shape=(
            jax.ShapeDtypeStruct(pair_act.shape, bf16),
            jax.ShapeDtypeStruct(pair_act.shape, bf16),
            jax.ShapeDtypeStruct(weights.shape, f32),
        ),
        in_specs=[vmem] * (4 + len(counts)),
        out_specs=(vmem, vmem, vmem),
        scratch_shapes=[
            pltpu.VMEM((5, pairs, channels), f32),
            pltpu.VMEM((pairs, channels), f32),
            pltpu.VMEM((pairs, channels), f32),
            pltpu.VMEM((pairs, channels), f32),
            pltpu.VMEM((pairs, channels), f32),
            pltpu.VMEM((pairs, channels), bf16),
            pltpu.VMEM((2, pairs, channels), f32),
            pltpu.VMEM((pairs, channels), bf16),
            pltpu.VMEM((pairs, channels), f32),
            pltpu.VMEM((5, pairs, channels), bf16),
        ],
        compiler_params=pltpu.CompilerParams(vmem_limit_bytes=32 * 1024 * 1024),
    )(pair_act, weights, in_gain.reshape(1, channels), out_gain.reshape(1, channels), *everyone)


def body(n_row, n_col, pair_act, *others):
    tile_rows, tile_cols, channels = pair_act.shape
    pairs = tile_rows * n_row * tile_cols * n_col
    small = pairs * channels * 4 <= 1024 * 1024 and channels == 128
    square = n_row == n_col and tile_rows == SUB and tile_cols == SUB and n_col & (n_col - 1) == 0
    if small and square:
        return gathered_body(n_row, n_col, pair_act, *others)
    return spread_body(pair_act, *others)


def solution(mesh):
    return jax.shard_map(
        functools.partial(body, mesh.shape["row"], mesh.shape["col"]),
        mesh=mesh,
        in_specs=(
            P(("parts", "row"), "col", None),
            P(("parts", "row"), "col"),
            P("parts"),
            P(),
            P(),
            P(),
            P(("parts", "row"), "col", None),
        ),
        out_specs=(
            P(("parts", "row"), "col", None),
            P(("parts", "row"), "col", None),
            P("parts", None, None),
        ),
        check_vma=False,
    )
```

```python
import functools

import jax
import jax.numpy as jnp
from jax import lax
from jax.experimental import pallas as pl
from jax.experimental.pallas import tpu as pltpu
from jax.sharding import PartitionSpec as P

SUB = 8
EPS = 1e-05


def normalize(values):
    average = jnp.mean(values, axis=-1, keepdims=True)
    centered = values - average
    inverse = lax.rsqrt(jnp.mean(centered * centered, axis=-1, keepdims=True) + 1e-05)
    return (centered * inverse, inverse)


def norm_back(grad_hat, values_hat, inverse):
    first = jnp.mean(grad_hat, axis=-1, keepdims=True)
    second = jnp.mean(grad_hat * values_hat, axis=-1, keepdims=True)
    return (grad_hat - first - values_hat * second) * inverse


def gate_back(grad_act, proj_value, proj_gate, keep_mask):
    gate_sig = jax.nn.sigmoid(proj_gate)
    masked = grad_act * keep_mask
    grad_value = (masked * gate_sig).astype(jnp.bfloat16)
    grad_gate = (masked * proj_value * gate_sig * (1.0 - gate_sig)).astype(jnp.bfloat16)
    return (grad_value, grad_gate)


def spread_body(pair_act, pair_mask, crop_length, weights, in_gain, out_gain, cotangent):
    tile_rows, tile_cols, channels = pair_act.shape
    residues = tile_rows * lax.axis_size("row")
    row_pos = lax.axis_index("row") * tile_rows + jnp.arange(tile_rows, dtype=jnp.int32)
    col_pos = lax.axis_index("col") * tile_cols + jnp.arange(tile_cols, dtype=jnp.int32)
    row_in = (row_pos < crop_length[0]).astype(jnp.float32)
    col_in = (col_pos < crop_length[0]).astype(jnp.float32)
    keep_mask = (pair_mask.astype(jnp.float32) * row_in[:, None] * col_in[None, :])[:, :, None]
    z_hat, z_inverse = normalize(pair_act.astype(jnp.float32))
    normed = (z_hat * in_gain).astype(jnp.bfloat16)
    flat_norm = normed.reshape(tile_rows * tile_cols, channels)
    projections = jnp.einsum(
        "pc,scd->spd", flat_norm, weights[:5], preferred_element_type=jnp.float32
    )
    projections = projections.reshape(5, tile_rows, tile_cols, channels)
    left_act = (jax.nn.sigmoid(projections[1]) * projections[0] * keep_mask).astype(jnp.bfloat16)
    right_act = (jax.nn.sigmoid(projections[3]) * projections[2] * keep_mask).astype(jnp.bfloat16)
    partial_value = jnp.einsum(
        "ikh,jkh->ijh",
        left_act,
        lax.all_gather(right_act, "row", axis=0, tiled=True),
        preferred_element_type=jnp.float32,
    )
    tri_sum = lax.psum_scatter(
        partial_value.astype(jnp.bfloat16), "col", scatter_dimension=1, tiled=True
    ).astype(jnp.float32)
    x_hat, x_inverse = normalize(tri_sum)
    normed_out = (x_hat * out_gain).astype(jnp.bfloat16)
    flat_out = normed_out.reshape(tile_rows * tile_cols, channels)
    update_lin = jnp.dot(flat_out, weights[5], preferred_element_type=jnp.float32)
    update_lin = update_lin.reshape(tile_rows, tile_cols, channels)
    out_gate = jax.nn.sigmoid(projections[4])
    update = (out_gate * update_lin).astype(jnp.bfloat16)
    cot_value = cotangent.astype(jnp.float32)
    grad_lin = (cot_value * out_gate).astype(jnp.bfloat16)
    grad_gate_out = (cot_value * update_lin * out_gate * (1.0 - out_gate)).astype(jnp.bfloat16)
    flat_lin = grad_lin.reshape(tile_rows * tile_cols, channels)
    grad_norm_out = jnp.einsum(
        "pd,cd->pc", flat_lin, weights[5], preferred_element_type=jnp.float32
    )
    grad_norm_out = grad_norm_out.reshape(tile_rows, tile_cols, channels)
    grad_tri = norm_back(grad_norm_out * out_gain, x_hat, x_inverse).astype(jnp.bfloat16)
    grad_full = lax.all_gather(grad_tri, "col", axis=1, tiled=True)
    grad_slab = grad_full
    grad_left = jnp.einsum(
        "ijh,jkh->ikh",
        grad_slab,
        lax.all_gather(right_act, "row", axis=0, tiled=True),
        preferred_element_type=jnp.float32,
    )
    grad_slab = grad_full
    grad_right = lax.psum_scatter(
        jnp.einsum("ijh,ikh->jkh", grad_slab, left_act, preferred_element_type=jnp.float32).astype(
            jnp.bfloat16
        ),
        "row",
        scatter_dimension=0,
        tiled=True,
    ).astype(jnp.float32)
    grad_pa, grad_ga = gate_back(grad_left, projections[0], projections[1], keep_mask)
    grad_pb, grad_gb = gate_back(grad_right, projections[2], projections[3], keep_mask)
    grads = jnp.stack([grad_pa, grad_ga, grad_pb, grad_gb, grad_gate_out]).reshape(
        5, tile_rows * tile_cols, channels
    )
    grad_normed = jnp.einsum("spd,scd->pc", grads, weights[:5], preferred_element_type=jnp.float32)
    grad_normed = grad_normed.reshape(tile_rows, tile_cols, channels)
    pair_grad = norm_back(grad_normed * in_gain, z_hat, z_inverse).astype(jnp.bfloat16)
    local_in = jnp.einsum("pc,spd->scd", flat_norm, grads, preferred_element_type=jnp.float32)
    local_out = jnp.dot(flat_out.T, flat_lin, preferred_element_type=jnp.float32)
    local_grads = jnp.concatenate([local_in, local_out[None]], axis=0) / residues
    weight_grad = lax.psum(local_grads, ("row", "col"))
    return (update, pair_grad, weight_grad)


def pack_kernel(crop_ref, act_ref, mask_ref, cot_ref, gain_ref, out_ref):
    tile_rows, tile_cols, channels = act_ref.shape
    pairs = tile_rows * tile_cols
    z_hat, _ = normalize(act_ref[...].astype(jnp.float32).reshape(pairs, channels))
    out_ref[0:pairs] = (z_hat * gain_ref[...]).astype(jnp.bfloat16)
    out_ref[pairs : 2 * pairs] = cot_ref[...].reshape(pairs, channels)
    row_at = lax.axis_index("row") * tile_rows
    col_at = lax.axis_index("col") * tile_cols
    rows = row_at + lax.broadcasted_iota(jnp.int32, (tile_rows, tile_cols), 0)
    cols = col_at + lax.broadcasted_iota(jnp.int32, (tile_rows, tile_cols), 1)
    inside = (rows < crop_ref[0]) & (cols < crop_ref[0])
    keep = jnp.where(inside, mask_ref[...], 0).astype(jnp.float32)
    wide = jnp.concatenate([keep, jnp.zeros((tile_rows, channels - tile_cols), jnp.float32)], axis=1)
    tall = jnp.concatenate([wide, jnp.zeros((channels - tile_rows, channels), jnp.float32)], axis=0)
    flipped = tall.T
    extra = out_ref.shape[0] - 2 * pairs
    out_ref[2 * pairs :] = flipped[0:extra].astype(jnp.bfloat16)


def triangle(groups, vectors_at, factors_at, store_at):
    def block(a, _):
        def step(q, totals):
            totals = list(totals)
            vectors = vectors_at(q)
            factors = factors_at(a, q)
            for inner in range(SUB):
                rows = [vectors(g, inner) for g in range(groups)]
                for lane in range(SUB):
                    factor = factors(lane, inner)
                    for g in range(groups):
                        at = lane * groups + g
                        totals[at] = totals[at] + factor * rows[g]
            return tuple(totals)

        zero = jnp.zeros((SUB, 128), jnp.float32)
        totals = lax.fori_loop(0, groups, step, (zero,) * (SUB * groups))
        for g in range(groups):
            store_at(a, g, [totals[lane * groups + g] for lane in range(SUB)])
        return 0

    lax.fori_loop(0, groups, block, 0)


def part_kernel(
    n_row, n_col, counts, slot_of, act_ref, weights_ref, in_gain_ref, out_gain_ref, *refs,
):
    pieces = [ref.at[b] for ref, count in zip(refs, counts) for b in range(count)]
    part_refs(n_row, n_col, slot_of, act_ref, weights_ref, in_gain_ref, out_gain_ref, pieces, *refs[len(counts) :])


def part_refs(
    n_row, n_col, slot_of, act_ref, weights_ref, in_gain_ref, out_gain_ref, all_refs,
    update_ref, pair_grad_ref, weight_grad_ref,
    proj_ref, left_ref, right_ref, keep_ref, tri_ref, lin_ref, gate_ref, hat_ref, upd_ref, d_ref,
):
    tile_rows, tile_cols, channels = act_ref.shape
    tile = tile_rows * tile_cols
    residues = n_row * tile_rows
    pairs = residues * residues
    chunk = 4 * tile
    bf16, f32 = jnp.bfloat16, jnp.float32

    row_me, col_me = lax.axis_index("row"), lax.axis_index("col")

    def base(row, col):
        return pl.multiple_of(slot_of(row, col, row_me, col_me) * tile, tile)

    def spread(ref, row):
        return jnp.broadcast_to(ref[pl.ds(row, 1), :], (SUB, channels))

    def line(ref, row):
        return ref[pl.ds(pl.multiple_of(row, SUB), SUB), :]

    def lines(ref):
        def store(row, col, values):
            first = base(row, col)
            for lane in range(SUB):
                ref[pl.ds(pl.multiple_of(first + lane * SUB, SUB), SUB), :] = values[lane]
        return store

    def across(ref):
        def at(q):
            firsts = [base(q, g) for g in range(n_col)]
            return lambda g, inner: line(ref, firsts[g] + inner * SUB)
        return at

    def chunks():
        return [(at, slice(at, at + chunk)) for at in range(0, pairs, chunk)]

    def normed_rows(at):
        return jnp.concatenate([all_refs[b][0:tile] for b in range(at // tile, (at + chunk) // tile)], axis=0)

    def cot_rows(at):
        return jnp.concatenate([all_refs[b][tile : 2 * tile] for b in range(at // tile, (at + chunk) // tile)], axis=0)

    for at, rows in chunks():
        normed = normed_rows(at)
        for s in range(5):
            proj_ref[s, rows, :] = jnp.dot(normed, weights_ref[s], preferred_element_type=f32)
        for b in range(at // tile, (at + chunk) // tile):
            keep = all_refs[b][2 * tile : 2 * tile + 16, :].astype(f32)[0:tile_cols]
            for ii in range(tile_rows):
                spot = (b * tile_rows + ii) * tile_cols
                keep_ref[spot : spot + tile_cols, :] = jnp.broadcast_to(keep[:, ii : ii + 1], (tile_cols, channels))
        kept = keep_ref[rows, :]
        left = jax.nn.sigmoid(proj_ref[1, rows, :]) * proj_ref[0, rows, :] * kept
        right = jax.nn.sigmoid(proj_ref[3, rows, :]) * proj_ref[2, rows, :] * kept
        left_ref[rows, :] = left.astype(bf16).astype(f32)
        right_ref[rows, :] = right.astype(bf16).astype(f32)

    def flipped(q):
        firsts = [base(g, q) for g in range(n_row)]
        return lambda g, inner: right_ref[pl.ds(firsts[g] + inner, SUB, stride=SUB), :]

    def along(ref):
        def at(a, q):
            first = base(a, q)
            return lambda lane, inner: spread(ref, first + lane * SUB + inner)
        return at

    def down(ref):
        def at(a, q):
            first = base(q, a)
            return lambda lane, inner: spread(ref, first + inner * SUB + lane)
        return at

    triangle(n_row, flipped, along(left_ref), lines(tri_ref))

    out_gain = out_gain_ref[...]
    for at, rows in chunks():
        x_hat, inverse = normalize(tri_ref[rows, :])
        normed_out = (x_hat * out_gain).astype(bf16)
        hat_ref[rows, :] = normed_out
        lin = jnp.dot(normed_out, weights_ref[5], preferred_element_type=f32)
        out_gate = jax.nn.sigmoid(proj_ref[4, rows, :])
        cot = cot_rows(at).astype(f32)
        upd_ref[rows, :] = out_gate * lin
        grad_lin = (cot * out_gate).astype(bf16)
        lin_ref[rows, :] = grad_lin
        d_ref[4, rows, :] = (cot * lin * out_gate * (1.0 - out_gate)).astype(bf16)
        back = lax.dot_general(grad_lin, weights_ref[5], (((1,), (1,)), ((), ())), preferred_element_type=f32)
        tri_ref[rows, :] = norm_back(back * out_gain, x_hat, inverse).astype(bf16).astype(f32)

    triangle(n_row, across(right_ref), along(tri_ref), lines(gate_ref.at[0]))
    triangle(n_row, across(left_ref), down(tri_ref), lines(gate_ref.at[1]))

    for at, rows in chunks():
        kept = keep_ref[rows, :]
        for side in range(2):
            value, gate = gate_back(gate_ref[side, rows, :], proj_ref[2 * side, rows, :], proj_ref[2 * side + 1, rows, :], kept)
            d_ref[2 * side, rows, :] = value
            d_ref[2 * side + 1, rows, :] = gate

    normed_all = jnp.concatenate([ref[0:tile] for ref in all_refs], axis=0)
    for s in range(5):
        weight_grad_ref[s] = lax.dot_general(
            normed_all, d_ref[s], (((0,), (0,)), ((), ())), preferred_element_type=f32
        ) / residues
    weight_grad_ref[5] = lax.dot_general(
        hat_ref[...], lin_ref[...], (((0,), (0,)), ((), ())), preferred_element_type=f32
    ) / residues

    own = pl.ds(base(row_me, col_me), tile)
    update_ref[...] = upd_ref[own, :].astype(bf16).reshape(update_ref.shape)
    total = jnp.zeros((tile, channels), f32)
    for s in range(5):
        total = total + lax.dot_general(d_ref[s, own, :], weights_ref[s], (((1,), (1,)), ((), ())), preferred_element_type=f32)
    z_hat, z_inverse = normalize(act_ref[...].astype(f32).reshape(tile, channels))
    grad = norm_back(total * in_gain_ref[...], z_hat, z_inverse)
    pair_grad_ref[...] = grad.astype(bf16).reshape(pair_grad_ref.shape)


def gather(own, n_row, n_col):
    repeated = jnp.broadcast_to(own, (n_row * n_col,) + own.shape)
    everyone = lax.all_to_all(repeated, ("row", "col"), split_axis=0, concat_axis=0, tiled=True)

    def slot_of(row, col, row_me, col_me):
        return row * n_col + col

    return [everyone], slot_of


def gathered_body(n_row, n_col, pair_act, pair_mask, crop_length, weights, in_gain, out_gain, cotangent):
    tile_rows, tile_cols, channels = pair_act.shape
    tile = tile_rows * tile_cols
    pairs = tile * n_row * n_col
    vmem = pl.BlockSpec(memory_space=pltpu.VMEM)
    smem = pl.BlockSpec(memory_space=pltpu.SMEM)
    packed = pl.pallas_call(
        pack_kernel,
        name="pack",
        out_shape=jax.ShapeDtypeStruct((2 * tile + 16, channels), jnp.bfloat16),
        in_specs=[smem, vmem, vmem, vmem, vmem],
        out_specs=vmem,
    )(crop_length, pair_act, pair_mask, cotangent, in_gain.reshape(1, channels))
    everyone, slot_of = gather(packed, n_row, n_col)
    counts = tuple(piece.shape[0] for piece in everyone)
    f32, bf16 = jnp.float32, jnp.bfloat16
    return pl.pallas_call(
        functools.partial(part_kernel, n_row, n_col, counts, slot_of),
        name="part",
        out_shape=(
            jax.ShapeDtypeStruct(pair_act.shape, bf16),
            jax.ShapeDtypeStruct(pair_act.shape, bf16),
            jax.ShapeDtypeStruct(weights.shape, f32),
        ),
        in_specs=[vmem] * (4 + len(counts)),
        out_specs=(vmem, vmem, vmem),
        scratch_shapes=[
            pltpu.VMEM((5, pairs, channels), f32),
            pltpu.VMEM((pairs, channels), f32),
            pltpu.VMEM((pairs, channels), f32),
            pltpu.VMEM((pairs, channels), f32),
            pltpu.VMEM((pairs, channels), f32),
            pltpu.VMEM((pairs, channels), bf16),
            pltpu.VMEM((2, pairs, channels), f32),
            pltpu.VMEM((pairs, channels), bf16),
            pltpu.VMEM((pairs, channels), f32),
            pltpu.VMEM((5, pairs, channels), bf16),
        ],
        compiler_params=pltpu.CompilerParams(vmem_limit_bytes=32 * 1024 * 1024),
    )(pair_act, weights, in_gain.reshape(1, channels), out_gain.reshape(1, channels), *everyone)


def body(n_row, n_col, pair_act, *others):
    tile_rows, tile_cols, channels = pair_act.shape
    pairs = tile_rows * n_row * tile_cols * n_col
    small = pairs * channels * 4 <= 1024 * 1024 and channels == 128
    square = n_row == n_col and tile_rows == SUB and tile_cols == SUB and n_col & (n_col - 1) == 0
    if small and square:
        return gathered_body(n_row, n_col, pair_act, *others)
    return spread_body(pair_act, *others)


def solution(mesh):
    return jax.shard_map(
        functools.partial(body, mesh.shape["row"], mesh.shape["col"]),
        mesh=mesh,
        in_specs=(
            P(("parts", "row"), "col", None),
            P(("parts", "row"), "col"),
            P("parts"),
            P(),
            P(),
            P(),
            P(("parts", "row"), "col", None),
        ),
        out_specs=(
            P(("parts", "row"), "col", None),
            P(("parts", "row"), "col", None),
            P("parts", None, None),
        ),
        check_vma=False,
    )
```

```python
import functools

import jax
import jax.numpy as jnp
from jax import lax
from jax.experimental import pallas as pl
from jax.experimental.pallas import tpu as pltpu
from jax.sharding import PartitionSpec as P

SUB = 8
EPS = 1e-05


def normalize(values):
    average = jnp.mean(values, axis=-1, keepdims=True)
    centered = values - average
    inverse = lax.rsqrt(jnp.mean(centered * centered, axis=-1, keepdims=True) + 1e-05)
    return (centered * inverse, inverse)


def norm_back(grad_hat, values_hat, inverse):
    first = jnp.mean(grad_hat, axis=-1, keepdims=True)
    second = jnp.mean(grad_hat * values_hat, axis=-1, keepdims=True)
    return (grad_hat - first - values_hat * second) * inverse


def gate_back(grad_act, proj_value, proj_gate, keep_mask):
    gate_sig = jax.nn.sigmoid(proj_gate)
    masked = grad_act * keep_mask
    grad_value = (masked * gate_sig).astype(jnp.bfloat16)
    grad_gate = (masked * proj_value * gate_sig * (1.0 - gate_sig)).astype(jnp.bfloat16)
    return (grad_value, grad_gate)


def spread_body(pair_act, pair_mask, crop_length, weights, in_gain, out_gain, cotangent):
    tile_rows, tile_cols, channels = pair_act.shape
    residues = tile_rows * lax.axis_size("row")
    row_pos = lax.axis_index("row") * tile_rows + jnp.arange(tile_rows, dtype=jnp.int32)
    col_pos = lax.axis_index("col") * tile_cols + jnp.arange(tile_cols, dtype=jnp.int32)
    row_in = (row_pos < crop_length[0]).astype(jnp.float32)
    col_in = (col_pos < crop_length[0]).astype(jnp.float32)
    keep_mask = (pair_mask.astype(jnp.float32) * row_in[:, None] * col_in[None, :])[:, :, None]
    z_hat, z_inverse = normalize(pair_act.astype(jnp.float32))
    normed = (z_hat * in_gain).astype(jnp.bfloat16)
    flat_norm = normed.reshape(tile_rows * tile_cols, channels)
    projections = jnp.einsum(
        "pc,scd->spd", flat_norm, weights[:5], preferred_element_type=jnp.float32
    )
    projections = projections.reshape(5, tile_rows, tile_cols, channels)
    left_act = (jax.nn.sigmoid(projections[1]) * projections[0] * keep_mask).astype(jnp.bfloat16)
    right_act = (jax.nn.sigmoid(projections[3]) * projections[2] * keep_mask).astype(jnp.bfloat16)
    partial_value = jnp.einsum(
        "ikh,jkh->ijh",
        left_act,
        lax.all_gather(right_act, "row", axis=0, tiled=True),
        preferred_element_type=jnp.float32,
    )
    tri_sum = lax.psum_scatter(
        partial_value.astype(jnp.bfloat16), "col", scatter_dimension=1, tiled=True
    ).astype(jnp.float32)
    x_hat, x_inverse = normalize(tri_sum)
    normed_out = (x_hat * out_gain).astype(jnp.bfloat16)
    flat_out = normed_out.reshape(tile_rows * tile_cols, channels)
    update_lin = jnp.dot(flat_out, weights[5], preferred_element_type=jnp.float32)
    update_lin = update_lin.reshape(tile_rows, tile_cols, channels)
    out_gate = jax.nn.sigmoid(projections[4])
    update = (out_gate * update_lin).astype(jnp.bfloat16)
    cot_value = cotangent.astype(jnp.float32)
    grad_lin = (cot_value * out_gate).astype(jnp.bfloat16)
    grad_gate_out = (cot_value * update_lin * out_gate * (1.0 - out_gate)).astype(jnp.bfloat16)
    flat_lin = grad_lin.reshape(tile_rows * tile_cols, channels)
    grad_norm_out = jnp.einsum(
        "pd,cd->pc", flat_lin, weights[5], preferred_element_type=jnp.float32
    )
    grad_norm_out = grad_norm_out.reshape(tile_rows, tile_cols, channels)
    grad_tri = norm_back(grad_norm_out * out_gain, x_hat, x_inverse).astype(jnp.bfloat16)
    grad_full = lax.all_gather(grad_tri, "col", axis=1, tiled=True)
    grad_slab = grad_full
    grad_left = jnp.einsum(
        "ijh,jkh->ikh",
        grad_slab,
        lax.all_gather(right_act, "row", axis=0, tiled=True),
        preferred_element_type=jnp.float32,
    )
    grad_slab = grad_full
    grad_right = lax.psum_scatter(
        jnp.einsum("ijh,ikh->jkh", grad_slab, left_act, preferred_element_type=jnp.float32).astype(
            jnp.bfloat16
        ),
        "row",
        scatter_dimension=0,
        tiled=True,
    ).astype(jnp.float32)
    grad_pa, grad_ga = gate_back(grad_left, projections[0], projections[1], keep_mask)
    grad_pb, grad_gb = gate_back(grad_right, projections[2], projections[3], keep_mask)
    grads = jnp.stack([grad_pa, grad_ga, grad_pb, grad_gb, grad_gate_out]).reshape(
        5, tile_rows * tile_cols, channels
    )
    grad_normed = jnp.einsum("spd,scd->pc", grads, weights[:5], preferred_element_type=jnp.float32)
    grad_normed = grad_normed.reshape(tile_rows, tile_cols, channels)
    pair_grad = norm_back(grad_normed * in_gain, z_hat, z_inverse).astype(jnp.bfloat16)
    local_in = jnp.einsum("pc,spd->scd", flat_norm, grads, preferred_element_type=jnp.float32)
    local_out = jnp.dot(flat_out.T, flat_lin, preferred_element_type=jnp.float32)
    local_grads = jnp.concatenate([local_in, local_out[None]], axis=0) / residues
    weight_grad = lax.psum(local_grads, ("row", "col"))
    return (update, pair_grad, weight_grad)


def pack_kernel(crop_ref, act_ref, mask_ref, cot_ref, gain_ref, out_ref):
    tile_rows, tile_cols, channels = act_ref.shape
    pairs = tile_rows * tile_cols
    z_hat, _ = normalize(act_ref[...].astype(jnp.float32).reshape(pairs, channels))
    out_ref[0:pairs] = (z_hat * gain_ref[...]).astype(jnp.bfloat16)
    out_ref[pairs : 2 * pairs] = cot_ref[...].reshape(pairs, channels)
    row_at = lax.axis_index("row") * tile_rows
    col_at = lax.axis_index("col") * tile_cols
    rows = row_at + lax.broadcasted_iota(jnp.int32, (tile_rows, tile_cols), 0)
    cols = col_at + lax.broadcasted_iota(jnp.int32, (tile_rows, tile_cols), 1)
    inside = (rows < crop_ref[0]) & (cols < crop_ref[0])
    keep = jnp.where(inside, mask_ref[...], 0).astype(jnp.float32)
    wide = jnp.concatenate([keep, jnp.zeros((tile_rows, channels - tile_cols), jnp.float32)], axis=1)
    tall = jnp.concatenate([wide, jnp.zeros((channels - tile_rows, channels), jnp.float32)], axis=0)
    flipped = tall.T
    extra = out_ref.shape[0] - 2 * pairs
    out_ref[2 * pairs :] = flipped[0:extra].astype(jnp.bfloat16)


def triangle(groups, vectors_at, factors_at, store_at):
    def block(a, _):
        def step(q, totals):
            totals = list(totals)
            vectors = vectors_at(q)
            factors = factors_at(a, q)
            for inner in range(SUB):
                rows = [vectors(g, inner) for g in range(groups)]
                for lane in range(SUB):
                    factor = factors(lane, inner)
                    for g in range(groups):
                        at = lane * groups + g
                        totals[at] = totals[at] + factor * rows[g]
            return tuple(totals)

        zero = jnp.zeros((SUB, 128), jnp.float32)
        totals = lax.fori_loop(0, groups, step, (zero,) * (SUB * groups))
        for g in range(groups):
            store_at(a, g, [totals[lane * groups + g] for lane in range(SUB)])
        return 0

    lax.fori_loop(0, groups, block, 0)


def part_kernel(
    n_row, n_col, counts, owners, act_ref, weights_ref, in_gain_ref, out_gain_ref, *refs,
):
    pieces = [ref.at[b] for ref, count in zip(refs, counts) for b in range(count)]
    part_refs(n_row, n_col, owners, act_ref, weights_ref, in_gain_ref, out_gain_ref, pieces, *refs[len(counts) :])


def part_refs(
    n_row, n_col, owners, act_ref, weights_ref, in_gain_ref, out_gain_ref, all_refs,
    update_ref, pair_grad_ref, weight_grad_ref,
    proj_ref, left_ref, right_ref, keep_ref, tri_ref, lin_ref, gate_ref, hat_ref, upd_ref, d_ref, slot_ref,
):
    tile_rows, tile_cols, channels = act_ref.shape
    tile = tile_rows * tile_cols
    residues = n_row * tile_rows
    pairs = residues * residues
    chunk = 4 * tile
    bf16, f32 = jnp.bfloat16, jnp.float32

    row_me, col_me = lax.axis_index("row"), lax.axis_index("col")

    core_me = col_me % 2
    for slot, (near, far) in enumerate(owners):
        shift = [jnp.where(core_me == 0, a, b) for a, b in zip(near, far)]
        slot_ref[(row_me ^ shift[0]) * n_col + (col_me ^ shift[1])] = slot * tile

    def base(row, col):
        return pl.multiple_of(slot_ref[row * n_col + col], tile)

    def spread(ref, row):
        return jnp.broadcast_to(ref[pl.ds(row, 1), :], (SUB, channels))

    def line(ref, row):
        return ref[pl.ds(pl.multiple_of(row, SUB), SUB), :]

    def lines(ref):
        def store(row, col, values):
            first = base(row, col)
            for lane in range(SUB):
                ref[pl.ds(pl.multiple_of(first + lane * SUB, SUB), SUB), :] = values[lane]
        return store

    def across(ref):
        def at(q):
            firsts = [base(q, g) for g in range(n_col)]
            return lambda g, inner: line(ref, firsts[g] + inner * SUB)
        return at

    def chunks():
        return [(at, slice(at, at + chunk)) for at in range(0, pairs, chunk)]

    def normed_rows(at):
        return jnp.concatenate([all_refs[b][0:tile] for b in range(at // tile, (at + chunk) // tile)], axis=0)

    def cot_rows(at):
        return jnp.concatenate([all_refs[b][tile : 2 * tile] for b in range(at // tile, (at + chunk) // tile)], axis=0)

    for at, rows in chunks():
        normed = normed_rows(at)
        for s in range(5):
            proj_ref[s, rows, :] = jnp.dot(normed, weights_ref[s], preferred_element_type=f32)
        for b in range(at // tile, (at + chunk) // tile):
            keep = all_refs[b][2 * tile : 2 * tile + 16, :].astype(f32)[0:tile_cols]
            for ii in range(tile_rows):
                spot = (b * tile_rows + ii) * tile_cols
                keep_ref[spot : spot + tile_cols, :] = jnp.broadcast_to(keep[:, ii : ii + 1], (tile_cols, channels))
        kept = keep_ref[rows, :]
        left = jax.nn.sigmoid(proj_ref[1, rows, :]) * proj_ref[0, rows, :] * kept
        right = jax.nn.sigmoid(proj_ref[3, rows, :]) * proj_ref[2, rows, :] * kept
        left_ref[rows, :] = left.astype(bf16).astype(f32)
        right_ref[rows, :] = right.astype(bf16).astype(f32)

    def flipped(q):
        firsts = [base(g, q) for g in range(n_row)]
        return lambda g, inner: right_ref[pl.ds(firsts[g] + inner, SUB, stride=SUB), :]

    def along(ref):
        def at(a, q):
            first = base(a, q)
            return lambda lane, inner: spread(ref, first + lane * SUB + inner)
        return at

    def down(ref):
        def at(a, q):
            first = base(q, a)
            return lambda lane, inner: spread(ref, first + inner * SUB + lane)
        return at

    triangle(n_row, flipped, along(left_ref), lines(tri_ref))

    out_gain = out_gain_ref[...]
    for at, rows in chunks():
        x_hat, inverse = normalize(tri_ref[rows, :])
        normed_out = (x_hat * out_gain).astype(bf16)
        hat_ref[rows, :] = normed_out
        lin = jnp.dot(normed_out, weights_ref[5], preferred_element_type=f32)
        out_gate = jax.nn.sigmoid(proj_ref[4, rows, :])
        cot = cot_rows(at).astype(f32)
        upd_ref[rows, :] = out_gate * lin
        grad_lin = (cot * out_gate).astype(bf16)
        lin_ref[rows, :] = grad_lin
        d_ref[4, rows, :] = (cot * lin * out_gate * (1.0 - out_gate)).astype(bf16)
        back = lax.dot_general(grad_lin, weights_ref[5], (((1,), (1,)), ((), ())), preferred_element_type=f32)
        tri_ref[rows, :] = norm_back(back * out_gain, x_hat, inverse).astype(bf16).astype(f32)

    triangle(n_row, across(right_ref), along(tri_ref), lines(gate_ref.at[0]))
    triangle(n_row, across(left_ref), down(tri_ref), lines(gate_ref.at[1]))

    for at, rows in chunks():
        kept = keep_ref[rows, :]
        for side in range(2):
            value, gate = gate_back(gate_ref[side, rows, :], proj_ref[2 * side, rows, :], proj_ref[2 * side + 1, rows, :], kept)
            d_ref[2 * side, rows, :] = value
            d_ref[2 * side + 1, rows, :] = gate

    normed_all = jnp.concatenate([ref[0:tile] for ref in all_refs], axis=0)
    for s in range(5):
        weight_grad_ref[s] = lax.dot_general(
            normed_all, d_ref[s], (((0,), (0,)), ((), ())), preferred_element_type=f32
        ) / residues
    weight_grad_ref[5] = lax.dot_general(
        hat_ref[...], lin_ref[...], (((0,), (0,)), ((), ())), preferred_element_type=f32
    ) / residues

    own = slice(0, tile)
    update_ref[...] = upd_ref[own, :].astype(bf16).reshape(update_ref.shape)
    total = jnp.zeros((tile, channels), f32)
    for s in range(5):
        total = total + lax.dot_general(d_ref[s, own, :], weights_ref[s], (((1,), (1,)), ((), ())), preferred_element_type=f32)
    z_hat, z_inverse = normalize(act_ref[...].astype(f32).reshape(tile, channels))
    grad = norm_back(total * in_gain_ref[...], z_hat, z_inverse)
    pair_grad_ref[...] = grad.astype(bf16).reshape(pair_grad_ref.shape)


def flip_by(block, n_row, n_col, near, far):
    pairs = []
    for row in range(n_row):
        for col in range(n_col):
            shift = near if col % 2 == 0 else far
            pairs.append((row * n_col + col, (row ^ shift[0]) * n_col + (col ^ shift[1])))
    return lax.ppermute(block, ("row", "col"), pairs)


def gather(own, n_row, n_col):
    def other(block):
        return flip_by(block, n_row, n_col, (0, 1), (0, 1))

    both = jnp.stack([own, other(own)])
    chips = [(row, col) for row in range(n_row) for col in range(0, n_col, 2) if row + col > 0]
    chips.sort(key=lambda chip: (bin(chip[0]).count("1") + chip[1] // 2, chip))
    pieces = [both]
    owners = [((0, 0), (0, 0)), ((0, 1), (0, 1))]
    while len(chips) > 1:
        near, far = chips.pop(0), chips.pop(0)
        piece = flip_by(both, n_row, n_col, near, far)
        pieces += [piece, other(piece)]
        for a, b, core in ((near, far, 0), (near, far, 1), (far, near, 1), (far, near, 0)):
            owners.append(((a[0], a[1] ^ core), (b[0], b[1] ^ core)))
    for last in chips:
        piece = flip_by(own[None], n_row, n_col, last, last)
        pieces += [piece, other(piece)]
        owners += [(last, last), ((last[0], last[1] ^ 1),) * 2]
    return pieces, tuple(owners)


def gathered_body(n_row, n_col, pair_act, pair_mask, crop_length, weights, in_gain, out_gain, cotangent):
    tile_rows, tile_cols, channels = pair_act.shape
    tile = tile_rows * tile_cols
    pairs = tile * n_row * n_col
    vmem = pl.BlockSpec(memory_space=pltpu.VMEM)
    smem = pl.BlockSpec(memory_space=pltpu.SMEM)
    packed = pl.pallas_call(
        pack_kernel,
        name="pack",
        out_shape=jax.ShapeDtypeStruct((2 * tile + 16, channels), jnp.bfloat16),
        in_specs=[smem, vmem, vmem, vmem, vmem],
        out_specs=vmem,
        compiler_params=pltpu.CompilerParams(vmem_limit_bytes=2 * 1024 * 1024),
    )(crop_length, pair_act, pair_mask, cotangent, in_gain.reshape(1, channels))
    everyone, owners = gather(packed, n_row, n_col)
    counts = tuple(piece.shape[0] for piece in everyone)
    f32, bf16 = jnp.float32, jnp.bfloat16
    return pl.pallas_call(
        functools.partial(part_kernel, n_row, n_col, counts, owners),
        name="part",
        out_shape=(
            jax.ShapeDtypeStruct(pair_act.shape, bf16),
            jax.ShapeDtypeStruct(pair_act.shape, bf16),
            jax.ShapeDtypeStruct(weights.shape, f32),
        ),
        in_specs=[vmem] * (4 + len(counts)),
        out_specs=(vmem, vmem, vmem),
        scratch_shapes=[
            pltpu.VMEM((5, pairs, channels), f32),
            pltpu.VMEM((pairs, channels), f32),
            pltpu.VMEM((pairs, channels), f32),
            pltpu.VMEM((pairs, channels), f32),
            pltpu.VMEM((pairs, channels), f32),
            pltpu.VMEM((pairs, channels), bf16),
            pltpu.VMEM((2, pairs, channels), f32),
            pltpu.VMEM((pairs, channels), bf16),
            pltpu.VMEM((pairs, channels), f32),
            pltpu.VMEM((5, pairs, channels), bf16),
            pltpu.SMEM((n_row * n_col,), jnp.int32),
        ],
        compiler_params=pltpu.CompilerParams(vmem_limit_bytes=24 * 1024 * 1024),
    )(pair_act, weights, in_gain.reshape(1, channels), out_gain.reshape(1, channels), *everyone)


def body(n_row, n_col, pair_act, *others):
    tile_rows, tile_cols, channels = pair_act.shape
    pairs = tile_rows * n_row * tile_cols * n_col
    small = pairs * channels * 4 <= 1024 * 1024 and channels == 128
    square = n_row == n_col and tile_rows == SUB and tile_cols == SUB and n_col & (n_col - 1) == 0
    if small and square:
        return gathered_body(n_row, n_col, pair_act, *others)
    return spread_body(pair_act, *others)


def solution(mesh):
    return jax.shard_map(
        functools.partial(body, mesh.shape["row"], mesh.shape["col"]),
        mesh=mesh,
        in_specs=(
            P(("parts", "row"), "col", None),
            P(("parts", "row"), "col"),
            P("parts"),
            P(),
            P(),
            P(),
            P(("parts", "row"), "col", None),
        ),
        out_specs=(
            P(("parts", "row"), "col", None),
            P(("parts", "row"), "col", None),
            P("parts", None, None),
        ),
        check_vma=False,
    )
```

```python
import functools

import jax
import jax.numpy as jnp
from jax import lax
from jax.experimental import pallas as pl
from jax.experimental.pallas import tpu as pltpu
from jax.sharding import PartitionSpec as P

SUB = 8
EPS = 1e-05


def normalize(values):
    average = jnp.mean(values, axis=-1, keepdims=True)
    centered = values - average
    inverse = lax.rsqrt(jnp.mean(centered * centered, axis=-1, keepdims=True) + 1e-05)
    return (centered * inverse, inverse)


def norm_back(grad_hat, values_hat, inverse):
    first = jnp.mean(grad_hat, axis=-1, keepdims=True)
    second = jnp.mean(grad_hat * values_hat, axis=-1, keepdims=True)
    return (grad_hat - first - values_hat * second) * inverse


def gate_back(grad_act, proj_value, proj_gate, keep_mask):
    gate_sig = jax.nn.sigmoid(proj_gate)
    masked = grad_act * keep_mask
    grad_value = (masked * gate_sig).astype(jnp.bfloat16)
    grad_gate = (masked * proj_value * gate_sig * (1.0 - gate_sig)).astype(jnp.bfloat16)
    return (grad_value, grad_gate)


def spread_body(pair_act, pair_mask, crop_length, weights, in_gain, out_gain, cotangent):
    tile_rows, tile_cols, channels = pair_act.shape
    residues = tile_rows * lax.axis_size("row")
    row_pos = lax.axis_index("row") * tile_rows + jnp.arange(tile_rows, dtype=jnp.int32)
    col_pos = lax.axis_index("col") * tile_cols + jnp.arange(tile_cols, dtype=jnp.int32)
    row_in = (row_pos < crop_length[0]).astype(jnp.float32)
    col_in = (col_pos < crop_length[0]).astype(jnp.float32)
    keep_mask = (pair_mask.astype(jnp.float32) * row_in[:, None] * col_in[None, :])[:, :, None]
    z_hat, z_inverse = normalize(pair_act.astype(jnp.float32))
    normed = (z_hat * in_gain).astype(jnp.bfloat16)
    flat_norm = normed.reshape(tile_rows * tile_cols, channels)
    projections = jnp.einsum(
        "pc,scd->spd", flat_norm, weights[:5], preferred_element_type=jnp.float32
    )
    projections = projections.reshape(5, tile_rows, tile_cols, channels)
    left_act = (jax.nn.sigmoid(projections[1]) * projections[0] * keep_mask).astype(jnp.bfloat16)
    right_act = (jax.nn.sigmoid(projections[3]) * projections[2] * keep_mask).astype(jnp.bfloat16)
    partial_value = jnp.einsum(
        "ikh,jkh->ijh",
        left_act,
        lax.all_gather(right_act, "row", axis=0, tiled=True),
        preferred_element_type=jnp.float32,
    )
    tri_sum = lax.psum_scatter(
        partial_value.astype(jnp.bfloat16), "col", scatter_dimension=1, tiled=True
    ).astype(jnp.float32)
    x_hat, x_inverse = normalize(tri_sum)
    normed_out = (x_hat * out_gain).astype(jnp.bfloat16)
    flat_out = normed_out.reshape(tile_rows * tile_cols, channels)
    update_lin = jnp.dot(flat_out, weights[5], preferred_element_type=jnp.float32)
    update_lin = update_lin.reshape(tile_rows, tile_cols, channels)
    out_gate = jax.nn.sigmoid(projections[4])
    update = (out_gate * update_lin).astype(jnp.bfloat16)
    cot_value = cotangent.astype(jnp.float32)
    grad_lin = (cot_value * out_gate).astype(jnp.bfloat16)
    grad_gate_out = (cot_value * update_lin * out_gate * (1.0 - out_gate)).astype(jnp.bfloat16)
    flat_lin = grad_lin.reshape(tile_rows * tile_cols, channels)
    grad_norm_out = jnp.einsum(
        "pd,cd->pc", flat_lin, weights[5], preferred_element_type=jnp.float32
    )
    grad_norm_out = grad_norm_out.reshape(tile_rows, tile_cols, channels)
    grad_tri = norm_back(grad_norm_out * out_gain, x_hat, x_inverse).astype(jnp.bfloat16)
    grad_full = lax.all_gather(grad_tri, "col", axis=1, tiled=True)
    grad_slab = grad_full
    grad_left = jnp.einsum(
        "ijh,jkh->ikh",
        grad_slab,
        lax.all_gather(right_act, "row", axis=0, tiled=True),
        preferred_element_type=jnp.float32,
    )
    grad_slab = grad_full
    grad_right = lax.psum_scatter(
        jnp.einsum("ijh,ikh->jkh", grad_slab, left_act, preferred_element_type=jnp.float32).astype(
            jnp.bfloat16
        ),
        "row",
        scatter_dimension=0,
        tiled=True,
    ).astype(jnp.float32)
    grad_pa, grad_ga = gate_back(grad_left, projections[0], projections[1], keep_mask)
    grad_pb, grad_gb = gate_back(grad_right, projections[2], projections[3], keep_mask)
    grads = jnp.stack([grad_pa, grad_ga, grad_pb, grad_gb, grad_gate_out]).reshape(
        5, tile_rows * tile_cols, channels
    )
    grad_normed = jnp.einsum("spd,scd->pc", grads, weights[:5], preferred_element_type=jnp.float32)
    grad_normed = grad_normed.reshape(tile_rows, tile_cols, channels)
    pair_grad = norm_back(grad_normed * in_gain, z_hat, z_inverse).astype(jnp.bfloat16)
    local_in = jnp.einsum("pc,spd->scd", flat_norm, grads, preferred_element_type=jnp.float32)
    local_out = jnp.dot(flat_out.T, flat_lin, preferred_element_type=jnp.float32)
    local_grads = jnp.concatenate([local_in, local_out[None]], axis=0) / residues
    weight_grad = lax.psum(local_grads, ("row", "col"))
    return (update, pair_grad, weight_grad)


def pack_kernel(
    act_hbm, mask_hbm, cot_hbm, gain_hbm, out_ref, act_ref, mask_ref, gain_ref, sems
):
    tile_rows, tile_cols, channels = act_ref.shape
    pairs = tile_rows * tile_cols
    pack_copies = [
        pltpu.make_async_copy(act_hbm, act_ref, sems.at[0]),
        pltpu.make_async_copy(gain_hbm, gain_ref, sems.at[1]),
        pltpu.make_async_copy(mask_hbm, mask_ref, sems.at[2]),
        pltpu.make_async_copy(cot_hbm, out_ref.at[pairs : 2 * pairs], sems.at[3]),
    ]
    for copy in pack_copies:
        copy.start()
    for copy in pack_copies:
        copy.wait()
    z_hat, _ = normalize(act_ref[...].astype(jnp.float32).reshape(pairs, channels))
    out_ref[0:pairs] = (z_hat * gain_ref[...]).astype(jnp.bfloat16)
    keep = mask_ref[...].astype(jnp.float32)
    wide = jnp.concatenate([keep, jnp.zeros((tile_rows, channels - tile_cols), jnp.float32)], axis=1)
    tall = jnp.concatenate([wide, jnp.zeros((channels - tile_rows, channels), jnp.float32)], axis=0)
    flipped = tall.T
    extra = out_ref.shape[0] - 2 * pairs
    out_ref[2 * pairs :] = flipped[0:extra].astype(jnp.bfloat16)


def triangle(groups, vectors_at, factors_at, store_at):
    def block(a, _):
        def step(q, totals):
            totals = list(totals)
            vectors = vectors_at(q)
            factors = factors_at(a, q)
            for inner in range(SUB):
                rows = [vectors(g, inner) for g in range(groups)]
                for lane in range(SUB):
                    factor = factors(lane, inner)
                    for g in range(groups):
                        at = lane * groups + g
                        totals[at] = totals[at] + factor * rows[g]
            return tuple(totals)

        zero = jnp.zeros((SUB, 128), jnp.float32)
        totals = lax.fori_loop(0, groups, step, (zero,) * (SUB * groups))
        for g in range(groups):
            store_at(a, g, [totals[lane * groups + g] for lane in range(SUB)])
        return 0

    lax.fori_loop(0, groups, block, 0)


def part_kernel(
    n_row, n_col, counts, owners, crop_ref, act_ref, weights_ref, in_gain_ref, out_gain_ref, *refs,
):
    pieces = [ref.at[b] for ref, count in zip(refs, counts) for b in range(count)]
    part_refs(n_row, n_col, owners, crop_ref, act_ref, weights_ref, in_gain_ref, out_gain_ref, pieces, *refs[len(counts) :])


def part_refs(
    n_row, n_col, owners, crop_ref, act_ref, weights_ref, in_gain_ref, out_gain_ref, all_refs,
    update_ref, pair_grad_ref, weight_grad_ref,
    proj_ref, left_ref, right_ref, keep_ref, tri_ref, lin_ref, gate_ref, hat_ref, upd_ref, d_ref, slot_ref,
):
    tile_rows, tile_cols, channels = act_ref.shape
    tile = tile_rows * tile_cols
    residues = n_row * tile_rows
    pairs = residues * residues
    chunk = 4 * tile
    bf16, f32 = jnp.bfloat16, jnp.float32

    row_me, col_me = lax.axis_index("row"), lax.axis_index("col")

    core_me = col_me % 2
    crop = crop_ref[0]
    spots = []
    for slot, (near, far) in enumerate(owners):
        shift = [jnp.where(core_me == 0, a, b) for a, b in zip(near, far)]
        spots.append((row_me ^ shift[0], col_me ^ shift[1]))
        slot_ref[spots[slot][0] * n_col + spots[slot][1]] = slot * tile
    col_offset = lax.broadcasted_iota(jnp.int32, (tile_cols, channels), 0)
    row_offset = lax.broadcasted_iota(jnp.int32, (tile_cols, channels), 1)

    def base(row, col):
        return pl.multiple_of(slot_ref[row * n_col + col], tile)

    def spread(ref, row):
        return jnp.broadcast_to(ref[pl.ds(row, 1), :], (SUB, channels))

    def line(ref, row):
        return ref[pl.ds(pl.multiple_of(row, SUB), SUB), :]

    def lines(ref):
        def store(row, col, values):
            first = base(row, col)
            for lane in range(SUB):
                ref[pl.ds(pl.multiple_of(first + lane * SUB, SUB), SUB), :] = values[lane]
        return store

    def across(ref):
        def at(q):
            firsts = [base(q, g) for g in range(n_col)]
            return lambda g, inner: line(ref, firsts[g] + inner * SUB)
        return at

    def chunks():
        return [(at, slice(at, at + chunk)) for at in range(0, pairs, chunk)]

    def normed_rows(at):
        return jnp.concatenate([all_refs[b][0:tile] for b in range(at // tile, (at + chunk) // tile)], axis=0)

    def cot_rows(at):
        return jnp.concatenate([all_refs[b][tile : 2 * tile] for b in range(at // tile, (at + chunk) // tile)], axis=0)

    for at, rows in chunks():
        normed = normed_rows(at)
        for s in range(5):
            proj_ref[s, rows, :] = jnp.dot(normed, weights_ref[s], preferred_element_type=f32)
        for b in range(at // tile, (at + chunk) // tile):
            keep = all_refs[b][2 * tile : 2 * tile + 16, :].astype(f32)[0:tile_cols]
            rows_in = row_offset < crop - spots[b][0] * tile_rows
            cols_in = col_offset < crop - spots[b][1] * tile_cols
            keep = jnp.where(rows_in & cols_in, keep, 0.0)
            for ii in range(tile_rows):
                spot = (b * tile_rows + ii) * tile_cols
                keep_ref[spot : spot + tile_cols, :] = jnp.broadcast_to(keep[:, ii : ii + 1], (tile_cols, channels))
        kept = keep_ref[rows, :]
        left = jax.nn.sigmoid(proj_ref[1, rows, :]) * proj_ref[0, rows, :] * kept
        right = jax.nn.sigmoid(proj_ref[3, rows, :]) * proj_ref[2, rows, :] * kept
        left_ref[rows, :] = left.astype(bf16).astype(f32)
        right_ref[rows, :] = right.astype(bf16).astype(f32)

    def flipped(q):
        firsts = [base(g, q) for g in range(n_row)]
        return lambda g, inner: right_ref[pl.ds(firsts[g] + inner, SUB, stride=SUB), :]

    def along(ref):
        def at(a, q):
            first = base(a, q)
            return lambda lane, inner: spread(ref, first + lane * SUB + inner)
        return at

    def down(ref):
        def at(a, q):
            first = base(q, a)
            return lambda lane, inner: spread(ref, first + inner * SUB + lane)
        return at

    triangle(n_row, flipped, along(left_ref), lines(tri_ref))

    out_gain = out_gain_ref[...]
    for at, rows in chunks():
        x_hat, inverse = normalize(tri_ref[rows, :])
        normed_out = (x_hat * out_gain).astype(bf16)
        hat_ref[rows, :] = normed_out
        lin = jnp.dot(normed_out, weights_ref[5], preferred_element_type=f32)
        out_gate = jax.nn.sigmoid(proj_ref[4, rows, :])
        cot = cot_rows(at).astype(f32)
        upd_ref[rows, :] = out_gate * lin
        grad_lin = (cot * out_gate).astype(bf16)
        lin_ref[rows, :] = grad_lin
        d_ref[4, rows, :] = (cot * lin * out_gate * (1.0 - out_gate)).astype(bf16)
        back = lax.dot_general(grad_lin, weights_ref[5], (((1,), (1,)), ((), ())), preferred_element_type=f32)
        tri_ref[rows, :] = norm_back(back * out_gain, x_hat, inverse).astype(bf16).astype(f32)

    triangle(n_row, across(right_ref), along(tri_ref), lines(gate_ref.at[0]))
    triangle(n_row, across(left_ref), down(tri_ref), lines(gate_ref.at[1]))

    for at, rows in chunks():
        kept = keep_ref[rows, :]
        for side in range(2):
            value, gate = gate_back(gate_ref[side, rows, :], proj_ref[2 * side, rows, :], proj_ref[2 * side + 1, rows, :], kept)
            d_ref[2 * side, rows, :] = value
            d_ref[2 * side + 1, rows, :] = gate

    normed_all = jnp.concatenate([ref[0:tile] for ref in all_refs], axis=0)
    for s in range(5):
        weight_grad_ref[s] = lax.dot_general(
            normed_all, d_ref[s], (((0,), (0,)), ((), ())), preferred_element_type=f32
        ) / residues
    weight_grad_ref[5] = lax.dot_general(
        hat_ref[...], lin_ref[...], (((0,), (0,)), ((), ())), preferred_element_type=f32
    ) / residues

    own = slice(0, tile)
    update_ref[...] = upd_ref[own, :].astype(bf16).reshape(update_ref.shape)
    total = jnp.zeros((tile, channels), f32)
    for s in range(5):
        total = total + lax.dot_general(d_ref[s, own, :], weights_ref[s], (((1,), (1,)), ((), ())), preferred_element_type=f32)
    z_hat, z_inverse = normalize(act_ref[...].astype(f32).reshape(tile, channels))
    grad = norm_back(total * in_gain_ref[...], z_hat, z_inverse)
    pair_grad_ref[...] = grad.astype(bf16).reshape(pair_grad_ref.shape)


def flip_by(block, n_row, n_col, near, far):
    pairs = []
    for row in range(n_row):
        for col in range(n_col):
            shift = near if col % 2 == 0 else far
            pairs.append((row * n_col + col, (row ^ shift[0]) * n_col + (col ^ shift[1])))
    return lax.ppermute(block, ("row", "col"), pairs)


def gather(own, n_row, n_col):
    def other(block):
        return flip_by(block, n_row, n_col, (0, 1), (0, 1))

    both = jnp.stack([own, other(own)])
    chips = [(row, col) for row in range(n_row) for col in range(0, n_col, 2) if row + col > 0]
    chips.sort(key=lambda chip: (bin(chip[0]).count("1") + chip[1] // 2, chip))
    pieces = [both]
    owners = [((0, 0), (0, 0)), ((0, 1), (0, 1))]
    while len(chips) > 1:
        near, far = chips.pop(0), chips.pop(0)
        piece = flip_by(both, n_row, n_col, near, far)
        pieces += [piece, other(piece)]
        for a, b, core in ((near, far, 0), (near, far, 1), (far, near, 1), (far, near, 0)):
            owners.append(((a[0], a[1] ^ core), (b[0], b[1] ^ core)))
    for last in chips:
        piece = flip_by(own[None], n_row, n_col, last, last)
        pieces += [piece, other(piece)]
        owners += [(last, last), ((last[0], last[1] ^ 1),) * 2]
    return pieces, tuple(owners)


def gathered_body(n_row, n_col, pair_act, pair_mask, crop_length, weights, in_gain, out_gain, cotangent):
    tile_rows, tile_cols, channels = pair_act.shape
    tile = tile_rows * tile_cols
    pairs = tile * n_row * n_col
    vmem = pl.BlockSpec(memory_space=pltpu.VMEM)
    smem = pl.BlockSpec(memory_space=pltpu.SMEM)
    hbm = pl.BlockSpec(memory_space=pltpu.HBM)
    packed = pl.pallas_call(
        pack_kernel,
        name="pack",
        out_shape=jax.ShapeDtypeStruct((2 * tile + 16, channels), jnp.bfloat16),
        in_specs=[hbm] * 4,
        out_specs=vmem,
        scratch_shapes=[
            pltpu.VMEM(pair_act.shape, pair_act.dtype),
            pltpu.VMEM(pair_mask.shape, jnp.int32),
            pltpu.VMEM((1, channels), jnp.float32),
            pltpu.SemaphoreType.DMA((4,)),
        ],
        compiler_params=pltpu.CompilerParams(vmem_limit_bytes=60 * 1024 * 1024),
    )(pair_act, pair_mask, cotangent.reshape(tile, channels), in_gain.reshape(1, channels))
    crop_length, packed = lax.optimization_barrier((crop_length, packed))
    everyone, owners = gather(packed, n_row, n_col)
    counts = tuple(piece.shape[0] for piece in everyone)
    f32, bf16 = jnp.float32, jnp.bfloat16
    return pl.pallas_call(
        functools.partial(part_kernel, n_row, n_col, counts, owners),
        name="part",
        out_shape=(
            jax.ShapeDtypeStruct(pair_act.shape, bf16),
            jax.ShapeDtypeStruct(pair_act.shape, bf16),
            jax.ShapeDtypeStruct(weights.shape, f32),
        ),
        in_specs=[smem] + [vmem] * (4 + len(counts)),
        out_specs=(vmem, vmem, vmem),
        scratch_shapes=[
            pltpu.VMEM((5, pairs, channels), f32),
            pltpu.VMEM((pairs, channels), f32),
            pltpu.VMEM((pairs, channels), f32),
            pltpu.VMEM((pairs, channels), f32),
            pltpu.VMEM((pairs, channels), f32),
            pltpu.VMEM((pairs, channels), bf16),
            pltpu.VMEM((2, pairs, channels), f32),
            pltpu.VMEM((pairs, channels), bf16),
            pltpu.VMEM((pairs, channels), f32),
            pltpu.VMEM((5, pairs, channels), bf16),
            pltpu.SMEM((n_row * n_col,), jnp.int32),
        ],
        compiler_params=pltpu.CompilerParams(vmem_limit_bytes=24 * 1024 * 1024),
    )(crop_length, pair_act, weights, in_gain.reshape(1, channels), out_gain.reshape(1, channels), *everyone)


def body(n_row, n_col, pair_act, *others):
    tile_rows, tile_cols, channels = pair_act.shape
    pairs = tile_rows * n_row * tile_cols * n_col
    small = pairs * channels * 4 <= 1024 * 1024 and channels == 128
    square = n_row == n_col and tile_rows == SUB and tile_cols == SUB and n_col & (n_col - 1) == 0
    if small and square:
        return gathered_body(n_row, n_col, pair_act, *others)
    return spread_body(pair_act, *others)


def solution(mesh):
    return jax.shard_map(
        functools.partial(body, mesh.shape["row"], mesh.shape["col"]),
        mesh=mesh,
        in_specs=(
            P(("parts", "row"), "col", None),
            P(("parts", "row"), "col"),
            P("parts"),
            P(),
            P(),
            P(),
            P(("parts", "row"), "col", None),
        ),
        out_specs=(
            P(("parts", "row"), "col", None),
            P(("parts", "row"), "col", None),
            P("parts", None, None),
        ),
        check_vma=False,
    )
```

```python
import functools

import jax
import jax.numpy as jnp
from jax import lax
from jax.experimental import pallas as pl
from jax.experimental.pallas import tpu as pltpu
from jax.sharding import PartitionSpec as P

SUB = 8
EPS = 1e-05


def normalize(values):
    average = jnp.mean(values, axis=-1, keepdims=True)
    centered = values - average
    inverse = lax.rsqrt(jnp.mean(centered * centered, axis=-1, keepdims=True) + 1e-05)
    return (centered * inverse, inverse)


def norm_back(grad_hat, values_hat, inverse):
    first = jnp.mean(grad_hat, axis=-1, keepdims=True)
    second = jnp.mean(grad_hat * values_hat, axis=-1, keepdims=True)
    return (grad_hat - first - values_hat * second) * inverse


def gate_back(grad_act, proj_value, proj_gate, keep_mask):
    gate_sig = jax.nn.sigmoid(proj_gate)
    masked = grad_act * keep_mask
    grad_value = (masked * gate_sig).astype(jnp.bfloat16)
    grad_gate = (masked * proj_value * gate_sig * (1.0 - gate_sig)).astype(jnp.bfloat16)
    return (grad_value, grad_gate)


def spread_body(pair_act, pair_mask, crop_length, weights, in_gain, out_gain, cotangent):
    tile_rows, tile_cols, channels = pair_act.shape
    residues = tile_rows * lax.axis_size("row")
    row_pos = lax.axis_index("row") * tile_rows + jnp.arange(tile_rows, dtype=jnp.int32)
    col_pos = lax.axis_index("col") * tile_cols + jnp.arange(tile_cols, dtype=jnp.int32)
    row_in = (row_pos < crop_length[0]).astype(jnp.float32)
    col_in = (col_pos < crop_length[0]).astype(jnp.float32)
    keep_mask = (pair_mask.astype(jnp.float32) * row_in[:, None] * col_in[None, :])[:, :, None]
    z_hat, z_inverse = normalize(pair_act.astype(jnp.float32))
    normed = (z_hat * in_gain).astype(jnp.bfloat16)
    flat_norm = normed.reshape(tile_rows * tile_cols, channels)
    projections = jnp.einsum(
        "pc,scd->spd", flat_norm, weights[:5], preferred_element_type=jnp.float32
    )
    projections = projections.reshape(5, tile_rows, tile_cols, channels)
    left_act = (jax.nn.sigmoid(projections[1]) * projections[0] * keep_mask).astype(jnp.bfloat16)
    right_act = (jax.nn.sigmoid(projections[3]) * projections[2] * keep_mask).astype(jnp.bfloat16)
    partial_value = jnp.einsum(
        "ikh,jkh->ijh",
        left_act,
        lax.all_gather(right_act, "row", axis=0, tiled=True),
        preferred_element_type=jnp.float32,
    )
    tri_sum = lax.psum_scatter(
        partial_value.astype(jnp.bfloat16), "col", scatter_dimension=1, tiled=True
    ).astype(jnp.float32)
    x_hat, x_inverse = normalize(tri_sum)
    normed_out = (x_hat * out_gain).astype(jnp.bfloat16)
    flat_out = normed_out.reshape(tile_rows * tile_cols, channels)
    update_lin = jnp.dot(flat_out, weights[5], preferred_element_type=jnp.float32)
    update_lin = update_lin.reshape(tile_rows, tile_cols, channels)
    out_gate = jax.nn.sigmoid(projections[4])
    update = (out_gate * update_lin).astype(jnp.bfloat16)
    cot_value = cotangent.astype(jnp.float32)
    grad_lin = (cot_value * out_gate).astype(jnp.bfloat16)
    grad_gate_out = (cot_value * update_lin * out_gate * (1.0 - out_gate)).astype(jnp.bfloat16)
    flat_lin = grad_lin.reshape(tile_rows * tile_cols, channels)
    grad_norm_out = jnp.einsum(
        "pd,cd->pc", flat_lin, weights[5], preferred_element_type=jnp.float32
    )
    grad_norm_out = grad_norm_out.reshape(tile_rows, tile_cols, channels)
    grad_tri = norm_back(grad_norm_out * out_gain, x_hat, x_inverse).astype(jnp.bfloat16)
    grad_full = lax.all_gather(grad_tri, "col", axis=1, tiled=True)
    grad_slab = grad_full
    grad_left = jnp.einsum(
        "ijh,jkh->ikh",
        grad_slab,
        lax.all_gather(right_act, "row", axis=0, tiled=True),
        preferred_element_type=jnp.float32,
    )
    grad_slab = grad_full
    grad_right = lax.psum_scatter(
        jnp.einsum("ijh,ikh->jkh", grad_slab, left_act, preferred_element_type=jnp.float32).astype(
            jnp.bfloat16
        ),
        "row",
        scatter_dimension=0,
        tiled=True,
    ).astype(jnp.float32)
    grad_pa, grad_ga = gate_back(grad_left, projections[0], projections[1], keep_mask)
    grad_pb, grad_gb = gate_back(grad_right, projections[2], projections[3], keep_mask)
    grads = jnp.stack([grad_pa, grad_ga, grad_pb, grad_gb, grad_gate_out]).reshape(
        5, tile_rows * tile_cols, channels
    )
    grad_normed = jnp.einsum("spd,scd->pc", grads, weights[:5], preferred_element_type=jnp.float32)
    grad_normed = grad_normed.reshape(tile_rows, tile_cols, channels)
    pair_grad = norm_back(grad_normed * in_gain, z_hat, z_inverse).astype(jnp.bfloat16)
    local_in = jnp.einsum("pc,spd->scd", flat_norm, grads, preferred_element_type=jnp.float32)
    local_out = jnp.dot(flat_out.T, flat_lin, preferred_element_type=jnp.float32)
    local_grads = jnp.concatenate([local_in, local_out[None]], axis=0) / residues
    weight_grad = lax.psum(local_grads, ("row", "col"))
    return (update, pair_grad, weight_grad)


def pack_kernel(
    act_hbm, mask_hbm, cot_hbm, gain_hbm, out_ref, act_ref, mask_ref, gain_ref, sems
):
    tile_rows, tile_cols, channels = act_ref.shape
    pairs = tile_rows * tile_cols
    pack_copies = [
        pltpu.make_async_copy(act_hbm, act_ref, sems.at[0]),
        pltpu.make_async_copy(gain_hbm, gain_ref, sems.at[1]),
        pltpu.make_async_copy(mask_hbm, mask_ref, sems.at[2]),
        pltpu.make_async_copy(cot_hbm, out_ref.at[pairs : 2 * pairs], sems.at[3]),
    ]
    for copy in pack_copies:
        copy.start()
    for copy in pack_copies:
        copy.wait()
    z_hat, _ = normalize(act_ref[...].astype(jnp.float32).reshape(pairs, channels))
    out_ref[0:pairs] = (z_hat * gain_ref[...]).astype(jnp.bfloat16)
    keep = mask_ref[...].astype(jnp.float32)
    wide = jnp.concatenate([keep, jnp.zeros((tile_rows, channels - tile_cols), jnp.float32)], axis=1)
    tall = jnp.concatenate([wide, jnp.zeros((channels - tile_rows, channels), jnp.float32)], axis=0)
    flipped = tall.T
    extra = out_ref.shape[0] - 2 * pairs
    out_ref[2 * pairs :] = flipped[0:extra].astype(jnp.bfloat16)


def triangle(groups, vectors_at, factors_at, store_at):
    def block(a, _):
        def step(q, totals):
            totals = list(totals)
            vectors = vectors_at(q)
            factors = factors_at(a, q)
            for inner in range(SUB):
                rows = [vectors(g, inner) for g in range(groups)]
                for lane in range(SUB):
                    factor = factors(lane, inner)
                    for g in range(groups):
                        at = lane * groups + g
                        totals[at] = totals[at] + factor * rows[g]
            return tuple(totals)

        zero = jnp.zeros((SUB, 128), jnp.float32)
        totals = lax.fori_loop(0, groups, step, (zero,) * (SUB * groups))
        for g in range(groups):
            store_at(a, g, [totals[lane * groups + g] for lane in range(SUB)])
        return 0

    lax.fori_loop(0, groups, block, 0)


def part_kernel(
    n_row, n_col, counts, owners, crop_ref, act_ref, weights_ref, in_gain_ref, out_gain_ref, *refs,
):
    pieces = [ref.at[b] for ref, count in zip(refs, counts) for b in range(count)]
    part_refs(n_row, n_col, owners, crop_ref, act_ref, weights_ref, in_gain_ref, out_gain_ref, pieces, *refs[len(counts) :])


def part_refs(
    n_row, n_col, owners, crop_ref, act_ref, weights_ref, in_gain_ref, out_gain_ref, all_refs,
    update_ref, pair_grad_ref, weight_grad_ref,
    proj_ref, left_ref, right_ref, keep_ref, tri_ref, lin_ref, gate_ref, hat_ref, upd_ref, d_ref, slot_ref,
):
    tile_rows, tile_cols, channels = act_ref.shape
    tile = tile_rows * tile_cols
    residues = n_row * tile_rows
    pairs = residues * residues
    chunk = 4 * tile
    bf16, f32 = jnp.bfloat16, jnp.float32

    row_me, col_me = lax.axis_index("row"), lax.axis_index("col")

    core_me = col_me % 2
    crop = crop_ref[0]
    spots = []
    for slot, (near, far) in enumerate(owners):
        shift = [jnp.where(core_me == 0, a, b) for a, b in zip(near, far)]
        spots.append((row_me ^ shift[0], col_me ^ shift[1]))
        slot_ref[spots[slot][0] * n_col + spots[slot][1]] = slot * tile
    col_offset = lax.broadcasted_iota(jnp.int32, (tile_cols, channels), 0)
    row_offset = lax.broadcasted_iota(jnp.int32, (tile_cols, channels), 1)

    def base(row, col):
        return pl.multiple_of(slot_ref[row * n_col + col], tile)

    def spread(ref, row):
        return jnp.broadcast_to(ref[pl.ds(row, 1), :], (SUB, channels))

    def line(ref, row):
        return ref[pl.ds(pl.multiple_of(row, SUB), SUB), :]

    def lines(ref):
        def store(row, col, values):
            first = base(row, col)
            for lane in range(SUB):
                ref[pl.ds(pl.multiple_of(first + lane * SUB, SUB), SUB), :] = values[lane]
        return store

    def across(ref):
        def at(q):
            firsts = [base(q, g) for g in range(n_col)]
            return lambda g, inner: line(ref, firsts[g] + inner * SUB)
        return at

    def chunks():
        return [(at, slice(at, at + chunk)) for at in range(0, pairs, chunk)]

    def normed_rows(at):
        return jnp.concatenate([all_refs[b][0:tile] for b in range(at // tile, (at + chunk) // tile)], axis=0)

    def cot_rows(at):
        return jnp.concatenate([all_refs[b][tile : 2 * tile] for b in range(at // tile, (at + chunk) // tile)], axis=0)

    for at, rows in chunks():
        normed = normed_rows(at)
        for s in range(5):
            proj_ref[s, rows, :] = jnp.dot(normed, weights_ref[s], preferred_element_type=f32)
        for b in range(at // tile, (at + chunk) // tile):
            keep = all_refs[b][2 * tile : 2 * tile + 16, :].astype(f32)[0:tile_cols]
            rows_in = row_offset < crop - spots[b][0] * tile_rows
            cols_in = col_offset < crop - spots[b][1] * tile_cols
            keep = jnp.where(rows_in & cols_in, keep, 0.0)
            for ii in range(tile_rows):
                spot = (b * tile_rows + ii) * tile_cols
                keep_ref[spot : spot + tile_cols, :] = jnp.broadcast_to(keep[:, ii : ii + 1], (tile_cols, channels))
        kept = keep_ref[rows, :]
        left = jax.nn.sigmoid(proj_ref[1, rows, :]) * proj_ref[0, rows, :] * kept
        right = jax.nn.sigmoid(proj_ref[3, rows, :]) * proj_ref[2, rows, :] * kept
        left_ref[rows, :] = left.astype(bf16).astype(f32)
        right_ref[rows, :] = right.astype(bf16).astype(f32)

    def flipped(q):
        firsts = [base(g, q) for g in range(n_row)]
        return lambda g, inner: right_ref[pl.ds(firsts[g] + inner, SUB, stride=SUB), :]

    def along(ref):
        def at(a, q):
            first = base(a, q)
            return lambda lane, inner: spread(ref, first + lane * SUB + inner)
        return at

    def down(ref):
        def at(a, q):
            first = base(q, a)
            return lambda lane, inner: spread(ref, first + inner * SUB + lane)
        return at

    triangle(n_row, flipped, along(left_ref), lines(tri_ref))

    out_gain = out_gain_ref[...]
    for at, rows in chunks():
        x_hat, inverse = normalize(tri_ref[rows, :])
        normed_out = (x_hat * out_gain).astype(bf16)
        hat_ref[rows, :] = normed_out
        lin = jnp.dot(normed_out, weights_ref[5], preferred_element_type=f32)
        out_gate = jax.nn.sigmoid(proj_ref[4, rows, :])
        cot = cot_rows(at).astype(f32)
        upd_ref[rows, :] = out_gate * lin
        grad_lin = (cot * out_gate).astype(bf16)
        lin_ref[rows, :] = grad_lin
        d_ref[4, rows, :] = (cot * lin * out_gate * (1.0 - out_gate)).astype(bf16)
        back = lax.dot_general(grad_lin, weights_ref[5], (((1,), (1,)), ((), ())), preferred_element_type=f32)
        tri_ref[rows, :] = norm_back(back * out_gain, x_hat, inverse).astype(bf16).astype(f32)

    triangle(n_row, across(right_ref), along(tri_ref), lines(gate_ref.at[0]))
    triangle(n_row, across(left_ref), down(tri_ref), lines(gate_ref.at[1]))

    for at, rows in chunks():
        kept = keep_ref[rows, :]
        for side in range(2):
            value, gate = gate_back(gate_ref[side, rows, :], proj_ref[2 * side, rows, :], proj_ref[2 * side + 1, rows, :], kept)
            d_ref[2 * side, rows, :] = value
            d_ref[2 * side + 1, rows, :] = gate

    normed_all = jnp.concatenate([ref[0:tile] for ref in all_refs], axis=0)
    for s in range(5):
        weight_grad_ref[s] = lax.dot_general(
            normed_all, d_ref[s], (((0,), (0,)), ((), ())), preferred_element_type=f32
        ) / residues
    weight_grad_ref[5] = lax.dot_general(
        hat_ref[...], lin_ref[...], (((0,), (0,)), ((), ())), preferred_element_type=f32
    ) / residues

    own = slice(0, tile)
    update_ref[...] = upd_ref[own, :].astype(bf16).reshape(update_ref.shape)
    total = jnp.zeros((tile, channels), f32)
    for s in range(5):
        total = total + lax.dot_general(d_ref[s, own, :], weights_ref[s], (((1,), (1,)), ((), ())), preferred_element_type=f32)
    z_hat, z_inverse = normalize(act_ref[...].astype(f32).reshape(tile, channels))
    grad = norm_back(total * in_gain_ref[...], z_hat, z_inverse)
    pair_grad_ref[...] = grad.astype(bf16).reshape(pair_grad_ref.shape)


def flip_by(block, n_row, n_col, near, far):
    pairs = []
    for row in range(n_row):
        for col in range(n_col):
            shift = near if col % 2 == 0 else far
            pairs.append((row * n_col + col, (row ^ shift[0]) * n_col + (col ^ shift[1])))
    return lax.ppermute(block, ("row", "col"), pairs)


def gather(own, n_row, n_col):
    def flip(block, row, col):
        return flip_by(block, n_row, n_col, (row, col), (row, col))

    along = [flip(own, shift, 0) for shift in reversed(range(1, n_row))]
    stacks = {0: [own[None]]}
    bit = n_col // 2
    while bit > 0:
        stacks.update({col ^ bit: [flip(stack[0], 0, bit)] for col, stack in stacks.items()})
        bit //= 2
    stacks[0].append(jnp.stack(along))
    bit = n_col // 2
    while bit > 0:
        for col in [col for col, stack in stacks.items() if len(stack) == 2]:
            stacks[col ^ bit].append(flip(stacks[col][1], 0, bit))
        bit //= 2
    pieces, owners = [], []
    for col, stack in sorted(stacks.items()):
        pieces += stack
        owners += [((row, col),) * 2 for row in (0, *reversed(range(1, n_row)))]
    return pieces, tuple(owners)


def gathered_body(n_row, n_col, pair_act, pair_mask, crop_length, weights, in_gain, out_gain, cotangent):
    tile_rows, tile_cols, channels = pair_act.shape
    tile = tile_rows * tile_cols
    pairs = tile * n_row * n_col
    vmem = pl.BlockSpec(memory_space=pltpu.VMEM)
    smem = pl.BlockSpec(memory_space=pltpu.SMEM)
    hbm = pl.BlockSpec(memory_space=pltpu.HBM)
    packed = pl.pallas_call(
        pack_kernel,
        name="pack",
        out_shape=jax.ShapeDtypeStruct((2 * tile + 16, channels), jnp.bfloat16),
        in_specs=[hbm] * 4,
        out_specs=vmem,
        scratch_shapes=[
            pltpu.VMEM(pair_act.shape, pair_act.dtype),
            pltpu.VMEM(pair_mask.shape, jnp.int32),
            pltpu.VMEM((1, channels), jnp.float32),
            pltpu.SemaphoreType.DMA((4,)),
        ],
        compiler_params=pltpu.CompilerParams(vmem_limit_bytes=60 * 1024 * 1024),
    )(pair_act, pair_mask, cotangent.reshape(tile, channels), in_gain.reshape(1, channels))
    crop_length, packed = lax.optimization_barrier((crop_length, packed))
    everyone, owners = gather(packed, n_row, n_col)
    counts = tuple(piece.shape[0] for piece in everyone)
    f32, bf16 = jnp.float32, jnp.bfloat16
    return pl.pallas_call(
        functools.partial(part_kernel, n_row, n_col, counts, owners),
        name="part",
        out_shape=(
            jax.ShapeDtypeStruct(pair_act.shape, bf16),
            jax.ShapeDtypeStruct(pair_act.shape, bf16),
            jax.ShapeDtypeStruct(weights.shape, f32),
        ),
        in_specs=[smem] + [vmem] * (4 + len(counts)),
        out_specs=(vmem, vmem, vmem),
        scratch_shapes=[
            pltpu.VMEM((5, pairs, channels), f32),
            pltpu.VMEM((pairs, channels), f32),
            pltpu.VMEM((pairs, channels), f32),
            pltpu.VMEM((pairs, channels), f32),
            pltpu.VMEM((pairs, channels), f32),
            pltpu.VMEM((pairs, channels), bf16),
            pltpu.VMEM((2, pairs, channels), f32),
            pltpu.VMEM((pairs, channels), bf16),
            pltpu.VMEM((pairs, channels), f32),
            pltpu.VMEM((5, pairs, channels), bf16),
            pltpu.SMEM((n_row * n_col,), jnp.int32),
        ],
        compiler_params=pltpu.CompilerParams(vmem_limit_bytes=24 * 1024 * 1024),
    )(crop_length, pair_act, weights, in_gain.reshape(1, channels), out_gain.reshape(1, channels), *everyone)


def body(n_row, n_col, pair_act, *others):
    tile_rows, tile_cols, channels = pair_act.shape
    pairs = tile_rows * n_row * tile_cols * n_col
    small = pairs * channels * 4 <= 1024 * 1024 and channels == 128
    square = n_row == n_col and tile_rows == SUB and tile_cols == SUB and n_col & (n_col - 1) == 0
    if small and square:
        return gathered_body(n_row, n_col, pair_act, *others)
    return spread_body(pair_act, *others)


def solution(mesh):
    return jax.shard_map(
        functools.partial(body, mesh.shape["row"], mesh.shape["col"]),
        mesh=mesh,
        in_specs=(
            P(("parts", "row"), "col", None),
            P(("parts", "row"), "col"),
            P("parts"),
            P(),
            P(),
            P(),
            P(("parts", "row"), "col", None),
        ),
        out_specs=(
            P(("parts", "row"), "col", None),
            P(("parts", "row"), "col", None),
            P("parts", None, None),
        ),
        check_vma=False,
    )
```

```python
import functools

import jax
import jax.numpy as jnp
from jax import lax
from jax.experimental import pallas as pl
from jax.experimental.pallas import tpu as pltpu
from jax.sharding import PartitionSpec as P

SUB = 8
EPS = 1e-05


def normalize(values):
    average = jnp.mean(values, axis=-1, keepdims=True)
    centered = values - average
    inverse = lax.rsqrt(jnp.mean(centered * centered, axis=-1, keepdims=True) + 1e-05)
    return (centered * inverse, inverse)


def norm_back(grad_hat, values_hat, inverse):
    first = jnp.mean(grad_hat, axis=-1, keepdims=True)
    second = jnp.mean(grad_hat * values_hat, axis=-1, keepdims=True)
    return (grad_hat - first - values_hat * second) * inverse


def gate_back(grad_act, proj_value, proj_gate, keep_mask):
    gate_sig = jax.nn.sigmoid(proj_gate)
    masked = grad_act * keep_mask
    grad_value = (masked * gate_sig).astype(jnp.bfloat16)
    grad_gate = (masked * proj_value * gate_sig * (1.0 - gate_sig)).astype(jnp.bfloat16)
    return (grad_value, grad_gate)


def spread_body(pair_act, pair_mask, crop_length, weights, in_gain, out_gain, cotangent):
    tile_rows, tile_cols, channels = pair_act.shape
    residues = tile_rows * lax.axis_size("row")
    row_pos = lax.axis_index("row") * tile_rows + jnp.arange(tile_rows, dtype=jnp.int32)
    col_pos = lax.axis_index("col") * tile_cols + jnp.arange(tile_cols, dtype=jnp.int32)
    row_in = (row_pos < crop_length[0]).astype(jnp.float32)
    col_in = (col_pos < crop_length[0]).astype(jnp.float32)
    keep_mask = (pair_mask.astype(jnp.float32) * row_in[:, None] * col_in[None, :])[:, :, None]
    z_hat, z_inverse = normalize(pair_act.astype(jnp.float32))
    normed = (z_hat * in_gain).astype(jnp.bfloat16)
    flat_norm = normed.reshape(tile_rows * tile_cols, channels)
    projections = jnp.einsum(
        "pc,scd->spd", flat_norm, weights[:5], preferred_element_type=jnp.float32
    )
    projections = projections.reshape(5, tile_rows, tile_cols, channels)
    left_act = (jax.nn.sigmoid(projections[1]) * projections[0] * keep_mask).astype(jnp.bfloat16)
    right_act = (jax.nn.sigmoid(projections[3]) * projections[2] * keep_mask).astype(jnp.bfloat16)
    partial_value = jnp.einsum(
        "ikh,jkh->ijh",
        left_act,
        lax.all_gather(right_act, "row", axis=0, tiled=True),
        preferred_element_type=jnp.float32,
    )
    tri_sum = lax.psum_scatter(
        partial_value.astype(jnp.bfloat16), "col", scatter_dimension=1, tiled=True
    ).astype(jnp.float32)
    x_hat, x_inverse = normalize(tri_sum)
    normed_out = (x_hat * out_gain).astype(jnp.bfloat16)
    flat_out = normed_out.reshape(tile_rows * tile_cols, channels)
    update_lin = jnp.dot(flat_out, weights[5], preferred_element_type=jnp.float32)
    update_lin = update_lin.reshape(tile_rows, tile_cols, channels)
    out_gate = jax.nn.sigmoid(projections[4])
    update = (out_gate * update_lin).astype(jnp.bfloat16)
    cot_value = cotangent.astype(jnp.float32)
    grad_lin = (cot_value * out_gate).astype(jnp.bfloat16)
    grad_gate_out = (cot_value * update_lin * out_gate * (1.0 - out_gate)).astype(jnp.bfloat16)
    flat_lin = grad_lin.reshape(tile_rows * tile_cols, channels)
    grad_norm_out = jnp.einsum(
        "pd,cd->pc", flat_lin, weights[5], preferred_element_type=jnp.float32
    )
    grad_norm_out = grad_norm_out.reshape(tile_rows, tile_cols, channels)
    grad_tri = norm_back(grad_norm_out * out_gain, x_hat, x_inverse).astype(jnp.bfloat16)
    grad_full = lax.all_gather(grad_tri, "col", axis=1, tiled=True)
    grad_slab = grad_full
    grad_left = jnp.einsum(
        "ijh,jkh->ikh",
        grad_slab,
        lax.all_gather(right_act, "row", axis=0, tiled=True),
        preferred_element_type=jnp.float32,
    )
    grad_slab = grad_full
    grad_right = lax.psum_scatter(
        jnp.einsum("ijh,ikh->jkh", grad_slab, left_act, preferred_element_type=jnp.float32).astype(
            jnp.bfloat16
        ),
        "row",
        scatter_dimension=0,
        tiled=True,
    ).astype(jnp.float32)
    grad_pa, grad_ga = gate_back(grad_left, projections[0], projections[1], keep_mask)
    grad_pb, grad_gb = gate_back(grad_right, projections[2], projections[3], keep_mask)
    grads = jnp.stack([grad_pa, grad_ga, grad_pb, grad_gb, grad_gate_out]).reshape(
        5, tile_rows * tile_cols, channels
    )
    grad_normed = jnp.einsum("spd,scd->pc", grads, weights[:5], preferred_element_type=jnp.float32)
    grad_normed = grad_normed.reshape(tile_rows, tile_cols, channels)
    pair_grad = norm_back(grad_normed * in_gain, z_hat, z_inverse).astype(jnp.bfloat16)
    local_in = jnp.einsum("pc,spd->scd", flat_norm, grads, preferred_element_type=jnp.float32)
    local_out = jnp.dot(flat_out.T, flat_lin, preferred_element_type=jnp.float32)
    local_grads = jnp.concatenate([local_in, local_out[None]], axis=0) / residues
    weight_grad = lax.psum(local_grads, ("row", "col"))
    return (update, pair_grad, weight_grad)


def pack_kernel(act_hbm, mask_hbm, cot_hbm, gain_hbm, out_ref, act_ref, mask_ref, gain_ref, sems):
    tile_rows, tile_cols, channels = act_ref.shape
    pairs = tile_rows * tile_cols
    head = out_ref.shape[0] - pairs
    pack_copies = [
        pltpu.make_async_copy(act_hbm, act_ref, sems.at[0]),
        pltpu.make_async_copy(gain_hbm, gain_ref, sems.at[1]),
        pltpu.make_async_copy(mask_hbm, mask_ref, sems.at[2]),
        pltpu.make_async_copy(cot_hbm, out_ref.at[head : head + pairs], sems.at[3]),
    ]
    for copy in pack_copies:
        copy.start()
    for copy in pack_copies:
        copy.wait()
    z_hat, _ = normalize(act_ref[...].astype(jnp.float32).reshape(pairs, channels))
    out_ref[0:pairs] = (z_hat * gain_ref[...]).astype(jnp.bfloat16)
    keep = mask_ref[...].astype(jnp.float32)
    wide = jnp.concatenate([keep, jnp.zeros((tile_rows, channels - tile_cols), jnp.float32)], axis=1)
    tall = jnp.concatenate([wide, jnp.zeros((channels - tile_rows, channels), jnp.float32)], axis=0)
    out_ref[pairs:head] = tall.T[0 : head - pairs].astype(jnp.bfloat16)


def join_kernel(head, count, *refs):
    blocks, (front_ref, back_ref) = refs[:count], refs[-2:]
    for at, block in enumerate(blocks):
        front_ref[at] = block[0:head]
        back_ref[at] = block[head:]


def triangle(blocks, groups, steps, vectors_at, factors_at, start_at, store_at):
    def block(a, _):
        def step(q, totals):
            totals = list(totals)
            vectors = vectors_at(q)
            factors = factors_at(a, q)
            for inner in range(SUB):
                rows = [vectors(g, inner) for g in range(groups)]
                for lane in range(SUB):
                    factor = factors(lane, inner)
                    for g in range(groups):
                        at = lane * groups + g
                        totals[at] = totals[at] + factor * rows[g]
            return tuple(totals)

        totals = tuple(start_at(a, g, lane) for lane in range(SUB) for g in range(groups))
        totals = step(0, totals) if steps == 1 else lax.fori_loop(0, steps, step, totals)
        for g in range(groups):
            store_at(a, g, [totals[lane * groups + g] for lane in range(SUB)])
        return 0

    lax.fori_loop(0, blocks, block, 0)


def spread(ref, row):
    return jnp.broadcast_to(ref[pl.ds(row, 1), :], (SUB, ref.shape[-1]))


def line(ref, row):
    return ref[pl.ds(pl.multiple_of(row, SUB), SUB), :]


def column_kernel(n_row, n_col, col, crop_ref, first_ref, rest_ref, weights_ref, *refs):
    tri_in, (tri_ref, left_ref, right_ref, side_ref, gate_ref, flip_ref) = refs[:-6], refs[-6:]
    channels = first_ref.shape[-1]
    tile = SUB * SUB
    size = n_row * tile
    bf16, f32 = jnp.bfloat16, jnp.float32
    row_me, col_me = lax.axis_index("row"), lax.axis_index("col")
    blocks = [first_ref] + [rest_ref.at[b] for b in range(n_row - 1)]
    normed = jnp.concatenate([block[0:tile] for block in blocks], axis=0)
    flip_ref[...] = normed.astype(f32).T.astype(bf16)
    crop = crop_ref[0]
    col_offset = lax.broadcasted_iota(jnp.int32, (SUB, channels), 0)
    row_offset = lax.broadcasted_iota(jnp.int32, (SUB, channels), 1)
    cols_in = col_offset < crop - (col_me ^ col) * SUB
    kept = []
    for b, block in enumerate(blocks):
        keep = block[tile : tile + 2 * SUB].astype(f32)[0:SUB]
        rows_in = row_offset < crop - (row_me ^ b) * SUB
        keep = jnp.where(rows_in & cols_in, keep, 0.0)
        kept += [jnp.broadcast_to(keep[:, at : at + 1], (SUB, channels)) for at in range(SUB)]
    kept = jnp.concatenate(kept, axis=0)
    for side, act_ref in enumerate((left_ref, right_ref)):
        pair = jnp.concatenate([weights_ref[2 * side], weights_ref[2 * side + 1]], axis=1)
        proj = jnp.dot(normed, pair, preferred_element_type=f32)
        gate = jax.nn.sigmoid(proj[:, channels:])
        masked = gate * kept
        act = masked * proj[:, :channels]
        act_ref[...] = act.astype(bf16).astype(f32)
        side_ref[2 * side] = masked
        side_ref[2 * side + 1] = act * (1.0 - gate)
    gate_ref[...] = jax.nn.sigmoid(jnp.dot(normed, weights_ref[4], preferred_element_type=f32))
    turn = row_me ^ col_me

    def flipped(q):
        firsts = [(turn ^ g) * tile for g in range(n_col)]
        return lambda g, inner: right_ref[pl.ds(firsts[g] + inner, SUB, stride=SUB), :]

    def along(a, q):
        return lambda lane, inner: spread(left_ref, a * tile + lane * SUB + inner)

    def start(a, g, lane):
        if len(tri_in) == 0:
            return jnp.zeros((SUB, channels), f32)
        return line(tri_in[0], g * size + a * tile + lane * SUB)

    def store(a, g, values):
        for lane in range(SUB):
            tri_ref[pl.ds(pl.multiple_of(g * size + a * tile + lane * SUB, SUB), SUB), :] = values[lane]

    triangle(n_row, n_col, 1, flipped, along, start, store)


def rest_kernel(n_row, n_col, act_ref, weights_ref, in_gain_ref, out_gain_ref, tri_ref, *refs):
    parts = [refs[at * 7 : at * 7 + 7] for at in range(n_col)]
    update_ref, pair_grad_ref, weight_grad_ref, back_ref, hat_ref, lin_ref, d_ref = refs[7 * n_col :]
    channels = act_ref.shape[-1]
    tile = SUB * SUB
    size = n_row * tile
    residues = n_row * SUB
    bf16, f32 = jnp.bfloat16, jnp.float32
    turn = lax.axis_index("row") ^ lax.axis_index("col")
    out_gain = out_gain_ref[...]
    for col, (first_ref, cots_ref, _, _, _, gate_ref, _) in enumerate(parts):
        rows = slice(col * size, (col + 1) * size)
        x_hat, inverse = normalize(tri_ref[rows, :])
        normed_out = (x_hat * out_gain).astype(bf16)
        hat_ref[rows, :] = normed_out
        lin = jnp.dot(normed_out, weights_ref[5], preferred_element_type=f32)
        out_gate = gate_ref[...]
        if col == 0:
            update_ref[...] = (out_gate[0:tile] * lin[0:tile]).astype(bf16).reshape(update_ref.shape)
        head = first_ref.shape[0] - tile
        cot = jnp.concatenate([first_ref[head:]] + [cots_ref[b] for b in range(n_row - 1)], axis=0).astype(f32)
        grad = cot * out_gate
        grad_lin = grad.astype(bf16)
        lin_ref[rows, :] = grad_lin
        d_ref[rows, 4 * channels : 5 * channels] = (grad * lin * (1.0 - out_gate)).astype(bf16)
        back = lax.dot_general(grad_lin, weights_ref[5], (((1,), (1,)), ((), ())), preferred_element_type=f32)
        back_ref[rows, :] = norm_back(back * out_gain, x_hat, inverse).astype(bf16).astype(f32)

    lefts, rights, sides = [[part[at] for part in parts] for at in (2, 3, 4)]

    def zero(a, g, lane):
        return jnp.zeros((SUB, channels), f32)

    def store(side):
        def put(a, g, values):
            for lane in range(0, SUB, 2):
                at = pl.multiple_of(a * tile + lane * SUB, 2 * SUB)
                both = jnp.concatenate(values[lane : lane + 2], axis=0)
                rows = pl.ds(pl.multiple_of(g * size + at, 2 * SUB), 2 * SUB)
                for kind in range(2):
                    spot = (2 * side + kind) * channels
                    scaled = both * sides[g][2 * side + kind, pl.ds(at, 2 * SUB), :]
                    d_ref[rows, spot : spot + channels] = scaled.astype(bf16)
        return put

    def by_right(q):
        return lambda g, inner: line(rights[g], (q ^ turn) * tile + inner * SUB)

    def by_left(q):
        return lambda g, inner: line(lefts[g], q * tile + inner * SUB)

    def along(a, q):
        return lambda lane, inner: spread(back_ref, q * size + a * tile + lane * SUB + inner)

    def down(a, q):
        return lambda lane, inner: spread(back_ref, (a ^ turn) * size + q * tile + inner * SUB + lane)

    triangle(n_row, n_col, n_col, by_right, along, zero, store(0))
    triangle(n_row, n_col, n_row, by_left, down, zero, store(1))

    scale = 1.0 / residues
    flipped = jnp.concatenate([part[6][...] for part in parts], axis=1)
    sums = jnp.dot(flipped, d_ref[...], preferred_element_type=f32) * scale
    for s in range(5):
        weight_grad_ref[s] = sums[:, s * channels : (s + 1) * channels]
    weight_grad_ref[5] = scale * lax.dot_general(
        hat_ref[...], lin_ref[...], (((0,), (0,)), ((), ())), preferred_element_type=f32
    )
    total = jnp.zeros((tile, channels), f32)
    for s in range(5):
        total = total + lax.dot_general(
            d_ref[0:tile, s * channels : (s + 1) * channels], weights_ref[s],
            (((1,), (1,)), ((), ())), preferred_element_type=f32,
        )
    z_hat, z_inverse = normalize(act_ref[...].astype(f32).reshape(tile, channels))
    grad = norm_back(total * in_gain_ref[...], z_hat, z_inverse)
    pair_grad_ref[...] = grad.astype(bf16).reshape(pair_grad_ref.shape)


def flip(block, n_row, n_col, row, col):
    pairs = [(r * n_col + c, (r ^ row) * n_col + (c ^ col)) for r in range(n_row) for c in range(n_col)]
    return lax.ppermute(block, ("row", "col"), pairs)


def gathered_body(n_row, n_col, pair_act, pair_mask, crop_length, weights, in_gain, out_gain, cotangent):
    tile_rows, tile_cols, channels = pair_act.shape
    tile = tile_rows * tile_cols
    size = n_row * tile
    pairs = size * n_col
    head = tile + 2 * SUB
    f32, bf16 = jnp.float32, jnp.bfloat16
    vmem = pl.BlockSpec(memory_space=pltpu.VMEM)
    smem = pl.BlockSpec(memory_space=pltpu.SMEM)
    hbm = pl.BlockSpec(memory_space=pltpu.HBM)
    in_gain, out_gain = in_gain.reshape(1, channels), out_gain.reshape(1, channels)

    def limit(mib):
        return pltpu.CompilerParams(vmem_limit_bytes=mib * 1024 * 1024)

    own = pl.pallas_call(
        pack_kernel,
        name="pack",
        out_shape=jax.ShapeDtypeStruct((head + tile, channels), bf16),
        in_specs=[hbm] * 4,
        out_specs=vmem,
        scratch_shapes=[
            pltpu.VMEM(pair_act.shape, pair_act.dtype),
            pltpu.VMEM(pair_mask.shape, jnp.int32),
            pltpu.VMEM((1, channels), f32),
            pltpu.SemaphoreType.DMA((4,)),
        ],
        compiler_params=limit(60),
    )(pair_act, pair_mask, cotangent.reshape(tile, channels), in_gain)
    crop_length, own = lax.optimization_barrier((crop_length, own))

    firsts = {0: own}
    along = [flip(own, n_row, n_col, shift, 0) for shift in reversed(range(1, n_row))]
    bit = n_col // 2
    while bit > 0:
        firsts.update({col ^ bit: flip(first, n_row, n_col, 0, bit) for col, first in firsts.items()})
        bit //= 2
    direct = [firsts[1 << at] for at in range(n_col.bit_length() - 1)]
    front, back = pl.pallas_call(
        functools.partial(join_kernel, head, n_row - 1),
        name="join",
        out_shape=(
            jax.ShapeDtypeStruct((n_row - 1, head, channels), bf16),
            jax.ShapeDtypeStruct((n_row - 1, tile, channels), bf16),
        ),
        in_specs=[vmem] * (n_row - 1) + [pl.BlockSpec(memory_space=pl.ANY)] * len(direct),
        out_specs=(vmem, vmem),
        compiler_params=limit(2),
    )(*reversed(along), *direct)
    fronts, backs = {0: front}, {0: back}
    bit = n_col // 2
    while bit > 0:
        fronts.update({col ^ bit: flip(stack, n_row, n_col, 0, bit) for col, stack in fronts.items()})
        backs.update({col ^ bit: flip(stack, n_row, n_col, 0, bit) for col, stack in backs.items()})
        bit //= 2

    tri, parts = [], []
    for col in range(n_col):
        last = len(tri) > 0
        results = pl.pallas_call(
            functools.partial(column_kernel, n_row, n_col, col),
            name=f"column_{col}",
            out_shape=(
                jax.ShapeDtypeStruct((pairs, channels), f32),
                jax.ShapeDtypeStruct((size, channels), f32),
                jax.ShapeDtypeStruct((size, channels), f32),
                jax.ShapeDtypeStruct((4, size, channels), f32),
                jax.ShapeDtypeStruct((size, channels), f32),
                jax.ShapeDtypeStruct((channels, size), bf16),
            ),
            in_specs=[smem] + [vmem] * (3 + len(tri)),
            out_specs=(vmem,) * 6,
            input_output_aliases={4: 0} if last else {},
            compiler_params=limit(8),
            cost_estimate=pl.CostEstimate(flops=400_000_000, bytes_accessed=1_000_000, transcendentals=0),
        )(crop_length, firsts[col], fronts[col], weights, *tri)
        tri = [results[0]]
        parts += [firsts[col], backs[col], *results[1:]]

    return pl.pallas_call(
        functools.partial(rest_kernel, n_row, n_col),
        name="rest",
        out_shape=(
            jax.ShapeDtypeStruct(pair_act.shape, bf16),
            jax.ShapeDtypeStruct(pair_act.shape, bf16),
            jax.ShapeDtypeStruct(weights.shape, f32),
        ),
        in_specs=[vmem] * (5 + len(parts)),
        out_specs=(vmem, vmem, vmem),
        scratch_shapes=[
            pltpu.VMEM((pairs, channels), f32),
            pltpu.VMEM((pairs, channels), bf16),
            pltpu.VMEM((pairs, channels), bf16),
            pltpu.VMEM((pairs, 5 * channels), bf16),
        ],
        compiler_params=limit(16),
    )(pair_act, weights, in_gain, out_gain, *tri, *parts)


def body(n_row, n_col, pair_act, *others):
    tile_rows, tile_cols, channels = pair_act.shape
    pairs = tile_rows * n_row * tile_cols * n_col
    small = pairs * channels * 4 <= 1024 * 1024 and channels == 128
    square = n_row == n_col and tile_rows == SUB and tile_cols == SUB and n_col & (n_col - 1) == 0 and n_col > 1
    if small and square:
        return gathered_body(n_row, n_col, pair_act, *others)
    return spread_body(pair_act, *others)


def solution(mesh):
    return jax.shard_map(
        functools.partial(body, mesh.shape["row"], mesh.shape["col"]),
        mesh=mesh,
        in_specs=(
            P(("parts", "row"), "col", None),
            P(("parts", "row"), "col"),
            P("parts"),
            P(),
            P(),
            P(),
            P(("parts", "row"), "col", None),
        ),
        out_specs=(
            P(("parts", "row"), "col", None),
            P(("parts", "row"), "col", None),
            P("parts", None, None),
        ),
        check_vma=False,
    )
```

```python
import functools

import jax
import jax.numpy as jnp
from jax import lax
from jax.experimental import pallas as pl
from jax.experimental.pallas import tpu as pltpu
from jax.sharding import PartitionSpec as P

SUB = 8
EPS = 1e-05


def normalize(values):
    average = jnp.mean(values, axis=-1, keepdims=True)
    centered = values - average
    inverse = lax.rsqrt(jnp.mean(centered * centered, axis=-1, keepdims=True) + 1e-05)
    return (centered * inverse, inverse)


def norm_back(grad_hat, values_hat, inverse):
    first = jnp.mean(grad_hat, axis=-1, keepdims=True)
    second = jnp.mean(grad_hat * values_hat, axis=-1, keepdims=True)
    return (grad_hat - first - values_hat * second) * inverse


def gate_back(grad_act, proj_value, proj_gate, keep_mask):
    gate_sig = jax.nn.sigmoid(proj_gate)
    masked = grad_act * keep_mask
    grad_value = (masked * gate_sig).astype(jnp.bfloat16)
    grad_gate = (masked * proj_value * gate_sig * (1.0 - gate_sig)).astype(jnp.bfloat16)
    return (grad_value, grad_gate)


def spread_body(pair_act, pair_mask, crop_length, weights, in_gain, out_gain, cotangent):
    tile_rows, tile_cols, channels = pair_act.shape
    residues = tile_rows * lax.axis_size("row")
    row_pos = lax.axis_index("row") * tile_rows + jnp.arange(tile_rows, dtype=jnp.int32)
    col_pos = lax.axis_index("col") * tile_cols + jnp.arange(tile_cols, dtype=jnp.int32)
    row_in = (row_pos < crop_length[0]).astype(jnp.float32)
    col_in = (col_pos < crop_length[0]).astype(jnp.float32)
    keep_mask = (pair_mask.astype(jnp.float32) * row_in[:, None] * col_in[None, :])[:, :, None]
    z_hat, z_inverse = normalize(pair_act.astype(jnp.float32))
    normed = (z_hat * in_gain).astype(jnp.bfloat16)
    flat_norm = normed.reshape(tile_rows * tile_cols, channels)
    projections = jnp.einsum(
        "pc,scd->spd", flat_norm, weights[:5], preferred_element_type=jnp.float32
    )
    projections = projections.reshape(5, tile_rows, tile_cols, channels)
    left_act = (jax.nn.sigmoid(projections[1]) * projections[0] * keep_mask).astype(jnp.bfloat16)
    right_act = (jax.nn.sigmoid(projections[3]) * projections[2] * keep_mask).astype(jnp.bfloat16)
    partial_value = jnp.einsum(
        "ikh,jkh->ijh",
        left_act,
        lax.all_gather(right_act, "row", axis=0, tiled=True),
        preferred_element_type=jnp.float32,
    )
    tri_sum = lax.psum_scatter(
        partial_value.astype(jnp.bfloat16), "col", scatter_dimension=1, tiled=True
    ).astype(jnp.float32)
    x_hat, x_inverse = normalize(tri_sum)
    normed_out = (x_hat * out_gain).astype(jnp.bfloat16)
    flat_out = normed_out.reshape(tile_rows * tile_cols, channels)
    update_lin = jnp.dot(flat_out, weights[5], preferred_element_type=jnp.float32)
    update_lin = update_lin.reshape(tile_rows, tile_cols, channels)
    out_gate = jax.nn.sigmoid(projections[4])
    update = (out_gate * update_lin).astype(jnp.bfloat16)
    cot_value = cotangent.astype(jnp.float32)
    grad_lin = (cot_value * out_gate).astype(jnp.bfloat16)
    grad_gate_out = (cot_value * update_lin * out_gate * (1.0 - out_gate)).astype(jnp.bfloat16)
    flat_lin = grad_lin.reshape(tile_rows * tile_cols, channels)
    grad_norm_out = jnp.einsum(
        "pd,cd->pc", flat_lin, weights[5], preferred_element_type=jnp.float32
    )
    grad_norm_out = grad_norm_out.reshape(tile_rows, tile_cols, channels)
    grad_tri = norm_back(grad_norm_out * out_gain, x_hat, x_inverse).astype(jnp.bfloat16)
    grad_full = lax.all_gather(grad_tri, "col", axis=1, tiled=True)
    grad_slab = grad_full
    grad_left = jnp.einsum(
        "ijh,jkh->ikh",
        grad_slab,
        lax.all_gather(right_act, "row", axis=0, tiled=True),
        preferred_element_type=jnp.float32,
    )
    grad_slab = grad_full
    grad_right = lax.psum_scatter(
        jnp.einsum("ijh,ikh->jkh", grad_slab, left_act, preferred_element_type=jnp.float32).astype(
            jnp.bfloat16
        ),
        "row",
        scatter_dimension=0,
        tiled=True,
    ).astype(jnp.float32)
    grad_pa, grad_ga = gate_back(grad_left, projections[0], projections[1], keep_mask)
    grad_pb, grad_gb = gate_back(grad_right, projections[2], projections[3], keep_mask)
    grads = jnp.stack([grad_pa, grad_ga, grad_pb, grad_gb, grad_gate_out]).reshape(
        5, tile_rows * tile_cols, channels
    )
    grad_normed = jnp.einsum("spd,scd->pc", grads, weights[:5], preferred_element_type=jnp.float32)
    grad_normed = grad_normed.reshape(tile_rows, tile_cols, channels)
    pair_grad = norm_back(grad_normed * in_gain, z_hat, z_inverse).astype(jnp.bfloat16)
    local_in = jnp.einsum("pc,spd->scd", flat_norm, grads, preferred_element_type=jnp.float32)
    local_out = jnp.dot(flat_out.T, flat_lin, preferred_element_type=jnp.float32)
    local_grads = jnp.concatenate([local_in, local_out[None]], axis=0) / residues
    weight_grad = lax.psum(local_grads, ("row", "col"))
    return (update, pair_grad, weight_grad)


def pack_kernel(act_hbm, mask_hbm, cot_hbm, gain_hbm, out_ref, act_ref, mask_ref, gain_ref, sems):
    tile_rows, tile_cols, channels = act_ref.shape
    pairs = tile_rows * tile_cols
    head = out_ref.shape[0] - pairs
    pack_copies = [
        pltpu.make_async_copy(act_hbm, act_ref, sems.at[0]),
        pltpu.make_async_copy(gain_hbm, gain_ref, sems.at[1]),
        pltpu.make_async_copy(mask_hbm, mask_ref, sems.at[2]),
        pltpu.make_async_copy(cot_hbm, out_ref.at[head : head + pairs], sems.at[3]),
    ]
    for copy in pack_copies:
        copy.start()
    for copy in pack_copies:
        copy.wait()
    z_hat, _ = normalize(act_ref[...].astype(jnp.float32).reshape(pairs, channels))
    out_ref[0:pairs] = (z_hat * gain_ref[...]).astype(jnp.bfloat16)
    keep = mask_ref[...].astype(jnp.float32)
    wide = jnp.concatenate([keep, jnp.zeros((tile_rows, channels - tile_cols), jnp.float32)], axis=1)
    tall = jnp.concatenate([wide, jnp.zeros((channels - tile_rows, channels), jnp.float32)], axis=0)
    out_ref[pairs:head] = tall.T[0 : head - pairs].astype(jnp.bfloat16)


def join_kernel(head, far_3, far_2, over, near, cross, twin, front_ref, back_ref, near_ref):
    for at, block in enumerate((far_2, far_3)):
        front_ref[at] = block[0:head]
        back_ref[at] = block[head:]
    for at, block in enumerate((over, near, cross)):
        near_ref[at] = block[...]


def triangle(blocks, groups, steps, vectors_at, factors_at, start_at, store_at):
    def block(a, _):
        def step(q, totals):
            totals = list(totals)
            vectors = vectors_at(q)
            factors = factors_at(a, q)
            for inner in range(SUB):
                rows = [vectors(g, inner) for g in range(groups)]
                for lane in range(SUB):
                    factor = factors(lane, inner)
                    for g in range(groups):
                        at = lane * groups + g
                        totals[at] = totals[at] + factor * rows[g]
            return tuple(totals)

        totals = tuple(start_at(a, g, lane) for lane in range(SUB) for g in range(groups))
        totals = step(0, totals) if steps == 1 else lax.fori_loop(0, steps, step, totals)
        for g in range(groups):
            store_at(a, g, [totals[lane * groups + g] for lane in range(SUB)])
        return 0

    lax.fori_loop(0, blocks, block, 0)


def spread(ref, row):
    return jnp.broadcast_to(ref[pl.ds(row, 1), :], (SUB, ref.shape[-1]))


def line(ref, row):
    return ref[pl.ds(pl.multiple_of(row, SUB), SUB), :]


def column_kernel(n_row, n_col, col, spots, crop_ref, first_ref, second_ref, rest_ref, weights_ref, *refs):
    if col == 0:
        act_ref, in_gain_ref, out_gain_ref, *refs, own_ref, gains_ref = refs
        z_hat, z_inverse = normalize(act_ref[...].astype(jnp.float32).reshape(own_ref.shape[1:]))
        own_ref[0] = z_hat
        own_ref[1] = jnp.broadcast_to(z_inverse, z_hat.shape)
        gains_ref[0:1] = in_gain_ref[...]
        gains_ref[1:2] = out_gain_ref[...]
    tri_in, (tri_ref, left_ref, right_ref, side_ref, gate_ref, flip_ref) = refs[:-6], refs[-6:]
    channels = rest_ref.shape[-1]
    tile = SUB * SUB
    size = n_row * tile
    bf16, f32 = jnp.bfloat16, jnp.float32
    row_me, col_me = lax.axis_index("row"), lax.axis_index("col")
    blocks = [ref if at is None else ref.at[at] for ref, at in zip((first_ref, second_ref), spots)]
    blocks += [rest_ref.at[b] for b in range(n_row - 2)]
    normed = jnp.concatenate([block[0:tile] for block in blocks], axis=0)
    flip_ref[...] = normed.astype(f32).T.astype(bf16)
    crop = crop_ref[0]
    col_offset = lax.broadcasted_iota(jnp.int32, (SUB, channels), 0)
    row_offset = lax.broadcasted_iota(jnp.int32, (SUB, channels), 1)
    cols_in = col_offset < crop - (col_me ^ col) * SUB
    kept = []
    for b, block in enumerate(blocks):
        keep = block[tile : tile + 2 * SUB].astype(f32)[0:SUB]
        rows_in = row_offset < crop - (row_me ^ b) * SUB
        keep = jnp.where(rows_in & cols_in, keep, 0.0)
        kept += [jnp.broadcast_to(keep[:, at : at + 1], (SUB, channels)) for at in range(SUB)]
    kept = jnp.concatenate(kept, axis=0)
    for side, act_ref in enumerate((left_ref, right_ref)):
        pair = jnp.concatenate([weights_ref[2 * side], weights_ref[2 * side + 1]], axis=1)
        proj = jnp.dot(normed, pair, preferred_element_type=f32)
        gate = jax.nn.sigmoid(proj[:, channels:])
        masked = gate * kept
        act = masked * proj[:, :channels]
        act_ref[...] = act.astype(bf16).astype(f32)
        side_ref[2 * side] = masked
        side_ref[2 * side + 1] = act * (1.0 - gate)
    gate_ref[...] = jax.nn.sigmoid(jnp.dot(normed, weights_ref[4], preferred_element_type=f32))
    turn = row_me ^ col_me

    def flipped(q):
        firsts = [(turn ^ g) * tile for g in range(n_col)]
        return lambda g, inner: right_ref[pl.ds(firsts[g] + inner, SUB, stride=SUB), :]

    def along(a, q):
        return lambda lane, inner: spread(left_ref, a * tile + lane * SUB + inner)

    def start(a, g, lane):
        if len(tri_in) == 0:
            return jnp.zeros((SUB, channels), f32)
        return line(tri_in[0], g * size + a * tile + lane * SUB)

    def store(a, g, values):
        for lane in range(SUB):
            tri_ref[pl.ds(pl.multiple_of(g * size + a * tile + lane * SUB, SUB), SUB), :] = values[lane]

    triangle(n_row, n_col, 1, flipped, along, start, store)


def rest_kernel(n_row, n_col, spots, weights_ref, own_ref, gains_ref, tri_ref, *refs):
    parts = [refs[at * 8 : at * 8 + 8] for at in range(n_col)]
    update_ref, pair_grad_ref, weight_grad_ref, back_ref, hat_ref, lin_ref, d_ref = refs[8 * n_col :]
    channels = tri_ref.shape[-1]
    tile = SUB * SUB
    size = n_row * tile
    residues = n_row * SUB
    bf16, f32 = jnp.bfloat16, jnp.float32
    turn = lax.axis_index("row") ^ lax.axis_index("col")
    out_gain = gains_ref[1:2]
    for col, (first_ref, second_ref, cots_ref, _, _, _, gate_ref, _) in enumerate(parts):
        rows = slice(col * size, (col + 1) * size)
        x_hat, inverse = normalize(tri_ref[rows, :])
        normed_out = (x_hat * out_gain).astype(bf16)
        hat_ref[rows, :] = normed_out
        lin = jnp.dot(normed_out, weights_ref[5], preferred_element_type=f32)
        out_gate = gate_ref[...]
        if col == 0:
            update_ref[...] = (out_gate[0:tile] * lin[0:tile]).astype(bf16).reshape(update_ref.shape)
        blocks = [ref if at is None else ref.at[at] for ref, at in zip((first_ref, second_ref), spots[col])]
        cots = [block[block.shape[0] - tile :] for block in blocks] + [cots_ref[b] for b in range(n_row - 2)]
        cot = jnp.concatenate(cots, axis=0).astype(f32)
        grad = cot * out_gate
        grad_lin = grad.astype(bf16)
        lin_ref[rows, :] = grad_lin
        d_ref[rows, 4 * channels : 5 * channels] = (grad * lin * (1.0 - out_gate)).astype(bf16)
        back = lax.dot_general(grad_lin, weights_ref[5], (((1,), (1,)), ((), ())), preferred_element_type=f32)
        back_ref[rows, :] = norm_back(back * out_gain, x_hat, inverse).astype(bf16).astype(f32)

    lefts, rights, sides = [[part[at] for part in parts] for at in (3, 4, 5)]

    def zero(a, g, lane):
        return jnp.zeros((SUB, channels), f32)

    def store(side):
        def put(a, g, values):
            for lane in range(0, SUB, 2):
                at = pl.multiple_of(a * tile + lane * SUB, 2 * SUB)
                both = jnp.concatenate(values[lane : lane + 2], axis=0)
                rows = pl.ds(pl.multiple_of(g * size + at, 2 * SUB), 2 * SUB)
                for kind in range(2):
                    spot = (2 * side + kind) * channels
                    scaled = both * sides[g][2 * side + kind, pl.ds(at, 2 * SUB), :]
                    d_ref[rows, spot : spot + channels] = scaled.astype(bf16)
        return put

    def by_right(q):
        return lambda g, inner: line(rights[g], (q ^ turn) * tile + inner * SUB)

    def by_left(q):
        return lambda g, inner: line(lefts[g], q * tile + inner * SUB)

    def along(a, q):
        return lambda lane, inner: spread(back_ref, q * size + a * tile + lane * SUB + inner)

    def down(a, q):
        return lambda lane, inner: spread(back_ref, (a ^ turn) * size + q * tile + inner * SUB + lane)

    triangle(n_row, n_col, n_col, by_right, along, zero, store(0))
    triangle(n_row, n_col, n_row, by_left, down, zero, store(1))

    scale = 1.0 / residues
    flipped = jnp.concatenate([part[7][...] for part in parts], axis=1)
    sums = jnp.dot(flipped, d_ref[...], preferred_element_type=f32) * scale
    for s in range(5):
        weight_grad_ref[s] = sums[:, s * channels : (s + 1) * channels]
    weight_grad_ref[5] = scale * lax.dot_general(
        hat_ref[...], lin_ref[...], (((0,), (0,)), ((), ())), preferred_element_type=f32
    )
    total = jnp.zeros((tile, channels), f32)
    for s in range(5):
        total = total + lax.dot_general(
            d_ref[0:tile, s * channels : (s + 1) * channels], weights_ref[s],
            (((1,), (1,)), ((), ())), preferred_element_type=f32,
        )
    grad = norm_back(total * gains_ref[0:1], own_ref[0], own_ref[1])
    pair_grad_ref[...] = grad.astype(bf16).reshape(pair_grad_ref.shape)


def flip(block, n_row, n_col, row, col):
    pairs = [(r * n_col + c, (r ^ row) * n_col + (c ^ col)) for r in range(n_row) for c in range(n_col)]
    return lax.ppermute(block, ("row", "col"), pairs)


def gathered_body(n_row, n_col, pair_act, pair_mask, crop_length, weights, in_gain, out_gain, cotangent):
    tile_rows, tile_cols, channels = pair_act.shape
    tile = tile_rows * tile_cols
    size = n_row * tile
    pairs = size * n_col
    head = tile + 2 * SUB
    f32, bf16 = jnp.float32, jnp.bfloat16
    vmem = pl.BlockSpec(memory_space=pltpu.VMEM)
    smem = pl.BlockSpec(memory_space=pltpu.SMEM)
    hbm = pl.BlockSpec(memory_space=pltpu.HBM)
    in_gain, out_gain = in_gain.reshape(1, channels), out_gain.reshape(1, channels)

    def limit(mib):
        return pltpu.CompilerParams(vmem_limit_bytes=mib * 1024 * 1024)

    own = pl.pallas_call(
        pack_kernel,
        name="pack",
        out_shape=jax.ShapeDtypeStruct((head + tile, channels), bf16),
        in_specs=[hbm] * 4,
        out_specs=vmem,
        scratch_shapes=[
            pltpu.VMEM(pair_act.shape, pair_act.dtype),
            pltpu.VMEM(pair_mask.shape, jnp.int32),
            pltpu.VMEM((1, channels), f32),
            pltpu.SemaphoreType.DMA((4,)),
        ],
        compiler_params=limit(60),
    )(pair_act, pair_mask, cotangent.reshape(tile, channels), in_gain)
    crop_length, own = lax.optimization_barrier((crop_length, own))

    def move(block, row, col):
        return flip(block, n_row, n_col, row, col)

    twin = move(own, 0, 1)
    front, back, near = pl.pallas_call(
        functools.partial(join_kernel, head),
        name="join",
        out_shape=(
            jax.ShapeDtypeStruct((2, head, channels), bf16),
            jax.ShapeDtypeStruct((2, tile, channels), bf16),
            jax.ShapeDtypeStruct((3,) + own.shape, bf16),
        ),
        in_specs=[vmem] * 5 + [pl.BlockSpec(memory_space=pl.ANY)],
        out_specs=(vmem, vmem, vmem),
        compiler_params=limit(2),
    )(move(own, 3, 0), move(own, 2, 0), move(own, 0, 2), move(own, 1, 0), move(own, 1, 2), twin)
    near_twin = move(near, 0, 1)
    fronts, backs = {0: front}, {0: back}
    for bit in (2, 1):
        fronts.update({col ^ bit: move(stack, 0, bit) for col, stack in fronts.items()})
        backs.update({col ^ bit: move(stack, 0, bit) for col, stack in backs.items()})
    heads = {0: (own, near), 1: (twin, near_twin), 2: (near, near), 3: (near_twin, near_twin)}
    spots = ((None, 1), (None, 1), (0, 2), (0, 2))

    tri, parts, extra = [], [], []
    for col in range(n_col):
        more = (pair_act, in_gain, out_gain) if col == 0 else tri
        more_shapes = () if col > 0 else (
            jax.ShapeDtypeStruct((2, tile, channels), f32),
            jax.ShapeDtypeStruct((SUB, channels), f32),
        )
        tri, *results = pl.pallas_call(
            functools.partial(column_kernel, n_row, n_col, col, spots[col]),
            name=f"column_{col}",
            out_shape=(
                jax.ShapeDtypeStruct((pairs, channels), f32),
                jax.ShapeDtypeStruct((size, channels), f32),
                jax.ShapeDtypeStruct((size, channels), f32),
                jax.ShapeDtypeStruct((4, size, channels), f32),
                jax.ShapeDtypeStruct((size, channels), f32),
                jax.ShapeDtypeStruct((channels, size), bf16),
                *more_shapes,
            ),
            in_specs=[smem] + [vmem] * (4 + len(more)),
            out_specs=(vmem,) * (6 + len(more_shapes)),
            input_output_aliases={5: 0} if col > 0 else {},
            compiler_params=limit(8),
            cost_estimate=pl.CostEstimate(flops=400_000_000, bytes_accessed=1_000_000, transcendentals=0),
        )(crop_length, *heads[col], fronts[col], weights, *more)
        tri = [tri]
        parts += [*heads[col], backs[col], *results[:5]]
        extra += results[5:]

    return pl.pallas_call(
        functools.partial(rest_kernel, n_row, n_col, spots),
        name="rest",
        out_shape=(
            jax.ShapeDtypeStruct(pair_act.shape, bf16),
            jax.ShapeDtypeStruct(pair_act.shape, bf16),
            jax.ShapeDtypeStruct(weights.shape, f32),
        ),
        in_specs=[vmem] * (4 + len(parts)),
        out_specs=(vmem, vmem, vmem),
        scratch_shapes=[
            pltpu.VMEM((pairs, channels), f32),
            pltpu.VMEM((pairs, channels), bf16),
            pltpu.VMEM((pairs, channels), bf16),
            pltpu.VMEM((pairs, 5 * channels), bf16),
        ],
        compiler_params=limit(16),
    )(weights, *extra, *tri, *parts)


def body(n_row, n_col, pair_act, *others):
    tile_rows, tile_cols, channels = pair_act.shape
    pairs = tile_rows * n_row * tile_cols * n_col
    small = pairs * channels * 4 <= 1024 * 1024 and channels == 128
    square = n_row == 4 and n_col == 4 and tile_rows == SUB and tile_cols == SUB
    if small and square:
        return gathered_body(n_row, n_col, pair_act, *others)
    return spread_body(pair_act, *others)


def solution(mesh):
    return jax.shard_map(
        functools.partial(body, mesh.shape["row"], mesh.shape["col"]),
        mesh=mesh,
        in_specs=(
            P(("parts", "row"), "col", None),
            P(("parts", "row"), "col"),
            P("parts"),
            P(),
            P(),
            P(),
            P(("parts", "row"), "col", None),
        ),
        out_specs=(
            P(("parts", "row"), "col", None),
            P(("parts", "row"), "col", None),
            P("parts", None, None),
        ),
        check_vma=False,
    )
```

```python
import functools

import jax
import jax.numpy as jnp
from jax import lax
from jax.experimental import pallas as pl
from jax.experimental.pallas import tpu as pltpu
from jax.sharding import PartitionSpec as P

SUB = 8
EPS = 1e-05


def normalize(values):
    average = jnp.mean(values, axis=-1, keepdims=True)
    centered = values - average
    inverse = lax.rsqrt(jnp.mean(centered * centered, axis=-1, keepdims=True) + 1e-05)
    return (centered * inverse, inverse)


def norm_back(grad_hat, values_hat, inverse):
    first = jnp.mean(grad_hat, axis=-1, keepdims=True)
    second = jnp.mean(grad_hat * values_hat, axis=-1, keepdims=True)
    return (grad_hat - first - values_hat * second) * inverse


def gate_back(grad_act, proj_value, proj_gate, keep_mask):
    gate_sig = jax.nn.sigmoid(proj_gate)
    masked = grad_act * keep_mask
    grad_value = (masked * gate_sig).astype(jnp.bfloat16)
    grad_gate = (masked * proj_value * gate_sig * (1.0 - gate_sig)).astype(jnp.bfloat16)
    return (grad_value, grad_gate)


def spread_body(pair_act, pair_mask, crop_length, weights, in_gain, out_gain, cotangent):
    tile_rows, tile_cols, channels = pair_act.shape
    residues = tile_rows * lax.axis_size("row")
    row_pos = lax.axis_index("row") * tile_rows + jnp.arange(tile_rows, dtype=jnp.int32)
    col_pos = lax.axis_index("col") * tile_cols + jnp.arange(tile_cols, dtype=jnp.int32)
    row_in = (row_pos < crop_length[0]).astype(jnp.float32)
    col_in = (col_pos < crop_length[0]).astype(jnp.float32)
    keep_mask = (pair_mask.astype(jnp.float32) * row_in[:, None] * col_in[None, :])[:, :, None]
    z_hat, z_inverse = normalize(pair_act.astype(jnp.float32))
    normed = (z_hat * in_gain).astype(jnp.bfloat16)
    flat_norm = normed.reshape(tile_rows * tile_cols, channels)
    projections = jnp.einsum(
        "pc,scd->spd", flat_norm, weights[:5], preferred_element_type=jnp.float32
    )
    projections = projections.reshape(5, tile_rows, tile_cols, channels)
    left_act = (jax.nn.sigmoid(projections[1]) * projections[0] * keep_mask).astype(jnp.bfloat16)
    right_act = (jax.nn.sigmoid(projections[3]) * projections[2] * keep_mask).astype(jnp.bfloat16)
    partial_value = jnp.einsum(
        "ikh,jkh->ijh",
        left_act,
        lax.all_gather(right_act, "row", axis=0, tiled=True),
        preferred_element_type=jnp.float32,
    )
    tri_sum = lax.psum_scatter(
        partial_value.astype(jnp.bfloat16), "col", scatter_dimension=1, tiled=True
    ).astype(jnp.float32)
    x_hat, x_inverse = normalize(tri_sum)
    normed_out = (x_hat * out_gain).astype(jnp.bfloat16)
    flat_out = normed_out.reshape(tile_rows * tile_cols, channels)
    update_lin = jnp.dot(flat_out, weights[5], preferred_element_type=jnp.float32)
    update_lin = update_lin.reshape(tile_rows, tile_cols, channels)
    out_gate = jax.nn.sigmoid(projections[4])
    update = (out_gate * update_lin).astype(jnp.bfloat16)
    cot_value = cotangent.astype(jnp.float32)
    grad_lin = (cot_value * out_gate).astype(jnp.bfloat16)
    grad_gate_out = (cot_value * update_lin * out_gate * (1.0 - out_gate)).astype(jnp.bfloat16)
    flat_lin = grad_lin.reshape(tile_rows * tile_cols, channels)
    grad_norm_out = jnp.einsum(
        "pd,cd->pc", flat_lin, weights[5], preferred_element_type=jnp.float32
    )
    grad_norm_out = grad_norm_out.reshape(tile_rows, tile_cols, channels)
    grad_tri = norm_back(grad_norm_out * out_gain, x_hat, x_inverse).astype(jnp.bfloat16)
    grad_full = lax.all_gather(grad_tri, "col", axis=1, tiled=True)
    grad_slab = grad_full
    grad_left = jnp.einsum(
        "ijh,jkh->ikh",
        grad_slab,
        lax.all_gather(right_act, "row", axis=0, tiled=True),
        preferred_element_type=jnp.float32,
    )
    grad_slab = grad_full
    grad_right = lax.psum_scatter(
        jnp.einsum("ijh,ikh->jkh", grad_slab, left_act, preferred_element_type=jnp.float32).astype(
            jnp.bfloat16
        ),
        "row",
        scatter_dimension=0,
        tiled=True,
    ).astype(jnp.float32)
    grad_pa, grad_ga = gate_back(grad_left, projections[0], projections[1], keep_mask)
    grad_pb, grad_gb = gate_back(grad_right, projections[2], projections[3], keep_mask)
    grads = jnp.stack([grad_pa, grad_ga, grad_pb, grad_gb, grad_gate_out]).reshape(
        5, tile_rows * tile_cols, channels
    )
    grad_normed = jnp.einsum("spd,scd->pc", grads, weights[:5], preferred_element_type=jnp.float32)
    grad_normed = grad_normed.reshape(tile_rows, tile_cols, channels)
    pair_grad = norm_back(grad_normed * in_gain, z_hat, z_inverse).astype(jnp.bfloat16)
    local_in = jnp.einsum("pc,spd->scd", flat_norm, grads, preferred_element_type=jnp.float32)
    local_out = jnp.dot(flat_out.T, flat_lin, preferred_element_type=jnp.float32)
    local_grads = jnp.concatenate([local_in, local_out[None]], axis=0) / residues
    weight_grad = lax.psum(local_grads, ("row", "col"))
    return (update, pair_grad, weight_grad)


def pack_kernel(act_hbm, mask_hbm, cot_hbm, gain_hbm, out_ref, act_ref, mask_ref, gain_ref, sems):
    tile_rows, tile_cols, channels = act_ref.shape
    pairs = tile_rows * tile_cols
    head = out_ref.shape[0] - pairs
    pack_copies = [
        pltpu.make_async_copy(act_hbm, act_ref, sems.at[0]),
        pltpu.make_async_copy(gain_hbm, gain_ref, sems.at[1]),
        pltpu.make_async_copy(mask_hbm, mask_ref, sems.at[2]),
        pltpu.make_async_copy(cot_hbm, out_ref.at[head : head + pairs], sems.at[3]),
    ]
    for copy in pack_copies:
        copy.start()
    for copy in pack_copies:
        copy.wait()
    z_hat, _ = normalize(act_ref[...].astype(jnp.float32).reshape(pairs, channels))
    out_ref[0:pairs] = (z_hat * gain_ref[...]).astype(jnp.bfloat16)
    keep = mask_ref[...].astype(jnp.float32)
    wide = jnp.concatenate([keep, jnp.zeros((tile_rows, channels - tile_cols), jnp.float32)], axis=1)
    tall = jnp.concatenate([wide, jnp.zeros((channels - tile_rows, channels), jnp.float32)], axis=0)
    out_ref[pairs:head] = tall.T[0 : head - pairs].astype(jnp.bfloat16)


def join_kernel(own_ref, twin_ref, out_ref):
    tile = SUB * SUB
    refs = (own_ref, twin_ref)
    for at, ref in enumerate(refs):
        out_ref[at * tile : (at + 1) * tile] = ref[0:tile]
        spot = 2 * tile + 2 * SUB + at * tile
        out_ref[spot : spot + tile] = ref[tile + 2 * SUB :]
    masks = [ref[tile : tile + 2 * SUB].astype(jnp.float32)[0:SUB] for ref in refs]
    out_ref[2 * tile : 2 * tile + 2 * SUB] = jnp.concatenate(masks, axis=0).astype(jnp.bfloat16)


def normed_rows(ref, sub):
    return ref[sub * SUB * SUB : (sub + 1) * SUB * SUB]


def mask_rows(ref, sub):
    at = ref.shape[0] // 2 // (SUB * SUB) * SUB * SUB
    return ref[at : at + 2 * SUB].astype(jnp.float32)[sub * SUB : (sub + 1) * SUB]


def cot_rows(ref, sub):
    at = ref.shape[0] // 2 // (SUB * SUB) * SUB * SUB + 2 * SUB
    return ref[at + sub * SUB * SUB : at + (sub + 1) * SUB * SUB]


def chip_rows(rows_of, refs, core, direct_on):
    if direct_on is None:
        return rows_of(refs[min(core, len(refs) - 1)], core if len(refs) == 1 else 0)
    here = lax.axis_index("col") % 2 == direct_on
    return jnp.where(here, rows_of(refs[0], core), rows_of(refs[1], 1 - core))


def split_chips(refs, chips):
    split, at = [], 0
    for width, direct_on in chips:
        split.append((refs[at : at + width], direct_on))
        at += width
    return split


def triangle(blocks, groups, steps, vectors_at, factors_at, start_at, store_at):
    def block(a, _):
        def step(q, totals):
            totals = list(totals)
            vectors = vectors_at(q)
            factors = factors_at(a, q)
            for inner in range(SUB):
                rows = [vectors(g, inner) for g in range(groups)]
                for lane in range(SUB):
                    factor = factors(lane, inner)
                    for g in range(groups):
                        at = lane * groups + g
                        totals[at] = totals[at] + factor * rows[g]
            return tuple(totals)

        totals = tuple(start_at(a, g, lane) for lane in range(SUB) for g in range(groups))
        totals = step(0, totals) if steps == 1 else lax.fori_loop(0, steps, step, totals)
        for g in range(groups):
            store_at(a, g, [totals[lane * groups + g] for lane in range(SUB)])
        return 0

    lax.fori_loop(0, blocks, block, 0)


def spread(ref, row):
    return jnp.broadcast_to(ref[pl.ds(row, 1), :], (SUB, ref.shape[-1]))


def line(ref, row):
    return ref[pl.ds(pl.multiple_of(row, SUB), SUB), :]


def column_kernel(n_row, n_col, col, chips, crop_ref, weights_ref, *refs):
    count = sum(width for width, _ in chips)
    chip_refs, refs = refs[:count], refs[count:]
    if col == 0:
        act_ref, in_gain_ref, out_gain_ref, *refs, own_ref, gains_ref = refs
        z_hat, z_inverse = normalize(act_ref[...].astype(jnp.float32).reshape(own_ref.shape[1:]))
        own_ref[0] = z_hat
        own_ref[1] = jnp.broadcast_to(z_inverse, z_hat.shape)
        gains_ref[0:1] = in_gain_ref[...]
        gains_ref[1:2] = out_gain_ref[...]
    tri_in, (tri_ref, left_ref, right_ref, side_ref, gate_ref, flip_ref) = refs[:-6], refs[-6:]
    channels = weights_ref.shape[-1]
    tile = SUB * SUB
    size = n_row * tile
    bf16, f32 = jnp.bfloat16, jnp.float32
    row_me, col_me = lax.axis_index("row"), lax.axis_index("col")
    chip_list = split_chips(chip_refs, chips)
    normed = jnp.concatenate([chip_rows(normed_rows, chip, col % 2, on) for chip, on in chip_list], axis=0)
    flip_ref[...] = normed.astype(f32).T.astype(bf16)
    crop = crop_ref[0]
    col_offset = lax.broadcasted_iota(jnp.int32, (SUB, channels), 0)
    row_offset = lax.broadcasted_iota(jnp.int32, (SUB, channels), 1)
    cols_in = col_offset < crop - (col_me ^ col) * SUB
    kept = []
    for b, (chip, on) in enumerate(chip_list):
        keep = chip_rows(mask_rows, chip, col % 2, on)
        rows_in = row_offset < crop - (row_me ^ b) * SUB
        keep = jnp.where(rows_in & cols_in, keep, 0.0)
        kept += [jnp.broadcast_to(keep[:, at : at + 1], (SUB, channels)) for at in range(SUB)]
    kept = jnp.concatenate(kept, axis=0)
    for side, act_ref in enumerate((left_ref, right_ref)):
        pair = jnp.concatenate([weights_ref[2 * side], weights_ref[2 * side + 1]], axis=1)
        proj = jnp.dot(normed, pair, preferred_element_type=f32)
        gate = jax.nn.sigmoid(proj[:, channels:])
        masked = gate * kept
        act = masked * proj[:, :channels]
        act_ref[...] = act.astype(bf16).astype(f32)
        side_ref[2 * side] = masked
        side_ref[2 * side + 1] = act * (1.0 - gate)
    gate_ref[...] = jax.nn.sigmoid(jnp.dot(normed, weights_ref[4], preferred_element_type=f32))
    turn = row_me ^ col_me

    def flipped(q):
        firsts = [(turn ^ g) * tile for g in range(n_col)]
        return lambda g, inner: right_ref[pl.ds(firsts[g] + inner, SUB, stride=SUB), :]

    def along(a, q):
        return lambda lane, inner: spread(left_ref, a * tile + lane * SUB + inner)

    def start(a, g, lane):
        if len(tri_in) == 0:
            return jnp.zeros((SUB, channels), f32)
        return line(tri_in[0], g * size + a * tile + lane * SUB)

    def store(a, g, values):
        for lane in range(SUB):
            tri_ref[pl.ds(pl.multiple_of(g * size + a * tile + lane * SUB, SUB), SUB), :] = values[lane]

    triangle(n_row, n_col, 1, flipped, along, start, store)


def rest_kernel(n_row, n_col, chips, weights_ref, own_ref, gains_ref, tri_ref, *refs):
    chip_lists, columns = [], []
    for col in range(n_col):
        count = sum(width for width, _ in chips[col // 2])
        chip_lists.append(split_chips(refs[:count], chips[col // 2]))
        columns.append(refs[count : count + 5])
        refs = refs[count + 5 :]
    update_ref, pair_grad_ref, weight_grad_ref, back_ref, hat_ref, lin_ref, d_ref = refs
    channels = tri_ref.shape[-1]
    tile = SUB * SUB
    size = n_row * tile
    residues = n_row * SUB
    bf16, f32 = jnp.bfloat16, jnp.float32
    turn = lax.axis_index("row") ^ lax.axis_index("col")
    out_gain = gains_ref[1:2]
    for col, (_, _, _, gate_ref, _) in enumerate(columns):
        rows = slice(col * size, (col + 1) * size)
        x_hat, inverse = normalize(tri_ref[rows, :])
        normed_out = (x_hat * out_gain).astype(bf16)
        hat_ref[rows, :] = normed_out
        lin = jnp.dot(normed_out, weights_ref[5], preferred_element_type=f32)
        out_gate = gate_ref[...]
        if col == 0:
            update_ref[...] = (out_gate[0:tile] * lin[0:tile]).astype(bf16).reshape(update_ref.shape)
        cots = [chip_rows(cot_rows, chip, col % 2, on) for chip, on in chip_lists[col]]
        cot = jnp.concatenate(cots, axis=0).astype(f32)
        grad = cot * out_gate
        grad_lin = grad.astype(bf16)
        lin_ref[rows, :] = grad_lin
        d_ref[rows, 4 * channels : 5 * channels] = (grad * lin * (1.0 - out_gate)).astype(bf16)
        back = lax.dot_general(grad_lin, weights_ref[5], (((1,), (1,)), ((), ())), preferred_element_type=f32)
        back_ref[rows, :] = norm_back(back * out_gain, x_hat, inverse).astype(bf16).astype(f32)

    lefts, rights, sides = [[column[at] for column in columns] for at in (0, 1, 2)]

    def zero(a, g, lane):
        return jnp.zeros((SUB, channels), f32)

    def store(side):
        def put(a, g, values):
            for lane in range(0, SUB, 2):
                at = pl.multiple_of(a * tile + lane * SUB, 2 * SUB)
                both = jnp.concatenate(values[lane : lane + 2], axis=0)
                rows = pl.ds(pl.multiple_of(g * size + at, 2 * SUB), 2 * SUB)
                for kind in range(2):
                    spot = (2 * side + kind) * channels
                    scaled = both * sides[g][2 * side + kind, pl.ds(at, 2 * SUB), :]
                    d_ref[rows, spot : spot + channels] = scaled.astype(bf16)
        return put

    def by_right(q):
        return lambda g, inner: line(rights[g], (q ^ turn) * tile + inner * SUB)

    def by_left(q):
        return lambda g, inner: line(lefts[g], q * tile + inner * SUB)

    def along(a, q):
        return lambda lane, inner: spread(back_ref, q * size + a * tile + lane * SUB + inner)

    def down(a, q):
        return lambda lane, inner: spread(back_ref, (a ^ turn) * size + q * tile + inner * SUB + lane)

    triangle(n_row, n_col, n_col, by_right, along, zero, store(0))
    triangle(n_row, n_col, n_row, by_left, down, zero, store(1))

    scale = 1.0 / residues
    flipped = jnp.concatenate([column[4][...] for column in columns], axis=1)
    sums = jnp.dot(flipped, d_ref[...], preferred_element_type=f32) * scale
    for s in range(5):
        weight_grad_ref[s] = sums[:, s * channels : (s + 1) * channels]
    weight_grad_ref[5] = scale * lax.dot_general(
        hat_ref[...], lin_ref[...], (((0,), (0,)), ((), ())), preferred_element_type=f32
    )
    total = jnp.zeros((tile, channels), f32)
    for s in range(5):
        total = total + lax.dot_general(
            d_ref[0:tile, s * channels : (s + 1) * channels], weights_ref[s],
            (((1,), (1,)), ((), ())), preferred_element_type=f32,
        )
    grad = norm_back(total * gains_ref[0:1], own_ref[0], own_ref[1])
    pair_grad_ref[...] = grad.astype(bf16).reshape(pair_grad_ref.shape)


def flip(block, n_row, n_col, even, odd):
    pairs = []
    for row in range(n_row):
        for col in range(n_col):
            shift = odd if col % 2 else even
            pairs.append((row * n_col + col, (row ^ shift[0]) * n_col + (col ^ shift[1])))
    return lax.ppermute(block, ("row", "col"), pairs)


def gathered_body(n_row, n_col, pair_act, pair_mask, crop_length, weights, in_gain, out_gain, cotangent):
    tile_rows, tile_cols, channels = pair_act.shape
    tile = tile_rows * tile_cols
    size = n_row * tile
    pairs = size * n_col
    head = tile + 2 * SUB
    f32, bf16 = jnp.float32, jnp.bfloat16
    vmem = pl.BlockSpec(memory_space=pltpu.VMEM)
    smem = pl.BlockSpec(memory_space=pltpu.SMEM)
    hbm = pl.BlockSpec(memory_space=pltpu.HBM)
    in_gain, out_gain = in_gain.reshape(1, channels), out_gain.reshape(1, channels)

    def limit(mib):
        return pltpu.CompilerParams(vmem_limit_bytes=mib * 1024 * 1024)

    own = pl.pallas_call(
        pack_kernel,
        name="pack",
        out_shape=jax.ShapeDtypeStruct((head + tile, channels), bf16),
        in_specs=[hbm] * 4,
        out_specs=vmem,
        scratch_shapes=[
            pltpu.VMEM(pair_act.shape, pair_act.dtype),
            pltpu.VMEM(pair_mask.shape, jnp.int32),
            pltpu.VMEM((1, channels), f32),
            pltpu.SemaphoreType.DMA((4,)),
        ],
        compiler_params=limit(60),
    )(pair_act, pair_mask, cotangent.reshape(tile, channels), in_gain)
    crop_length, own = lax.optimization_barrier((crop_length, own))

    def move(block, even, odd):
        return flip(block, n_row, n_col, even, odd)

    def other(block):
        return move(block, (0, 1), (0, 1))

    both = pl.pallas_call(
        join_kernel,
        name="join",
        out_shape=jax.ShapeDtypeStruct((2 * own.shape[0] - 2 * SUB, channels), bf16),
        in_specs=[vmem] * 2,
        out_specs=vmem,
        compiler_params=limit(2),
    )(own, other(own))
    far = move(both, (2, 0), (3, 0))
    near = move(both, (1, 0), (0, 2))
    cross = move(both, (1, 2), (2, 2))
    last = move(own, (3, 2), (3, 2))
    far, near, cross, last = [(block, other(block)) for block in (far, near, cross, last)]
    chips = (((1, None), (2, 0), (2, 0), (2, 1)), ((2, 1), (2, 0), (2, 1), (2, None)))
    sources = ((both, *near, *far, *far), (*near, *cross, *cross, *last))

    tri, parts, extra = [], [], []
    for col in range(n_col):
        more = (pair_act, in_gain, out_gain) if col == 0 else tri
        more_shapes = () if col > 0 else (
            jax.ShapeDtypeStruct((2, tile, channels), f32),
            jax.ShapeDtypeStruct((SUB, channels), f32),
        )
        tri, *results = pl.pallas_call(
            functools.partial(column_kernel, n_row, n_col, col, chips[col // 2]),
            name=f"column_{col}",
            out_shape=(
                jax.ShapeDtypeStruct((pairs, channels), f32),
                jax.ShapeDtypeStruct((size, channels), f32),
                jax.ShapeDtypeStruct((size, channels), f32),
                jax.ShapeDtypeStruct((4, size, channels), f32),
                jax.ShapeDtypeStruct((size, channels), f32),
                jax.ShapeDtypeStruct((channels, size), bf16),
                *more_shapes,
            ),
            in_specs=[smem] + [vmem] * (1 + len(sources[col // 2]) + len(more)),
            out_specs=(vmem,) * (6 + len(more_shapes)),
            input_output_aliases={2 + len(sources[col // 2]): 0} if col > 0 else {},
            compiler_params=limit(8),
            cost_estimate=pl.CostEstimate(flops=400_000_000, bytes_accessed=1_000_000, transcendentals=0),
        )(crop_length, weights, *sources[col // 2], *more)
        tri = [tri]
        parts += [*sources[col // 2], *results[:5]]
        extra += results[5:]

    return pl.pallas_call(
        functools.partial(rest_kernel, n_row, n_col, chips),
        name="rest",
        out_shape=(
            jax.ShapeDtypeStruct(pair_act.shape, bf16),
            jax.ShapeDtypeStruct(pair_act.shape, bf16),
            jax.ShapeDtypeStruct(weights.shape, f32),
        ),
        in_specs=[vmem] * (4 + len(parts)),
        out_specs=(vmem, vmem, vmem),
        scratch_shapes=[
            pltpu.VMEM((pairs, channels), f32),
            pltpu.VMEM((pairs, channels), bf16),
            pltpu.VMEM((pairs, channels), bf16),
            pltpu.VMEM((pairs, 5 * channels), bf16),
        ],
        compiler_params=limit(16),
    )(weights, *extra, *tri, *parts)


def body(n_row, n_col, pair_act, *others):
    tile_rows, tile_cols, channels = pair_act.shape
    pairs = tile_rows * n_row * tile_cols * n_col
    small = pairs * channels * 4 <= 1024 * 1024 and channels == 128
    square = n_row == 4 and n_col == 4 and tile_rows == SUB and tile_cols == SUB
    if small and square:
        return gathered_body(n_row, n_col, pair_act, *others)
    return spread_body(pair_act, *others)


def solution(mesh):
    return jax.shard_map(
        functools.partial(body, mesh.shape["row"], mesh.shape["col"]),
        mesh=mesh,
        in_specs=(
            P(("parts", "row"), "col", None),
            P(("parts", "row"), "col"),
            P("parts"),
            P(),
            P(),
            P(),
            P(("parts", "row"), "col", None),
        ),
        out_specs=(
            P(("parts", "row"), "col", None),
            P(("parts", "row"), "col", None),
            P("parts", None, None),
        ),
        check_vma=False,
    )
```

```python
import functools

import jax
import jax.numpy as jnp
from jax import lax
from jax.experimental import pallas as pl
from jax.experimental.pallas import tpu as pltpu
from jax.sharding import PartitionSpec as P

SUB = 8
EPS = 1e-05


def normalize(values):
    average = jnp.mean(values, axis=-1, keepdims=True)
    centered = values - average
    inverse = lax.rsqrt(jnp.mean(centered * centered, axis=-1, keepdims=True) + 1e-05)
    return (centered * inverse, inverse)


def norm_back(grad_hat, values_hat, inverse):
    first = jnp.mean(grad_hat, axis=-1, keepdims=True)
    second = jnp.mean(grad_hat * values_hat, axis=-1, keepdims=True)
    return (grad_hat - first - values_hat * second) * inverse


def gate_back(grad_act, proj_value, proj_gate, keep_mask):
    gate_sig = jax.nn.sigmoid(proj_gate)
    masked = grad_act * keep_mask
    grad_value = (masked * gate_sig).astype(jnp.bfloat16)
    grad_gate = (masked * proj_value * gate_sig * (1.0 - gate_sig)).astype(jnp.bfloat16)
    return (grad_value, grad_gate)


def spread_body(pair_act, pair_mask, crop_length, weights, in_gain, out_gain, cotangent):
    tile_rows, tile_cols, channels = pair_act.shape
    residues = tile_rows * lax.axis_size("row")
    row_pos = lax.axis_index("row") * tile_rows + jnp.arange(tile_rows, dtype=jnp.int32)
    col_pos = lax.axis_index("col") * tile_cols + jnp.arange(tile_cols, dtype=jnp.int32)
    row_in = (row_pos < crop_length[0]).astype(jnp.float32)
    col_in = (col_pos < crop_length[0]).astype(jnp.float32)
    keep_mask = (pair_mask.astype(jnp.float32) * row_in[:, None] * col_in[None, :])[:, :, None]
    z_hat, z_inverse = normalize(pair_act.astype(jnp.float32))
    normed = (z_hat * in_gain).astype(jnp.bfloat16)
    flat_norm = normed.reshape(tile_rows * tile_cols, channels)
    projections = jnp.einsum(
        "pc,scd->spd", flat_norm, weights[:5], preferred_element_type=jnp.float32
    )
    projections = projections.reshape(5, tile_rows, tile_cols, channels)
    left_act = (jax.nn.sigmoid(projections[1]) * projections[0] * keep_mask).astype(jnp.bfloat16)
    right_act = (jax.nn.sigmoid(projections[3]) * projections[2] * keep_mask).astype(jnp.bfloat16)
    partial_value = jnp.einsum(
        "ikh,jkh->ijh",
        left_act,
        lax.all_gather(right_act, "row", axis=0, tiled=True),
        preferred_element_type=jnp.float32,
    )
    tri_sum = lax.psum_scatter(
        partial_value.astype(jnp.bfloat16), "col", scatter_dimension=1, tiled=True
    ).astype(jnp.float32)
    x_hat, x_inverse = normalize(tri_sum)
    normed_out = (x_hat * out_gain).astype(jnp.bfloat16)
    flat_out = normed_out.reshape(tile_rows * tile_cols, channels)
    update_lin = jnp.dot(flat_out, weights[5], preferred_element_type=jnp.float32)
    update_lin = update_lin.reshape(tile_rows, tile_cols, channels)
    out_gate = jax.nn.sigmoid(projections[4])
    update = (out_gate * update_lin).astype(jnp.bfloat16)
    cot_value = cotangent.astype(jnp.float32)
    grad_lin = (cot_value * out_gate).astype(jnp.bfloat16)
    grad_gate_out = (cot_value * update_lin * out_gate * (1.0 - out_gate)).astype(jnp.bfloat16)
    flat_lin = grad_lin.reshape(tile_rows * tile_cols, channels)
    grad_norm_out = jnp.einsum(
        "pd,cd->pc", flat_lin, weights[5], preferred_element_type=jnp.float32
    )
    grad_norm_out = grad_norm_out.reshape(tile_rows, tile_cols, channels)
    grad_tri = norm_back(grad_norm_out * out_gain, x_hat, x_inverse).astype(jnp.bfloat16)
    grad_full = lax.all_gather(grad_tri, "col", axis=1, tiled=True)
    grad_slab = grad_full
    grad_left = jnp.einsum(
        "ijh,jkh->ikh",
        grad_slab,
        lax.all_gather(right_act, "row", axis=0, tiled=True),
        preferred_element_type=jnp.float32,
    )
    grad_slab = grad_full
    grad_right = lax.psum_scatter(
        jnp.einsum("ijh,ikh->jkh", grad_slab, left_act, preferred_element_type=jnp.float32).astype(
            jnp.bfloat16
        ),
        "row",
        scatter_dimension=0,
        tiled=True,
    ).astype(jnp.float32)
    grad_pa, grad_ga = gate_back(grad_left, projections[0], projections[1], keep_mask)
    grad_pb, grad_gb = gate_back(grad_right, projections[2], projections[3], keep_mask)
    grads = jnp.stack([grad_pa, grad_ga, grad_pb, grad_gb, grad_gate_out]).reshape(
        5, tile_rows * tile_cols, channels
    )
    grad_normed = jnp.einsum("spd,scd->pc", grads, weights[:5], preferred_element_type=jnp.float32)
    grad_normed = grad_normed.reshape(tile_rows, tile_cols, channels)
    pair_grad = norm_back(grad_normed * in_gain, z_hat, z_inverse).astype(jnp.bfloat16)
    local_in = jnp.einsum("pc,spd->scd", flat_norm, grads, preferred_element_type=jnp.float32)
    local_out = jnp.dot(flat_out.T, flat_lin, preferred_element_type=jnp.float32)
    local_grads = jnp.concatenate([local_in, local_out[None]], axis=0) / residues
    weight_grad = lax.psum(local_grads, ("row", "col"))
    return (update, pair_grad, weight_grad)


def pack_kernel(act_hbm, mask_hbm, cot_hbm, gain_hbm, out_ref, act_ref, mask_ref, gain_ref, sems):
    tile_rows, tile_cols, channels = act_ref.shape
    pairs = tile_rows * tile_cols
    head = out_ref.shape[0] - pairs
    pack_copies = [
        pltpu.make_async_copy(act_hbm, act_ref, sems.at[0]),
        pltpu.make_async_copy(gain_hbm, gain_ref, sems.at[1]),
        pltpu.make_async_copy(mask_hbm, mask_ref, sems.at[2]),
        pltpu.make_async_copy(cot_hbm, out_ref.at[head : head + pairs], sems.at[3]),
    ]
    for copy in pack_copies:
        copy.start()
    for copy in pack_copies:
        copy.wait()
    z_hat, _ = normalize(act_ref[...].astype(jnp.float32).reshape(pairs, channels))
    out_ref[0:pairs] = (z_hat * gain_ref[...]).astype(jnp.bfloat16)
    keep = mask_ref[...].astype(jnp.float32)
    wide = jnp.concatenate([keep, jnp.zeros((tile_rows, channels - tile_cols), jnp.float32)], axis=1)
    tall = jnp.concatenate([wide, jnp.zeros((channels - tile_rows, channels), jnp.float32)], axis=0)
    out_ref[pairs:head] = tall.T[0 : head - pairs].astype(jnp.bfloat16)


def copy_kernel(in_ref, out_ref):
    out_ref[...] = in_ref[...]


def join_kernel(own_ref, twin_ref, out_ref):
    tile = SUB * SUB
    refs = (own_ref, twin_ref)
    for at, ref in enumerate(refs):
        out_ref[at * tile : (at + 1) * tile] = ref[0:tile]
        spot = 2 * tile + 2 * SUB + at * tile
        out_ref[spot : spot + tile] = ref[tile + 2 * SUB :]
    masks = [ref[tile : tile + 2 * SUB].astype(jnp.float32)[0:SUB] for ref in refs]
    out_ref[2 * tile : 2 * tile + 2 * SUB] = jnp.concatenate(masks, axis=0).astype(jnp.bfloat16)


def normed_rows(ref, sub):
    return ref[sub * SUB * SUB : (sub + 1) * SUB * SUB]


def mask_rows(ref, sub):
    at = ref.shape[0] // 2 // (SUB * SUB) * SUB * SUB
    return ref[at : at + 2 * SUB].astype(jnp.float32)[sub * SUB : (sub + 1) * SUB]


def cot_rows(ref, sub):
    at = ref.shape[0] // 2 // (SUB * SUB) * SUB * SUB + 2 * SUB
    return ref[at + sub * SUB * SUB : at + (sub + 1) * SUB * SUB]


def chip_rows(rows_of, refs, core, direct_on):
    if direct_on is None:
        return rows_of(refs[min(core, len(refs) - 1)], core if len(refs) == 1 else 0)
    here = lax.axis_index("col") % 2 == direct_on
    return jnp.where(here, rows_of(refs[0], core), rows_of(refs[1], 1 - core))


def split_chips(refs, chips):
    split, at = [], 0
    for width, direct_on in chips:
        split.append((refs[at : at + width], direct_on))
        at += width
    return split


def triangle(blocks, groups, steps, vectors_at, factors_at, start_at, store_at):
    def block(a, _):
        def step(q, totals):
            totals = list(totals)
            vectors = vectors_at(q)
            factors = factors_at(a, q)
            for inner in range(SUB):
                rows = [vectors(g, inner) for g in range(groups)]
                for lane in range(SUB):
                    factor = factors(lane, inner)
                    for g in range(groups):
                        at = lane * groups + g
                        totals[at] = totals[at] + factor * rows[g]
            return tuple(totals)

        totals = tuple(start_at(a, g, lane) for lane in range(SUB) for g in range(groups))
        totals = step(0, totals) if steps == 1 else lax.fori_loop(0, steps, step, totals)
        for g in range(groups):
            store_at(a, g, [totals[lane * groups + g] for lane in range(SUB)])
        return 0

    lax.fori_loop(0, blocks, block, 0)


def spread(ref, row):
    return jnp.broadcast_to(ref[pl.ds(row, 1), :], (SUB, ref.shape[-1]))


def line(ref, row):
    return ref[pl.ds(pl.multiple_of(row, SUB), SUB), :]


def column_kernel(n_row, n_col, col, chips, crop_ref, weights_ref, *refs):
    count = sum(width for width, _ in chips)
    chip_refs, refs = refs[:count], refs[count:]
    if col == 0:
        act_ref, in_gain_ref, out_gain_ref, *refs, own_ref, gains_ref = refs
        z_hat, z_inverse = normalize(act_ref[...].astype(jnp.float32).reshape(own_ref.shape[1:]))
        own_ref[0] = z_hat
        own_ref[1] = jnp.broadcast_to(z_inverse, z_hat.shape)
        gains_ref[0:1] = in_gain_ref[...]
        gains_ref[1:2] = out_gain_ref[...]
    tri_in, (tri_ref, left_ref, right_ref, side_ref, gate_ref, flip_ref) = refs[:-6], refs[-6:]
    channels = weights_ref.shape[-1]
    tile = SUB * SUB
    size = n_row * tile
    bf16, f32 = jnp.bfloat16, jnp.float32
    row_me, col_me = lax.axis_index("row"), lax.axis_index("col")
    chip_list = split_chips(chip_refs, chips)
    normed = jnp.concatenate([chip_rows(normed_rows, chip, col % 2, on) for chip, on in chip_list], axis=0)
    flip_ref[...] = normed.astype(f32).T.astype(bf16)
    crop = crop_ref[0]
    col_offset = lax.broadcasted_iota(jnp.int32, (SUB, channels), 0)
    row_offset = lax.broadcasted_iota(jnp.int32, (SUB, channels), 1)
    cols_in = col_offset < crop - (col_me ^ col) * SUB
    kept = []
    for b, (chip, on) in enumerate(chip_list):
        keep = chip_rows(mask_rows, chip, col % 2, on)
        rows_in = row_offset < crop - (row_me ^ b) * SUB
        keep = jnp.where(rows_in & cols_in, keep, 0.0)
        kept += [jnp.broadcast_to(keep[:, at : at + 1], (SUB, channels)) for at in range(SUB)]
    kept = jnp.concatenate(kept, axis=0)
    for side, act_ref in enumerate((left_ref, right_ref)):
        pair = jnp.concatenate([weights_ref[2 * side], weights_ref[2 * side + 1]], axis=1)
        proj = jnp.dot(normed, pair, preferred_element_type=f32)
        gate = jax.nn.sigmoid(proj[:, channels:])
        masked = gate * kept
        act = masked * proj[:, :channels]
        act_ref[...] = act.astype(bf16).astype(f32)
        side_ref[2 * side] = masked
        side_ref[2 * side + 1] = act * (1.0 - gate)
    gate_ref[...] = jax.nn.sigmoid(jnp.dot(normed, weights_ref[4], preferred_element_type=f32))
    turn = row_me ^ col_me

    def flipped(q):
        firsts = [(turn ^ g) * tile for g in range(n_col)]
        return lambda g, inner: right_ref[pl.ds(firsts[g] + inner, SUB, stride=SUB), :]

    def along(a, q):
        return lambda lane, inner: spread(left_ref, a * tile + lane * SUB + inner)

    def start(a, g, lane):
        if len(tri_in) == 0:
            return jnp.zeros((SUB, channels), f32)
        return line(tri_in[0], g * size + a * tile + lane * SUB)

    def store(a, g, values):
        for lane in range(SUB):
            tri_ref[pl.ds(pl.multiple_of(g * size + a * tile + lane * SUB, SUB), SUB), :] = values[lane]

    triangle(n_row, n_col, 1, flipped, along, start, store)


def rest_kernel(n_row, n_col, chips, weights_ref, own_ref, gains_ref, tri_ref, *refs):
    chip_lists, columns = [], []
    for col in range(n_col):
        count = sum(width for width, _ in chips[col // 2])
        chip_lists.append(split_chips(refs[:count], chips[col // 2]))
        columns.append(refs[count : count + 5])
        refs = refs[count + 5 :]
    update_ref, pair_grad_ref, weight_grad_ref, back_ref, hat_ref, lin_ref, d_ref = refs
    channels = tri_ref.shape[-1]
    tile = SUB * SUB
    size = n_row * tile
    residues = n_row * SUB
    bf16, f32 = jnp.bfloat16, jnp.float32
    turn = lax.axis_index("row") ^ lax.axis_index("col")
    out_gain = gains_ref[1:2]
    for col, (_, _, _, gate_ref, _) in enumerate(columns):
        rows = slice(col * size, (col + 1) * size)
        x_hat, inverse = normalize(tri_ref[rows, :])
        normed_out = (x_hat * out_gain).astype(bf16)
        hat_ref[rows, :] = normed_out
        lin = jnp.dot(normed_out, weights_ref[5], preferred_element_type=f32)
        out_gate = gate_ref[...]
        if col == 0:
            update_ref[...] = (out_gate[0:tile] * lin[0:tile]).astype(bf16).reshape(update_ref.shape)
        cots = [chip_rows(cot_rows, chip, col % 2, on) for chip, on in chip_lists[col]]
        cot = jnp.concatenate(cots, axis=0).astype(f32)
        grad = cot * out_gate
        grad_lin = grad.astype(bf16)
        lin_ref[rows, :] = grad_lin
        d_ref[rows, 4 * channels : 5 * channels] = (grad * lin * (1.0 - out_gate)).astype(bf16)
        back = lax.dot_general(grad_lin, weights_ref[5], (((1,), (1,)), ((), ())), preferred_element_type=f32)
        back_ref[rows, :] = norm_back(back * out_gain, x_hat, inverse).astype(bf16).astype(f32)

    lefts, rights, sides = [[column[at] for column in columns] for at in (0, 1, 2)]

    def zero(a, g, lane):
        return jnp.zeros((SUB, channels), f32)

    def store(side):
        def put(a, g, values):
            for lane in range(0, SUB, 2):
                at = pl.multiple_of(a * tile + lane * SUB, 2 * SUB)
                both = jnp.concatenate(values[lane : lane + 2], axis=0)
                rows = pl.ds(pl.multiple_of(g * size + at, 2 * SUB), 2 * SUB)
                for kind in range(2):
                    spot = (2 * side + kind) * channels
                    scaled = both * sides[g][2 * side + kind, pl.ds(at, 2 * SUB), :]
                    d_ref[rows, spot : spot + channels] = scaled.astype(bf16)
        return put

    def by_right(q):
        return lambda g, inner: line(rights[g], (q ^ turn) * tile + inner * SUB)

    def by_left(q):
        return lambda g, inner: line(lefts[g], q * tile + inner * SUB)

    def along(a, q):
        return lambda lane, inner: spread(back_ref, q * size + a * tile + lane * SUB + inner)

    def down(a, q):
        return lambda lane, inner: spread(back_ref, (a ^ turn) * size + q * tile + inner * SUB + lane)

    triangle(n_row, n_col, n_col, by_right, along, zero, store(0))
    triangle(n_row, n_col, n_row, by_left, down, zero, store(1))

    scale = 1.0 / residues
    flipped = jnp.concatenate([column[4][...] for column in columns], axis=1)
    sums = jnp.dot(flipped, d_ref[...], preferred_element_type=f32) * scale
    for s in range(5):
        weight_grad_ref[s] = sums[:, s * channels : (s + 1) * channels]
    weight_grad_ref[5] = scale * lax.dot_general(
        hat_ref[...], lin_ref[...], (((0,), (0,)), ((), ())), preferred_element_type=f32
    )
    total = jnp.zeros((tile, channels), f32)
    for s in range(5):
        total = total + lax.dot_general(
            d_ref[0:tile, s * channels : (s + 1) * channels], weights_ref[s],
            (((1,), (1,)), ((), ())), preferred_element_type=f32,
        )
    grad = norm_back(total * gains_ref[0:1], own_ref[0], own_ref[1])
    pair_grad_ref[...] = grad.astype(bf16).reshape(pair_grad_ref.shape)


def flip(block, n_row, n_col, even, odd):
    pairs = []
    for row in range(n_row):
        for col in range(n_col):
            shift = odd if col % 2 else even
            if shift is not None:
                pairs.append((row * n_col + col, (row ^ shift[0]) * n_col + (col ^ shift[1])))
    return lax.ppermute(block, ("row", "col"), pairs)


def gathered_body(n_row, n_col, pair_act, pair_mask, crop_length, weights, in_gain, out_gain, cotangent):
    tile_rows, tile_cols, channels = pair_act.shape
    tile = tile_rows * tile_cols
    size = n_row * tile
    pairs = size * n_col
    head = tile + 2 * SUB
    f32, bf16 = jnp.float32, jnp.bfloat16
    vmem = pl.BlockSpec(memory_space=pltpu.VMEM)
    smem = pl.BlockSpec(memory_space=pltpu.SMEM)
    hbm = pl.BlockSpec(memory_space=pltpu.HBM)
    in_gain, out_gain = in_gain.reshape(1, channels), out_gain.reshape(1, channels)

    def limit(mib):
        return pltpu.CompilerParams(vmem_limit_bytes=mib * 1024 * 1024)

    own = pl.pallas_call(
        pack_kernel,
        name="pack",
        out_shape=jax.ShapeDtypeStruct((head + tile, channels), bf16),
        in_specs=[hbm] * 4,
        out_specs=vmem,
        scratch_shapes=[
            pltpu.VMEM(pair_act.shape, pair_act.dtype),
            pltpu.VMEM(pair_mask.shape, jnp.int32),
            pltpu.VMEM((1, channels), f32),
            pltpu.SemaphoreType.DMA((4,)),
        ],
        compiler_params=limit(60),
    )(pair_act, pair_mask, cotangent.reshape(tile, channels), in_gain)
    crop_length, own = lax.optimization_barrier((crop_length, own))

    def move(block, even, odd):
        return flip(block, n_row, n_col, even, odd)

    def other(block, odd=(0, 1)):
        return move(block, (0, 1), odd)

    held = pl.pallas_call(
        copy_kernel,
        name="hold",
        out_shape=jax.ShapeDtypeStruct(own.shape, bf16),
        in_specs=[vmem],
        out_specs=vmem,
        compiler_params=limit(2),
        cost_estimate=pl.CostEstimate(flops=100_000_000, bytes_accessed=1_000_000, transcendentals=0),
    )(own)
    both = pl.pallas_call(
        join_kernel,
        name="join",
        out_shape=jax.ShapeDtypeStruct((2 * own.shape[0] - 2 * SUB, channels), bf16),
        in_specs=[vmem] * 2,
        out_specs=vmem,
        compiler_params=limit(2),
    )(held, other(own))
    first = move(both, (2, 0), (3, 0))
    second = move(both, (3, 2), (0, 2))
    third = move(both, (2, 2), (1, 0))
    fourth = move(both, (1, 2), None)
    first, second, third = [(block, other(block)) for block in (first, second, third)]
    fourth = fourth, other(fourth, None)
    chips = (((1, None), (2, 1), (2, 0), (2, 1)), ((2, 1), (2, 0), (2, 0), (2, 0)))
    sources = ((both, *third, *first, *first), (*second, *fourth, *third, *second))

    tri, parts, extra = [], [], []
    for col in range(n_col):
        more = (pair_act, in_gain, out_gain) if col == 0 else tri
        more_shapes = () if col > 0 else (
            jax.ShapeDtypeStruct((2, tile, channels), f32),
            jax.ShapeDtypeStruct((SUB, channels), f32),
        )
        tri, *results = pl.pallas_call(
            functools.partial(column_kernel, n_row, n_col, col, chips[col // 2]),
            name=f"column_{col}",
            out_shape=(
                jax.ShapeDtypeStruct((pairs, channels), f32),
                jax.ShapeDtypeStruct((size, channels), f32),
                jax.ShapeDtypeStruct((size, channels), f32),
                jax.ShapeDtypeStruct((4, size, channels), f32),
                jax.ShapeDtypeStruct((size, channels), f32),
                jax.ShapeDtypeStruct((channels, size), bf16),
                *more_shapes,
            ),
            in_specs=[smem] + [vmem] * (1 + len(sources[col // 2]) + len(more)),
            out_specs=(vmem,) * (6 + len(more_shapes)),
            input_output_aliases={2 + len(sources[col // 2]): 0} if col > 0 else {},
            compiler_params=limit(8),
            cost_estimate=pl.CostEstimate(flops=400_000_000, bytes_accessed=1_000_000, transcendentals=0),
        )(crop_length, weights, *sources[col // 2], *more)
        tri = [tri]
        parts += [*sources[col // 2], *results[:5]]
        extra += results[5:]

    return pl.pallas_call(
        functools.partial(rest_kernel, n_row, n_col, chips),
        name="rest",
        out_shape=(
            jax.ShapeDtypeStruct(pair_act.shape, bf16),
            jax.ShapeDtypeStruct(pair_act.shape, bf16),
            jax.ShapeDtypeStruct(weights.shape, f32),
        ),
        in_specs=[vmem] * (4 + len(parts)),
        out_specs=(vmem, vmem, vmem),
        scratch_shapes=[
            pltpu.VMEM((pairs, channels), f32),
            pltpu.VMEM((pairs, channels), bf16),
            pltpu.VMEM((pairs, channels), bf16),
            pltpu.VMEM((pairs, 5 * channels), bf16),
        ],
        compiler_params=limit(16),
    )(weights, *extra, *tri, *parts)


def body(n_row, n_col, pair_act, *others):
    tile_rows, tile_cols, channels = pair_act.shape
    pairs = tile_rows * n_row * tile_cols * n_col
    small = pairs * channels * 4 <= 1024 * 1024 and channels == 128
    square = n_row == 4 and n_col == 4 and tile_rows == SUB and tile_cols == SUB
    if small and square:
        return gathered_body(n_row, n_col, pair_act, *others)
    return spread_body(pair_act, *others)


def solution(mesh):
    return jax.shard_map(
        functools.partial(body, mesh.shape["row"], mesh.shape["col"]),
        mesh=mesh,
        in_specs=(
            P(("parts", "row"), "col", None),
            P(("parts", "row"), "col"),
            P("parts"),
            P(),
            P(),
            P(),
            P(("parts", "row"), "col", None),
        ),
        out_specs=(
            P(("parts", "row"), "col", None),
            P(("parts", "row"), "col", None),
            P("parts", None, None),
        ),
        check_vma=False,
    )
```

```python
import functools

import jax
import jax.numpy as jnp
from jax import lax
from jax.experimental import pallas as pl
from jax.experimental.pallas import tpu as pltpu
from jax.sharding import PartitionSpec as P

SUB = 8
EPS = 1e-05


def normalize(values):
    average = jnp.mean(values, axis=-1, keepdims=True)
    centered = values - average
    inverse = lax.rsqrt(jnp.mean(centered * centered, axis=-1, keepdims=True) + 1e-05)
    return (centered * inverse, inverse)


def norm_back(grad_hat, values_hat, inverse):
    first = jnp.mean(grad_hat, axis=-1, keepdims=True)
    second = jnp.mean(grad_hat * values_hat, axis=-1, keepdims=True)
    return (grad_hat - first - values_hat * second) * inverse


def gate_back(grad_act, proj_value, proj_gate, keep_mask):
    gate_sig = jax.nn.sigmoid(proj_gate)
    masked = grad_act * keep_mask
    grad_value = (masked * gate_sig).astype(jnp.bfloat16)
    grad_gate = (masked * proj_value * gate_sig * (1.0 - gate_sig)).astype(jnp.bfloat16)
    return (grad_value, grad_gate)


def spread_body(pair_act, pair_mask, crop_length, weights, in_gain, out_gain, cotangent):
    tile_rows, tile_cols, channels = pair_act.shape
    residues = tile_rows * lax.axis_size("row")
    row_pos = lax.axis_index("row") * tile_rows + jnp.arange(tile_rows, dtype=jnp.int32)
    col_pos = lax.axis_index("col") * tile_cols + jnp.arange(tile_cols, dtype=jnp.int32)
    row_in = (row_pos < crop_length[0]).astype(jnp.float32)
    col_in = (col_pos < crop_length[0]).astype(jnp.float32)
    keep_mask = (pair_mask.astype(jnp.float32) * row_in[:, None] * col_in[None, :])[:, :, None]
    z_hat, z_inverse = normalize(pair_act.astype(jnp.float32))
    normed = (z_hat * in_gain).astype(jnp.bfloat16)
    flat_norm = normed.reshape(tile_rows * tile_cols, channels)
    projections = jnp.einsum(
        "pc,scd->spd", flat_norm, weights[:5], preferred_element_type=jnp.float32
    )
    projections = projections.reshape(5, tile_rows, tile_cols, channels)
    left_act = (jax.nn.sigmoid(projections[1]) * projections[0] * keep_mask).astype(jnp.bfloat16)
    right_act = (jax.nn.sigmoid(projections[3]) * projections[2] * keep_mask).astype(jnp.bfloat16)
    partial_value = jnp.einsum(
        "ikh,jkh->ijh",
        left_act,
        lax.all_gather(right_act, "row", axis=0, tiled=True),
        preferred_element_type=jnp.float32,
    )
    tri_sum = lax.psum_scatter(
        partial_value.astype(jnp.bfloat16), "col", scatter_dimension=1, tiled=True
    ).astype(jnp.float32)
    x_hat, x_inverse = normalize(tri_sum)
    normed_out = (x_hat * out_gain).astype(jnp.bfloat16)
    flat_out = normed_out.reshape(tile_rows * tile_cols, channels)
    update_lin = jnp.dot(flat_out, weights[5], preferred_element_type=jnp.float32)
    update_lin = update_lin.reshape(tile_rows, tile_cols, channels)
    out_gate = jax.nn.sigmoid(projections[4])
    update = (out_gate * update_lin).astype(jnp.bfloat16)
    cot_value = cotangent.astype(jnp.float32)
    grad_lin = (cot_value * out_gate).astype(jnp.bfloat16)
    grad_gate_out = (cot_value * update_lin * out_gate * (1.0 - out_gate)).astype(jnp.bfloat16)
    flat_lin = grad_lin.reshape(tile_rows * tile_cols, channels)
    grad_norm_out = jnp.einsum(
        "pd,cd->pc", flat_lin, weights[5], preferred_element_type=jnp.float32
    )
    grad_norm_out = grad_norm_out.reshape(tile_rows, tile_cols, channels)
    grad_tri = norm_back(grad_norm_out * out_gain, x_hat, x_inverse).astype(jnp.bfloat16)
    grad_full = lax.all_gather(grad_tri, "col", axis=1, tiled=True)
    grad_slab = grad_full
    grad_left = jnp.einsum(
        "ijh,jkh->ikh",
        grad_slab,
        lax.all_gather(right_act, "row", axis=0, tiled=True),
        preferred_element_type=jnp.float32,
    )
    grad_slab = grad_full
    grad_right = lax.psum_scatter(
        jnp.einsum("ijh,ikh->jkh", grad_slab, left_act, preferred_element_type=jnp.float32).astype(
            jnp.bfloat16
        ),
        "row",
        scatter_dimension=0,
        tiled=True,
    ).astype(jnp.float32)
    grad_pa, grad_ga = gate_back(grad_left, projections[0], projections[1], keep_mask)
    grad_pb, grad_gb = gate_back(grad_right, projections[2], projections[3], keep_mask)
    grads = jnp.stack([grad_pa, grad_ga, grad_pb, grad_gb, grad_gate_out]).reshape(
        5, tile_rows * tile_cols, channels
    )
    grad_normed = jnp.einsum("spd,scd->pc", grads, weights[:5], preferred_element_type=jnp.float32)
    grad_normed = grad_normed.reshape(tile_rows, tile_cols, channels)
    pair_grad = norm_back(grad_normed * in_gain, z_hat, z_inverse).astype(jnp.bfloat16)
    local_in = jnp.einsum("pc,spd->scd", flat_norm, grads, preferred_element_type=jnp.float32)
    local_out = jnp.dot(flat_out.T, flat_lin, preferred_element_type=jnp.float32)
    local_grads = jnp.concatenate([local_in, local_out[None]], axis=0) / residues
    weight_grad = lax.psum(local_grads, ("row", "col"))
    return (update, pair_grad, weight_grad)


def pack_kernel(act_hbm, mask_hbm, cot_hbm, gain_hbm, out_ref, act_ref, mask_ref, gain_ref, sems):
    tile_rows, tile_cols, channels = act_ref.shape
    pairs = tile_rows * tile_cols
    head = out_ref.shape[0] - pairs
    pack_copies = [
        pltpu.make_async_copy(act_hbm, act_ref, sems.at[0]),
        pltpu.make_async_copy(gain_hbm, gain_ref, sems.at[1]),
        pltpu.make_async_copy(mask_hbm, mask_ref, sems.at[2]),
        pltpu.make_async_copy(cot_hbm, out_ref.at[head : head + pairs], sems.at[3]),
    ]
    for copy in pack_copies:
        copy.start()
    for copy in pack_copies:
        copy.wait()
    z_hat, _ = normalize(act_ref[...].astype(jnp.float32).reshape(pairs, channels))
    out_ref[0:pairs] = (z_hat * gain_ref[...]).astype(jnp.bfloat16)
    keep = mask_ref[...].astype(jnp.float32)
    wide = jnp.concatenate([keep, jnp.zeros((tile_rows, channels - tile_cols), jnp.float32)], axis=1)
    tall = jnp.concatenate([wide, jnp.zeros((channels - tile_rows, channels), jnp.float32)], axis=0)
    out_ref[pairs:head] = tall.T[0 : head - pairs].astype(jnp.bfloat16)


def copy_kernel(in_ref, out_ref):
    out_ref[...] = in_ref[...]


def join_kernel(own_ref, twin_ref, out_ref):
    tile = SUB * SUB
    refs = (own_ref, twin_ref)
    for at, ref in enumerate(refs):
        out_ref[at * tile : (at + 1) * tile] = ref[0:tile]
        spot = 2 * tile + 2 * SUB + at * tile
        out_ref[spot : spot + tile] = ref[tile + 2 * SUB :]
    masks = [ref[tile : tile + 2 * SUB].astype(jnp.float32)[0:SUB] for ref in refs]
    out_ref[2 * tile : 2 * tile + 2 * SUB] = jnp.concatenate(masks, axis=0).astype(jnp.bfloat16)


def normed_rows(ref, sub):
    return ref[sub * SUB * SUB : (sub + 1) * SUB * SUB]


def mask_rows(ref, sub):
    at = ref.shape[0] // 2 // (SUB * SUB) * SUB * SUB
    return ref[at : at + 2 * SUB].astype(jnp.float32)[sub * SUB : (sub + 1) * SUB]


def cot_rows(ref, sub):
    at = ref.shape[0] // 2 // (SUB * SUB) * SUB * SUB + 2 * SUB
    return ref[at + sub * SUB * SUB : at + (sub + 1) * SUB * SUB]


def chip_rows(rows_of, refs, core, direct_on):
    if direct_on is None:
        return rows_of(refs[min(core, len(refs) - 1)], core if len(refs) == 1 else 0)
    here = lax.axis_index("col") % 2 == direct_on
    return jnp.where(here, rows_of(refs[0], core), rows_of(refs[1], 1 - core))


def split_chips(refs, chips):
    split, at = [], 0
    for width, direct_on in chips:
        split.append((refs[at : at + width], direct_on))
        at += width
    return split


def triangle(blocks, groups, steps, vectors_at, factors_at, start_at, store_at):
    def block(a, _):
        def step(q, totals):
            totals = list(totals)
            vectors = vectors_at(q)
            factors = factors_at(a, q)
            for inner in range(SUB):
                rows = [vectors(g, inner) for g in range(groups)]
                for lane in range(SUB):
                    factor = factors(lane, inner)
                    for g in range(groups):
                        at = lane * groups + g
                        totals[at] = totals[at] + factor * rows[g]
            return tuple(totals)

        totals = tuple(start_at(a, g, lane) for lane in range(SUB) for g in range(groups))
        totals = step(0, totals) if steps == 1 else lax.fori_loop(0, steps, step, totals)
        for g in range(groups):
            store_at(a, g, [totals[lane * groups + g] for lane in range(SUB)])
        return 0

    lax.fori_loop(0, blocks, block, 0)


def spread(ref, row):
    return jnp.broadcast_to(ref[pl.ds(row, 1), :], (SUB, ref.shape[-1]))


def line(ref, row):
    return ref[pl.ds(pl.multiple_of(row, SUB), SUB), :]


def column_kernel(n_row, n_col, col, chips, crop_ref, weights_ref, *refs):
    count = sum(width for width, _ in chips)
    chip_refs, refs = refs[:count], refs[count:]
    if col == 0:
        act_ref, in_gain_ref, out_gain_ref, *refs, own_ref, gains_ref = refs
        z_hat, z_inverse = normalize(act_ref[...].astype(jnp.float32).reshape(own_ref.shape[1:]))
        own_ref[0] = z_hat
        own_ref[1] = jnp.broadcast_to(z_inverse, z_hat.shape)
        gains_ref[0:1] = in_gain_ref[...]
        gains_ref[1:2] = out_gain_ref[...]
    tri_in, (tri_ref, left_ref, right_ref, side_ref, gate_ref, flip_ref) = refs[:-6], refs[-6:]
    channels = weights_ref.shape[-1]
    tile = SUB * SUB
    size = n_row * tile
    bf16, f32 = jnp.bfloat16, jnp.float32
    row_me, col_me = lax.axis_index("row"), lax.axis_index("col")
    chip_list = split_chips(chip_refs, chips)
    normed = jnp.concatenate([chip_rows(normed_rows, chip, col % 2, on) for chip, on in chip_list], axis=0)
    flip_ref[...] = normed.astype(f32).T.astype(bf16)
    crop = crop_ref[0]
    col_offset = lax.broadcasted_iota(jnp.int32, (SUB, channels), 0)
    row_offset = lax.broadcasted_iota(jnp.int32, (SUB, channels), 1)
    cols_in = col_offset < crop - (col_me ^ col) * SUB
    kept = []
    for b, (chip, on) in enumerate(chip_list):
        keep = chip_rows(mask_rows, chip, col % 2, on)
        rows_in = row_offset < crop - (row_me ^ b) * SUB
        keep = jnp.where(rows_in & cols_in, keep, 0.0)
        kept += [jnp.broadcast_to(keep[:, at : at + 1], (SUB, channels)) for at in range(SUB)]
    kept = jnp.concatenate(kept, axis=0)
    for side, act_ref in enumerate((left_ref, right_ref)):
        pair = jnp.concatenate([weights_ref[2 * side], weights_ref[2 * side + 1]], axis=1)
        proj = jnp.dot(normed, pair, preferred_element_type=f32)
        gate = jax.nn.sigmoid(proj[:, channels:])
        masked = gate * kept
        act = masked * proj[:, :channels]
        act_ref[...] = act.astype(bf16).astype(f32)
        side_ref[2 * side] = masked
        side_ref[2 * side + 1] = act * (1.0 - gate)
    gate_ref[...] = jax.nn.sigmoid(jnp.dot(normed, weights_ref[4], preferred_element_type=f32))
    turn = row_me ^ col_me

    def flipped(q):
        firsts = [(turn ^ g) * tile for g in range(n_col)]
        return lambda g, inner: right_ref[pl.ds(firsts[g] + inner, SUB, stride=SUB), :]

    def along(a, q):
        return lambda lane, inner: spread(left_ref, a * tile + lane * SUB + inner)

    def start(a, g, lane):
        if len(tri_in) == 0:
            return jnp.zeros((SUB, channels), f32)
        return line(tri_in[0], g * size + a * tile + lane * SUB)

    def store(a, g, values):
        for lane in range(SUB):
            tri_ref[pl.ds(pl.multiple_of(g * size + a * tile + lane * SUB, SUB), SUB), :] = values[lane]

    triangle(n_row, n_col, 1, flipped, along, start, store)


def rest_kernel(n_row, n_col, chips, weights_ref, own_ref, gains_ref, tri_ref, *refs):
    chip_lists, columns = [], []
    for col in range(n_col):
        count = sum(width for width, _ in chips[col // 2])
        chip_lists.append(split_chips(refs[:count], chips[col // 2]))
        columns.append(refs[count : count + 5])
        refs = refs[count + 5 :]
    update_ref, pair_grad_ref, weight_grad_ref, back_ref, hat_ref, lin_ref, d_ref = refs
    channels = tri_ref.shape[-1]
    tile = SUB * SUB
    size = n_row * tile
    residues = n_row * SUB
    bf16, f32 = jnp.bfloat16, jnp.float32
    turn = lax.axis_index("row") ^ lax.axis_index("col")
    out_gain = gains_ref[1:2]
    for col, (_, _, _, gate_ref, _) in enumerate(columns):
        rows = slice(col * size, (col + 1) * size)
        x_hat, inverse = normalize(tri_ref[rows, :])
        normed_out = (x_hat * out_gain).astype(bf16)
        hat_ref[rows, :] = normed_out
        lin = jnp.dot(normed_out, weights_ref[5], preferred_element_type=f32)
        out_gate = gate_ref[...]
        if col == 0:
            update_ref[...] = (out_gate[0:tile] * lin[0:tile]).astype(bf16).reshape(update_ref.shape)
        cots = [chip_rows(cot_rows, chip, col % 2, on) for chip, on in chip_lists[col]]
        cot = jnp.concatenate(cots, axis=0).astype(f32)
        grad = cot * out_gate
        grad_lin = grad.astype(bf16)
        lin_ref[rows, :] = grad_lin
        d_ref[rows, 4 * channels : 5 * channels] = (grad * lin * (1.0 - out_gate)).astype(bf16)
        back = lax.dot_general(grad_lin, weights_ref[5], (((1,), (1,)), ((), ())), preferred_element_type=f32)
        back_ref[rows, :] = norm_back(back * out_gain, x_hat, inverse).astype(bf16).astype(f32)

    lefts, rights, sides = [[column[at] for column in columns] for at in (0, 1, 2)]

    def zero(a, g, lane):
        return jnp.zeros((SUB, channels), f32)

    def store(side):
        def put(a, g, values):
            for lane in range(0, SUB, 2):
                at = pl.multiple_of(a * tile + lane * SUB, 2 * SUB)
                both = jnp.concatenate(values[lane : lane + 2], axis=0)
                rows = pl.ds(pl.multiple_of(g * size + at, 2 * SUB), 2 * SUB)
                for kind in range(2):
                    spot = (2 * side + kind) * channels
                    scaled = both * sides[g][2 * side + kind, pl.ds(at, 2 * SUB), :]
                    d_ref[rows, spot : spot + channels] = scaled.astype(bf16)
        return put

    def by_right(q):
        return lambda g, inner: line(rights[g], (q ^ turn) * tile + inner * SUB)

    def by_left(q):
        return lambda g, inner: line(lefts[g], q * tile + inner * SUB)

    def along(a, q):
        return lambda lane, inner: spread(back_ref, q * size + a * tile + lane * SUB + inner)

    def down(a, q):
        return lambda lane, inner: spread(back_ref, (a ^ turn) * size + q * tile + inner * SUB + lane)

    triangle(n_row, n_col, n_col, by_right, along, zero, store(0))
    triangle(n_row, n_col, n_row, by_left, down, zero, store(1))

    scale = 1.0 / residues
    flipped = jnp.concatenate([column[4][...] for column in columns], axis=1)
    sums = jnp.dot(flipped, d_ref[...], preferred_element_type=f32) * scale
    for s in range(5):
        weight_grad_ref[s] = sums[:, s * channels : (s + 1) * channels]
    weight_grad_ref[5] = scale * lax.dot_general(
        hat_ref[...], lin_ref[...], (((0,), (0,)), ((), ())), preferred_element_type=f32
    )
    total = jnp.zeros((tile, channels), f32)
    for s in range(5):
        total = total + lax.dot_general(
            d_ref[0:tile, s * channels : (s + 1) * channels], weights_ref[s],
            (((1,), (1,)), ((), ())), preferred_element_type=f32,
        )
    grad = norm_back(total * gains_ref[0:1], own_ref[0], own_ref[1])
    pair_grad_ref[...] = grad.astype(bf16).reshape(pair_grad_ref.shape)


def flip(block, n_row, n_col, even, odd):
    pairs = []
    for row in range(n_row):
        for col in range(n_col):
            shift = odd if col % 2 else even
            pairs.append((row * n_col + col, (row ^ shift[0]) * n_col + (col ^ shift[1])))
    return lax.ppermute(block, ("row", "col"), pairs)


def gathered_body(n_row, n_col, pair_act, pair_mask, crop_length, weights, in_gain, out_gain, cotangent):
    tile_rows, tile_cols, channels = pair_act.shape
    tile = tile_rows * tile_cols
    size = n_row * tile
    pairs = size * n_col
    head = tile + 2 * SUB
    f32, bf16 = jnp.float32, jnp.bfloat16
    vmem = pl.BlockSpec(memory_space=pltpu.VMEM)
    smem = pl.BlockSpec(memory_space=pltpu.SMEM)
    hbm = pl.BlockSpec(memory_space=pltpu.HBM)
    in_gain, out_gain = in_gain.reshape(1, channels), out_gain.reshape(1, channels)

    def limit(mib):
        return pltpu.CompilerParams(vmem_limit_bytes=mib * 1024 * 1024)

    own = pl.pallas_call(
        pack_kernel,
        name="pack",
        out_shape=jax.ShapeDtypeStruct((head + tile, channels), bf16),
        in_specs=[hbm] * 4,
        out_specs=vmem,
        scratch_shapes=[
            pltpu.VMEM(pair_act.shape, pair_act.dtype),
            pltpu.VMEM(pair_mask.shape, jnp.int32),
            pltpu.VMEM((1, channels), f32),
            pltpu.SemaphoreType.DMA((4,)),
        ],
        compiler_params=limit(60),
    )(pair_act, pair_mask, cotangent.reshape(tile, channels), in_gain)
    crop_length, own = lax.optimization_barrier((crop_length, own))

    def move(block, even, odd):
        return flip(block, n_row, n_col, even, odd)

    def other(block):
        return move(block, (0, 1), (0, 1))

    held = pl.pallas_call(
        copy_kernel,
        name="hold",
        out_shape=jax.ShapeDtypeStruct(own.shape, bf16),
        in_specs=[vmem],
        out_specs=vmem,
        compiler_params=limit(2),
        cost_estimate=pl.CostEstimate(flops=100_000_000, bytes_accessed=1_000_000, transcendentals=0),
    )(own)
    both = pl.pallas_call(
        join_kernel,
        name="join",
        out_shape=jax.ShapeDtypeStruct((2 * own.shape[0] - 2 * SUB, channels), bf16),
        in_specs=[vmem] * 2,
        out_specs=vmem,
        compiler_params=limit(2),
    )(held, other(own))
    straight = move(own, (3, 0), (3, 0))
    first = move(both, (2, 0), (1, 0))
    second = move(both, (0, 2), (2, 2))
    third = move(both, (1, 2), (3, 2))
    straight, first, second, third = [(block, other(block)) for block in (straight, first, second, third)]
    chips = (((1, None), (2, 1), (2, 0), (2, None)), ((2, 0), (2, 0), (2, 1), (2, 1)))
    sources = ((both, *first, *first, *straight), (*second, *third, *second, *third))

    tri, parts, extra = [], [], []
    for col in range(n_col):
        more = (pair_act, in_gain, out_gain) if col == 0 else tri
        more_shapes = () if col > 0 else (
            jax.ShapeDtypeStruct((2, tile, channels), f32),
            jax.ShapeDtypeStruct((SUB, channels), f32),
        )
        tri, *results = pl.pallas_call(
            functools.partial(column_kernel, n_row, n_col, col, chips[col // 2]),
            name=f"column_{col}",
            out_shape=(
                jax.ShapeDtypeStruct((pairs, channels), f32),
                jax.ShapeDtypeStruct((size, channels), f32),
                jax.ShapeDtypeStruct((size, channels), f32),
                jax.ShapeDtypeStruct((4, size, channels), f32),
                jax.ShapeDtypeStruct((size, channels), f32),
                jax.ShapeDtypeStruct((channels, size), bf16),
                *more_shapes,
            ),
            in_specs=[smem] + [vmem] * (1 + len(sources[col // 2]) + len(more)),
            out_specs=(vmem,) * (6 + len(more_shapes)),
            input_output_aliases={2 + len(sources[col // 2]): 0} if col > 0 else {},
            compiler_params=limit(8),
            cost_estimate=pl.CostEstimate(flops=400_000_000, bytes_accessed=1_000_000, transcendentals=0),
        )(crop_length, weights, *sources[col // 2], *more)
        tri = [tri]
        parts += [*sources[col // 2], *results[:5]]
        extra += results[5:]

    return pl.pallas_call(
        functools.partial(rest_kernel, n_row, n_col, chips),
        name="rest",
        out_shape=(
            jax.ShapeDtypeStruct(pair_act.shape, bf16),
            jax.ShapeDtypeStruct(pair_act.shape, bf16),
            jax.ShapeDtypeStruct(weights.shape, f32),
        ),
        in_specs=[vmem] * (4 + len(parts)),
        out_specs=(vmem, vmem, vmem),
        scratch_shapes=[
            pltpu.VMEM((pairs, channels), f32),
            pltpu.VMEM((pairs, channels), bf16),
            pltpu.VMEM((pairs, channels), bf16),
            pltpu.VMEM((pairs, 5 * channels), bf16),
        ],
        compiler_params=limit(16),
    )(weights, *extra, *tri, *parts)


def body(n_row, n_col, pair_act, *others):
    tile_rows, tile_cols, channels = pair_act.shape
    pairs = tile_rows * n_row * tile_cols * n_col
    small = pairs * channels * 4 <= 1024 * 1024 and channels == 128
    square = n_row == 4 and n_col == 4 and tile_rows == SUB and tile_cols == SUB
    if small and square:
        return gathered_body(n_row, n_col, pair_act, *others)
    return spread_body(pair_act, *others)


def solution(mesh):
    return jax.shard_map(
        functools.partial(body, mesh.shape["row"], mesh.shape["col"]),
        mesh=mesh,
        in_specs=(
            P(("parts", "row"), "col", None),
            P(("parts", "row"), "col"),
            P("parts"),
            P(),
            P(),
            P(),
            P(("parts", "row"), "col", None),
        ),
        out_specs=(
            P(("parts", "row"), "col", None),
            P(("parts", "row"), "col", None),
            P("parts", None, None),
        ),
        check_vma=False,
    )
```

```python
import functools

import jax
import jax.numpy as jnp
from jax import lax
from jax.experimental import pallas as pl
from jax.experimental.pallas import tpu as pltpu
from jax.sharding import PartitionSpec as P

SUB = 8
EPS = 1e-05


def normalize(values):
    average = jnp.mean(values, axis=-1, keepdims=True)
    centered = values - average
    inverse = lax.rsqrt(jnp.mean(centered * centered, axis=-1, keepdims=True) + 1e-05)
    return (centered * inverse, inverse)


def norm_back(grad_hat, values_hat, inverse):
    first = jnp.mean(grad_hat, axis=-1, keepdims=True)
    second = jnp.mean(grad_hat * values_hat, axis=-1, keepdims=True)
    return (grad_hat - first - values_hat * second) * inverse


def gate_back(grad_act, proj_value, proj_gate, keep_mask):
    gate_sig = jax.nn.sigmoid(proj_gate)
    masked = grad_act * keep_mask
    grad_value = (masked * gate_sig).astype(jnp.bfloat16)
    grad_gate = (masked * proj_value * gate_sig * (1.0 - gate_sig)).astype(jnp.bfloat16)
    return (grad_value, grad_gate)


def spread_body(pair_act, pair_mask, crop_length, weights, in_gain, out_gain, cotangent):
    tile_rows, tile_cols, channels = pair_act.shape
    residues = tile_rows * lax.axis_size("row")
    row_pos = lax.axis_index("row") * tile_rows + jnp.arange(tile_rows, dtype=jnp.int32)
    col_pos = lax.axis_index("col") * tile_cols + jnp.arange(tile_cols, dtype=jnp.int32)
    row_in = (row_pos < crop_length[0]).astype(jnp.float32)
    col_in = (col_pos < crop_length[0]).astype(jnp.float32)
    keep_mask = (pair_mask.astype(jnp.float32) * row_in[:, None] * col_in[None, :])[:, :, None]
    z_hat, z_inverse = normalize(pair_act.astype(jnp.float32))
    normed = (z_hat * in_gain).astype(jnp.bfloat16)
    flat_norm = normed.reshape(tile_rows * tile_cols, channels)
    projections = jnp.einsum(
        "pc,scd->spd", flat_norm, weights[:5], preferred_element_type=jnp.float32
    )
    projections = projections.reshape(5, tile_rows, tile_cols, channels)
    left_act = (jax.nn.sigmoid(projections[1]) * projections[0] * keep_mask).astype(jnp.bfloat16)
    right_act = (jax.nn.sigmoid(projections[3]) * projections[2] * keep_mask).astype(jnp.bfloat16)
    partial_value = jnp.einsum(
        "ikh,jkh->ijh",
        left_act,
        lax.all_gather(right_act, "row", axis=0, tiled=True),
        preferred_element_type=jnp.float32,
    )
    tri_sum = lax.psum_scatter(
        partial_value.astype(jnp.bfloat16), "col", scatter_dimension=1, tiled=True
    ).astype(jnp.float32)
    x_hat, x_inverse = normalize(tri_sum)
    normed_out = (x_hat * out_gain).astype(jnp.bfloat16)
    flat_out = normed_out.reshape(tile_rows * tile_cols, channels)
    update_lin = jnp.dot(flat_out, weights[5], preferred_element_type=jnp.float32)
    update_lin = update_lin.reshape(tile_rows, tile_cols, channels)
    out_gate = jax.nn.sigmoid(projections[4])
    update = (out_gate * update_lin).astype(jnp.bfloat16)
    cot_value = cotangent.astype(jnp.float32)
    grad_lin = (cot_value * out_gate).astype(jnp.bfloat16)
    grad_gate_out = (cot_value * update_lin * out_gate * (1.0 - out_gate)).astype(jnp.bfloat16)
    flat_lin = grad_lin.reshape(tile_rows * tile_cols, channels)
    grad_norm_out = jnp.einsum(
        "pd,cd->pc", flat_lin, weights[5], preferred_element_type=jnp.float32
    )
    grad_norm_out = grad_norm_out.reshape(tile_rows, tile_cols, channels)
    grad_tri = norm_back(grad_norm_out * out_gain, x_hat, x_inverse).astype(jnp.bfloat16)
    grad_full = lax.all_gather(grad_tri, "col", axis=1, tiled=True)
    grad_slab = grad_full
    grad_left = jnp.einsum(
        "ijh,jkh->ikh",
        grad_slab,
        lax.all_gather(right_act, "row", axis=0, tiled=True),
        preferred_element_type=jnp.float32,
    )
    grad_slab = grad_full
    grad_right = lax.psum_scatter(
        jnp.einsum("ijh,ikh->jkh", grad_slab, left_act, preferred_element_type=jnp.float32).astype(
            jnp.bfloat16
        ),
        "row",
        scatter_dimension=0,
        tiled=True,
    ).astype(jnp.float32)
    grad_pa, grad_ga = gate_back(grad_left, projections[0], projections[1], keep_mask)
    grad_pb, grad_gb = gate_back(grad_right, projections[2], projections[3], keep_mask)
    grads = jnp.stack([grad_pa, grad_ga, grad_pb, grad_gb, grad_gate_out]).reshape(
        5, tile_rows * tile_cols, channels
    )
    grad_normed = jnp.einsum("spd,scd->pc", grads, weights[:5], preferred_element_type=jnp.float32)
    grad_normed = grad_normed.reshape(tile_rows, tile_cols, channels)
    pair_grad = norm_back(grad_normed * in_gain, z_hat, z_inverse).astype(jnp.bfloat16)
    local_in = jnp.einsum("pc,spd->scd", flat_norm, grads, preferred_element_type=jnp.float32)
    local_out = jnp.dot(flat_out.T, flat_lin, preferred_element_type=jnp.float32)
    local_grads = jnp.concatenate([local_in, local_out[None]], axis=0) / residues
    weight_grad = lax.psum(local_grads, ("row", "col"))
    return (update, pair_grad, weight_grad)


def pack_kernel(act_hbm, mask_hbm, cot_hbm, gain_hbm, out_ref, act_ref, mask_ref, gain_ref, sems):
    tile_rows, tile_cols, channels = act_ref.shape
    pairs = tile_rows * tile_cols
    head = out_ref.shape[0] - pairs
    pack_copies = [
        pltpu.make_async_copy(act_hbm, act_ref, sems.at[0]),
        pltpu.make_async_copy(gain_hbm, gain_ref, sems.at[1]),
        pltpu.make_async_copy(mask_hbm, mask_ref, sems.at[2]),
        pltpu.make_async_copy(cot_hbm, out_ref.at[head : head + pairs], sems.at[3]),
    ]
    for copy in pack_copies:
        copy.start()
    for copy in pack_copies:
        copy.wait()
    z_hat, _ = normalize(act_ref[...].astype(jnp.float32).reshape(pairs, channels))
    out_ref[0:pairs] = (z_hat * gain_ref[...]).astype(jnp.bfloat16)
    keep = mask_ref[...].astype(jnp.float32)
    wide = jnp.concatenate([keep, jnp.zeros((tile_rows, channels - tile_cols), jnp.float32)], axis=1)
    tall = jnp.concatenate([wide, jnp.zeros((channels - tile_rows, channels), jnp.float32)], axis=0)
    out_ref[pairs:head] = tall.T[0 : head - pairs].astype(jnp.bfloat16)


def copy_kernel(in_ref, out_ref):
    out_ref[...] = in_ref[...]


def pair_kernel(one_ref, two_ref, one_out, two_out):
    one_out[...] = one_ref[...]
    two_out[...] = two_ref[...]


def join_kernel(own_ref, twin_ref, out_ref):
    tile = SUB * SUB
    refs = (own_ref, twin_ref)
    for at, ref in enumerate(refs):
        out_ref[at * tile : (at + 1) * tile] = ref[0:tile]
        spot = 2 * tile + 2 * SUB + at * tile
        out_ref[spot : spot + tile] = ref[tile + 2 * SUB :]
    masks = [ref[tile : tile + 2 * SUB].astype(jnp.float32)[0:SUB] for ref in refs]
    out_ref[2 * tile : 2 * tile + 2 * SUB] = jnp.concatenate(masks, axis=0).astype(jnp.bfloat16)


def normed_rows(ref, sub):
    return ref[sub * SUB * SUB : (sub + 1) * SUB * SUB]


def mask_rows(ref, sub):
    at = ref.shape[0] // 2 // (SUB * SUB) * SUB * SUB
    return ref[at : at + 2 * SUB].astype(jnp.float32)[sub * SUB : (sub + 1) * SUB]


def cot_rows(ref, sub):
    at = ref.shape[0] // 2 // (SUB * SUB) * SUB * SUB + 2 * SUB
    return ref[at + sub * SUB * SUB : at + (sub + 1) * SUB * SUB]


def chip_rows(rows_of, refs, core, direct_on):
    if direct_on is None:
        return rows_of(refs[min(core, len(refs) - 1)], core if len(refs) == 1 else 0)
    here = lax.axis_index("col") % 2 == direct_on
    return jnp.where(here, rows_of(refs[0], core), rows_of(refs[1], 1 - core))


def split_chips(refs, chips):
    split, at = [], 0
    for width, direct_on in chips:
        split.append((refs[at : at + width], direct_on))
        at += width
    return split


def triangle(blocks, groups, steps, vectors_at, factors_at, start_at, store_at):
    def block(a, _):
        def step(q, totals):
            totals = list(totals)
            vectors = vectors_at(q)
            factors = factors_at(a, q)
            for inner in range(SUB):
                rows = [vectors(g, inner) for g in range(groups)]
                for lane in range(SUB):
                    factor = factors(lane, inner)
                    for g in range(groups):
                        at = lane * groups + g
                        totals[at] = totals[at] + factor * rows[g]
            return tuple(totals)

        totals = tuple(start_at(a, g, lane) for lane in range(SUB) for g in range(groups))
        totals = step(0, totals) if steps == 1 else lax.fori_loop(0, steps, step, totals)
        for g in range(groups):
            store_at(a, g, [totals[lane * groups + g] for lane in range(SUB)])
        return 0

    lax.fori_loop(0, blocks, block, 0)


def spread(ref, row):
    return jnp.broadcast_to(ref[pl.ds(row, 1), :], (SUB, ref.shape[-1]))


def line(ref, row):
    return ref[pl.ds(pl.multiple_of(row, SUB), SUB), :]


def column_kernel(n_row, n_col, col, chips, crop_ref, weights_ref, *refs):
    count = sum(width for width, _ in chips)
    chip_refs, refs = refs[:count], refs[count:]
    if col == 0:
        act_ref, in_gain_ref, out_gain_ref, *refs, own_ref, gains_ref = refs
        z_hat, z_inverse = normalize(act_ref[...].astype(jnp.float32).reshape(own_ref.shape[1:]))
        own_ref[0] = z_hat
        own_ref[1] = jnp.broadcast_to(z_inverse, z_hat.shape)
        gains_ref[0:1] = in_gain_ref[...]
        gains_ref[1:2] = out_gain_ref[...]
    tri_in, (tri_ref, left_ref, right_ref, side_ref, gate_ref, flip_ref) = refs[:-6], refs[-6:]
    channels = weights_ref.shape[-1]
    tile = SUB * SUB
    size = n_row * tile
    bf16, f32 = jnp.bfloat16, jnp.float32
    row_me, col_me = lax.axis_index("row"), lax.axis_index("col")
    chip_list = split_chips(chip_refs, chips)
    normed = jnp.concatenate([chip_rows(normed_rows, chip, col % 2, on) for chip, on in chip_list], axis=0)
    flip_ref[...] = normed.astype(f32).T.astype(bf16)
    crop = crop_ref[0]
    col_offset = lax.broadcasted_iota(jnp.int32, (SUB, channels), 0)
    row_offset = lax.broadcasted_iota(jnp.int32, (SUB, channels), 1)
    cols_in = col_offset < crop - (col_me ^ col) * SUB
    kept = []
    for b, (chip, on) in enumerate(chip_list):
        keep = chip_rows(mask_rows, chip, col % 2, on)
        rows_in = row_offset < crop - (row_me ^ b) * SUB
        keep = jnp.where(rows_in & cols_in, keep, 0.0)
        kept += [jnp.broadcast_to(keep[:, at : at + 1], (SUB, channels)) for at in range(SUB)]
    kept = jnp.concatenate(kept, axis=0)
    for side, act_ref in enumerate((left_ref, right_ref)):
        pair = jnp.concatenate([weights_ref[2 * side], weights_ref[2 * side + 1]], axis=1)
        proj = jnp.dot(normed, pair, preferred_element_type=f32)
        gate = jax.nn.sigmoid(proj[:, channels:])
        masked = gate * kept
        act = masked * proj[:, :channels]
        act_ref[...] = act.astype(bf16).astype(f32)
        side_ref[2 * side] = masked
        side_ref[2 * side + 1] = act * (1.0 - gate)
    gate_ref[...] = jax.nn.sigmoid(jnp.dot(normed, weights_ref[4], preferred_element_type=f32))
    turn = row_me ^ col_me

    def flipped(q):
        firsts = [(turn ^ g) * tile for g in range(n_col)]
        return lambda g, inner: right_ref[pl.ds(firsts[g] + inner, SUB, stride=SUB), :]

    def along(a, q):
        return lambda lane, inner: spread(left_ref, a * tile + lane * SUB + inner)

    def start(a, g, lane):
        if len(tri_in) == 0:
            return jnp.zeros((SUB, channels), f32)
        return line(tri_in[0], g * size + a * tile + lane * SUB)

    def store(a, g, values):
        for lane in range(SUB):
            tri_ref[pl.ds(pl.multiple_of(g * size + a * tile + lane * SUB, SUB), SUB), :] = values[lane]

    triangle(n_row, n_col, 1, flipped, along, start, store)


def rest_kernel(n_row, n_col, chips, weights_ref, own_ref, gains_ref, tri_ref, *refs):
    chip_lists, columns = [], []
    for col in range(n_col):
        count = sum(width for width, _ in chips[col // 2])
        chip_lists.append(split_chips(refs[:count], chips[col // 2]))
        columns.append(refs[count : count + 5])
        refs = refs[count + 5 :]
    update_ref, pair_grad_ref, weight_grad_ref, back_ref, hat_ref, lin_ref, d_ref = refs
    channels = tri_ref.shape[-1]
    tile = SUB * SUB
    size = n_row * tile
    residues = n_row * SUB
    bf16, f32 = jnp.bfloat16, jnp.float32
    turn = lax.axis_index("row") ^ lax.axis_index("col")
    out_gain = gains_ref[1:2]
    for col, (_, _, _, gate_ref, _) in enumerate(columns):
        rows = slice(col * size, (col + 1) * size)
        x_hat, inverse = normalize(tri_ref[rows, :])
        normed_out = (x_hat * out_gain).astype(bf16)
        hat_ref[rows, :] = normed_out
        lin = jnp.dot(normed_out, weights_ref[5], preferred_element_type=f32)
        out_gate = gate_ref[...]
        if col == 0:
            update_ref[...] = (out_gate[0:tile] * lin[0:tile]).astype(bf16).reshape(update_ref.shape)
        cots = [chip_rows(cot_rows, chip, col % 2, on) for chip, on in chip_lists[col]]
        cot = jnp.concatenate(cots, axis=0).astype(f32)
        grad = cot * out_gate
        grad_lin = grad.astype(bf16)
        lin_ref[rows, :] = grad_lin
        d_ref[rows, 4 * channels : 5 * channels] = (grad * lin * (1.0 - out_gate)).astype(bf16)
        back = lax.dot_general(grad_lin, weights_ref[5], (((1,), (1,)), ((), ())), preferred_element_type=f32)
        back_ref[rows, :] = norm_back(back * out_gain, x_hat, inverse).astype(bf16).astype(f32)

    lefts, rights, sides = [[column[at] for column in columns] for at in (0, 1, 2)]

    def zero(a, g, lane):
        return jnp.zeros((SUB, channels), f32)

    def store(side):
        def put(a, g, values):
            for lane in range(0, SUB, 2):
                at = pl.multiple_of(a * tile + lane * SUB, 2 * SUB)
                both = jnp.concatenate(values[lane : lane + 2], axis=0)
                rows = pl.ds(pl.multiple_of(g * size + at, 2 * SUB), 2 * SUB)
                for kind in range(2):
                    spot = (2 * side + kind) * channels
                    scaled = both * sides[g][2 * side + kind, pl.ds(at, 2 * SUB), :]
                    d_ref[rows, spot : spot + channels] = scaled.astype(bf16)
        return put

    def by_right(q):
        return lambda g, inner: line(rights[g], (q ^ turn) * tile + inner * SUB)

    def by_left(q):
        return lambda g, inner: line(lefts[g], q * tile + inner * SUB)

    def along(a, q):
        return lambda lane, inner: spread(back_ref, q * size + a * tile + lane * SUB + inner)

    def down(a, q):
        return lambda lane, inner: spread(back_ref, (a ^ turn) * size + q * tile + inner * SUB + lane)

    triangle(n_row, n_col, n_col, by_right, along, zero, store(0))
    triangle(n_row, n_col, n_row, by_left, down, zero, store(1))

    scale = 1.0 / residues
    flipped = jnp.concatenate([column[4][...] for column in columns], axis=1)
    sums = jnp.dot(flipped, d_ref[...], preferred_element_type=f32) * scale
    for s in range(5):
        weight_grad_ref[s] = sums[:, s * channels : (s + 1) * channels]
    weight_grad_ref[5] = scale * lax.dot_general(
        hat_ref[...], lin_ref[...], (((0,), (0,)), ((), ())), preferred_element_type=f32
    )
    total = jnp.zeros((tile, channels), f32)
    for s in range(5):
        total = total + lax.dot_general(
            d_ref[0:tile, s * channels : (s + 1) * channels], weights_ref[s],
            (((1,), (1,)), ((), ())), preferred_element_type=f32,
        )
    grad = norm_back(total * gains_ref[0:1], own_ref[0], own_ref[1])
    pair_grad_ref[...] = grad.astype(bf16).reshape(pair_grad_ref.shape)


def flip(block, n_row, n_col, even, odd):
    pairs = []
    for row in range(n_row):
        for col in range(n_col):
            shift = odd if col % 2 else even
            pairs.append((row * n_col + col, (row ^ shift[0]) * n_col + (col ^ shift[1])))
    return lax.ppermute(block, ("row", "col"), pairs)


def gathered_body(n_row, n_col, pair_act, pair_mask, crop_length, weights, in_gain, out_gain, cotangent):
    tile_rows, tile_cols, channels = pair_act.shape
    tile = tile_rows * tile_cols
    size = n_row * tile
    pairs = size * n_col
    head = tile + 2 * SUB
    f32, bf16 = jnp.float32, jnp.bfloat16
    vmem = pl.BlockSpec(memory_space=pltpu.VMEM)
    smem = pl.BlockSpec(memory_space=pltpu.SMEM)
    hbm = pl.BlockSpec(memory_space=pltpu.HBM)
    in_gain, out_gain = in_gain.reshape(1, channels), out_gain.reshape(1, channels)

    def limit(mib):
        return pltpu.CompilerParams(vmem_limit_bytes=mib * 1024 * 1024)

    own = pl.pallas_call(
        pack_kernel,
        name="pack",
        out_shape=jax.ShapeDtypeStruct((head + tile, channels), bf16),
        in_specs=[hbm] * 4,
        out_specs=vmem,
        scratch_shapes=[
            pltpu.VMEM(pair_act.shape, pair_act.dtype),
            pltpu.VMEM(pair_mask.shape, jnp.int32),
            pltpu.VMEM((1, channels), f32),
            pltpu.SemaphoreType.DMA((4,)),
        ],
        compiler_params=limit(60),
    )(pair_act, pair_mask, cotangent.reshape(tile, channels), in_gain)
    crop_length, own = lax.optimization_barrier((crop_length, own))

    def move(block, even, odd):
        return flip(block, n_row, n_col, even, odd)

    def other(block):
        return move(block, (0, 1), (0, 1))

    held = pl.pallas_call(
        copy_kernel,
        name="hold",
        out_shape=jax.ShapeDtypeStruct(own.shape, bf16),
        in_specs=[vmem],
        out_specs=vmem,
        compiler_params=limit(2),
        cost_estimate=pl.CostEstimate(flops=100_000_000, bytes_accessed=1_000_000, transcendentals=0),
    )(own)
    both = pl.pallas_call(
        join_kernel,
        name="join",
        out_shape=jax.ShapeDtypeStruct((2 * own.shape[0] - 2 * SUB, channels), bf16),
        in_specs=[vmem] * 2,
        out_specs=vmem,
        compiler_params=limit(2),
    )(held, other(own))
    straight = move(own, (3, 0), (3, 0))
    first = move(both, (2, 0), (1, 0))
    second = move(both, (0, 2), (2, 2))
    third = move(both, (1, 2), (3, 2))
    straight, first, second, third = [(block, other(block)) for block in (straight, first, second, third)]
    straight = pl.pallas_call(
        pair_kernel,
        name="pair",
        out_shape=(jax.ShapeDtypeStruct(own.shape, bf16),) * 2,
        in_specs=[vmem] * 2,
        out_specs=(vmem, vmem),
        compiler_params=limit(2),
        cost_estimate=pl.CostEstimate(flops=1_000_000_000, bytes_accessed=1_000_000, transcendentals=0),
    )(*straight)
    chips = (((1, None), (2, 1), (2, 0), (2, None)), ((2, 0), (2, 0), (2, 1), (2, 1)))
    sources = ((both, *first, *first, *straight), (*second, *third, *second, *third))

    tri, parts, extra = [], [], []
    for col in range(n_col):
        more = (pair_act, in_gain, out_gain) if col == 0 else tri
        more_shapes = () if col > 0 else (
            jax.ShapeDtypeStruct((2, tile, channels), f32),
            jax.ShapeDtypeStruct((SUB, channels), f32),
        )
        tri, *results = pl.pallas_call(
            functools.partial(column_kernel, n_row, n_col, col, chips[col // 2]),
            name=f"column_{col}",
            out_shape=(
                jax.ShapeDtypeStruct((pairs, channels), f32),
                jax.ShapeDtypeStruct((size, channels), f32),
                jax.ShapeDtypeStruct((size, channels), f32),
                jax.ShapeDtypeStruct((4, size, channels), f32),
                jax.ShapeDtypeStruct((size, channels), f32),
                jax.ShapeDtypeStruct((channels, size), bf16),
                *more_shapes,
            ),
            in_specs=[smem] + [vmem] * (1 + len(sources[col // 2]) + len(more)),
            out_specs=(vmem,) * (6 + len(more_shapes)),
            input_output_aliases={2 + len(sources[col // 2]): 0} if col > 0 else {},
            compiler_params=limit(8),
            cost_estimate=pl.CostEstimate(flops=400_000_000, bytes_accessed=1_000_000, transcendentals=0),
        )(crop_length, weights, *sources[col // 2], *more)
        tri = [tri]
        parts += [*sources[col // 2], *results[:5]]
        extra += results[5:]

    return pl.pallas_call(
        functools.partial(rest_kernel, n_row, n_col, chips),
        name="rest",
        out_shape=(
            jax.ShapeDtypeStruct(pair_act.shape, bf16),
            jax.ShapeDtypeStruct(pair_act.shape, bf16),
            jax.ShapeDtypeStruct(weights.shape, f32),
        ),
        in_specs=[vmem] * (4 + len(parts)),
        out_specs=(vmem, vmem, vmem),
        scratch_shapes=[
            pltpu.VMEM((pairs, channels), f32),
            pltpu.VMEM((pairs, channels), bf16),
            pltpu.VMEM((pairs, channels), bf16),
            pltpu.VMEM((pairs, 5 * channels), bf16),
        ],
        compiler_params=limit(16),
    )(weights, *extra, *tri, *parts)


def body(n_row, n_col, pair_act, *others):
    tile_rows, tile_cols, channels = pair_act.shape
    pairs = tile_rows * n_row * tile_cols * n_col
    small = pairs * channels * 4 <= 1024 * 1024 and channels == 128
    square = n_row == 4 and n_col == 4 and tile_rows == SUB and tile_cols == SUB
    if small and square:
        return gathered_body(n_row, n_col, pair_act, *others)
    return spread_body(pair_act, *others)


def solution(mesh):
    return jax.shard_map(
        functools.partial(body, mesh.shape["row"], mesh.shape["col"]),
        mesh=mesh,
        in_specs=(
            P(("parts", "row"), "col", None),
            P(("parts", "row"), "col"),
            P("parts"),
            P(),
            P(),
            P(),
            P(("parts", "row"), "col", None),
        ),
        out_specs=(
            P(("parts", "row"), "col", None),
            P(("parts", "row"), "col", None),
            P("parts", None, None),
        ),
        check_vma=False,
    )
```

```python
import functools

import jax
import jax.numpy as jnp
from jax import lax
from jax.experimental import pallas as pl
from jax.experimental.pallas import tpu as pltpu
from jax.sharding import PartitionSpec as P

SUB = 8
EPS = 1e-05


def normalize(values):
    average = jnp.mean(values, axis=-1, keepdims=True)
    centered = values - average
    inverse = lax.rsqrt(jnp.mean(centered * centered, axis=-1, keepdims=True) + 1e-05)
    return (centered * inverse, inverse)


def norm_back(grad_hat, values_hat, inverse):
    first = jnp.mean(grad_hat, axis=-1, keepdims=True)
    second = jnp.mean(grad_hat * values_hat, axis=-1, keepdims=True)
    return (grad_hat - first - values_hat * second) * inverse


def gate_back(grad_act, proj_value, proj_gate, keep_mask):
    gate_sig = jax.nn.sigmoid(proj_gate)
    masked = grad_act * keep_mask
    grad_value = (masked * gate_sig).astype(jnp.bfloat16)
    grad_gate = (masked * proj_value * gate_sig * (1.0 - gate_sig)).astype(jnp.bfloat16)
    return (grad_value, grad_gate)


def spread_body(pair_act, pair_mask, crop_length, weights, in_gain, out_gain, cotangent):
    tile_rows, tile_cols, channels = pair_act.shape
    residues = tile_rows * lax.axis_size("row")
    row_pos = lax.axis_index("row") * tile_rows + jnp.arange(tile_rows, dtype=jnp.int32)
    col_pos = lax.axis_index("col") * tile_cols + jnp.arange(tile_cols, dtype=jnp.int32)
    row_in = (row_pos < crop_length[0]).astype(jnp.float32)
    col_in = (col_pos < crop_length[0]).astype(jnp.float32)
    keep_mask = (pair_mask.astype(jnp.float32) * row_in[:, None] * col_in[None, :])[:, :, None]
    z_hat, z_inverse = normalize(pair_act.astype(jnp.float32))
    normed = (z_hat * in_gain).astype(jnp.bfloat16)
    flat_norm = normed.reshape(tile_rows * tile_cols, channels)
    projections = jnp.einsum(
        "pc,scd->spd", flat_norm, weights[:5], preferred_element_type=jnp.float32
    )
    projections = projections.reshape(5, tile_rows, tile_cols, channels)
    left_act = (jax.nn.sigmoid(projections[1]) * projections[0] * keep_mask).astype(jnp.bfloat16)
    right_act = (jax.nn.sigmoid(projections[3]) * projections[2] * keep_mask).astype(jnp.bfloat16)
    partial_value = jnp.einsum(
        "ikh,jkh->ijh",
        left_act,
        lax.all_gather(right_act, "row", axis=0, tiled=True),
        preferred_element_type=jnp.float32,
    )
    tri_sum = lax.psum_scatter(
        partial_value.astype(jnp.bfloat16), "col", scatter_dimension=1, tiled=True
    ).astype(jnp.float32)
    x_hat, x_inverse = normalize(tri_sum)
    normed_out = (x_hat * out_gain).astype(jnp.bfloat16)
    flat_out = normed_out.reshape(tile_rows * tile_cols, channels)
    update_lin = jnp.dot(flat_out, weights[5], preferred_element_type=jnp.float32)
    update_lin = update_lin.reshape(tile_rows, tile_cols, channels)
    out_gate = jax.nn.sigmoid(projections[4])
    update = (out_gate * update_lin).astype(jnp.bfloat16)
    cot_value = cotangent.astype(jnp.float32)
    grad_lin = (cot_value * out_gate).astype(jnp.bfloat16)
    grad_gate_out = (cot_value * update_lin * out_gate * (1.0 - out_gate)).astype(jnp.bfloat16)
    flat_lin = grad_lin.reshape(tile_rows * tile_cols, channels)
    grad_norm_out = jnp.einsum(
        "pd,cd->pc", flat_lin, weights[5], preferred_element_type=jnp.float32
    )
    grad_norm_out = grad_norm_out.reshape(tile_rows, tile_cols, channels)
    grad_tri = norm_back(grad_norm_out * out_gain, x_hat, x_inverse).astype(jnp.bfloat16)
    grad_full = lax.all_gather(grad_tri, "col", axis=1, tiled=True)
    grad_slab = grad_full
    grad_left = jnp.einsum(
        "ijh,jkh->ikh",
        grad_slab,
        lax.all_gather(right_act, "row", axis=0, tiled=True),
        preferred_element_type=jnp.float32,
    )
    grad_slab = grad_full
    grad_right = lax.psum_scatter(
        jnp.einsum("ijh,ikh->jkh", grad_slab, left_act, preferred_element_type=jnp.float32).astype(
            jnp.bfloat16
        ),
        "row",
        scatter_dimension=0,
        tiled=True,
    ).astype(jnp.float32)
    grad_pa, grad_ga = gate_back(grad_left, projections[0], projections[1], keep_mask)
    grad_pb, grad_gb = gate_back(grad_right, projections[2], projections[3], keep_mask)
    grads = jnp.stack([grad_pa, grad_ga, grad_pb, grad_gb, grad_gate_out]).reshape(
        5, tile_rows * tile_cols, channels
    )
    grad_normed = jnp.einsum("spd,scd->pc", grads, weights[:5], preferred_element_type=jnp.float32)
    grad_normed = grad_normed.reshape(tile_rows, tile_cols, channels)
    pair_grad = norm_back(grad_normed * in_gain, z_hat, z_inverse).astype(jnp.bfloat16)
    local_in = jnp.einsum("pc,spd->scd", flat_norm, grads, preferred_element_type=jnp.float32)
    local_out = jnp.dot(flat_out.T, flat_lin, preferred_element_type=jnp.float32)
    local_grads = jnp.concatenate([local_in, local_out[None]], axis=0) / residues
    weight_grad = lax.psum(local_grads, ("row", "col"))
    return (update, pair_grad, weight_grad)


def pack_kernel(act_hbm, mask_hbm, cot_hbm, gain_hbm, out_ref, act_ref, mask_ref, gain_ref, sems):
    tile_rows, tile_cols, channels = act_ref.shape
    pairs = tile_rows * tile_cols
    head = out_ref.shape[0] - pairs
    pack_copies = [
        pltpu.make_async_copy(act_hbm, act_ref, sems.at[0]),
        pltpu.make_async_copy(gain_hbm, gain_ref, sems.at[1]),
        pltpu.make_async_copy(mask_hbm, mask_ref, sems.at[2]),
        pltpu.make_async_copy(cot_hbm, out_ref.at[head : head + pairs], sems.at[3]),
    ]
    for copy in pack_copies:
        copy.start()
    for copy in pack_copies:
        copy.wait()
    z_hat, _ = normalize(act_ref[...].astype(jnp.float32).reshape(pairs, channels))
    out_ref[0:pairs] = (z_hat * gain_ref[...]).astype(jnp.bfloat16)
    keep = mask_ref[...].astype(jnp.float32)
    wide = jnp.concatenate([keep, jnp.zeros((tile_rows, channels - tile_cols), jnp.float32)], axis=1)
    tall = jnp.concatenate([wide, jnp.zeros((channels - tile_rows, channels), jnp.float32)], axis=0)
    out_ref[pairs:head] = tall.T[0 : head - pairs].astype(jnp.bfloat16)


def copy_kernel(in_ref, out_ref):
    out_ref[...] = in_ref[...]


def join_kernel(own_ref, twin_ref, out_ref):
    tile = SUB * SUB
    refs = (own_ref, twin_ref)
    for at, ref in enumerate(refs):
        out_ref[at * tile : (at + 1) * tile] = ref[0:tile]
        spot = 2 * tile + 2 * SUB + at * tile
        out_ref[spot : spot + tile] = ref[tile + 2 * SUB :]
    masks = [ref[tile : tile + 2 * SUB].astype(jnp.float32)[0:SUB] for ref in refs]
    out_ref[2 * tile : 2 * tile + 2 * SUB] = jnp.concatenate(masks, axis=0).astype(jnp.bfloat16)


def normed_rows(ref, sub):
    return ref[sub * SUB * SUB : (sub + 1) * SUB * SUB]


def mask_rows(ref, sub):
    at = ref.shape[0] // 2 // (SUB * SUB) * SUB * SUB
    return ref[at : at + 2 * SUB].astype(jnp.float32)[sub * SUB : (sub + 1) * SUB]


def cot_rows(ref, sub):
    at = ref.shape[0] // 2 // (SUB * SUB) * SUB * SUB + 2 * SUB
    return ref[at + sub * SUB * SUB : at + (sub + 1) * SUB * SUB]


def chip_rows(rows_of, refs, core, direct_on):
    if direct_on is None:
        return rows_of(refs[min(core, len(refs) - 1)], core if len(refs) == 1 else 0)
    here = lax.axis_index("col") % 2 == direct_on
    return jnp.where(here, rows_of(refs[0], core), rows_of(refs[1], 1 - core))


def split_chips(refs, chips):
    split, at = [], 0
    for width, direct_on in chips:
        split.append((refs[at : at + width], direct_on))
        at += width
    return split


def triangle(blocks, groups, steps, vectors_at, factors_at, start_at, store_at):
    def block(a, _):
        def step(q, totals):
            totals = list(totals)
            vectors = vectors_at(q)
            factors = factors_at(a, q)
            for inner in range(SUB):
                rows = [vectors(g, inner) for g in range(groups)]
                for lane in range(SUB):
                    factor = factors(lane, inner)
                    for g in range(groups):
                        at = lane * groups + g
                        totals[at] = totals[at] + factor * rows[g]
            return tuple(totals)

        totals = tuple(start_at(a, g, lane) for lane in range(SUB) for g in range(groups))
        totals = step(0, totals) if steps == 1 else lax.fori_loop(0, steps, step, totals)
        for g in range(groups):
            store_at(a, g, [totals[lane * groups + g] for lane in range(SUB)])
        return 0

    lax.fori_loop(0, blocks, block, 0)


def spread(ref, row):
    return jnp.broadcast_to(ref[pl.ds(row, 1), :], (SUB, ref.shape[-1]))


def line(ref, row):
    return ref[pl.ds(pl.multiple_of(row, SUB), SUB), :]


def column_kernel(n_row, n_col, col, chips, crop_ref, weights_ref, *refs):
    count = sum(width for width, _ in chips)
    chip_refs, refs = refs[:count], refs[count:]
    own_ref = None
    if col == 0:
        act_ref, in_gain_ref, out_gain_ref, *refs, own_ref, gains_ref = refs
        z_hat, z_inverse = normalize(act_ref[...].astype(jnp.float32).reshape(own_ref.shape[1:]))
        own_ref[0] = z_hat
        own_ref[1] = jnp.broadcast_to(z_inverse, z_hat.shape)
        gains_ref[0:1] = in_gain_ref[...]
        gains_ref[1:2] = out_gain_ref[...]
    else:
        gains_ref, *refs = refs
    tri_in, (tri_ref, left_ref, right_ref, side_ref, back_ref, flip_ref) = refs[:-6], refs[-6:]
    channels = weights_ref.shape[-1]
    tile = SUB * SUB
    size = n_row * tile
    bf16, f32 = jnp.bfloat16, jnp.float32
    row_me, col_me = lax.axis_index("row"), lax.axis_index("col")
    chip_list = split_chips(chip_refs, chips)
    normed = jnp.concatenate([chip_rows(normed_rows, chip, col % 2, on) for chip, on in chip_list], axis=0)
    flip_ref[0] = normed.astype(f32).T.astype(bf16)
    crop = crop_ref[0]
    col_offset = lax.broadcasted_iota(jnp.int32, (SUB, channels), 0)
    row_offset = lax.broadcasted_iota(jnp.int32, (SUB, channels), 1)
    cols_in = col_offset < crop - (col_me ^ col) * SUB
    kept = []
    for b, (chip, on) in enumerate(chip_list):
        keep = chip_rows(mask_rows, chip, col % 2, on)
        rows_in = row_offset < crop - (row_me ^ b) * SUB
        keep = jnp.where(rows_in & cols_in, keep, 0.0)
        kept += [jnp.broadcast_to(keep[:, at : at + 1], (SUB, channels)) for at in range(SUB)]
    kept = jnp.concatenate(kept, axis=0)
    for side, act_ref in enumerate((left_ref, right_ref)):
        pair = jnp.concatenate([weights_ref[2 * side], weights_ref[2 * side + 1]], axis=1)
        proj = jnp.dot(normed, pair, preferred_element_type=f32)
        gate = jax.nn.sigmoid(proj[:, channels:])
        masked = gate * kept
        act = masked * proj[:, :channels]
        act_ref[...] = act.astype(bf16).astype(f32)
        side_ref[2 * side] = masked
        side_ref[2 * side + 1] = act * (1.0 - gate)
    out_gate = jax.nn.sigmoid(jnp.dot(normed, weights_ref[4], preferred_element_type=f32))
    if own_ref is not None:
        own_ref[2] = out_gate[0:tile]
    cot = jnp.concatenate([chip_rows(cot_rows, chip, col % 2, on) for chip, on in chip_list], axis=0)
    grad = cot.astype(f32) * out_gate
    grad_lin = grad.astype(bf16)
    flip_ref[1] = grad_lin.astype(f32).T.astype(bf16)
    back_ref[0] = grad * (1.0 - out_gate)
    back = lax.dot_general(grad_lin, weights_ref[5], (((1,), (1,)), ((), ())), preferred_element_type=f32)
    back = back * gains_ref[1:2]
    back_ref[1] = back - jnp.mean(back, axis=-1, keepdims=True)
    turn = row_me ^ col_me

    def flipped(q):
        firsts = [(turn ^ g) * tile for g in range(n_col)]
        return lambda g, inner: right_ref[pl.ds(firsts[g] + inner, SUB, stride=SUB), :]

    def along(a, q):
        return lambda lane, inner: spread(left_ref, a * tile + lane * SUB + inner)

    def start(a, g, lane):
        if len(tri_in) == 0:
            return jnp.zeros((SUB, channels), f32)
        return line(tri_in[0], g * size + a * tile + lane * SUB)

    def store(a, g, values):
        for lane in range(SUB):
            tri_ref[pl.ds(pl.multiple_of(g * size + a * tile + lane * SUB, SUB), SUB), :] = values[lane]

    triangle(n_row, n_col, 1, flipped, along, start, store)


def rest_kernel(n_row, n_col, weights_ref, own_ref, gains_ref, tri_ref, *refs):
    columns = [refs[at * 5 : at * 5 + 5] for at in range(n_col)]
    update_ref, pair_grad_ref, weight_grad_ref, back_ref, hat_ref, d_ref = refs[5 * n_col :]
    channels = tri_ref.shape[-1]
    tile = SUB * SUB
    size = n_row * tile
    residues = n_row * SUB
    bf16, f32 = jnp.bfloat16, jnp.float32
    turn = lax.axis_index("row") ^ lax.axis_index("col")
    out_gain = gains_ref[1:2]
    for col, (_, _, _, backs_ref, _) in enumerate(columns):
        rows = slice(col * size, (col + 1) * size)
        x_hat, inverse = normalize(tri_ref[rows, :])
        normed_out = (x_hat * out_gain).astype(bf16)
        hat_ref[rows, :] = normed_out
        lin = jnp.dot(normed_out, weights_ref[5], preferred_element_type=f32)
        if col == 0:
            update_ref[...] = (own_ref[2] * lin[0:tile]).astype(bf16).reshape(update_ref.shape)
        d_ref[rows, 4 * channels : 5 * channels] = (backs_ref[0] * lin).astype(bf16)
        back = backs_ref[1]
        second = jnp.mean(back * x_hat, axis=-1, keepdims=True)
        back_ref[rows, :] = ((back - x_hat * second) * inverse).astype(bf16).astype(f32)

    lefts, rights, sides = [[column[at] for column in columns] for at in (0, 1, 2)]

    def zero(a, g, lane):
        return jnp.zeros((SUB, channels), f32)

    def store(side):
        def put(a, g, values):
            for lane in range(0, SUB, 2):
                at = pl.multiple_of(a * tile + lane * SUB, 2 * SUB)
                both = jnp.concatenate(values[lane : lane + 2], axis=0)
                rows = pl.ds(pl.multiple_of(g * size + at, 2 * SUB), 2 * SUB)
                for kind in range(2):
                    spot = (2 * side + kind) * channels
                    scaled = both * sides[g][2 * side + kind, pl.ds(at, 2 * SUB), :]
                    d_ref[rows, spot : spot + channels] = scaled.astype(bf16)
        return put

    def by_right(q):
        return lambda g, inner: line(rights[g], (q ^ turn) * tile + inner * SUB)

    def by_left(q):
        return lambda g, inner: line(lefts[g], q * tile + inner * SUB)

    def along(a, q):
        return lambda lane, inner: spread(back_ref, q * size + a * tile + lane * SUB + inner)

    def down(a, q):
        return lambda lane, inner: spread(back_ref, (a ^ turn) * size + q * tile + inner * SUB + lane)

    triangle(n_row, n_col, n_col, by_right, along, zero, store(0))
    triangle(n_row, n_col, n_row, by_left, down, zero, store(1))

    scale = 1.0 / residues
    flipped, lin_flipped = [jnp.concatenate([column[4][at] for column in columns], axis=1) for at in range(2)]
    sums = jnp.dot(flipped, d_ref[...], preferred_element_type=f32) * scale
    for s in range(5):
        weight_grad_ref[s] = sums[:, s * channels : (s + 1) * channels]
    weight_grad_ref[5] = jnp.dot(lin_flipped, hat_ref[...], preferred_element_type=f32).T * scale
    total = jnp.zeros((tile, channels), f32)
    for s in range(5):
        total = total + lax.dot_general(
            d_ref[0:tile, s * channels : (s + 1) * channels], weights_ref[s],
            (((1,), (1,)), ((), ())), preferred_element_type=f32,
        )
    grad = norm_back(total * gains_ref[0:1], own_ref[0], own_ref[1])
    pair_grad_ref[...] = grad.astype(bf16).reshape(pair_grad_ref.shape)


def flip(block, n_row, n_col, even, odd):
    pairs = []
    for row in range(n_row):
        for col in range(n_col):
            shift = odd if col % 2 else even
            pairs.append((row * n_col + col, (row ^ shift[0]) * n_col + (col ^ shift[1])))
    return lax.ppermute(block, ("row", "col"), pairs)


def gathered_body(n_row, n_col, pair_act, pair_mask, crop_length, weights, in_gain, out_gain, cotangent):
    tile_rows, tile_cols, channels = pair_act.shape
    tile = tile_rows * tile_cols
    size = n_row * tile
    pairs = size * n_col
    head = tile + 2 * SUB
    f32, bf16 = jnp.float32, jnp.bfloat16
    vmem = pl.BlockSpec(memory_space=pltpu.VMEM)
    smem = pl.BlockSpec(memory_space=pltpu.SMEM)
    hbm = pl.BlockSpec(memory_space=pltpu.HBM)
    in_gain, out_gain = in_gain.reshape(1, channels), out_gain.reshape(1, channels)

    def limit(mib):
        return pltpu.CompilerParams(vmem_limit_bytes=mib * 1024 * 1024)

    own = pl.pallas_call(
        pack_kernel,
        name="pack",
        out_shape=jax.ShapeDtypeStruct((head + tile, channels), bf16),
        in_specs=[hbm] * 4,
        out_specs=vmem,
        scratch_shapes=[
            pltpu.VMEM(pair_act.shape, pair_act.dtype),
            pltpu.VMEM(pair_mask.shape, jnp.int32),
            pltpu.VMEM((1, channels), f32),
            pltpu.SemaphoreType.DMA((4,)),
        ],
        compiler_params=limit(60),
    )(pair_act, pair_mask, cotangent.reshape(tile, channels), in_gain)
    crop_length, own = lax.optimization_barrier((crop_length, own))

    def move(block, even, odd):
        return flip(block, n_row, n_col, even, odd)

    def other(block):
        return move(block, (0, 1), (0, 1))

    held = pl.pallas_call(
        copy_kernel,
        name="hold",
        out_shape=jax.ShapeDtypeStruct(own.shape, bf16),
        in_specs=[vmem],
        out_specs=vmem,
        compiler_params=limit(2),
        cost_estimate=pl.CostEstimate(flops=100_000_000, bytes_accessed=1_000_000, transcendentals=0),
    )(own)
    both = pl.pallas_call(
        join_kernel,
        name="join",
        out_shape=jax.ShapeDtypeStruct((2 * own.shape[0] - 2 * SUB, channels), bf16),
        in_specs=[vmem] * 2,
        out_specs=vmem,
        compiler_params=limit(2),
    )(held, other(own))
    straight = move(own, (3, 0), (3, 0))
    first = move(both, (2, 0), (1, 0))
    second = move(both, (0, 2), (2, 2))
    third = move(both, (1, 2), (3, 2))
    straight, first, second, third = [(block, other(block)) for block in (straight, first, second, third)]
    chips = (((1, None), (2, 1), (2, 0), (2, None)), ((2, 0), (2, 0), (2, 1), (2, 1)))
    sources = ((both, *first, *first, *straight), (*second, *third, *second, *third))

    tri, parts, extra = [], [], []
    for col in range(n_col):
        more = (pair_act, in_gain, out_gain) if col == 0 else (extra[1], *tri)
        more_shapes = () if col > 0 else (
            jax.ShapeDtypeStruct((3, tile, channels), f32),
            jax.ShapeDtypeStruct((SUB, channels), f32),
        )
        tri, *results = pl.pallas_call(
            functools.partial(column_kernel, n_row, n_col, col, chips[col // 2]),
            name=f"column_{col}",
            out_shape=(
                jax.ShapeDtypeStruct((pairs, channels), f32),
                jax.ShapeDtypeStruct((size, channels), f32),
                jax.ShapeDtypeStruct((size, channels), f32),
                jax.ShapeDtypeStruct((4, size, channels), f32),
                jax.ShapeDtypeStruct((2, size, channels), f32),
                jax.ShapeDtypeStruct((2, channels, size), bf16),
                *more_shapes,
            ),
            in_specs=[smem] + [vmem] * (1 + len(sources[col // 2]) + len(more)),
            out_specs=(vmem,) * (6 + len(more_shapes)),
            input_output_aliases={3 + len(sources[col // 2]): 0} if col > 0 else {},
            compiler_params=limit(8),
            cost_estimate=pl.CostEstimate(flops=400_000_000, bytes_accessed=1_000_000, transcendentals=0),
        )(crop_length, weights, *sources[col // 2], *more)
        tri = [tri]
        parts += results[:5]
        extra += results[5:]

    return pl.pallas_call(
        functools.partial(rest_kernel, n_row, n_col),
        name="rest",
        out_shape=(
            jax.ShapeDtypeStruct(pair_act.shape, bf16),
            jax.ShapeDtypeStruct(pair_act.shape, bf16),
            jax.ShapeDtypeStruct(weights.shape, f32),
        ),
        in_specs=[vmem] * (4 + len(parts)),
        out_specs=(vmem, vmem, vmem),
        scratch_shapes=[
            pltpu.VMEM((pairs, channels), f32),
            pltpu.VMEM((pairs, channels), bf16),
            pltpu.VMEM((pairs, 5 * channels), bf16),
        ],
        compiler_params=limit(16),
    )(weights, *extra, *tri, *parts)


def body(n_row, n_col, pair_act, *others):
    tile_rows, tile_cols, channels = pair_act.shape
    pairs = tile_rows * n_row * tile_cols * n_col
    small = pairs * channels * 4 <= 1024 * 1024 and channels == 128
    square = n_row == 4 and n_col == 4 and tile_rows == SUB and tile_cols == SUB
    if small and square:
        return gathered_body(n_row, n_col, pair_act, *others)
    return spread_body(pair_act, *others)


def solution(mesh):
    return jax.shard_map(
        functools.partial(body, mesh.shape["row"], mesh.shape["col"]),
        mesh=mesh,
        in_specs=(
            P(("parts", "row"), "col", None),
            P(("parts", "row"), "col"),
            P("parts"),
            P(),
            P(),
            P(),
            P(("parts", "row"), "col", None),
        ),
        out_specs=(
            P(("parts", "row"), "col", None),
            P(("parts", "row"), "col", None),
            P("parts", None, None),
        ),
        check_vma=False,
    )
```

```python
import functools

import jax
import jax.numpy as jnp
from jax import lax
from jax.experimental import pallas as pl
from jax.experimental.pallas import tpu as pltpu
from jax.sharding import PartitionSpec as P

SUB = 8
EPS = 1e-05


def normalize(values):
    average = jnp.mean(values, axis=-1, keepdims=True)
    centered = values - average
    inverse = lax.rsqrt(jnp.mean(centered * centered, axis=-1, keepdims=True) + 1e-05)
    return (centered * inverse, inverse)


def norm_back(grad_hat, values_hat, inverse):
    first = jnp.mean(grad_hat, axis=-1, keepdims=True)
    second = jnp.mean(grad_hat * values_hat, axis=-1, keepdims=True)
    return (grad_hat - first - values_hat * second) * inverse


def gate_back(grad_act, proj_value, proj_gate, keep_mask):
    gate_sig = jax.nn.sigmoid(proj_gate)
    masked = grad_act * keep_mask
    grad_value = (masked * gate_sig).astype(jnp.bfloat16)
    grad_gate = (masked * proj_value * gate_sig * (1.0 - gate_sig)).astype(jnp.bfloat16)
    return (grad_value, grad_gate)


def spread_body(pair_act, pair_mask, crop_length, weights, in_gain, out_gain, cotangent):
    tile_rows, tile_cols, channels = pair_act.shape
    residues = tile_rows * lax.axis_size("row")
    row_pos = lax.axis_index("row") * tile_rows + jnp.arange(tile_rows, dtype=jnp.int32)
    col_pos = lax.axis_index("col") * tile_cols + jnp.arange(tile_cols, dtype=jnp.int32)
    row_in = (row_pos < crop_length[0]).astype(jnp.float32)
    col_in = (col_pos < crop_length[0]).astype(jnp.float32)
    keep_mask = (pair_mask.astype(jnp.float32) * row_in[:, None] * col_in[None, :])[:, :, None]
    z_hat, z_inverse = normalize(pair_act.astype(jnp.float32))
    normed = (z_hat * in_gain).astype(jnp.bfloat16)
    flat_norm = normed.reshape(tile_rows * tile_cols, channels)
    projections = jnp.einsum(
        "pc,scd->spd", flat_norm, weights[:5], preferred_element_type=jnp.float32
    )
    projections = projections.reshape(5, tile_rows, tile_cols, channels)
    left_act = (jax.nn.sigmoid(projections[1]) * projections[0] * keep_mask).astype(jnp.bfloat16)
    right_act = (jax.nn.sigmoid(projections[3]) * projections[2] * keep_mask).astype(jnp.bfloat16)
    partial_value = jnp.einsum(
        "ikh,jkh->ijh",
        left_act,
        lax.all_gather(right_act, "row", axis=0, tiled=True),
        preferred_element_type=jnp.float32,
    )
    tri_sum = lax.psum_scatter(
        partial_value.astype(jnp.bfloat16), "col", scatter_dimension=1, tiled=True
    ).astype(jnp.float32)
    x_hat, x_inverse = normalize(tri_sum)
    normed_out = (x_hat * out_gain).astype(jnp.bfloat16)
    flat_out = normed_out.reshape(tile_rows * tile_cols, channels)
    update_lin = jnp.dot(flat_out, weights[5], preferred_element_type=jnp.float32)
    update_lin = update_lin.reshape(tile_rows, tile_cols, channels)
    out_gate = jax.nn.sigmoid(projections[4])
    update = (out_gate * update_lin).astype(jnp.bfloat16)
    cot_value = cotangent.astype(jnp.float32)
    grad_lin = (cot_value * out_gate).astype(jnp.bfloat16)
    grad_gate_out = (cot_value * update_lin * out_gate * (1.0 - out_gate)).astype(jnp.bfloat16)
    flat_lin = grad_lin.reshape(tile_rows * tile_cols, channels)
    grad_norm_out = jnp.einsum(
        "pd,cd->pc", flat_lin, weights[5], preferred_element_type=jnp.float32
    )
    grad_norm_out = grad_norm_out.reshape(tile_rows, tile_cols, channels)
    grad_tri = norm_back(grad_norm_out * out_gain, x_hat, x_inverse).astype(jnp.bfloat16)
    grad_full = lax.all_gather(grad_tri, "col", axis=1, tiled=True)
    grad_slab = grad_full
    grad_left = jnp.einsum(
        "ijh,jkh->ikh",
        grad_slab,
        lax.all_gather(right_act, "row", axis=0, tiled=True),
        preferred_element_type=jnp.float32,
    )
    grad_slab = grad_full
    grad_right = lax.psum_scatter(
        jnp.einsum("ijh,ikh->jkh", grad_slab, left_act, preferred_element_type=jnp.float32).astype(
            jnp.bfloat16
        ),
        "row",
        scatter_dimension=0,
        tiled=True,
    ).astype(jnp.float32)
    grad_pa, grad_ga = gate_back(grad_left, projections[0], projections[1], keep_mask)
    grad_pb, grad_gb = gate_back(grad_right, projections[2], projections[3], keep_mask)
    grads = jnp.stack([grad_pa, grad_ga, grad_pb, grad_gb, grad_gate_out]).reshape(
        5, tile_rows * tile_cols, channels
    )
    grad_normed = jnp.einsum("spd,scd->pc", grads, weights[:5], preferred_element_type=jnp.float32)
    grad_normed = grad_normed.reshape(tile_rows, tile_cols, channels)
    pair_grad = norm_back(grad_normed * in_gain, z_hat, z_inverse).astype(jnp.bfloat16)
    local_in = jnp.einsum("pc,spd->scd", flat_norm, grads, preferred_element_type=jnp.float32)
    local_out = jnp.dot(flat_out.T, flat_lin, preferred_element_type=jnp.float32)
    local_grads = jnp.concatenate([local_in, local_out[None]], axis=0) / residues
    weight_grad = lax.psum(local_grads, ("row", "col"))
    return (update, pair_grad, weight_grad)


def pack_kernel(act_hbm, mask_hbm, cot_hbm, gain_hbm, out_ref, act_ref, mask_ref, gain_ref, sems):
    tile_rows, tile_cols, channels = act_ref.shape
    pairs = tile_rows * tile_cols
    head = out_ref.shape[0] - pairs
    pack_copies = [
        pltpu.make_async_copy(act_hbm, act_ref, sems.at[0]),
        pltpu.make_async_copy(gain_hbm, gain_ref, sems.at[1]),
        pltpu.make_async_copy(mask_hbm, mask_ref, sems.at[2]),
        pltpu.make_async_copy(cot_hbm, out_ref.at[head : head + pairs], sems.at[3]),
    ]
    for copy in pack_copies:
        copy.start()
    for copy in pack_copies:
        copy.wait()
    z_hat, _ = normalize(act_ref[...].astype(jnp.float32).reshape(pairs, channels))
    out_ref[0:pairs] = (z_hat * gain_ref[...]).astype(jnp.bfloat16)
    keep = mask_ref[...].astype(jnp.float32)
    wide = jnp.concatenate([keep, jnp.zeros((tile_rows, channels - tile_cols), jnp.float32)], axis=1)
    tall = jnp.concatenate([wide, jnp.zeros((channels - tile_rows, channels), jnp.float32)], axis=0)
    out_ref[pairs:head] = tall.T[0 : head - pairs].astype(jnp.bfloat16)


def copy_kernel(in_ref, out_ref):
    out_ref[...] = in_ref[...]


def join_kernel(own_ref, twin_ref, out_ref):
    tile = SUB * SUB
    refs = (own_ref, twin_ref)
    for at, ref in enumerate(refs):
        out_ref[at * tile : (at + 1) * tile] = ref[0:tile]
        spot = 2 * tile + 2 * SUB + at * tile
        out_ref[spot : spot + tile] = ref[tile + 2 * SUB :]
    masks = [ref[tile : tile + 2 * SUB].astype(jnp.float32)[0:SUB] for ref in refs]
    out_ref[2 * tile : 2 * tile + 2 * SUB] = jnp.concatenate(masks, axis=0).astype(jnp.bfloat16)


def normed_rows(ref, sub):
    return ref[sub * SUB * SUB : (sub + 1) * SUB * SUB]


def mask_rows(ref, sub):
    at = ref.shape[0] // 2 // (SUB * SUB) * SUB * SUB
    return ref[at : at + 2 * SUB].astype(jnp.float32)[sub * SUB : (sub + 1) * SUB]


def cot_rows(ref, sub):
    at = ref.shape[0] // 2 // (SUB * SUB) * SUB * SUB + 2 * SUB
    return ref[at + sub * SUB * SUB : at + (sub + 1) * SUB * SUB]


def chip_rows(rows_of, refs, core, direct_on):
    if direct_on is None:
        return rows_of(refs[min(core, len(refs) - 1)], core if len(refs) == 1 else 0)
    here = lax.axis_index("col") % 2 == direct_on
    return jnp.where(here, rows_of(refs[0], core), rows_of(refs[1], 1 - core))


def split_chips(refs, chips):
    split, at = [], 0
    for width, direct_on in chips:
        split.append((refs[at : at + width], direct_on))
        at += width
    return split


def triangle(blocks, groups, steps, vectors_at, factors_at, start_at, store_at):
    def block(a, _):
        def step(q, totals):
            totals = list(totals)
            vectors = vectors_at(q)
            factors = factors_at(a, q)
            for inner in range(SUB):
                rows = [vectors(g, inner) for g in range(groups)]
                for lane in range(SUB):
                    factor = factors(lane, inner)
                    for g in range(groups):
                        at = lane * groups + g
                        totals[at] = totals[at] + factor * rows[g]
            return tuple(totals)

        totals = tuple(start_at(a, g, lane) for lane in range(SUB) for g in range(groups))
        if steps > 2:
            totals = lax.fori_loop(0, steps, step, totals)
        else:
            for q in range(steps):
                totals = step(q, totals)
        for g in range(groups):
            store_at(a, g, [totals[lane * groups + g] for lane in range(SUB)])
        return 0

    lax.fori_loop(0, blocks, block, 0)


def spread(ref, row):
    return jnp.broadcast_to(ref[pl.ds(row, 1), :], (SUB, ref.shape[-1]))


def line(ref, row):
    return ref[pl.ds(pl.multiple_of(row, SUB), SUB), :]


def columns_kernel(n_row, n_col, side_x, chips, crop_ref, weights_ref, *refs):
    count = sum(width for width, _ in chips)
    chip_list, refs = split_chips(refs[:count], chips), refs[count:]
    own_ref = None
    if side_x == 0:
        act_ref, in_gain_ref, out_gain_ref, *refs, own_ref, gains_ref = refs
        z_hat, z_inverse = normalize(act_ref[...].astype(jnp.float32).reshape(own_ref.shape[1:]))
        own_ref[0] = z_hat
        own_ref[1] = jnp.broadcast_to(z_inverse, z_hat.shape)
        gains_ref[0:1] = in_gain_ref[...]
        gains_ref[1:2] = out_gain_ref[...]
    else:
        gains_ref, *refs = refs
    tri_in, (tri_ref, left_ref, right_ref, side_ref, back_ref, flip_ref) = refs[:-6], refs[-6:]
    channels = weights_ref.shape[-1]
    tile = SUB * SUB
    size = n_row * tile
    bf16, f32 = jnp.bfloat16, jnp.float32
    row_me, col_me = lax.axis_index("row"), lax.axis_index("col")
    chip_list = [(chip, on, core, b) for core in range(2) for b, (chip, on) in enumerate(chip_list)]
    normed = jnp.concatenate([chip_rows(normed_rows, chip, core, on) for chip, on, core, _ in chip_list], axis=0)
    flip_ref[0] = normed.astype(f32).T.astype(bf16)
    crop = crop_ref[0]
    col_offset = lax.broadcasted_iota(jnp.int32, (SUB, channels), 0)
    row_offset = lax.broadcasted_iota(jnp.int32, (SUB, channels), 1)
    kept = []
    for chip, on, core, b in chip_list:
        keep = chip_rows(mask_rows, chip, core, on)
        rows_in = row_offset < crop - (row_me ^ b) * SUB
        cols_in = col_offset < crop - (col_me ^ (2 * side_x + core)) * SUB
        keep = jnp.where(rows_in & cols_in, keep, 0.0)
        kept += [jnp.broadcast_to(keep[:, at : at + 1], (SUB, channels)) for at in range(SUB)]
    kept = jnp.concatenate(kept, axis=0)
    for side, act_ref in enumerate((left_ref, right_ref)):
        pair = jnp.concatenate([weights_ref[2 * side], weights_ref[2 * side + 1]], axis=1)
        proj = jnp.dot(normed, pair, preferred_element_type=f32)
        gate = jax.nn.sigmoid(proj[:, channels:])
        masked = gate * kept
        act = masked * proj[:, :channels]
        act_ref[...] = act.astype(bf16).astype(f32)
        side_ref[2 * side] = masked
        side_ref[2 * side + 1] = act * (1.0 - gate)
    out_gate = jax.nn.sigmoid(jnp.dot(normed, weights_ref[4], preferred_element_type=f32))
    if own_ref is not None:
        own_ref[2] = out_gate[0:tile]
    cot = jnp.concatenate([chip_rows(cot_rows, chip, core, on) for chip, on, core, _ in chip_list], axis=0)
    grad = cot.astype(f32) * out_gate
    grad_lin = grad.astype(bf16)
    flip_ref[1] = grad_lin.astype(f32).T.astype(bf16)
    back_ref[0] = grad * (1.0 - out_gate)
    back = lax.dot_general(grad_lin, weights_ref[5], (((1,), (1,)), ((), ())), preferred_element_type=f32)
    back = back * gains_ref[1:2]
    back_ref[1] = back - jnp.mean(back, axis=-1, keepdims=True)
    turn = row_me ^ col_me

    def flipped(q):
        firsts = [q * size + (turn ^ g) * tile for g in range(n_col)]
        return lambda g, inner: right_ref[pl.ds(firsts[g] + inner, SUB, stride=SUB), :]

    def along(a, q):
        return lambda lane, inner: spread(left_ref, q * size + a * tile + lane * SUB + inner)

    def start(a, g, lane):
        if len(tri_in) == 0:
            return jnp.zeros((SUB, channels), f32)
        return line(tri_in[0], g * size + a * tile + lane * SUB)

    def store(a, g, values):
        for lane in range(SUB):
            tri_ref[pl.ds(pl.multiple_of(g * size + a * tile + lane * SUB, SUB), SUB), :] = values[lane]

    triangle(n_row, n_col, 2, flipped, along, start, store)


def rest_kernel(n_row, n_col, weights_ref, own_ref, gains_ref, tri_ref, *refs):
    groups = [refs[at * 5 : at * 5 + 5] for at in range(n_col // 2)]
    update_ref, pair_grad_ref, weight_grad_ref, back_ref, hat_ref, d_ref = refs[5 * (n_col // 2) :]
    channels = tri_ref.shape[-1]
    tile = SUB * SUB
    size = n_row * tile
    columns = []
    for col in range(n_col):
        own = pl.ds(col % 2 * size, size)
        left, right, side, backs, _ = groups[col // 2]
        columns.append((left.at[own], right.at[own], side.at[:, own], backs.at[:, own]))
    residues = n_row * SUB
    bf16, f32 = jnp.bfloat16, jnp.float32
    turn = lax.axis_index("row") ^ lax.axis_index("col")
    out_gain = gains_ref[1:2]
    for col, (_, _, _, backs_ref) in enumerate(columns):
        rows = slice(col * size, (col + 1) * size)
        x_hat, inverse = normalize(tri_ref[rows, :])
        normed_out = (x_hat * out_gain).astype(bf16)
        hat_ref[rows, :] = normed_out
        lin = jnp.dot(normed_out, weights_ref[5], preferred_element_type=f32)
        if col == 0:
            update_ref[...] = (own_ref[2] * lin[0:tile]).astype(bf16).reshape(update_ref.shape)
        d_ref[rows, 4 * channels : 5 * channels] = (backs_ref[0] * lin).astype(bf16)
        back = backs_ref[1]
        second = jnp.mean(back * x_hat, axis=-1, keepdims=True)
        back_ref[rows, :] = ((back - x_hat * second) * inverse).astype(bf16).astype(f32)

    lefts, rights, sides = [[column[at] for column in columns] for at in (0, 1, 2)]

    def zero(a, g, lane):
        return jnp.zeros((SUB, channels), f32)

    def store(side):
        def put(a, g, values):
            for lane in range(0, SUB, 2):
                at = pl.multiple_of(a * tile + lane * SUB, 2 * SUB)
                both = jnp.concatenate(values[lane : lane + 2], axis=0)
                rows = pl.ds(pl.multiple_of(g * size + at, 2 * SUB), 2 * SUB)
                for kind in range(2):
                    spot = (2 * side + kind) * channels
                    scaled = both * sides[g][2 * side + kind, pl.ds(at, 2 * SUB), :]
                    d_ref[rows, spot : spot + channels] = scaled.astype(bf16)
        return put

    def by_right(q):
        return lambda g, inner: line(rights[g], (q ^ turn) * tile + inner * SUB)

    def by_left(q):
        return lambda g, inner: line(lefts[g], q * tile + inner * SUB)

    def along(a, q):
        return lambda lane, inner: spread(back_ref, q * size + a * tile + lane * SUB + inner)

    def down(a, q):
        return lambda lane, inner: spread(back_ref, (a ^ turn) * size + q * tile + inner * SUB + lane)

    triangle(n_row, n_col, n_col, by_right, along, zero, store(0))
    triangle(n_row, n_col, n_row, by_left, down, zero, store(1))

    scale = 1.0 / residues
    flipped, lin_flipped = [jnp.concatenate([group[4][at] for group in groups], axis=1) for at in range(2)]
    sums = jnp.dot(flipped, d_ref[...], preferred_element_type=f32) * scale
    for s in range(5):
        weight_grad_ref[s] = sums[:, s * channels : (s + 1) * channels]
    weight_grad_ref[5] = jnp.dot(lin_flipped, hat_ref[...], preferred_element_type=f32).T * scale
    total = jnp.zeros((tile, channels), f32)
    for s in range(5):
        total = total + lax.dot_general(
            d_ref[0:tile, s * channels : (s + 1) * channels], weights_ref[s],
            (((1,), (1,)), ((), ())), preferred_element_type=f32,
        )
    grad = norm_back(total * gains_ref[0:1], own_ref[0], own_ref[1])
    pair_grad_ref[...] = grad.astype(bf16).reshape(pair_grad_ref.shape)


def flip(block, n_row, n_col, even, odd):
    pairs = []
    for row in range(n_row):
        for col in range(n_col):
            shift = odd if col % 2 else even
            pairs.append((row * n_col + col, (row ^ shift[0]) * n_col + (col ^ shift[1])))
    return lax.ppermute(block, ("row", "col"), pairs)


def gathered_body(n_row, n_col, pair_act, pair_mask, crop_length, weights, in_gain, out_gain, cotangent):
    tile_rows, tile_cols, channels = pair_act.shape
    tile = tile_rows * tile_cols
    size = n_row * tile
    pairs = size * n_col
    head = tile + 2 * SUB
    f32, bf16 = jnp.float32, jnp.bfloat16
    vmem = pl.BlockSpec(memory_space=pltpu.VMEM)
    smem = pl.BlockSpec(memory_space=pltpu.SMEM)
    hbm = pl.BlockSpec(memory_space=pltpu.HBM)
    in_gain, out_gain = in_gain.reshape(1, channels), out_gain.reshape(1, channels)

    def limit(mib):
        return pltpu.CompilerParams(vmem_limit_bytes=mib * 1024 * 1024)

    own = pl.pallas_call(
        pack_kernel,
        name="pack",
        out_shape=jax.ShapeDtypeStruct((head + tile, channels), bf16),
        in_specs=[hbm] * 4,
        out_specs=vmem,
        scratch_shapes=[
            pltpu.VMEM(pair_act.shape, pair_act.dtype),
            pltpu.VMEM(pair_mask.shape, jnp.int32),
            pltpu.VMEM((1, channels), f32),
            pltpu.SemaphoreType.DMA((4,)),
        ],
        compiler_params=limit(60),
    )(pair_act, pair_mask, cotangent.reshape(tile, channels), in_gain)
    crop_length, own = lax.optimization_barrier((crop_length, own))

    def move(block, even, odd):
        return flip(block, n_row, n_col, even, odd)

    def other(block):
        return move(block, (0, 1), (0, 1))

    held = pl.pallas_call(
        copy_kernel,
        name="hold",
        out_shape=jax.ShapeDtypeStruct(own.shape, bf16),
        in_specs=[vmem],
        out_specs=vmem,
        compiler_params=limit(2),
        cost_estimate=pl.CostEstimate(flops=100_000_000, bytes_accessed=1_000_000, transcendentals=0),
    )(own)
    both = pl.pallas_call(
        join_kernel,
        name="join",
        out_shape=jax.ShapeDtypeStruct((2 * own.shape[0] - 2 * SUB, channels), bf16),
        in_specs=[vmem] * 2,
        out_specs=vmem,
        compiler_params=limit(2),
    )(held, other(own))
    straight = move(own, (3, 0), (3, 0))
    first = move(both, (2, 0), (1, 0))
    second = move(both, (0, 2), (2, 2))
    third = move(both, (1, 2), (3, 2))
    straight, first, second, third = [(block, other(block)) for block in (straight, first, second, third)]
    chips = (((1, None), (2, 1), (2, 0), (2, None)), ((2, 0), (2, 0), (2, 1), (2, 1)))
    sources = ((both, *first, *first, *straight), (*second, *third, *second, *third))

    tri, parts, extra = [], [], []
    for side_x in range(n_col // 2):
        more = (pair_act, in_gain, out_gain) if side_x == 0 else (extra[1], *tri)
        more_shapes = () if side_x > 0 else (
            jax.ShapeDtypeStruct((3, tile, channels), f32),
            jax.ShapeDtypeStruct((SUB, channels), f32),
        )
        tri, *results = pl.pallas_call(
            functools.partial(columns_kernel, n_row, n_col, side_x, chips[side_x]),
            name=f"columns_{side_x}",
            out_shape=(
                jax.ShapeDtypeStruct((pairs, channels), f32),
                jax.ShapeDtypeStruct((2 * size, channels), f32),
                jax.ShapeDtypeStruct((2 * size, channels), f32),
                jax.ShapeDtypeStruct((4, 2 * size, channels), f32),
                jax.ShapeDtypeStruct((2, 2 * size, channels), f32),
                jax.ShapeDtypeStruct((2, channels, 2 * size), bf16),
                *more_shapes,
            ),
            in_specs=[smem] + [vmem] * (1 + len(sources[side_x]) + len(more)),
            out_specs=(vmem,) * (6 + len(more_shapes)),
            input_output_aliases={3 + len(sources[side_x]): 0} if side_x > 0 else {},
            compiler_params=limit(12),
            cost_estimate=pl.CostEstimate(flops=800_000_000, bytes_accessed=1_000_000, transcendentals=0),
        )(crop_length, weights, *sources[side_x], *more)
        tri = [tri]
        parts += results[:5]
        extra += results[5:]

    return pl.pallas_call(
        functools.partial(rest_kernel, n_row, n_col),
        name="rest",
        out_shape=(
            jax.ShapeDtypeStruct(pair_act.shape, bf16),
            jax.ShapeDtypeStruct(pair_act.shape, bf16),
            jax.ShapeDtypeStruct(weights.shape, f32),
        ),
        in_specs=[vmem] * (4 + len(parts)),
        out_specs=(vmem, vmem, vmem),
        scratch_shapes=[
            pltpu.VMEM((pairs, channels), f32),
            pltpu.VMEM((pairs, channels), bf16),
            pltpu.VMEM((pairs, 5 * channels), bf16),
        ],
        compiler_params=limit(16),
    )(weights, *extra, *tri, *parts)


def body(n_row, n_col, pair_act, *others):
    tile_rows, tile_cols, channels = pair_act.shape
    pairs = tile_rows * n_row * tile_cols * n_col
    small = pairs * channels * 4 <= 1024 * 1024 and channels == 128
    square = n_row == 4 and n_col == 4 and tile_rows == SUB and tile_cols == SUB
    if small and square:
        return gathered_body(n_row, n_col, pair_act, *others)
    return spread_body(pair_act, *others)


def solution(mesh):
    return jax.shard_map(
        functools.partial(body, mesh.shape["row"], mesh.shape["col"]),
        mesh=mesh,
        in_specs=(
            P(("parts", "row"), "col", None),
            P(("parts", "row"), "col"),
            P("parts"),
            P(),
            P(),
            P(),
            P(("parts", "row"), "col", None),
        ),
        out_specs=(
            P(("parts", "row"), "col", None),
            P(("parts", "row"), "col", None),
            P("parts", None, None),
        ),
        check_vma=False,
    )
```

```python
import functools

import jax
import jax.numpy as jnp
from jax import lax
from jax.experimental import pallas as pl
from jax.experimental.pallas import tpu as pltpu
from jax.sharding import PartitionSpec as P

SUB = 8
EPS = 1e-05


def normalize(values):
    average = jnp.mean(values, axis=-1, keepdims=True)
    centered = values - average
    inverse = lax.rsqrt(jnp.mean(centered * centered, axis=-1, keepdims=True) + 1e-05)
    return (centered * inverse, inverse)


def norm_back(grad_hat, values_hat, inverse):
    first = jnp.mean(grad_hat, axis=-1, keepdims=True)
    second = jnp.mean(grad_hat * values_hat, axis=-1, keepdims=True)
    return (grad_hat - first - values_hat * second) * inverse


def gate_back(grad_act, proj_value, proj_gate, keep_mask):
    gate_sig = jax.nn.sigmoid(proj_gate)
    masked = grad_act * keep_mask
    grad_value = (masked * gate_sig).astype(jnp.bfloat16)
    grad_gate = (masked * proj_value * gate_sig * (1.0 - gate_sig)).astype(jnp.bfloat16)
    return (grad_value, grad_gate)


def spread_body(pair_act, pair_mask, crop_length, weights, in_gain, out_gain, cotangent):
    tile_rows, tile_cols, channels = pair_act.shape
    residues = tile_rows * lax.axis_size("row")
    row_pos = lax.axis_index("row") * tile_rows + jnp.arange(tile_rows, dtype=jnp.int32)
    col_pos = lax.axis_index("col") * tile_cols + jnp.arange(tile_cols, dtype=jnp.int32)
    row_in = (row_pos < crop_length[0]).astype(jnp.float32)
    col_in = (col_pos < crop_length[0]).astype(jnp.float32)
    keep_mask = (pair_mask.astype(jnp.float32) * row_in[:, None] * col_in[None, :])[:, :, None]
    z_hat, z_inverse = normalize(pair_act.astype(jnp.float32))
    normed = (z_hat * in_gain).astype(jnp.bfloat16)
    flat_norm = normed.reshape(tile_rows * tile_cols, channels)
    projections = jnp.einsum(
        "pc,scd->spd", flat_norm, weights[:5], preferred_element_type=jnp.float32
    )
    projections = projections.reshape(5, tile_rows, tile_cols, channels)
    left_act = (jax.nn.sigmoid(projections[1]) * projections[0] * keep_mask).astype(jnp.bfloat16)
    right_act = (jax.nn.sigmoid(projections[3]) * projections[2] * keep_mask).astype(jnp.bfloat16)
    partial_value = jnp.einsum(
        "ikh,jkh->ijh",
        left_act,
        lax.all_gather(right_act, "row", axis=0, tiled=True),
        preferred_element_type=jnp.float32,
    )
    tri_sum = lax.psum_scatter(
        partial_value.astype(jnp.bfloat16), "col", scatter_dimension=1, tiled=True
    ).astype(jnp.float32)
    x_hat, x_inverse = normalize(tri_sum)
    normed_out = (x_hat * out_gain).astype(jnp.bfloat16)
    flat_out = normed_out.reshape(tile_rows * tile_cols, channels)
    update_lin = jnp.dot(flat_out, weights[5], preferred_element_type=jnp.float32)
    update_lin = update_lin.reshape(tile_rows, tile_cols, channels)
    out_gate = jax.nn.sigmoid(projections[4])
    update = (out_gate * update_lin).astype(jnp.bfloat16)
    cot_value = cotangent.astype(jnp.float32)
    grad_lin = (cot_value * out_gate).astype(jnp.bfloat16)
    grad_gate_out = (cot_value * update_lin * out_gate * (1.0 - out_gate)).astype(jnp.bfloat16)
    flat_lin = grad_lin.reshape(tile_rows * tile_cols, channels)
    grad_norm_out = jnp.einsum(
        "pd,cd->pc", flat_lin, weights[5], preferred_element_type=jnp.float32
    )
    grad_norm_out = grad_norm_out.reshape(tile_rows, tile_cols, channels)
    grad_tri = norm_back(grad_norm_out * out_gain, x_hat, x_inverse).astype(jnp.bfloat16)
    grad_full = lax.all_gather(grad_tri, "col", axis=1, tiled=True)
    grad_slab = grad_full
    grad_left = jnp.einsum(
        "ijh,jkh->ikh",
        grad_slab,
        lax.all_gather(right_act, "row", axis=0, tiled=True),
        preferred_element_type=jnp.float32,
    )
    grad_slab = grad_full
    grad_right = lax.psum_scatter(
        jnp.einsum("ijh,ikh->jkh", grad_slab, left_act, preferred_element_type=jnp.float32).astype(
            jnp.bfloat16
        ),
        "row",
        scatter_dimension=0,
        tiled=True,
    ).astype(jnp.float32)
    grad_pa, grad_ga = gate_back(grad_left, projections[0], projections[1], keep_mask)
    grad_pb, grad_gb = gate_back(grad_right, projections[2], projections[3], keep_mask)
    grads = jnp.stack([grad_pa, grad_ga, grad_pb, grad_gb, grad_gate_out]).reshape(
        5, tile_rows * tile_cols, channels
    )
    grad_normed = jnp.einsum("spd,scd->pc", grads, weights[:5], preferred_element_type=jnp.float32)
    grad_normed = grad_normed.reshape(tile_rows, tile_cols, channels)
    pair_grad = norm_back(grad_normed * in_gain, z_hat, z_inverse).astype(jnp.bfloat16)
    local_in = jnp.einsum("pc,spd->scd", flat_norm, grads, preferred_element_type=jnp.float32)
    local_out = jnp.dot(flat_out.T, flat_lin, preferred_element_type=jnp.float32)
    local_grads = jnp.concatenate([local_in, local_out[None]], axis=0) / residues
    weight_grad = lax.psum(local_grads, ("row", "col"))
    return (update, pair_grad, weight_grad)


def pack_kernel(act_hbm, mask_hbm, cot_hbm, gain_hbm, out_ref, act_ref, mask_ref, gain_ref, sems):
    tile_rows, tile_cols, channels = act_ref.shape
    pairs = tile_rows * tile_cols
    head = out_ref.shape[0] - pairs
    pack_copies = [
        pltpu.make_async_copy(act_hbm, act_ref, sems.at[0]),
        pltpu.make_async_copy(gain_hbm, gain_ref, sems.at[1]),
        pltpu.make_async_copy(mask_hbm, mask_ref, sems.at[2]),
        pltpu.make_async_copy(cot_hbm, out_ref.at[head : head + pairs], sems.at[3]),
    ]
    for copy in pack_copies:
        copy.start()
    for copy in pack_copies:
        copy.wait()
    z_hat, _ = normalize(act_ref[...].astype(jnp.float32).reshape(pairs, channels))
    out_ref[0:pairs] = (z_hat * gain_ref[...]).astype(jnp.bfloat16)
    keep = mask_ref[...].astype(jnp.float32)
    wide = jnp.concatenate([keep, jnp.zeros((tile_rows, channels - tile_cols), jnp.float32)], axis=1)
    tall = jnp.concatenate([wide, jnp.zeros((channels - tile_rows, channels), jnp.float32)], axis=0)
    out_ref[pairs:head] = tall.T[0 : head - pairs].astype(jnp.bfloat16)


def copy_kernel(in_ref, out_ref):
    out_ref[...] = in_ref[...]


def join_kernel(own_ref, twin_ref, out_ref):
    tile = SUB * SUB
    refs = (own_ref, twin_ref)
    for at, ref in enumerate(refs):
        out_ref[at * tile : (at + 1) * tile] = ref[0:tile]
        spot = 2 * tile + 2 * SUB + at * tile
        out_ref[spot : spot + tile] = ref[tile + 2 * SUB :]
    masks = [ref[tile : tile + 2 * SUB].astype(jnp.float32)[0:SUB] for ref in refs]
    out_ref[2 * tile : 2 * tile + 2 * SUB] = jnp.concatenate(masks, axis=0).astype(jnp.bfloat16)


def normed_rows(ref, sub):
    return ref[sub * SUB * SUB : (sub + 1) * SUB * SUB]


def mask_rows(ref, sub):
    at = ref.shape[0] // 2 // (SUB * SUB) * SUB * SUB
    return ref[at : at + 2 * SUB].astype(jnp.float32)[sub * SUB : (sub + 1) * SUB]


def cot_rows(ref, sub):
    at = ref.shape[0] // 2 // (SUB * SUB) * SUB * SUB + 2 * SUB
    return ref[at + sub * SUB * SUB : at + (sub + 1) * SUB * SUB]


def chip_rows(rows_of, refs, core, direct_on):
    if direct_on is None:
        return rows_of(refs[min(core, len(refs) - 1)], core if len(refs) == 1 else 0)
    here = lax.axis_index("col") % 2 == direct_on
    return jnp.where(here, rows_of(refs[0], core), rows_of(refs[1], 1 - core))


def split_chips(refs, chips):
    split, at = [], 0
    for width, direct_on in chips:
        split.append((refs[at : at + width], direct_on))
        at += width
    return split


def triangle(blocks, groups, steps, vectors_at, factors_at, start_at, store_at):
    def block(a, _):
        def step(q, totals):
            totals = list(totals)
            vectors = vectors_at(q)
            factors = factors_at(a, q)
            for inner in range(SUB):
                rows = [vectors(g, inner) for g in range(groups)]
                for lane in range(SUB):
                    factor = factors(lane, inner)
                    for g in range(groups):
                        at = lane * groups + g
                        totals[at] = totals[at] + factor * rows[g]
            return tuple(totals)

        totals = tuple(start_at(a, g, lane) for lane in range(SUB) for g in range(groups))
        if steps > 4:
            totals = lax.fori_loop(0, steps, step, totals)
        else:
            for q in range(steps):
                totals = step(q, totals)
        for g in range(groups):
            store_at(a, g, [totals[lane * groups + g] for lane in range(SUB)])
        return 0

    lax.fori_loop(0, blocks, block, 0)


def spread(ref, row):
    return jnp.broadcast_to(ref[pl.ds(row, 1), :], (SUB, ref.shape[-1]))


def line(ref, row):
    return ref[pl.ds(pl.multiple_of(row, SUB), SUB), :]


def columns_kernel(n_row, n_col, side_x, chips, crop_ref, weights_ref, *refs):
    count = sum(width for width, _ in chips)
    chip_list, refs = split_chips(refs[:count], chips), refs[count:]
    own_ref = None
    if side_x == 0:
        act_ref, in_gain_ref, out_gain_ref, *refs, own_ref, gains_ref = refs
        z_hat, z_inverse = normalize(act_ref[...].astype(jnp.float32).reshape(own_ref.shape[1:]))
        own_ref[0] = z_hat
        own_ref[1] = jnp.broadcast_to(z_inverse, z_hat.shape)
        gains_ref[0:1] = in_gain_ref[...]
        gains_ref[1:2] = out_gain_ref[...]
    else:
        gains_ref, *refs = refs
    tri_in, (tri_ref, left_ref, right_ref, side_ref, back_ref, flip_ref) = refs[:-6], refs[-6:]
    channels = weights_ref.shape[-1]
    tile = SUB * SUB
    size = n_row * tile
    bf16, f32 = jnp.bfloat16, jnp.float32
    row_me, col_me = lax.axis_index("row"), lax.axis_index("col")
    chip_list = [(chip, on, core, b) for core in range(2) for b, (chip, on) in enumerate(chip_list)]
    normed = jnp.concatenate([chip_rows(normed_rows, chip, core, on) for chip, on, core, _ in chip_list], axis=0)
    same = lax.broadcasted_iota(jnp.int32, (channels, channels), 0) == lax.broadcasted_iota(jnp.int32, (channels, channels), 1)
    identity = jnp.where(same, 1.0, 0.0).astype(bf16)

    def turned(rows):
        return lax.dot_general(identity, rows, (((1,), (1,)), ((), ())), preferred_element_type=f32).astype(bf16)

    flip_ref[0] = turned(normed)
    crop = crop_ref[0]
    col_offset = lax.broadcasted_iota(jnp.int32, (SUB, channels), 0)
    row_offset = lax.broadcasted_iota(jnp.int32, (SUB, channels), 1)
    kept = []
    for chip, on, core, b in chip_list:
        keep = chip_rows(mask_rows, chip, core, on)
        rows_in = row_offset < crop - (row_me ^ b) * SUB
        cols_in = col_offset < crop - (col_me ^ (2 * side_x + core)) * SUB
        keep = jnp.where(rows_in & cols_in, keep, 0.0)
        kept += [jnp.broadcast_to(keep[:, at : at + 1], (SUB, channels)) for at in range(SUB)]
    kept = jnp.concatenate(kept, axis=0)
    for side, act_ref in enumerate((left_ref, right_ref)):
        pair = jnp.concatenate([weights_ref[2 * side], weights_ref[2 * side + 1]], axis=1)
        proj = jnp.dot(normed, pair, preferred_element_type=f32)
        gate = jax.nn.sigmoid(proj[:, channels:])
        masked = gate * kept
        act = masked * proj[:, :channels]
        act_ref[...] = act.astype(bf16).astype(f32)
        side_ref[2 * side] = masked
        side_ref[2 * side + 1] = act * (1.0 - gate)
    out_gate = jax.nn.sigmoid(jnp.dot(normed, weights_ref[4], preferred_element_type=f32))
    if own_ref is not None:
        own_ref[2] = out_gate[0:tile]
    cot = jnp.concatenate([chip_rows(cot_rows, chip, core, on) for chip, on, core, _ in chip_list], axis=0)
    grad = cot.astype(f32) * out_gate
    grad_lin = grad.astype(bf16)
    flip_ref[1] = turned(grad_lin)
    back_ref[0] = grad * (1.0 - out_gate)
    back = lax.dot_general(grad_lin, weights_ref[5], (((1,), (1,)), ((), ())), preferred_element_type=f32)
    back = back * gains_ref[1:2]
    back_ref[1] = back - jnp.mean(back, axis=-1, keepdims=True)
    turn = row_me ^ col_me

    def flipped(q):
        firsts = [q * size + (turn ^ g) * tile for g in range(n_col)]
        return lambda g, inner: right_ref[pl.ds(firsts[g] + inner, SUB, stride=SUB), :]

    def along(a, q):
        return lambda lane, inner: spread(left_ref, q * size + a * tile + lane * SUB + inner)

    def start(a, g, lane):
        if len(tri_in) == 0:
            return jnp.zeros((SUB, channels), f32)
        return line(tri_in[0], g * size + a * tile + lane * SUB)

    def store(a, g, values):
        for lane in range(SUB):
            tri_ref[pl.ds(pl.multiple_of(g * size + a * tile + lane * SUB, SUB), SUB), :] = values[lane]

    triangle(n_row, n_col, 2, flipped, along, start, store)


def rest_kernel(n_row, n_col, weights_ref, own_ref, gains_ref, tri_ref, *refs):
    groups = [refs[at * 5 : at * 5 + 5] for at in range(n_col // 2)]
    update_ref, pair_grad_ref, weight_grad_ref, back_ref, hat_ref, d_ref = refs[5 * (n_col // 2) :]
    channels = tri_ref.shape[-1]
    tile = SUB * SUB
    size = n_row * tile
    columns = []
    for col in range(n_col):
        own = pl.ds(col % 2 * size, size)
        left, right, side, backs, _ = groups[col // 2]
        columns.append((left.at[own], right.at[own], side.at[:, own], backs.at[:, own]))
    residues = n_row * SUB
    bf16, f32 = jnp.bfloat16, jnp.float32
    turn = lax.axis_index("row") ^ lax.axis_index("col")
    out_gain = gains_ref[1:2]
    for col, (_, _, _, backs_ref) in enumerate(columns):
        rows = slice(col * size, (col + 1) * size)
        x_hat, inverse = normalize(tri_ref[rows, :])
        normed_out = (x_hat * out_gain).astype(bf16)
        hat_ref[rows, :] = normed_out
        lin = jnp.dot(normed_out, weights_ref[5], preferred_element_type=f32)
        if col == 0:
            update_ref[...] = (own_ref[2] * lin[0:tile]).astype(bf16).reshape(update_ref.shape)
        d_ref[rows, 4 * channels : 5 * channels] = (backs_ref[0] * lin).astype(bf16)
        back = backs_ref[1]
        second = jnp.mean(back * x_hat, axis=-1, keepdims=True)
        back_ref[rows, :] = ((back - x_hat * second) * inverse).astype(bf16).astype(f32)

    lefts, rights, sides = [[column[at] for column in columns] for at in (0, 1, 2)]

    def zero(a, g, lane):
        return jnp.zeros((SUB, channels), f32)

    def store(side):
        def put(a, g, values):
            for lane in range(0, SUB, 2):
                at = pl.multiple_of(a * tile + lane * SUB, 2 * SUB)
                both = jnp.concatenate(values[lane : lane + 2], axis=0)
                rows = pl.ds(pl.multiple_of(g * size + at, 2 * SUB), 2 * SUB)
                for kind in range(2):
                    spot = (2 * side + kind) * channels
                    scaled = both * sides[g][2 * side + kind, pl.ds(at, 2 * SUB), :]
                    d_ref[rows, spot : spot + channels] = scaled.astype(bf16)
        return put

    def by_right(q):
        return lambda g, inner: line(rights[g], (q ^ turn) * tile + inner * SUB)

    def by_left(q):
        return lambda g, inner: line(lefts[g], q * tile + inner * SUB)

    def along(a, q):
        return lambda lane, inner: spread(back_ref, q * size + a * tile + lane * SUB + inner)

    def down(a, q):
        return lambda lane, inner: spread(back_ref, (a ^ turn) * size + q * tile + inner * SUB + lane)

    triangle(n_row, n_col, n_col, by_right, along, zero, store(0))
    triangle(n_row, n_col, n_row, by_left, down, zero, store(1))

    scale = 1.0 / residues
    flipped, lin_flipped = [jnp.concatenate([group[4][at] for group in groups], axis=1) for at in range(2)]
    sums = jnp.dot(flipped, d_ref[...], preferred_element_type=f32) * scale
    for s in range(5):
        weight_grad_ref[s] = sums[:, s * channels : (s + 1) * channels]
    weight_grad_ref[5] = jnp.dot(lin_flipped, hat_ref[...], preferred_element_type=f32).T * scale
    total = jnp.zeros((tile, channels), f32)
    for s in range(5):
        total = total + lax.dot_general(
            d_ref[0:tile, s * channels : (s + 1) * channels], weights_ref[s],
            (((1,), (1,)), ((), ())), preferred_element_type=f32,
        )
    grad = norm_back(total * gains_ref[0:1], own_ref[0], own_ref[1])
    pair_grad_ref[...] = grad.astype(bf16).reshape(pair_grad_ref.shape)


def flip(block, n_row, n_col, even, odd):
    pairs = []
    for row in range(n_row):
        for col in range(n_col):
            shift = odd if col % 2 else even
            pairs.append((row * n_col + col, (row ^ shift[0]) * n_col + (col ^ shift[1])))
    return lax.ppermute(block, ("row", "col"), pairs)


def gathered_body(n_row, n_col, pair_act, pair_mask, crop_length, weights, in_gain, out_gain, cotangent):
    tile_rows, tile_cols, channels = pair_act.shape
    tile = tile_rows * tile_cols
    size = n_row * tile
    pairs = size * n_col
    head = tile + 2 * SUB
    f32, bf16 = jnp.float32, jnp.bfloat16
    vmem = pl.BlockSpec(memory_space=pltpu.VMEM)
    smem = pl.BlockSpec(memory_space=pltpu.SMEM)
    hbm = pl.BlockSpec(memory_space=pltpu.HBM)
    in_gain, out_gain = in_gain.reshape(1, channels), out_gain.reshape(1, channels)

    def limit(mib):
        return pltpu.CompilerParams(vmem_limit_bytes=mib * 1024 * 1024)

    own = pl.pallas_call(
        pack_kernel,
        name="pack",
        out_shape=jax.ShapeDtypeStruct((head + tile, channels), bf16),
        in_specs=[hbm] * 4,
        out_specs=vmem,
        scratch_shapes=[
            pltpu.VMEM(pair_act.shape, pair_act.dtype),
            pltpu.VMEM(pair_mask.shape, jnp.int32),
            pltpu.VMEM((1, channels), f32),
            pltpu.SemaphoreType.DMA((4,)),
        ],
        compiler_params=limit(60),
    )(pair_act, pair_mask, cotangent.reshape(tile, channels), in_gain)
    crop_length, own = lax.optimization_barrier((crop_length, own))

    def move(block, even, odd):
        return flip(block, n_row, n_col, even, odd)

    def other(block):
        return move(block, (0, 1), (0, 1))

    held = pl.pallas_call(
        copy_kernel,
        name="hold",
        out_shape=jax.ShapeDtypeStruct(own.shape, bf16),
        in_specs=[vmem],
        out_specs=vmem,
        compiler_params=limit(2),
        cost_estimate=pl.CostEstimate(flops=100_000_000, bytes_accessed=1_000_000, transcendentals=0),
    )(own)
    both = pl.pallas_call(
        join_kernel,
        name="join",
        out_shape=jax.ShapeDtypeStruct((2 * own.shape[0] - 2 * SUB, channels), bf16),
        in_specs=[vmem] * 2,
        out_specs=vmem,
        compiler_params=limit(2),
    )(held, other(own))
    straight = move(own, (3, 0), (3, 0))
    first = move(both, (2, 0), (1, 0))
    second = move(both, (0, 2), (2, 2))
    third = move(both, (1, 2), (3, 2))
    straight, first, second, third = [(block, other(block)) for block in (straight, first, second, third)]
    chips = (((1, None), (2, 1), (2, 0), (2, None)), ((2, 0), (2, 0), (2, 1), (2, 1)))
    sources = ((both, *first, *first, *straight), (*second, *third, *second, *third))

    tri, parts, extra = [], [], []
    for side_x in range(n_col // 2):
        more = (pair_act, in_gain, out_gain) if side_x == 0 else (extra[1], *tri)
        more_shapes = () if side_x > 0 else (
            jax.ShapeDtypeStruct((3, tile, channels), f32),
            jax.ShapeDtypeStruct((SUB, channels), f32),
        )
        tri, *results = pl.pallas_call(
            functools.partial(columns_kernel, n_row, n_col, side_x, chips[side_x]),
            name=f"columns_{side_x}",
            out_shape=(
                jax.ShapeDtypeStruct((pairs, channels), f32),
                jax.ShapeDtypeStruct((2 * size, channels), f32),
                jax.ShapeDtypeStruct((2 * size, channels), f32),
                jax.ShapeDtypeStruct((4, 2 * size, channels), f32),
                jax.ShapeDtypeStruct((2, 2 * size, channels), f32),
                jax.ShapeDtypeStruct((2, channels, 2 * size), bf16),
                *more_shapes,
            ),
            in_specs=[smem] + [vmem] * (1 + len(sources[side_x]) + len(more)),
            out_specs=(vmem,) * (6 + len(more_shapes)),
            input_output_aliases={3 + len(sources[side_x]): 0} if side_x > 0 else {},
            compiler_params=limit(12),
            cost_estimate=pl.CostEstimate(flops=800_000_000, bytes_accessed=1_000_000, transcendentals=0),
        )(crop_length, weights, *sources[side_x], *more)
        tri = [tri]
        parts += results[:5]
        extra += results[5:]

    return pl.pallas_call(
        functools.partial(rest_kernel, n_row, n_col),
        name="rest",
        out_shape=(
            jax.ShapeDtypeStruct(pair_act.shape, bf16),
            jax.ShapeDtypeStruct(pair_act.shape, bf16),
            jax.ShapeDtypeStruct(weights.shape, f32),
        ),
        in_specs=[vmem] * (4 + len(parts)),
        out_specs=(vmem, vmem, vmem),
        scratch_shapes=[
            pltpu.VMEM((pairs, channels), f32),
            pltpu.VMEM((pairs, channels), bf16),
            pltpu.VMEM((pairs, 5 * channels), bf16),
        ],
        compiler_params=limit(16),
    )(weights, *extra, *tri, *parts)


def body(n_row, n_col, pair_act, *others):
    tile_rows, tile_cols, channels = pair_act.shape
    pairs = tile_rows * n_row * tile_cols * n_col
    small = pairs * channels * 4 <= 1024 * 1024 and channels == 128
    square = n_row == 4 and n_col == 4 and tile_rows == SUB and tile_cols == SUB
    if small and square:
        return gathered_body(n_row, n_col, pair_act, *others)
    return spread_body(pair_act, *others)


def solution(mesh):
    return jax.shard_map(
        functools.partial(body, mesh.shape["row"], mesh.shape["col"]),
        mesh=mesh,
        in_specs=(
            P(("parts", "row"), "col", None),
            P(("parts", "row"), "col"),
            P("parts"),
            P(),
            P(),
            P(),
            P(("parts", "row"), "col", None),
        ),
        out_specs=(
            P(("parts", "row"), "col", None),
            P(("parts", "row"), "col", None),
            P("parts", None, None),
        ),
        check_vma=False,
    )
```

```python
import functools

import jax
import jax.numpy as jnp
from jax import lax
from jax.experimental import pallas as pl
from jax.experimental.pallas import tpu as pltpu
from jax.sharding import PartitionSpec as P

SUB = 8
EPS = 1e-05


def normalize(values):
    average = jnp.mean(values, axis=-1, keepdims=True)
    centered = values - average
    inverse = lax.rsqrt(jnp.mean(centered * centered, axis=-1, keepdims=True) + 1e-05)
    return (centered * inverse, inverse)


def norm_back(grad_hat, values_hat, inverse):
    first = jnp.mean(grad_hat, axis=-1, keepdims=True)
    second = jnp.mean(grad_hat * values_hat, axis=-1, keepdims=True)
    return (grad_hat - first - values_hat * second) * inverse


def gate_back(grad_act, proj_value, proj_gate, keep_mask):
    gate_sig = jax.nn.sigmoid(proj_gate)
    masked = grad_act * keep_mask
    grad_value = (masked * gate_sig).astype(jnp.bfloat16)
    grad_gate = (masked * proj_value * gate_sig * (1.0 - gate_sig)).astype(jnp.bfloat16)
    return (grad_value, grad_gate)


def spread_body(pair_act, pair_mask, crop_length, weights, in_gain, out_gain, cotangent):
    tile_rows, tile_cols, channels = pair_act.shape
    residues = tile_rows * lax.axis_size("row")
    row_pos = lax.axis_index("row") * tile_rows + jnp.arange(tile_rows, dtype=jnp.int32)
    col_pos = lax.axis_index("col") * tile_cols + jnp.arange(tile_cols, dtype=jnp.int32)
    row_in = (row_pos < crop_length[0]).astype(jnp.float32)
    col_in = (col_pos < crop_length[0]).astype(jnp.float32)
    keep_mask = (pair_mask.astype(jnp.float32) * row_in[:, None] * col_in[None, :])[:, :, None]
    z_hat, z_inverse = normalize(pair_act.astype(jnp.float32))
    normed = (z_hat * in_gain).astype(jnp.bfloat16)
    flat_norm = normed.reshape(tile_rows * tile_cols, channels)
    projections = jnp.einsum(
        "pc,scd->spd", flat_norm, weights[:5], preferred_element_type=jnp.float32
    )
    projections = projections.reshape(5, tile_rows, tile_cols, channels)
    left_act = (jax.nn.sigmoid(projections[1]) * projections[0] * keep_mask).astype(jnp.bfloat16)
    right_act = (jax.nn.sigmoid(projections[3]) * projections[2] * keep_mask).astype(jnp.bfloat16)
    partial_value = jnp.einsum(
        "ikh,jkh->ijh",
        left_act,
        lax.all_gather(right_act, "row", axis=0, tiled=True),
        preferred_element_type=jnp.float32,
    )
    tri_sum = lax.psum_scatter(
        partial_value.astype(jnp.bfloat16), "col", scatter_dimension=1, tiled=True
    ).astype(jnp.float32)
    x_hat, x_inverse = normalize(tri_sum)
    normed_out = (x_hat * out_gain).astype(jnp.bfloat16)
    flat_out = normed_out.reshape(tile_rows * tile_cols, channels)
    update_lin = jnp.dot(flat_out, weights[5], preferred_element_type=jnp.float32)
    update_lin = update_lin.reshape(tile_rows, tile_cols, channels)
    out_gate = jax.nn.sigmoid(projections[4])
    update = (out_gate * update_lin).astype(jnp.bfloat16)
    cot_value = cotangent.astype(jnp.float32)
    grad_lin = (cot_value * out_gate).astype(jnp.bfloat16)
    grad_gate_out = (cot_value * update_lin * out_gate * (1.0 - out_gate)).astype(jnp.bfloat16)
    flat_lin = grad_lin.reshape(tile_rows * tile_cols, channels)
    grad_norm_out = jnp.einsum(
        "pd,cd->pc", flat_lin, weights[5], preferred_element_type=jnp.float32
    )
    grad_norm_out = grad_norm_out.reshape(tile_rows, tile_cols, channels)
    grad_tri = norm_back(grad_norm_out * out_gain, x_hat, x_inverse).astype(jnp.bfloat16)
    grad_full = lax.all_gather(grad_tri, "col", axis=1, tiled=True)
    grad_slab = grad_full
    grad_left = jnp.einsum(
        "ijh,jkh->ikh",
        grad_slab,
        lax.all_gather(right_act, "row", axis=0, tiled=True),
        preferred_element_type=jnp.float32,
    )
    grad_slab = grad_full
    grad_right = lax.psum_scatter(
        jnp.einsum("ijh,ikh->jkh", grad_slab, left_act, preferred_element_type=jnp.float32).astype(
            jnp.bfloat16
        ),
        "row",
        scatter_dimension=0,
        tiled=True,
    ).astype(jnp.float32)
    grad_pa, grad_ga = gate_back(grad_left, projections[0], projections[1], keep_mask)
    grad_pb, grad_gb = gate_back(grad_right, projections[2], projections[3], keep_mask)
    grads = jnp.stack([grad_pa, grad_ga, grad_pb, grad_gb, grad_gate_out]).reshape(
        5, tile_rows * tile_cols, channels
    )
    grad_normed = jnp.einsum("spd,scd->pc", grads, weights[:5], preferred_element_type=jnp.float32)
    grad_normed = grad_normed.reshape(tile_rows, tile_cols, channels)
    pair_grad = norm_back(grad_normed * in_gain, z_hat, z_inverse).astype(jnp.bfloat16)
    local_in = jnp.einsum("pc,spd->scd", flat_norm, grads, preferred_element_type=jnp.float32)
    local_out = jnp.dot(flat_out.T, flat_lin, preferred_element_type=jnp.float32)
    local_grads = jnp.concatenate([local_in, local_out[None]], axis=0) / residues
    weight_grad = lax.psum(local_grads, ("row", "col"))
    return (update, pair_grad, weight_grad)


def pack_kernel(act_hbm, mask_hbm, cot_hbm, gain_hbm, out_ref, act_ref, mask_ref, gain_ref, sems):
    tile_rows, tile_cols, channels = act_ref.shape
    pairs = tile_rows * tile_cols
    head = out_ref.shape[0] - pairs
    pack_copies = [
        pltpu.make_async_copy(act_hbm, act_ref, sems.at[0]),
        pltpu.make_async_copy(gain_hbm, gain_ref, sems.at[1]),
        pltpu.make_async_copy(mask_hbm, mask_ref, sems.at[2]),
        pltpu.make_async_copy(cot_hbm, out_ref.at[head : head + pairs], sems.at[3]),
    ]
    for copy in pack_copies:
        copy.start()
    for copy in pack_copies:
        copy.wait()
    z_hat, _ = normalize(act_ref[...].astype(jnp.float32).reshape(pairs, channels))
    out_ref[0:pairs] = (z_hat * gain_ref[...]).astype(jnp.bfloat16)
    keep = mask_ref[...].astype(jnp.float32)
    wide = jnp.concatenate([keep, jnp.zeros((tile_rows, channels - tile_cols), jnp.float32)], axis=1)
    tall = jnp.concatenate([wide, jnp.zeros((channels - tile_rows, channels), jnp.float32)], axis=0)
    out_ref[pairs:head] = tall.T[0 : head - pairs].astype(jnp.bfloat16)


def copy_kernel(in_ref, out_ref):
    out_ref[...] = in_ref[...]


def join_kernel(own_ref, twin_ref, out_ref):
    tile = SUB * SUB
    refs = (own_ref, twin_ref)
    for at, ref in enumerate(refs):
        out_ref[at * tile : (at + 1) * tile] = ref[0:tile]
        spot = 2 * tile + 2 * SUB + at * tile
        out_ref[spot : spot + tile] = ref[tile + 2 * SUB :]
    masks = [ref[tile : tile + 2 * SUB].astype(jnp.float32)[0:SUB] for ref in refs]
    out_ref[2 * tile : 2 * tile + 2 * SUB] = jnp.concatenate(masks, axis=0).astype(jnp.bfloat16)


def normed_rows(ref, sub):
    return ref[sub * SUB * SUB : (sub + 1) * SUB * SUB]


def mask_rows(ref, sub):
    at = ref.shape[0] // 2 // (SUB * SUB) * SUB * SUB
    return ref[at : at + 2 * SUB].astype(jnp.float32)[sub * SUB : (sub + 1) * SUB]


def cot_rows(ref, sub):
    at = ref.shape[0] // 2 // (SUB * SUB) * SUB * SUB + 2 * SUB
    return ref[at + sub * SUB * SUB : at + (sub + 1) * SUB * SUB]


def chip_rows(rows_of, refs, core, direct_on):
    if direct_on is None:
        return rows_of(refs[min(core, len(refs) - 1)], core if len(refs) == 1 else 0)
    here = lax.axis_index("col") % 2 == direct_on
    return jnp.where(here, rows_of(refs[0], core), rows_of(refs[1], 1 - core))


def split_chips(refs, chips):
    split, at = [], 0
    for width, direct_on in chips:
        split.append((refs[at : at + width], direct_on))
        at += width
    return split


def triangle(blocks, groups, steps, vectors_at, factors_at, start_at, store_at):
    def block(a, _):
        def step(q, totals):
            totals = list(totals)
            vectors = vectors_at(q)
            factors = factors_at(a, q)
            for inner in range(SUB):
                rows = [vectors(g, inner) for g in range(groups)]
                for lane in range(SUB):
                    factor = factors(lane, inner)
                    for g in range(groups):
                        at = lane * groups + g
                        totals[at] = totals[at] + factor * rows[g]
            return tuple(totals)

        totals = tuple(start_at(a, g, lane) for lane in range(SUB) for g in range(groups))
        if steps > 4:
            totals = lax.fori_loop(0, steps, step, totals)
        else:
            for q in range(steps):
                totals = step(q, totals)
        for g in range(groups):
            store_at(a, g, [totals[lane * groups + g] for lane in range(SUB)])
        return 0

    lax.fori_loop(0, blocks, block, 0)


def spread(ref, row):
    return jnp.broadcast_to(ref[pl.ds(row, 1), :], (SUB, ref.shape[-1]))


def line(ref, row):
    return ref[pl.ds(pl.multiple_of(row, SUB), SUB), :]


def columns_kernel(n_row, n_col, side_x, is_first, chips, crop_ref, weights_ref, *refs):
    count = sum(width for width, _ in chips)
    chip_list, refs = split_chips(refs[:count], chips), refs[count:]
    gate_ref = None
    if is_first:
        act_ref, in_gain_ref, out_gain_ref, *refs, gains_ref, own_ref = refs
        z_hat, z_inverse = normalize(act_ref[...].astype(jnp.float32).reshape(own_ref.shape[1:]))
        own_ref[0] = z_hat
        own_ref[1] = jnp.broadcast_to(z_inverse, z_hat.shape)
        gains_ref[0:1] = in_gain_ref[...]
        gains_ref[1:2] = out_gain_ref[...]
    else:
        gains_ref, *refs = refs
        if side_x == 0:
            *refs, gate_ref = refs
    tri_in, (tri_ref, left_ref, right_ref, side_ref, back_ref, flip_ref) = refs[:-6], refs[-6:]
    channels = weights_ref.shape[-1]
    tile = SUB * SUB
    size = n_row * tile
    bf16, f32 = jnp.bfloat16, jnp.float32
    row_me, col_me = lax.axis_index("row"), lax.axis_index("col")
    chip_list = [(chip, on, core, b) for core in range(2) for b, (chip, on) in enumerate(chip_list)]
    normed = jnp.concatenate([chip_rows(normed_rows, chip, core, on) for chip, on, core, _ in chip_list], axis=0)
    same = lax.broadcasted_iota(jnp.int32, (channels, channels), 0) == lax.broadcasted_iota(jnp.int32, (channels, channels), 1)
    identity = jnp.where(same, 1.0, 0.0).astype(bf16)

    def turned(rows):
        return lax.dot_general(identity, rows, (((1,), (1,)), ((), ())), preferred_element_type=f32).astype(bf16)

    flip_ref[0] = turned(normed)
    crop = crop_ref[0]
    col_offset = lax.broadcasted_iota(jnp.int32, (SUB, channels), 0)
    row_offset = lax.broadcasted_iota(jnp.int32, (SUB, channels), 1)
    kept = []
    for chip, on, core, b in chip_list:
        keep = chip_rows(mask_rows, chip, core, on)
        rows_in = row_offset < crop - (row_me ^ b) * SUB
        cols_in = col_offset < crop - (col_me ^ (2 * side_x + core)) * SUB
        keep = jnp.where(rows_in & cols_in, keep, 0.0)
        kept += [jnp.broadcast_to(keep[:, at : at + 1], (SUB, channels)) for at in range(SUB)]
    kept = jnp.concatenate(kept, axis=0)
    for side, act_ref in enumerate((left_ref, right_ref)):
        pair = jnp.concatenate([weights_ref[2 * side], weights_ref[2 * side + 1]], axis=1)
        proj = jnp.dot(normed, pair, preferred_element_type=f32)
        gate = jax.nn.sigmoid(proj[:, channels:])
        masked = gate * kept
        act = masked * proj[:, :channels]
        act_ref[...] = act.astype(bf16).astype(f32)
        side_ref[2 * side] = masked
        side_ref[2 * side + 1] = act * (1.0 - gate)
    out_gate = jax.nn.sigmoid(jnp.dot(normed, weights_ref[4], preferred_element_type=f32))
    if gate_ref is not None:
        gate_ref[...] = out_gate[0:tile]
    cot = jnp.concatenate([chip_rows(cot_rows, chip, core, on) for chip, on, core, _ in chip_list], axis=0)
    grad = cot.astype(f32) * out_gate
    grad_lin = grad.astype(bf16)
    flip_ref[1] = turned(grad_lin)
    back_ref[0] = grad * (1.0 - out_gate)
    back = lax.dot_general(grad_lin, weights_ref[5], (((1,), (1,)), ((), ())), preferred_element_type=f32)
    back = back * gains_ref[1:2]
    back_ref[1] = back - jnp.mean(back, axis=-1, keepdims=True)
    turn = row_me ^ col_me

    def flipped(q):
        firsts = [q * size + (turn ^ g) * tile for g in range(n_col)]
        return lambda g, inner: right_ref[pl.ds(firsts[g] + inner, SUB, stride=SUB), :]

    def along(a, q):
        return lambda lane, inner: spread(left_ref, q * size + a * tile + lane * SUB + inner)

    def start(a, g, lane):
        if len(tri_in) == 0:
            return jnp.zeros((SUB, channels), f32)
        return line(tri_in[0], g * size + a * tile + lane * SUB)

    def store(a, g, values):
        for lane in range(SUB):
            tri_ref[pl.ds(pl.multiple_of(g * size + a * tile + lane * SUB, SUB), SUB), :] = values[lane]

    triangle(n_row, n_col, 2, flipped, along, start, store)


def rest_kernel(n_row, n_col, weights_ref, gains_ref, own_ref, gate_ref, tri_ref, *refs):
    groups = [refs[at * 5 : at * 5 + 5] for at in range(n_col // 2)]
    update_ref, pair_grad_ref, weight_grad_ref, back_ref, hat_ref, d_ref = refs[5 * (n_col // 2) :]
    channels = tri_ref.shape[-1]
    tile = SUB * SUB
    size = n_row * tile
    columns = []
    for col in range(n_col):
        own = pl.ds(col % 2 * size, size)
        left, right, side, backs, _ = groups[col // 2]
        columns.append((left.at[own], right.at[own], side.at[:, own], backs.at[:, own]))
    residues = n_row * SUB
    bf16, f32 = jnp.bfloat16, jnp.float32
    turn = lax.axis_index("row") ^ lax.axis_index("col")
    out_gain = gains_ref[1:2]
    for col, (_, _, _, backs_ref) in enumerate(columns):
        rows = slice(col * size, (col + 1) * size)
        x_hat, inverse = normalize(tri_ref[rows, :])
        normed_out = (x_hat * out_gain).astype(bf16)
        hat_ref[rows, :] = normed_out
        lin = jnp.dot(normed_out, weights_ref[5], preferred_element_type=f32)
        if col == 0:
            update_ref[...] = (gate_ref[...] * lin[0:tile]).astype(bf16).reshape(update_ref.shape)
        d_ref[rows, 4 * channels : 5 * channels] = (backs_ref[0] * lin).astype(bf16)
        back = backs_ref[1]
        second = jnp.mean(back * x_hat, axis=-1, keepdims=True)
        back_ref[rows, :] = ((back - x_hat * second) * inverse).astype(bf16).astype(f32)

    lefts, rights, sides = [[column[at] for column in columns] for at in (0, 1, 2)]

    def zero(a, g, lane):
        return jnp.zeros((SUB, channels), f32)

    def store(side):
        def put(a, g, values):
            for lane in range(0, SUB, 2):
                at = pl.multiple_of(a * tile + lane * SUB, 2 * SUB)
                both = jnp.concatenate(values[lane : lane + 2], axis=0)
                rows = pl.ds(pl.multiple_of(g * size + at, 2 * SUB), 2 * SUB)
                for kind in range(2):
                    spot = (2 * side + kind) * channels
                    scaled = both * sides[g][2 * side + kind, pl.ds(at, 2 * SUB), :]
                    d_ref[rows, spot : spot + channels] = scaled.astype(bf16)
        return put

    def by_right(q):
        return lambda g, inner: line(rights[g], (q ^ turn) * tile + inner * SUB)

    def by_left(q):
        return lambda g, inner: line(lefts[g], q * tile + inner * SUB)

    def along(a, q):
        return lambda lane, inner: spread(back_ref, q * size + a * tile + lane * SUB + inner)

    def down(a, q):
        return lambda lane, inner: spread(back_ref, (a ^ turn) * size + q * tile + inner * SUB + lane)

    triangle(n_row, n_col, n_col, by_right, along, zero, store(0))
    triangle(n_row, n_col, n_row, by_left, down, zero, store(1))

    scale = 1.0 / residues
    flipped, lin_flipped = [jnp.concatenate([group[4][at] for group in groups], axis=1) for at in range(2)]
    sums = jnp.dot(flipped, d_ref[...], preferred_element_type=f32) * scale
    for s in range(5):
        weight_grad_ref[s] = sums[:, s * channels : (s + 1) * channels]
    weight_grad_ref[5] = jnp.dot(lin_flipped, hat_ref[...], preferred_element_type=f32).T * scale
    total = jnp.zeros((tile, channels), f32)
    for s in range(5):
        total = total + lax.dot_general(
            d_ref[0:tile, s * channels : (s + 1) * channels], weights_ref[s],
            (((1,), (1,)), ((), ())), preferred_element_type=f32,
        )
    grad = norm_back(total * gains_ref[0:1], own_ref[0], own_ref[1])
    pair_grad_ref[...] = grad.astype(bf16).reshape(pair_grad_ref.shape)


def flip(block, n_row, n_col, even, odd):
    pairs = []
    for row in range(n_row):
        for col in range(n_col):
            shift = odd if col % 2 else even
            if shift is not None:
                pairs.append((row * n_col + col, (row ^ shift[0]) * n_col + (col ^ shift[1])))
    return lax.ppermute(block, ("row", "col"), pairs)


def gathered_body(n_row, n_col, pair_act, pair_mask, crop_length, weights, in_gain, out_gain, cotangent):
    tile_rows, tile_cols, channels = pair_act.shape
    tile = tile_rows * tile_cols
    size = n_row * tile
    pairs = size * n_col
    head = tile + 2 * SUB
    f32, bf16 = jnp.float32, jnp.bfloat16
    vmem = pl.BlockSpec(memory_space=pltpu.VMEM)
    smem = pl.BlockSpec(memory_space=pltpu.SMEM)
    hbm = pl.BlockSpec(memory_space=pltpu.HBM)
    in_gain, out_gain = in_gain.reshape(1, channels), out_gain.reshape(1, channels)

    def limit(mib):
        return pltpu.CompilerParams(vmem_limit_bytes=mib * 1024 * 1024)

    own = pl.pallas_call(
        pack_kernel,
        name="pack",
        out_shape=jax.ShapeDtypeStruct((head + tile, channels), bf16),
        in_specs=[hbm] * 4,
        out_specs=vmem,
        scratch_shapes=[
            pltpu.VMEM(pair_act.shape, pair_act.dtype),
            pltpu.VMEM(pair_mask.shape, jnp.int32),
            pltpu.VMEM((1, channels), f32),
            pltpu.SemaphoreType.DMA((4,)),
        ],
        compiler_params=limit(60),
    )(pair_act, pair_mask, cotangent.reshape(tile, channels), in_gain)
    crop_length, own = lax.optimization_barrier((crop_length, own))

    def move(block, even, odd):
        return flip(block, n_row, n_col, even, odd)

    def other(block):
        return move(block, (0, 1), (0, 1))

    held = pl.pallas_call(
        copy_kernel,
        name="hold",
        out_shape=jax.ShapeDtypeStruct(own.shape, bf16),
        in_specs=[vmem],
        out_specs=vmem,
        compiler_params=limit(2),
        cost_estimate=pl.CostEstimate(flops=100_000_000, bytes_accessed=1_000_000, transcendentals=0),
    )(own)
    both = pl.pallas_call(
        join_kernel,
        name="join",
        out_shape=jax.ShapeDtypeStruct((2 * own.shape[0] - 2 * SUB, channels), bf16),
        in_specs=[vmem] * 2,
        out_specs=vmem,
        compiler_params=limit(2),
    )(held, other(own))
    first = move(both, (2, 0), (1, 0))
    second = move(both, (0, 2), (2, 2))
    third = move(both, (1, 2), (3, 2))
    relayed = move(first, (1, 0), None)
    first, second, third, relayed = [(block, other(block)) for block in (first, second, third, relayed)]
    chips = (((1, None), (2, 1), (2, 0), (2, 0)), ((2, 0), (2, 0), (2, 1), (2, 1)))
    sources = ((both, *first, *first, *relayed), (*second, *third, *second, *third))

    tri, parts, extra = [], {}, []
    for side_x in reversed(range(n_col // 2)):
        more = (pair_act, in_gain, out_gain) if len(tri) == 0 else (extra[0], *tri)
        shapes = (
            jax.ShapeDtypeStruct((pairs, channels), f32),
            jax.ShapeDtypeStruct((2 * size, channels), f32),
            jax.ShapeDtypeStruct((2 * size, channels), f32),
            jax.ShapeDtypeStruct((4, 2 * size, channels), f32),
            jax.ShapeDtypeStruct((2, 2 * size, channels), f32),
            jax.ShapeDtypeStruct((2, channels, 2 * size), bf16),
        )
        if len(tri) == 0:
            shapes += (jax.ShapeDtypeStruct((SUB, channels), f32), jax.ShapeDtypeStruct((2, tile, channels), f32))
        elif side_x == 0:
            shapes += (jax.ShapeDtypeStruct((tile, channels), f32),)
        alias = {3 + len(sources[side_x]): 0} if len(tri) > 0 else {}
        tri, *results = pl.pallas_call(
            functools.partial(columns_kernel, n_row, n_col, side_x, len(tri) == 0, chips[side_x]),
            name=f"columns_{side_x}",
            out_shape=shapes,
            in_specs=[smem] + [vmem] * (1 + len(sources[side_x]) + len(more)),
            out_specs=(vmem,) * len(shapes),
            input_output_aliases=alias,
            compiler_params=limit(12),
            cost_estimate=pl.CostEstimate(flops=800_000_000, bytes_accessed=1_000_000, transcendentals=0),
        )(crop_length, weights, *sources[side_x], *more)
        tri = [tri]
        parts[side_x] = results[:5]
        extra += results[5:]
    parts = [array for side_x in range(n_col // 2) for array in parts[side_x]]

    return pl.pallas_call(
        functools.partial(rest_kernel, n_row, n_col),
        name="rest",
        out_shape=(
            jax.ShapeDtypeStruct(pair_act.shape, bf16),
            jax.ShapeDtypeStruct(pair_act.shape, bf16),
            jax.ShapeDtypeStruct(weights.shape, f32),
        ),
        in_specs=[vmem] * (5 + len(parts)),
        out_specs=(vmem, vmem, vmem),
        scratch_shapes=[
            pltpu.VMEM((pairs, channels), f32),
            pltpu.VMEM((pairs, channels), bf16),
            pltpu.VMEM((pairs, 5 * channels), bf16),
        ],
        compiler_params=limit(16),
    )(weights, *extra, *tri, *parts)


def body(n_row, n_col, pair_act, *others):
    tile_rows, tile_cols, channels = pair_act.shape
    pairs = tile_rows * n_row * tile_cols * n_col
    small = pairs * channels * 4 <= 1024 * 1024 and channels == 128
    square = n_row == 4 and n_col == 4 and tile_rows == SUB and tile_cols == SUB
    if small and square:
        return gathered_body(n_row, n_col, pair_act, *others)
    return spread_body(pair_act, *others)


def solution(mesh):
    return jax.shard_map(
        functools.partial(body, mesh.shape["row"], mesh.shape["col"]),
        mesh=mesh,
        in_specs=(
            P(("parts", "row"), "col", None),
            P(("parts", "row"), "col"),
            P("parts"),
            P(),
            P(),
            P(),
            P(("parts", "row"), "col", None),
        ),
        out_specs=(
            P(("parts", "row"), "col", None),
            P(("parts", "row"), "col", None),
            P("parts", None, None),
        ),
        check_vma=False,
    )
```

```python
import functools

import jax
import jax.numpy as jnp
from jax import lax
from jax.experimental import pallas as pl
from jax.experimental.pallas import tpu as pltpu
from jax.sharding import PartitionSpec as P

SUB = 8
EPS = 1e-05


def normalize(values):
    average = jnp.mean(values, axis=-1, keepdims=True)
    centered = values - average
    inverse = lax.rsqrt(jnp.mean(centered * centered, axis=-1, keepdims=True) + 1e-05)
    return (centered * inverse, inverse)


def norm_back(grad_hat, values_hat, inverse):
    first = jnp.mean(grad_hat, axis=-1, keepdims=True)
    second = jnp.mean(grad_hat * values_hat, axis=-1, keepdims=True)
    return (grad_hat - first - values_hat * second) * inverse


def gate_back(grad_act, proj_value, proj_gate, keep_mask):
    gate_sig = jax.nn.sigmoid(proj_gate)
    masked = grad_act * keep_mask
    grad_value = (masked * gate_sig).astype(jnp.bfloat16)
    grad_gate = (masked * proj_value * gate_sig * (1.0 - gate_sig)).astype(jnp.bfloat16)
    return (grad_value, grad_gate)


def spread_body(pair_act, pair_mask, crop_length, weights, in_gain, out_gain, cotangent):
    tile_rows, tile_cols, channels = pair_act.shape
    residues = tile_rows * lax.axis_size("row")
    row_pos = lax.axis_index("row") * tile_rows + jnp.arange(tile_rows, dtype=jnp.int32)
    col_pos = lax.axis_index("col") * tile_cols + jnp.arange(tile_cols, dtype=jnp.int32)
    row_in = (row_pos < crop_length[0]).astype(jnp.float32)
    col_in = (col_pos < crop_length[0]).astype(jnp.float32)
    keep_mask = (pair_mask.astype(jnp.float32) * row_in[:, None] * col_in[None, :])[:, :, None]
    z_hat, z_inverse = normalize(pair_act.astype(jnp.float32))
    normed = (z_hat * in_gain).astype(jnp.bfloat16)
    flat_norm = normed.reshape(tile_rows * tile_cols, channels)
    projections = jnp.einsum(
        "pc,scd->spd", flat_norm, weights[:5], preferred_element_type=jnp.float32
    )
    projections = projections.reshape(5, tile_rows, tile_cols, channels)
    left_act = (jax.nn.sigmoid(projections[1]) * projections[0] * keep_mask).astype(jnp.bfloat16)
    right_act = (jax.nn.sigmoid(projections[3]) * projections[2] * keep_mask).astype(jnp.bfloat16)
    partial_value = jnp.einsum(
        "ikh,jkh->ijh",
        left_act,
        lax.all_gather(right_act, "row", axis=0, tiled=True),
        preferred_element_type=jnp.float32,
    )
    tri_sum = lax.psum_scatter(
        partial_value.astype(jnp.bfloat16), "col", scatter_dimension=1, tiled=True
    ).astype(jnp.float32)
    x_hat, x_inverse = normalize(tri_sum)
    normed_out = (x_hat * out_gain).astype(jnp.bfloat16)
    flat_out = normed_out.reshape(tile_rows * tile_cols, channels)
    update_lin = jnp.dot(flat_out, weights[5], preferred_element_type=jnp.float32)
    update_lin = update_lin.reshape(tile_rows, tile_cols, channels)
    out_gate = jax.nn.sigmoid(projections[4])
    update = (out_gate * update_lin).astype(jnp.bfloat16)
    cot_value = cotangent.astype(jnp.float32)
    grad_lin = (cot_value * out_gate).astype(jnp.bfloat16)
    grad_gate_out = (cot_value * update_lin * out_gate * (1.0 - out_gate)).astype(jnp.bfloat16)
    flat_lin = grad_lin.reshape(tile_rows * tile_cols, channels)
    grad_norm_out = jnp.einsum(
        "pd,cd->pc", flat_lin, weights[5], preferred_element_type=jnp.float32
    )
    grad_norm_out = grad_norm_out.reshape(tile_rows, tile_cols, channels)
    grad_tri = norm_back(grad_norm_out * out_gain, x_hat, x_inverse).astype(jnp.bfloat16)
    grad_full = lax.all_gather(grad_tri, "col", axis=1, tiled=True)
    grad_slab = grad_full
    grad_left = jnp.einsum(
        "ijh,jkh->ikh",
        grad_slab,
        lax.all_gather(right_act, "row", axis=0, tiled=True),
        preferred_element_type=jnp.float32,
    )
    grad_slab = grad_full
    grad_right = lax.psum_scatter(
        jnp.einsum("ijh,ikh->jkh", grad_slab, left_act, preferred_element_type=jnp.float32).astype(
            jnp.bfloat16
        ),
        "row",
        scatter_dimension=0,
        tiled=True,
    ).astype(jnp.float32)
    grad_pa, grad_ga = gate_back(grad_left, projections[0], projections[1], keep_mask)
    grad_pb, grad_gb = gate_back(grad_right, projections[2], projections[3], keep_mask)
    grads = jnp.stack([grad_pa, grad_ga, grad_pb, grad_gb, grad_gate_out]).reshape(
        5, tile_rows * tile_cols, channels
    )
    grad_normed = jnp.einsum("spd,scd->pc", grads, weights[:5], preferred_element_type=jnp.float32)
    grad_normed = grad_normed.reshape(tile_rows, tile_cols, channels)
    pair_grad = norm_back(grad_normed * in_gain, z_hat, z_inverse).astype(jnp.bfloat16)
    local_in = jnp.einsum("pc,spd->scd", flat_norm, grads, preferred_element_type=jnp.float32)
    local_out = jnp.dot(flat_out.T, flat_lin, preferred_element_type=jnp.float32)
    local_grads = jnp.concatenate([local_in, local_out[None]], axis=0) / residues
    weight_grad = lax.psum(local_grads, ("row", "col"))
    return (update, pair_grad, weight_grad)


def pack_kernel(act_hbm, mask_hbm, cot_hbm, gain_hbm, out_ref, act_ref, mask_ref, gain_ref, sems):
    tile_rows, tile_cols, channels = act_ref.shape
    pairs = tile_rows * tile_cols
    head = out_ref.shape[0] - pairs
    pack_copies = [
        pltpu.make_async_copy(act_hbm, act_ref, sems.at[0]),
        pltpu.make_async_copy(gain_hbm, gain_ref, sems.at[1]),
        pltpu.make_async_copy(mask_hbm, mask_ref, sems.at[2]),
        pltpu.make_async_copy(cot_hbm, out_ref.at[head : head + pairs], sems.at[3]),
    ]
    for copy in pack_copies:
        copy.start()
    for copy in pack_copies:
        copy.wait()
    z_hat, _ = normalize(act_ref[...].astype(jnp.float32).reshape(pairs, channels))
    out_ref[0:pairs] = (z_hat * gain_ref[...]).astype(jnp.bfloat16)
    keep = mask_ref[...].astype(jnp.float32)
    wide = jnp.concatenate([keep, jnp.zeros((tile_rows, channels - tile_cols), jnp.float32)], axis=1)
    tall = jnp.concatenate([wide, jnp.zeros((channels - tile_rows, channels), jnp.float32)], axis=0)
    out_ref[pairs:head] = tall.T[0 : head - pairs].astype(jnp.bfloat16)


def copy_kernel(in_ref, out_ref):
    out_ref[...] = in_ref[...]


def token_kernel(*refs):
    refs[-1][...] = jnp.zeros(refs[-1].shape, refs[-1].dtype)


def join_kernel(own_ref, twin_ref, out_ref):
    tile = SUB * SUB
    refs = (own_ref, twin_ref)
    for at, ref in enumerate(refs):
        out_ref[at * tile : (at + 1) * tile] = ref[0:tile]
        spot = 2 * tile + 2 * SUB + at * tile
        out_ref[spot : spot + tile] = ref[tile + 2 * SUB :]
    masks = [ref[tile : tile + 2 * SUB].astype(jnp.float32)[0:SUB] for ref in refs]
    out_ref[2 * tile : 2 * tile + 2 * SUB] = jnp.concatenate(masks, axis=0).astype(jnp.bfloat16)


def normed_rows(ref, sub):
    return ref[sub * SUB * SUB : (sub + 1) * SUB * SUB]


def mask_rows(ref, sub):
    at = ref.shape[0] // 2 // (SUB * SUB) * SUB * SUB
    return ref[at : at + 2 * SUB].astype(jnp.float32)[sub * SUB : (sub + 1) * SUB]


def cot_rows(ref, sub):
    at = ref.shape[0] // 2 // (SUB * SUB) * SUB * SUB + 2 * SUB
    return ref[at + sub * SUB * SUB : at + (sub + 1) * SUB * SUB]


def chip_rows(rows_of, refs, core, direct_on):
    if direct_on is None:
        return rows_of(refs[min(core, len(refs) - 1)], core if len(refs) == 1 else 0)
    here = lax.axis_index("col") % 2 == direct_on
    return jnp.where(here, rows_of(refs[0], core), rows_of(refs[1], 1 - core))


def split_chips(refs, chips):
    split, at = [], 0
    for width, direct_on in chips:
        split.append((refs[at : at + width], direct_on))
        at += width
    return split


def triangle(blocks, groups, steps, vectors_at, factors_at, start_at, store_at):
    def block(a, _):
        def step(q, totals):
            totals = list(totals)
            vectors = vectors_at(q)
            factors = factors_at(a, q)
            for inner in range(SUB):
                rows = [vectors(g, inner) for g in range(groups)]
                for lane in range(SUB):
                    factor = factors(lane, inner)
                    for g in range(groups):
                        at = lane * groups + g
                        totals[at] = totals[at] + factor * rows[g]
            return tuple(totals)

        totals = tuple(start_at(a, g, lane) for lane in range(SUB) for g in range(groups))
        if steps > 4:
            totals = lax.fori_loop(0, steps, step, totals)
        else:
            for q in range(steps):
                totals = step(q, totals)
        for g in range(groups):
            store_at(a, g, [totals[lane * groups + g] for lane in range(SUB)])
        return 0

    lax.fori_loop(0, blocks, block, 0)


def spread(ref, row):
    return jnp.broadcast_to(ref[pl.ds(row, 1), :], (SUB, ref.shape[-1]))


def line(ref, row):
    return ref[pl.ds(pl.multiple_of(row, SUB), SUB), :]


def columns_kernel(n_row, n_col, side_x, is_first, chips, crop_ref, weights_ref, *refs):
    count = sum(width for width, _ in chips)
    chip_list, refs = split_chips(refs[:count], chips), refs[count:]
    gate_ref = None
    if is_first:
        act_ref, in_gain_ref, out_gain_ref, *refs, gains_ref, own_ref = refs
        z_hat, z_inverse = normalize(act_ref[...].astype(jnp.float32).reshape(own_ref.shape[1:]))
        own_ref[0] = z_hat
        own_ref[1] = jnp.broadcast_to(z_inverse, z_hat.shape)
        gains_ref[0:1] = in_gain_ref[...]
        gains_ref[1:2] = out_gain_ref[...]
    else:
        _, gains_ref, *refs = refs
        if side_x == 0:
            *refs, gate_ref = refs
    tri_in, (tri_ref, left_ref, right_ref, side_ref, back_ref, flip_ref) = refs[:-6], refs[-6:]
    channels = weights_ref.shape[-1]
    tile = SUB * SUB
    size = n_row * tile
    bf16, f32 = jnp.bfloat16, jnp.float32
    row_me, col_me = lax.axis_index("row"), lax.axis_index("col")
    chip_list = [(chip, on, core, b) for core in range(2) for b, (chip, on) in enumerate(chip_list)]
    normed = jnp.concatenate([chip_rows(normed_rows, chip, core, on) for chip, on, core, _ in chip_list], axis=0)
    same = lax.broadcasted_iota(jnp.int32, (channels, channels), 0) == lax.broadcasted_iota(jnp.int32, (channels, channels), 1)
    identity = jnp.where(same, 1.0, 0.0).astype(bf16)

    def turned(rows):
        return lax.dot_general(identity, rows, (((1,), (1,)), ((), ())), preferred_element_type=f32).astype(bf16)

    flip_ref[0] = turned(normed)
    crop = crop_ref[0]
    col_offset = lax.broadcasted_iota(jnp.int32, (SUB, channels), 0)
    row_offset = lax.broadcasted_iota(jnp.int32, (SUB, channels), 1)
    kept = []
    for chip, on, core, b in chip_list:
        keep = chip_rows(mask_rows, chip, core, on)
        rows_in = row_offset < crop - (row_me ^ b) * SUB
        cols_in = col_offset < crop - (col_me ^ (2 * side_x + core)) * SUB
        keep = jnp.where(rows_in & cols_in, keep, 0.0)
        kept += [jnp.broadcast_to(keep[:, at : at + 1], (SUB, channels)) for at in range(SUB)]
    kept = jnp.concatenate(kept, axis=0)
    for side, act_ref in enumerate((left_ref, right_ref)):
        pair = jnp.concatenate([weights_ref[2 * side], weights_ref[2 * side + 1]], axis=1)
        proj = jnp.dot(normed, pair, preferred_element_type=f32)
        gate = jax.nn.sigmoid(proj[:, channels:])
        masked = gate * kept
        act = masked * proj[:, :channels]
        act_ref[...] = act.astype(bf16).astype(f32)
        side_ref[2 * side] = masked
        side_ref[2 * side + 1] = act * (1.0 - gate)
    out_gate = jax.nn.sigmoid(jnp.dot(normed, weights_ref[4], preferred_element_type=f32))
    if gate_ref is not None:
        gate_ref[...] = out_gate[0:tile]
    cot = jnp.concatenate([chip_rows(cot_rows, chip, core, on) for chip, on, core, _ in chip_list], axis=0)
    grad = cot.astype(f32) * out_gate
    grad_lin = grad.astype(bf16)
    flip_ref[1] = turned(grad_lin)
    back_ref[0] = grad * (1.0 - out_gate)
    back = lax.dot_general(grad_lin, weights_ref[5], (((1,), (1,)), ((), ())), preferred_element_type=f32)
    back = back * gains_ref[1:2]
    back_ref[1] = back - jnp.mean(back, axis=-1, keepdims=True)
    turn = row_me ^ col_me

    def flipped(q):
        firsts = [q * size + (turn ^ g) * tile for g in range(n_col)]
        return lambda g, inner: right_ref[pl.ds(firsts[g] + inner, SUB, stride=SUB), :]

    def along(a, q):
        return lambda lane, inner: spread(left_ref, q * size + a * tile + lane * SUB + inner)

    def start(a, g, lane):
        if len(tri_in) == 0:
            return jnp.zeros((SUB, channels), f32)
        return line(tri_in[0], g * size + a * tile + lane * SUB)

    def store(a, g, values):
        for lane in range(SUB):
            tri_ref[pl.ds(pl.multiple_of(g * size + a * tile + lane * SUB, SUB), SUB), :] = values[lane]

    triangle(n_row, n_col, 2, flipped, along, start, store)


def rest_kernel(n_row, n_col, weights_ref, gains_ref, own_ref, gate_ref, tri_ref, *refs):
    groups = [refs[at * 5 : at * 5 + 5] for at in range(n_col // 2)]
    update_ref, pair_grad_ref, weight_grad_ref, back_ref, hat_ref, d_ref = refs[5 * (n_col // 2) :]
    channels = tri_ref.shape[-1]
    tile = SUB * SUB
    size = n_row * tile
    columns = []
    for col in range(n_col):
        own = pl.ds(col % 2 * size, size)
        left, right, side, backs, _ = groups[col // 2]
        columns.append((left.at[own], right.at[own], side.at[:, own], backs.at[:, own]))
    residues = n_row * SUB
    bf16, f32 = jnp.bfloat16, jnp.float32
    turn = lax.axis_index("row") ^ lax.axis_index("col")
    out_gain = gains_ref[1:2]
    for col, (_, _, _, backs_ref) in enumerate(columns):
        rows = slice(col * size, (col + 1) * size)
        x_hat, inverse = normalize(tri_ref[rows, :])
        normed_out = (x_hat * out_gain).astype(bf16)
        hat_ref[rows, :] = normed_out
        lin = jnp.dot(normed_out, weights_ref[5], preferred_element_type=f32)
        if col == 0:
            update_ref[...] = (gate_ref[...] * lin[0:tile]).astype(bf16).reshape(update_ref.shape)
        d_ref[rows, 4 * channels : 5 * channels] = (backs_ref[0] * lin).astype(bf16)
        back = backs_ref[1]
        second = jnp.mean(back * x_hat, axis=-1, keepdims=True)
        back_ref[rows, :] = ((back - x_hat * second) * inverse).astype(bf16).astype(f32)

    lefts, rights, sides = [[column[at] for column in columns] for at in (0, 1, 2)]

    def zero(a, g, lane):
        return jnp.zeros((SUB, channels), f32)

    def store(side):
        def put(a, g, values):
            for lane in range(0, SUB, 2):
                at = pl.multiple_of(a * tile + lane * SUB, 2 * SUB)
                both = jnp.concatenate(values[lane : lane + 2], axis=0)
                rows = pl.ds(pl.multiple_of(g * size + at, 2 * SUB), 2 * SUB)
                for kind in range(2):
                    spot = (2 * side + kind) * channels
                    scaled = both * sides[g][2 * side + kind, pl.ds(at, 2 * SUB), :]
                    d_ref[rows, spot : spot + channels] = scaled.astype(bf16)
        return put

    def by_right(q):
        return lambda g, inner: line(rights[g], (q ^ turn) * tile + inner * SUB)

    def by_left(q):
        return lambda g, inner: line(lefts[g], q * tile + inner * SUB)

    def along(a, q):
        return lambda lane, inner: spread(back_ref, q * size + a * tile + lane * SUB + inner)

    def down(a, q):
        return lambda lane, inner: spread(back_ref, (a ^ turn) * size + q * tile + inner * SUB + lane)

    triangle(n_row, n_col, n_col, by_right, along, zero, store(0))
    triangle(n_row, n_col, n_row, by_left, down, zero, store(1))

    scale = 1.0 / residues
    flipped, lin_flipped = [jnp.concatenate([group[4][at] for group in groups], axis=1) for at in range(2)]
    sums = jnp.dot(flipped, d_ref[...], preferred_element_type=f32) * scale
    for s in range(5):
        weight_grad_ref[s] = sums[:, s * channels : (s + 1) * channels]
    weight_grad_ref[5] = jnp.dot(lin_flipped, hat_ref[...], preferred_element_type=f32).T * scale
    total = jnp.zeros((tile, channels), f32)
    for s in range(5):
        total = total + lax.dot_general(
            d_ref[0:tile, s * channels : (s + 1) * channels], weights_ref[s],
            (((1,), (1,)), ((), ())), preferred_element_type=f32,
        )
    grad = norm_back(total * gains_ref[0:1], own_ref[0], own_ref[1])
    pair_grad_ref[...] = grad.astype(bf16).reshape(pair_grad_ref.shape)


def flip(block, n_row, n_col, even, odd):
    pairs = []
    for row in range(n_row):
        for col in range(n_col):
            shift = odd if col % 2 else even
            if shift is not None:
                pairs.append((row * n_col + col, (row ^ shift[0]) * n_col + (col ^ shift[1])))
    return lax.ppermute(block, ("row", "col"), pairs)


def gathered_body(n_row, n_col, pair_act, pair_mask, crop_length, weights, in_gain, out_gain, cotangent):
    tile_rows, tile_cols, channels = pair_act.shape
    tile = tile_rows * tile_cols
    size = n_row * tile
    pairs = size * n_col
    head = tile + 2 * SUB
    f32, bf16 = jnp.float32, jnp.bfloat16
    vmem = pl.BlockSpec(memory_space=pltpu.VMEM)
    smem = pl.BlockSpec(memory_space=pltpu.SMEM)
    hbm = pl.BlockSpec(memory_space=pltpu.HBM)
    in_gain, out_gain = in_gain.reshape(1, channels), out_gain.reshape(1, channels)

    def limit(mib):
        return pltpu.CompilerParams(vmem_limit_bytes=mib * 1024 * 1024)

    own = pl.pallas_call(
        pack_kernel,
        name="pack",
        out_shape=jax.ShapeDtypeStruct((head + tile, channels), bf16),
        in_specs=[hbm] * 4,
        out_specs=vmem,
        scratch_shapes=[
            pltpu.VMEM(pair_act.shape, pair_act.dtype),
            pltpu.VMEM(pair_mask.shape, jnp.int32),
            pltpu.VMEM((1, channels), f32),
            pltpu.SemaphoreType.DMA((4,)),
        ],
        compiler_params=limit(60),
    )(pair_act, pair_mask, cotangent.reshape(tile, channels), in_gain)
    crop_length, own = lax.optimization_barrier((crop_length, own))

    def move(block, even, odd):
        return flip(block, n_row, n_col, even, odd)

    def other(block):
        return move(block, (0, 1), (0, 1))

    held = pl.pallas_call(
        copy_kernel,
        name="hold",
        out_shape=jax.ShapeDtypeStruct(own.shape, bf16),
        in_specs=[vmem],
        out_specs=vmem,
        compiler_params=limit(2),
        cost_estimate=pl.CostEstimate(flops=100_000_000, bytes_accessed=1_000_000, transcendentals=0),
    )(own)
    both = pl.pallas_call(
        join_kernel,
        name="join",
        out_shape=jax.ShapeDtypeStruct((2 * own.shape[0] - 2 * SUB, channels), bf16),
        in_specs=[vmem] * 2,
        out_specs=vmem,
        compiler_params=limit(2),
    )(held, other(own))
    straight = move(own, (3, 0), (3, 0))
    first = move(both, (2, 0), (1, 0))
    second = move(both, (0, 2), (2, 2))
    third = move(both, (1, 2), (3, 2))
    straight, first, second, third = [(block, other(block)) for block in (straight, first, second, third)]
    chips = (((1, None), (2, 1), (2, 0), (2, None)), ((2, 0), (2, 0), (2, 1), (2, 1)))
    sources = ((both, *first, *first, *straight), (*second, *third, *second, *third))
    anywhere = pl.BlockSpec(memory_space=pl.ANY)
    token = pl.pallas_call(
        token_kernel,
        name="token",
        out_shape=jax.ShapeDtypeStruct((SUB, channels), f32),
        in_specs=[anywhere] * 2,
        out_specs=vmem,
        compiler_params=limit(2),
        cost_estimate=pl.CostEstimate(flops=1_000_000_000, bytes_accessed=1_000_000, transcendentals=0),
    )(*straight)

    tri, parts, extra = [], {}, []
    for side_x in reversed(range(n_col // 2)):
        more = (pair_act, in_gain, out_gain) if len(tri) == 0 else (token, extra[0], *tri)
        shapes = (
            jax.ShapeDtypeStruct((pairs, channels), f32),
            jax.ShapeDtypeStruct((2 * size, channels), f32),
            jax.ShapeDtypeStruct((2 * size, channels), f32),
            jax.ShapeDtypeStruct((4, 2 * size, channels), f32),
            jax.ShapeDtypeStruct((2, 2 * size, channels), f32),
            jax.ShapeDtypeStruct((2, channels, 2 * size), bf16),
        )
        if len(tri) == 0:
            shapes += (jax.ShapeDtypeStruct((SUB, channels), f32), jax.ShapeDtypeStruct((2, tile, channels), f32))
        elif side_x == 0:
            shapes += (jax.ShapeDtypeStruct((tile, channels), f32),)
        alias = {4 + len(sources[side_x]): 0} if len(tri) > 0 else {}
        tri, *results = pl.pallas_call(
            functools.partial(columns_kernel, n_row, n_col, side_x, len(tri) == 0, chips[side_x]),
            name=f"columns_{side_x}",
            out_shape=shapes,
            in_specs=[smem] + [vmem] * (1 + len(sources[side_x]) + len(more)),
            out_specs=(vmem,) * len(shapes),
            input_output_aliases=alias,
            compiler_params=limit(12),
            cost_estimate=pl.CostEstimate(flops=800_000_000, bytes_accessed=1_000_000, transcendentals=0),
        )(crop_length, weights, *sources[side_x], *more)
        tri = [tri]
        parts[side_x] = results[:5]
        extra += results[5:]
    parts = [array for side_x in range(n_col // 2) for array in parts[side_x]]

    return pl.pallas_call(
        functools.partial(rest_kernel, n_row, n_col),
        name="rest",
        out_shape=(
            jax.ShapeDtypeStruct(pair_act.shape, bf16),
            jax.ShapeDtypeStruct(pair_act.shape, bf16),
            jax.ShapeDtypeStruct(weights.shape, f32),
        ),
        in_specs=[vmem] * (5 + len(parts)),
        out_specs=(vmem, vmem, vmem),
        scratch_shapes=[
            pltpu.VMEM((pairs, channels), f32),
            pltpu.VMEM((pairs, channels), bf16),
            pltpu.VMEM((pairs, 5 * channels), bf16),
        ],
        compiler_params=limit(16),
    )(weights, *extra, *tri, *parts)


def body(n_row, n_col, pair_act, *others):
    tile_rows, tile_cols, channels = pair_act.shape
    pairs = tile_rows * n_row * tile_cols * n_col
    small = pairs * channels * 4 <= 1024 * 1024 and channels == 128
    square = n_row == 4 and n_col == 4 and tile_rows == SUB and tile_cols == SUB
    if small and square:
        return gathered_body(n_row, n_col, pair_act, *others)
    return spread_body(pair_act, *others)


def solution(mesh):
    return jax.shard_map(
        functools.partial(body, mesh.shape["row"], mesh.shape["col"]),
        mesh=mesh,
        in_specs=(
            P(("parts", "row"), "col", None),
            P(("parts", "row"), "col"),
            P("parts"),
            P(),
            P(),
            P(),
            P(("parts", "row"), "col", None),
        ),
        out_specs=(
            P(("parts", "row"), "col", None),
            P(("parts", "row"), "col", None),
            P("parts", None, None),
        ),
        check_vma=False,
    )
```

```python
import functools

import jax
import jax.numpy as jnp
from jax import lax
from jax.experimental import pallas as pl
from jax.experimental.pallas import tpu as pltpu
from jax.sharding import PartitionSpec as P

SUB = 8
EPS = 1e-05


def normalize(values):
    average = jnp.mean(values, axis=-1, keepdims=True)
    centered = values - average
    inverse = lax.rsqrt(jnp.mean(centered * centered, axis=-1, keepdims=True) + 1e-05)
    return (centered * inverse, inverse)


def norm_back(grad_hat, values_hat, inverse):
    first = jnp.mean(grad_hat, axis=-1, keepdims=True)
    second = jnp.mean(grad_hat * values_hat, axis=-1, keepdims=True)
    return (grad_hat - first - values_hat * second) * inverse


def gate_back(grad_act, proj_value, proj_gate, keep_mask):
    gate_sig = jax.nn.sigmoid(proj_gate)
    masked = grad_act * keep_mask
    grad_value = (masked * gate_sig).astype(jnp.bfloat16)
    grad_gate = (masked * proj_value * gate_sig * (1.0 - gate_sig)).astype(jnp.bfloat16)
    return (grad_value, grad_gate)


def spread_body(pair_act, pair_mask, crop_length, weights, in_gain, out_gain, cotangent):
    tile_rows, tile_cols, channels = pair_act.shape
    residues = tile_rows * lax.axis_size("row")
    row_pos = lax.axis_index("row") * tile_rows + jnp.arange(tile_rows, dtype=jnp.int32)
    col_pos = lax.axis_index("col") * tile_cols + jnp.arange(tile_cols, dtype=jnp.int32)
    row_in = (row_pos < crop_length[0]).astype(jnp.float32)
    col_in = (col_pos < crop_length[0]).astype(jnp.float32)
    keep_mask = (pair_mask.astype(jnp.float32) * row_in[:, None] * col_in[None, :])[:, :, None]
    z_hat, z_inverse = normalize(pair_act.astype(jnp.float32))
    normed = (z_hat * in_gain).astype(jnp.bfloat16)
    flat_norm = normed.reshape(tile_rows * tile_cols, channels)
    projections = jnp.einsum(
        "pc,scd->spd", flat_norm, weights[:5], preferred_element_type=jnp.float32
    )
    projections = projections.reshape(5, tile_rows, tile_cols, channels)
    left_act = (jax.nn.sigmoid(projections[1]) * projections[0] * keep_mask).astype(jnp.bfloat16)
    right_act = (jax.nn.sigmoid(projections[3]) * projections[2] * keep_mask).astype(jnp.bfloat16)
    partial_value = jnp.einsum(
        "ikh,jkh->ijh",
        left_act,
        lax.all_gather(right_act, "row", axis=0, tiled=True),
        preferred_element_type=jnp.float32,
    )
    tri_sum = lax.psum_scatter(
        partial_value.astype(jnp.bfloat16), "col", scatter_dimension=1, tiled=True
    ).astype(jnp.float32)
    x_hat, x_inverse = normalize(tri_sum)
    normed_out = (x_hat * out_gain).astype(jnp.bfloat16)
    flat_out = normed_out.reshape(tile_rows * tile_cols, channels)
    update_lin = jnp.dot(flat_out, weights[5], preferred_element_type=jnp.float32)
    update_lin = update_lin.reshape(tile_rows, tile_cols, channels)
    out_gate = jax.nn.sigmoid(projections[4])
    update = (out_gate * update_lin).astype(jnp.bfloat16)
    cot_value = cotangent.astype(jnp.float32)
    grad_lin = (cot_value * out_gate).astype(jnp.bfloat16)
    grad_gate_out = (cot_value * update_lin * out_gate * (1.0 - out_gate)).astype(jnp.bfloat16)
    flat_lin = grad_lin.reshape(tile_rows * tile_cols, channels)
    grad_norm_out = jnp.einsum(
        "pd,cd->pc", flat_lin, weights[5], preferred_element_type=jnp.float32
    )
    grad_norm_out = grad_norm_out.reshape(tile_rows, tile_cols, channels)
    grad_tri = norm_back(grad_norm_out * out_gain, x_hat, x_inverse).astype(jnp.bfloat16)
    grad_full = lax.all_gather(grad_tri, "col", axis=1, tiled=True)
    grad_slab = grad_full
    grad_left = jnp.einsum(
        "ijh,jkh->ikh",
        grad_slab,
        lax.all_gather(right_act, "row", axis=0, tiled=True),
        preferred_element_type=jnp.float32,
    )
    grad_slab = grad_full
    grad_right = lax.psum_scatter(
        jnp.einsum("ijh,ikh->jkh", grad_slab, left_act, preferred_element_type=jnp.float32).astype(
            jnp.bfloat16
        ),
        "row",
        scatter_dimension=0,
        tiled=True,
    ).astype(jnp.float32)
    grad_pa, grad_ga = gate_back(grad_left, projections[0], projections[1], keep_mask)
    grad_pb, grad_gb = gate_back(grad_right, projections[2], projections[3], keep_mask)
    grads = jnp.stack([grad_pa, grad_ga, grad_pb, grad_gb, grad_gate_out]).reshape(
        5, tile_rows * tile_cols, channels
    )
    grad_normed = jnp.einsum("spd,scd->pc", grads, weights[:5], preferred_element_type=jnp.float32)
    grad_normed = grad_normed.reshape(tile_rows, tile_cols, channels)
    pair_grad = norm_back(grad_normed * in_gain, z_hat, z_inverse).astype(jnp.bfloat16)
    local_in = jnp.einsum("pc,spd->scd", flat_norm, grads, preferred_element_type=jnp.float32)
    local_out = jnp.dot(flat_out.T, flat_lin, preferred_element_type=jnp.float32)
    local_grads = jnp.concatenate([local_in, local_out[None]], axis=0) / residues
    weight_grad = lax.psum(local_grads, ("row", "col"))
    return (update, pair_grad, weight_grad)


def pack_kernel(act_hbm, mask_hbm, cot_hbm, gain_hbm, out_ref, act_ref, mask_ref, gain_ref, sems):
    tile_rows, tile_cols, channels = act_ref.shape
    pairs = tile_rows * tile_cols
    head = out_ref.shape[0] - pairs
    pack_copies = [
        pltpu.make_async_copy(act_hbm, act_ref, sems.at[0]),
        pltpu.make_async_copy(gain_hbm, gain_ref, sems.at[1]),
        pltpu.make_async_copy(mask_hbm, mask_ref, sems.at[2]),
        pltpu.make_async_copy(cot_hbm, out_ref.at[head : head + pairs], sems.at[3]),
    ]
    for copy in pack_copies:
        copy.start()
    for copy in pack_copies:
        copy.wait()
    z_hat, _ = normalize(act_ref[...].astype(jnp.float32).reshape(pairs, channels))
    out_ref[0:pairs] = (z_hat * gain_ref[...]).astype(jnp.bfloat16)
    keep = mask_ref[...].astype(jnp.float32)
    wide = jnp.concatenate([keep, jnp.zeros((tile_rows, channels - tile_cols), jnp.float32)], axis=1)
    tall = jnp.concatenate([wide, jnp.zeros((channels - tile_rows, channels), jnp.float32)], axis=0)
    out_ref[pairs:head] = tall.T[0 : head - pairs].astype(jnp.bfloat16)


def copy_kernel(in_ref, out_ref):
    out_ref[...] = in_ref[...]


def token_kernel(*refs):
    refs[-1][...] = jnp.zeros(refs[-1].shape, refs[-1].dtype)


def join_kernel(own_ref, twin_ref, out_ref):
    tile = SUB * SUB
    refs = (own_ref, twin_ref)
    for at, ref in enumerate(refs):
        out_ref[at * tile : (at + 1) * tile] = ref[0:tile]
        spot = 2 * tile + 2 * SUB + at * tile
        out_ref[spot : spot + tile] = ref[tile + 2 * SUB :]
    masks = [ref[tile : tile + 2 * SUB].astype(jnp.float32)[0:SUB] for ref in refs]
    out_ref[2 * tile : 2 * tile + 2 * SUB] = jnp.concatenate(masks, axis=0).astype(jnp.bfloat16)


def normed_rows(ref, sub):
    return ref[sub * SUB * SUB : (sub + 1) * SUB * SUB]


def mask_rows(ref, sub):
    at = ref.shape[0] // 2 // (SUB * SUB) * SUB * SUB
    return ref[at : at + 2 * SUB].astype(jnp.float32)[sub * SUB : (sub + 1) * SUB]


def cot_rows(ref, sub):
    at = ref.shape[0] // 2 // (SUB * SUB) * SUB * SUB + 2 * SUB
    return ref[at + sub * SUB * SUB : at + (sub + 1) * SUB * SUB]


def chip_rows(rows_of, refs, core, direct_on):
    if direct_on is None:
        return rows_of(refs[min(core, len(refs) - 1)], core if len(refs) == 1 else 0)
    here = lax.axis_index("col") % 2 == direct_on
    return jnp.where(here, rows_of(refs[0], core), rows_of(refs[1], 1 - core))


def split_chips(refs, chips):
    split, at = [], 0
    for width, direct_on in chips:
        split.append((refs[at : at + width], direct_on))
        at += width
    return split


def triangle(blocks, groups, steps, vectors_at, factors_at, start_at, store_at):
    def block(a, _):
        def step(q, totals):
            totals = list(totals)
            vectors = vectors_at(q)
            factors = factors_at(a, q)
            for inner in range(SUB):
                rows = [vectors(g, inner) for g in range(groups)]
                for lane in range(SUB):
                    factor = factors(lane, inner)
                    for g in range(groups):
                        at = lane * groups + g
                        totals[at] = totals[at] + factor * rows[g]
            return tuple(totals)

        totals = tuple(start_at(a, g, lane) for lane in range(SUB) for g in range(groups))
        if steps > 4:
            totals = lax.fori_loop(0, steps, step, totals)
        else:
            for q in range(steps):
                totals = step(q, totals)
        for g in range(groups):
            store_at(a, g, [totals[lane * groups + g] for lane in range(SUB)])
        return 0

    lax.fori_loop(0, blocks, block, 0)


def spread(ref, row):
    return jnp.broadcast_to(ref[pl.ds(row, 1), :], (SUB, ref.shape[-1]))


def line(ref, row):
    return ref[pl.ds(pl.multiple_of(row, SUB), SUB), :]


def columns_kernel(n_row, n_col, side_x, chips, crop_ref, weights_ref, *refs):
    count = sum(width for width, _ in chips)
    chip_list, refs = split_chips(refs[:count], chips), refs[count:]
    own_ref = None
    if side_x == 0:
        _, act_ref, in_gain_ref, out_gain_ref, *refs, own_ref, gains_ref = refs
        z_hat, z_inverse = normalize(act_ref[...].astype(jnp.float32).reshape(own_ref.shape[1:]))
        own_ref[0] = z_hat
        own_ref[1] = jnp.broadcast_to(z_inverse, z_hat.shape)
        gains_ref[0:1] = in_gain_ref[...]
        gains_ref[1:2] = out_gain_ref[...]
    else:
        _, gains_ref, *refs = refs
    tri_in, (tri_ref, left_ref, right_ref, side_ref, back_ref, flip_ref) = refs[:-6], refs[-6:]
    channels = weights_ref.shape[-1]
    tile = SUB * SUB
    size = n_row * tile
    bf16, f32 = jnp.bfloat16, jnp.float32
    row_me, col_me = lax.axis_index("row"), lax.axis_index("col")
    chip_list = [(chip, on, core, b) for core in range(2) for b, (chip, on) in enumerate(chip_list)]
    normed = jnp.concatenate([chip_rows(normed_rows, chip, core, on) for chip, on, core, _ in chip_list], axis=0)
    same = lax.broadcasted_iota(jnp.int32, (channels, channels), 0) == lax.broadcasted_iota(jnp.int32, (channels, channels), 1)
    identity = jnp.where(same, 1.0, 0.0).astype(bf16)

    def turned(rows):
        return lax.dot_general(identity, rows, (((1,), (1,)), ((), ())), preferred_element_type=f32).astype(bf16)

    flip_ref[0] = turned(normed)
    crop = crop_ref[0]
    col_offset = lax.broadcasted_iota(jnp.int32, (SUB, channels), 0)
    row_offset = lax.broadcasted_iota(jnp.int32, (SUB, channels), 1)
    kept = []
    for chip, on, core, b in chip_list:
        keep = chip_rows(mask_rows, chip, core, on)
        rows_in = row_offset < crop - (row_me ^ b) * SUB
        cols_in = col_offset < crop - (col_me ^ (2 * side_x + core)) * SUB
        keep = jnp.where(rows_in & cols_in, keep, 0.0)
        kept += [jnp.broadcast_to(keep[:, at : at + 1], (SUB, channels)) for at in range(SUB)]
    kept = jnp.concatenate(kept, axis=0)
    for side, act_ref in enumerate((left_ref, right_ref)):
        pair = jnp.concatenate([weights_ref[2 * side], weights_ref[2 * side + 1]], axis=1)
        proj = jnp.dot(normed, pair, preferred_element_type=f32)
        gate = jax.nn.sigmoid(proj[:, channels:])
        masked = gate * kept
        act = masked * proj[:, :channels]
        act_ref[...] = act.astype(bf16).astype(f32)
        side_ref[2 * side] = masked
        side_ref[2 * side + 1] = act * (1.0 - gate)
    out_gate = jax.nn.sigmoid(jnp.dot(normed, weights_ref[4], preferred_element_type=f32))
    if own_ref is not None:
        own_ref[2] = out_gate[0:tile]
    cot = jnp.concatenate([chip_rows(cot_rows, chip, core, on) for chip, on, core, _ in chip_list], axis=0)
    grad = cot.astype(f32) * out_gate
    grad_lin = grad.astype(bf16)
    flip_ref[1] = turned(grad_lin)
    back_ref[0] = grad * (1.0 - out_gate)
    back = lax.dot_general(grad_lin, weights_ref[5], (((1,), (1,)), ((), ())), preferred_element_type=f32)
    back = back * gains_ref[1:2]
    back_ref[1] = back - jnp.mean(back, axis=-1, keepdims=True)
    turn = row_me ^ col_me

    def flipped(q):
        firsts = [q * size + (turn ^ g) * tile for g in range(n_col)]
        return lambda g, inner: right_ref[pl.ds(firsts[g] + inner, SUB, stride=SUB), :]

    def along(a, q):
        return lambda lane, inner: spread(left_ref, q * size + a * tile + lane * SUB + inner)

    def start(a, g, lane):
        if len(tri_in) == 0:
            return jnp.zeros((SUB, channels), f32)
        return line(tri_in[0], g * size + a * tile + lane * SUB)

    def store(a, g, values):
        for lane in range(SUB):
            tri_ref[pl.ds(pl.multiple_of(g * size + a * tile + lane * SUB, SUB), SUB), :] = values[lane]

    triangle(n_row, n_col, 2, flipped, along, start, store)


def rest_kernel(n_row, n_col, weights_ref, own_ref, gains_ref, tri_ref, *refs):
    groups = [refs[at * 5 : at * 5 + 5] for at in range(n_col // 2)]
    update_ref, pair_grad_ref, weight_grad_ref, back_ref, hat_ref, d_ref = refs[5 * (n_col // 2) :]
    channels = tri_ref.shape[-1]
    tile = SUB * SUB
    size = n_row * tile
    columns = []
    for col in range(n_col):
        own = pl.ds(col % 2 * size, size)
        left, right, side, backs, _ = groups[col // 2]
        columns.append((left.at[own], right.at[own], side.at[:, own], backs.at[:, own]))
    residues = n_row * SUB
    bf16, f32 = jnp.bfloat16, jnp.float32
    turn = lax.axis_index("row") ^ lax.axis_index("col")
    out_gain = gains_ref[1:2]
    for col, (_, _, _, backs_ref) in enumerate(columns):
        rows = slice(col * size, (col + 1) * size)
        x_hat, inverse = normalize(tri_ref[rows, :])
        normed_out = (x_hat * out_gain).astype(bf16)
        hat_ref[rows, :] = normed_out
        lin = jnp.dot(normed_out, weights_ref[5], preferred_element_type=f32)
        if col == 0:
            update_ref[...] = (own_ref[2] * lin[0:tile]).astype(bf16).reshape(update_ref.shape)
        d_ref[rows, 4 * channels : 5 * channels] = (backs_ref[0] * lin).astype(bf16)
        back = backs_ref[1]
        second = jnp.mean(back * x_hat, axis=-1, keepdims=True)
        back_ref[rows, :] = ((back - x_hat * second) * inverse).astype(bf16).astype(f32)

    lefts, rights, sides = [[column[at] for column in columns] for at in (0, 1, 2)]

    def zero(a, g, lane):
        return jnp.zeros((SUB, channels), f32)

    def store(side):
        def put(a, g, values):
            for lane in range(0, SUB, 2):
                at = pl.multiple_of(a * tile + lane * SUB, 2 * SUB)
                both = jnp.concatenate(values[lane : lane + 2], axis=0)
                rows = pl.ds(pl.multiple_of(g * size + at, 2 * SUB), 2 * SUB)
                for kind in range(2):
                    spot = (2 * side + kind) * channels
                    scaled = both * sides[g][2 * side + kind, pl.ds(at, 2 * SUB), :]
                    d_ref[rows, spot : spot + channels] = scaled.astype(bf16)
        return put

    def by_right(q):
        return lambda g, inner: line(rights[g], (q ^ turn) * tile + inner * SUB)

    def by_left(q):
        return lambda g, inner: line(lefts[g], q * tile + inner * SUB)

    def along(a, q):
        return lambda lane, inner: spread(back_ref, q * size + a * tile + lane * SUB + inner)

    def down(a, q):
        return lambda lane, inner: spread(back_ref, (a ^ turn) * size + q * tile + inner * SUB + lane)

    triangle(n_row, n_col, n_col, by_right, along, zero, store(0))
    triangle(n_row, n_col, n_row, by_left, down, zero, store(1))

    scale = 1.0 / residues
    flipped, lin_flipped = [jnp.concatenate([group[4][at] for group in groups], axis=1) for at in range(2)]
    sums = jnp.dot(flipped, d_ref[...], preferred_element_type=f32) * scale
    for s in range(5):
        weight_grad_ref[s] = sums[:, s * channels : (s + 1) * channels]
    weight_grad_ref[5] = jnp.dot(lin_flipped, hat_ref[...], preferred_element_type=f32).T * scale
    total = jnp.zeros((tile, channels), f32)
    for s in range(5):
        total = total + lax.dot_general(
            d_ref[0:tile, s * channels : (s + 1) * channels], weights_ref[s],
            (((1,), (1,)), ((), ())), preferred_element_type=f32,
        )
    grad = norm_back(total * gains_ref[0:1], own_ref[0], own_ref[1])
    pair_grad_ref[...] = grad.astype(bf16).reshape(pair_grad_ref.shape)


def flip(block, n_row, n_col, even, odd):
    pairs = []
    for row in range(n_row):
        for col in range(n_col):
            shift = odd if col % 2 else even
            pairs.append((row * n_col + col, (row ^ shift[0]) * n_col + (col ^ shift[1])))
    return lax.ppermute(block, ("row", "col"), pairs)


def gathered_body(n_row, n_col, pair_act, pair_mask, crop_length, weights, in_gain, out_gain, cotangent):
    tile_rows, tile_cols, channels = pair_act.shape
    tile = tile_rows * tile_cols
    size = n_row * tile
    pairs = size * n_col
    head = tile + 2 * SUB
    f32, bf16 = jnp.float32, jnp.bfloat16
    vmem = pl.BlockSpec(memory_space=pltpu.VMEM)
    smem = pl.BlockSpec(memory_space=pltpu.SMEM)
    hbm = pl.BlockSpec(memory_space=pltpu.HBM)
    in_gain, out_gain = in_gain.reshape(1, channels), out_gain.reshape(1, channels)

    def limit(mib):
        return pltpu.CompilerParams(vmem_limit_bytes=mib * 1024 * 1024)

    own = pl.pallas_call(
        pack_kernel,
        name="pack",
        out_shape=jax.ShapeDtypeStruct((head + tile, channels), bf16),
        in_specs=[hbm] * 4,
        out_specs=vmem,
        scratch_shapes=[
            pltpu.VMEM(pair_act.shape, pair_act.dtype),
            pltpu.VMEM(pair_mask.shape, jnp.int32),
            pltpu.VMEM((1, channels), f32),
            pltpu.SemaphoreType.DMA((4,)),
        ],
        compiler_params=limit(60),
    )(pair_act, pair_mask, cotangent.reshape(tile, channels), in_gain)
    crop_length, own = lax.optimization_barrier((crop_length, own))

    def move(block, even, odd):
        return flip(block, n_row, n_col, even, odd)

    def other(block):
        return move(block, (0, 1), (0, 1))

    held = pl.pallas_call(
        copy_kernel,
        name="hold",
        out_shape=jax.ShapeDtypeStruct(own.shape, bf16),
        in_specs=[vmem],
        out_specs=vmem,
        compiler_params=limit(2),
        cost_estimate=pl.CostEstimate(flops=100_000_000, bytes_accessed=1_000_000, transcendentals=0),
    )(own)
    both = pl.pallas_call(
        join_kernel,
        name="join",
        out_shape=jax.ShapeDtypeStruct((2 * own.shape[0] - 2 * SUB, channels), bf16),
        in_specs=[vmem] * 2,
        out_specs=vmem,
        compiler_params=limit(2),
    )(held, other(own))
    straight = move(own, (3, 0), (3, 0))
    first = move(both, (2, 0), (1, 0))
    second = move(both, (0, 2), (2, 2))
    third = move(both, (1, 2), (3, 2))
    straight, first, second, third = [(block, other(block)) for block in (straight, first, second, third)]
    chips = (((1, None), (2, 1), (2, 0), (2, None)), ((2, 0), (2, 0), (2, 1), (2, 1)))
    sources = ((both, *first, *first, *straight), (*second, *third, *second, *third))

    anywhere = pl.BlockSpec(memory_space=pl.ANY)

    def token(cost, *pieces):
        return pl.pallas_call(
            token_kernel,
            name="token",
            out_shape=jax.ShapeDtypeStruct((SUB, channels), f32),
            in_specs=[anywhere] * len(pieces),
            out_specs=vmem,
            compiler_params=limit(2),
            cost_estimate=pl.CostEstimate(flops=cost, bytes_accessed=1_000_000, transcendentals=0),
        )(*pieces)

    tokens = (token(1_000_000_000, *straight), token(1_000_000, *second, *third))
    tri, parts, extra = [], [], []
    for side_x in range(n_col // 2):
        more = (tokens[0], pair_act, in_gain, out_gain) if side_x == 0 else (tokens[1], extra[1], *tri)
        more_shapes = () if side_x > 0 else (
            jax.ShapeDtypeStruct((3, tile, channels), f32),
            jax.ShapeDtypeStruct((SUB, channels), f32),
        )
        tri, *results = pl.pallas_call(
            functools.partial(columns_kernel, n_row, n_col, side_x, chips[side_x]),
            name=f"columns_{side_x}",
            out_shape=(
                jax.ShapeDtypeStruct((pairs, channels), f32),
                jax.ShapeDtypeStruct((2 * size, channels), f32),
                jax.ShapeDtypeStruct((2 * size, channels), f32),
                jax.ShapeDtypeStruct((4, 2 * size, channels), f32),
                jax.ShapeDtypeStruct((2, 2 * size, channels), f32),
                jax.ShapeDtypeStruct((2, channels, 2 * size), bf16),
                *more_shapes,
            ),
            in_specs=[smem] + [vmem] * (1 + len(sources[side_x]) + len(more)),
            out_specs=(vmem,) * (6 + len(more_shapes)),
            input_output_aliases={4 + len(sources[side_x]): 0} if side_x > 0 else {},
            compiler_params=limit(12),
            cost_estimate=pl.CostEstimate(flops=800_000_000, bytes_accessed=1_000_000, transcendentals=0),
        )(crop_length, weights, *sources[side_x], *more)
        tri = [tri]
        parts += results[:5]
        extra += results[5:]

    return pl.pallas_call(
        functools.partial(rest_kernel, n_row, n_col),
        name="rest",
        out_shape=(
            jax.ShapeDtypeStruct(pair_act.shape, bf16),
            jax.ShapeDtypeStruct(pair_act.shape, bf16),
            jax.ShapeDtypeStruct(weights.shape, f32),
        ),
        in_specs=[vmem] * (4 + len(parts)),
        out_specs=(vmem, vmem, vmem),
        scratch_shapes=[
            pltpu.VMEM((pairs, channels), f32),
            pltpu.VMEM((pairs, channels), bf16),
            pltpu.VMEM((pairs, 5 * channels), bf16),
        ],
        compiler_params=limit(16),
    )(weights, *extra, *tri, *parts)


def body(n_row, n_col, pair_act, *others):
    tile_rows, tile_cols, channels = pair_act.shape
    pairs = tile_rows * n_row * tile_cols * n_col
    small = pairs * channels * 4 <= 1024 * 1024 and channels == 128
    square = n_row == 4 and n_col == 4 and tile_rows == SUB and tile_cols == SUB
    if small and square:
        return gathered_body(n_row, n_col, pair_act, *others)
    return spread_body(pair_act, *others)


def solution(mesh):
    return jax.shard_map(
        functools.partial(body, mesh.shape["row"], mesh.shape["col"]),
        mesh=mesh,
        in_specs=(
            P(("parts", "row"), "col", None),
            P(("parts", "row"), "col"),
            P("parts"),
            P(),
            P(),
            P(),
            P(("parts", "row"), "col", None),
        ),
        out_specs=(
            P(("parts", "row"), "col", None),
            P(("parts", "row"), "col", None),
            P("parts", None, None),
        ),
        check_vma=False,
    )
```

```python
import functools

import jax
import jax.numpy as jnp
from jax import lax
from jax.experimental import pallas as pl
from jax.experimental.pallas import tpu as pltpu
from jax.sharding import PartitionSpec as P

SUB = 8
EPS = 1e-05


def normalize(values):
    average = jnp.mean(values, axis=-1, keepdims=True)
    centered = values - average
    inverse = lax.rsqrt(jnp.mean(centered * centered, axis=-1, keepdims=True) + 1e-05)
    return (centered * inverse, inverse)


def norm_back(grad_hat, values_hat, inverse):
    first = jnp.mean(grad_hat, axis=-1, keepdims=True)
    second = jnp.mean(grad_hat * values_hat, axis=-1, keepdims=True)
    return (grad_hat - first - values_hat * second) * inverse


def gate_back(grad_act, proj_value, proj_gate, keep_mask):
    gate_sig = jax.nn.sigmoid(proj_gate)
    masked = grad_act * keep_mask
    grad_value = (masked * gate_sig).astype(jnp.bfloat16)
    grad_gate = (masked * proj_value * gate_sig * (1.0 - gate_sig)).astype(jnp.bfloat16)
    return (grad_value, grad_gate)


def spread_body(pair_act, pair_mask, crop_length, weights, in_gain, out_gain, cotangent):
    tile_rows, tile_cols, channels = pair_act.shape
    residues = tile_rows * lax.axis_size("row")
    row_pos = lax.axis_index("row") * tile_rows + jnp.arange(tile_rows, dtype=jnp.int32)
    col_pos = lax.axis_index("col") * tile_cols + jnp.arange(tile_cols, dtype=jnp.int32)
    row_in = (row_pos < crop_length[0]).astype(jnp.float32)
    col_in = (col_pos < crop_length[0]).astype(jnp.float32)
    keep_mask = (pair_mask.astype(jnp.float32) * row_in[:, None] * col_in[None, :])[:, :, None]
    z_hat, z_inverse = normalize(pair_act.astype(jnp.float32))
    normed = (z_hat * in_gain).astype(jnp.bfloat16)
    flat_norm = normed.reshape(tile_rows * tile_cols, channels)
    projections = jnp.einsum(
        "pc,scd->spd", flat_norm, weights[:5], preferred_element_type=jnp.float32
    )
    projections = projections.reshape(5, tile_rows, tile_cols, channels)
    left_act = (jax.nn.sigmoid(projections[1]) * projections[0] * keep_mask).astype(jnp.bfloat16)
    right_act = (jax.nn.sigmoid(projections[3]) * projections[2] * keep_mask).astype(jnp.bfloat16)
    partial_value = jnp.einsum(
        "ikh,jkh->ijh",
        left_act,
        lax.all_gather(right_act, "row", axis=0, tiled=True),
        preferred_element_type=jnp.float32,
    )
    tri_sum = lax.psum_scatter(
        partial_value.astype(jnp.bfloat16), "col", scatter_dimension=1, tiled=True
    ).astype(jnp.float32)
    x_hat, x_inverse = normalize(tri_sum)
    normed_out = (x_hat * out_gain).astype(jnp.bfloat16)
    flat_out = normed_out.reshape(tile_rows * tile_cols, channels)
    update_lin = jnp.dot(flat_out, weights[5], preferred_element_type=jnp.float32)
    update_lin = update_lin.reshape(tile_rows, tile_cols, channels)
    out_gate = jax.nn.sigmoid(projections[4])
    update = (out_gate * update_lin).astype(jnp.bfloat16)
    cot_value = cotangent.astype(jnp.float32)
    grad_lin = (cot_value * out_gate).astype(jnp.bfloat16)
    grad_gate_out = (cot_value * update_lin * out_gate * (1.0 - out_gate)).astype(jnp.bfloat16)
    flat_lin = grad_lin.reshape(tile_rows * tile_cols, channels)
    grad_norm_out = jnp.einsum(
        "pd,cd->pc", flat_lin, weights[5], preferred_element_type=jnp.float32
    )
    grad_norm_out = grad_norm_out.reshape(tile_rows, tile_cols, channels)
    grad_tri = norm_back(grad_norm_out * out_gain, x_hat, x_inverse).astype(jnp.bfloat16)
    grad_full = lax.all_gather(grad_tri, "col", axis=1, tiled=True)
    grad_slab = grad_full
    grad_left = jnp.einsum(
        "ijh,jkh->ikh",
        grad_slab,
        lax.all_gather(right_act, "row", axis=0, tiled=True),
        preferred_element_type=jnp.float32,
    )
    grad_slab = grad_full
    grad_right = lax.psum_scatter(
        jnp.einsum("ijh,ikh->jkh", grad_slab, left_act, preferred_element_type=jnp.float32).astype(
            jnp.bfloat16
        ),
        "row",
        scatter_dimension=0,
        tiled=True,
    ).astype(jnp.float32)
    grad_pa, grad_ga = gate_back(grad_left, projections[0], projections[1], keep_mask)
    grad_pb, grad_gb = gate_back(grad_right, projections[2], projections[3], keep_mask)
    grads = jnp.stack([grad_pa, grad_ga, grad_pb, grad_gb, grad_gate_out]).reshape(
        5, tile_rows * tile_cols, channels
    )
    grad_normed = jnp.einsum("spd,scd->pc", grads, weights[:5], preferred_element_type=jnp.float32)
    grad_normed = grad_normed.reshape(tile_rows, tile_cols, channels)
    pair_grad = norm_back(grad_normed * in_gain, z_hat, z_inverse).astype(jnp.bfloat16)
    local_in = jnp.einsum("pc,spd->scd", flat_norm, grads, preferred_element_type=jnp.float32)
    local_out = jnp.dot(flat_out.T, flat_lin, preferred_element_type=jnp.float32)
    local_grads = jnp.concatenate([local_in, local_out[None]], axis=0) / residues
    weight_grad = lax.psum(local_grads, ("row", "col"))
    return (update, pair_grad, weight_grad)


def pack_kernel(act_hbm, mask_hbm, cot_hbm, gain_hbm, out_ref, act_ref, mask_ref, gain_ref, sems):
    tile_rows, tile_cols, channels = act_ref.shape
    pairs = tile_rows * tile_cols
    head = out_ref.shape[0] - pairs
    pack_copies = [
        pltpu.make_async_copy(act_hbm, act_ref, sems.at[0]),
        pltpu.make_async_copy(gain_hbm, gain_ref, sems.at[1]),
        pltpu.make_async_copy(mask_hbm, mask_ref, sems.at[2]),
        pltpu.make_async_copy(cot_hbm, out_ref.at[head : head + pairs], sems.at[3]),
    ]
    for copy in pack_copies:
        copy.start()
    for copy in pack_copies:
        copy.wait()
    z_hat, _ = normalize(act_ref[...].astype(jnp.float32).reshape(pairs, channels))
    out_ref[0:pairs] = (z_hat * gain_ref[...]).astype(jnp.bfloat16)
    keep = mask_ref[...].astype(jnp.float32)
    wide = jnp.concatenate([keep, jnp.zeros((tile_rows, channels - tile_cols), jnp.float32)], axis=1)
    tall = jnp.concatenate([wide, jnp.zeros((channels - tile_rows, channels), jnp.float32)], axis=0)
    out_ref[pairs:head] = tall.T[0 : head - pairs].astype(jnp.bfloat16)


def copy_kernel(in_ref, out_ref):
    out_ref[...] = in_ref[...]


def join_kernel(own_ref, twin_ref, out_ref):
    tile = SUB * SUB
    refs = (own_ref, twin_ref)
    for at, ref in enumerate(refs):
        out_ref[at * tile : (at + 1) * tile] = ref[0:tile]
        spot = 2 * tile + 2 * SUB + at * tile
        out_ref[spot : spot + tile] = ref[tile + 2 * SUB :]
    masks = [ref[tile : tile + 2 * SUB].astype(jnp.float32)[0:SUB] for ref in refs]
    out_ref[2 * tile : 2 * tile + 2 * SUB] = jnp.concatenate(masks, axis=0).astype(jnp.bfloat16)


def normed_rows(ref, sub):
    return ref[sub * SUB * SUB : (sub + 1) * SUB * SUB]


def mask_rows(ref, sub):
    at = ref.shape[0] // 2 // (SUB * SUB) * SUB * SUB
    return ref[at : at + 2 * SUB].astype(jnp.float32)[sub * SUB : (sub + 1) * SUB]


def cot_rows(ref, sub):
    at = ref.shape[0] // 2 // (SUB * SUB) * SUB * SUB + 2 * SUB
    return ref[at + sub * SUB * SUB : at + (sub + 1) * SUB * SUB]


def chip_rows(rows_of, refs, core, direct_on):
    if direct_on is None:
        return rows_of(refs[min(core, len(refs) - 1)], core if len(refs) == 1 else 0)
    here = lax.axis_index("col") % 2 == direct_on
    return jnp.where(here, rows_of(refs[0], core), rows_of(refs[1], 1 - core))


def split_chips(refs, chips):
    split, at = [], 0
    for width, direct_on in chips:
        split.append((refs[at : at + width], direct_on))
        at += width
    return split


def triangle(blocks, groups, steps, vectors_at, factors_at, start_at, store_at, beside=None):
    def block(a, _):
        if beside is not None:
            beside(a)
        def step(q, totals):
            totals = list(totals)
            vectors = vectors_at(q)
            factors = factors_at(a, q)
            for inner in range(SUB):
                rows = [vectors(g, inner) for g in range(groups)]
                for lane in range(SUB):
                    factor = factors(lane, inner)
                    for g in range(groups):
                        at = lane * groups + g
                        totals[at] = totals[at] + factor * rows[g]
            return tuple(totals)

        totals = tuple(start_at(a, g, lane) for lane in range(SUB) for g in range(groups))
        if steps > 4:
            totals = lax.fori_loop(0, steps, step, totals)
        else:
            for q in range(steps):
                totals = step(q, totals)
        for g in range(groups):
            store_at(a, g, [totals[lane * groups + g] for lane in range(SUB)])
        return 0

    lax.fori_loop(0, blocks, block, 0)


def spread(ref, row):
    return jnp.broadcast_to(ref[pl.ds(row, 1), :], (SUB, ref.shape[-1]))


def line(ref, row):
    return ref[pl.ds(pl.multiple_of(row, SUB), SUB), :]


def columns_kernel(n_row, n_col, side_x, chips, crop_ref, weights_ref, *refs):
    count = sum(width for width, _ in chips)
    chip_list, refs = split_chips(refs[:count], chips), refs[count:]
    own_ref = None
    if side_x == 0:
        act_ref, in_gain_ref, out_gain_ref, *refs, own_ref, gains_ref = refs
        z_hat, z_inverse = normalize(act_ref[...].astype(jnp.float32).reshape(own_ref.shape[1:]))
        own_ref[0] = z_hat
        own_ref[1] = jnp.broadcast_to(z_inverse, z_hat.shape)
        gains_ref[0:1] = in_gain_ref[...]
        gains_ref[1:2] = out_gain_ref[...]
    else:
        gains_ref, *refs = refs
    tri_in, (tri_ref, flip_ref, left_ref, right_ref, side_ref, back_ref) = refs[:-6], refs[-6:]
    channels = weights_ref.shape[-1]
    tile = SUB * SUB
    size = n_row * tile
    bf16, f32 = jnp.bfloat16, jnp.float32
    row_me, col_me = lax.axis_index("row"), lax.axis_index("col")
    chip_list = [(chip, on, core, b) for core in range(2) for b, (chip, on) in enumerate(chip_list)]
    normed = jnp.concatenate([chip_rows(normed_rows, chip, core, on) for chip, on, core, _ in chip_list], axis=0)
    same = lax.broadcasted_iota(jnp.int32, (channels, channels), 0) == lax.broadcasted_iota(jnp.int32, (channels, channels), 1)
    identity = jnp.where(same, 1.0, 0.0).astype(bf16)

    def turned(rows):
        return lax.dot_general(identity, rows, (((1,), (1,)), ((), ())), preferred_element_type=f32).astype(bf16)

    def put(kind, rows):
        both = turned(rows)
        for core in range(2):
            flip_ref[kind, 2 * side_x + core] = both[:, core * size : (core + 1) * size]

    put(0, normed)
    crop = crop_ref[0]
    col_offset = lax.broadcasted_iota(jnp.int32, (SUB, channels), 0)
    row_offset = lax.broadcasted_iota(jnp.int32, (SUB, channels), 1)
    kept = []
    for chip, on, core, b in chip_list:
        keep = chip_rows(mask_rows, chip, core, on)
        rows_in = row_offset < crop - (row_me ^ b) * SUB
        cols_in = col_offset < crop - (col_me ^ (2 * side_x + core)) * SUB
        keep = jnp.where(rows_in & cols_in, keep, 0.0)
        kept += [jnp.broadcast_to(keep[:, at : at + 1], (SUB, channels)) for at in range(SUB)]
    kept = jnp.concatenate(kept, axis=0)
    for side, act_ref in enumerate((left_ref, right_ref)):
        pair = jnp.concatenate([weights_ref[2 * side], weights_ref[2 * side + 1]], axis=1)
        proj = jnp.dot(normed, pair, preferred_element_type=f32)
        gate = jax.nn.sigmoid(proj[:, channels:])
        masked = gate * kept
        act = masked * proj[:, :channels]
        act_ref[...] = act.astype(bf16).astype(f32)
        side_ref[2 * side] = masked
        side_ref[2 * side + 1] = act * (1.0 - gate)
    out_gate = jax.nn.sigmoid(jnp.dot(normed, weights_ref[4], preferred_element_type=f32))
    if own_ref is not None:
        own_ref[2] = out_gate[0:tile]
    cot = jnp.concatenate([chip_rows(cot_rows, chip, core, on) for chip, on, core, _ in chip_list], axis=0)
    grad = cot.astype(f32) * out_gate
    grad_lin = grad.astype(bf16)
    put(1, grad_lin)
    back_ref[0] = grad * (1.0 - out_gate)
    back = lax.dot_general(grad_lin, weights_ref[5], (((1,), (1,)), ((), ())), preferred_element_type=f32)
    back = back * gains_ref[1:2]
    back_ref[1] = back - jnp.mean(back, axis=-1, keepdims=True)
    turn = row_me ^ col_me

    def flipped(q):
        firsts = [q * size + (turn ^ g) * tile for g in range(n_col)]
        return lambda g, inner: right_ref[pl.ds(firsts[g] + inner, SUB, stride=SUB), :]

    def along(a, q):
        return lambda lane, inner: spread(left_ref, q * size + a * tile + lane * SUB + inner)

    def start(a, g, lane):
        if len(tri_in) == 0:
            return jnp.zeros((SUB, channels), f32)
        return line(tri_in[0], g * size + a * tile + lane * SUB)

    def store(a, g, values):
        for lane in range(SUB):
            tri_ref[pl.ds(pl.multiple_of(g * size + a * tile + lane * SUB, SUB), SUB), :] = values[lane]

    triangle(n_row, n_col, 2, flipped, along, start, store)


def rest_kernel(n_row, n_col, weights_ref, own_ref, gains_ref, tri_ref, flip_ref, *refs):
    groups = [refs[at * 4 : at * 4 + 4] for at in range(n_col // 2)]
    update_ref, pair_grad_ref, weight_grad_ref, back_ref, hat_ref, d_ref, sum_ref = refs[4 * (n_col // 2) :]
    channels = tri_ref.shape[-1]
    tile = SUB * SUB
    size = n_row * tile
    columns = []
    for col in range(n_col):
        own = pl.ds(col % 2 * size, size)
        left, right, side, backs = groups[col // 2]
        columns.append((left.at[own], right.at[own], side.at[:, own], backs.at[:, own]))
    residues = n_row * SUB
    bf16, f32 = jnp.bfloat16, jnp.float32
    turn = lax.axis_index("row") ^ lax.axis_index("col")
    out_gain = gains_ref[1:2]
    for col, (_, _, _, backs_ref) in enumerate(columns):
        rows = slice(col * size, (col + 1) * size)
        x_hat, inverse = normalize(tri_ref[rows, :])
        normed_out = (x_hat * out_gain).astype(bf16)
        hat_ref[rows, :] = normed_out
        lin = jnp.dot(normed_out, weights_ref[5], preferred_element_type=f32)
        if col == 0:
            update_ref[...] = (own_ref[2] * lin[0:tile]).astype(bf16).reshape(update_ref.shape)
        d_ref[rows, 4 * channels : 5 * channels] = (backs_ref[0] * lin).astype(bf16)
        back = backs_ref[1]
        second = jnp.mean(back * x_hat, axis=-1, keepdims=True)
        back_ref[rows, :] = ((back - x_hat * second) * inverse).astype(bf16).astype(f32)

    lefts, rights, sides = [[column[at] for column in columns] for at in (0, 1, 2)]

    def zero(a, g, lane):
        return jnp.zeros((SUB, channels), f32)

    def store(side):
        def put(a, g, values):
            for lane in range(0, SUB, 2):
                at = pl.multiple_of(a * tile + lane * SUB, 2 * SUB)
                both = jnp.concatenate(values[lane : lane + 2], axis=0)
                rows = pl.ds(pl.multiple_of(g * size + at, 2 * SUB), 2 * SUB)
                for kind in range(2):
                    spot = (2 * side + kind) * channels
                    scaled = both * sides[g][2 * side + kind, pl.ds(at, 2 * SUB), :]
                    d_ref[rows, spot : spot + channels] = scaled.astype(bf16)
        return put

    def by_right(q):
        return lambda g, inner: line(rights[g], (q ^ turn) * tile + inner * SUB)

    def by_left(q):
        return lambda g, inner: line(lefts[g], q * tile + inner * SUB)

    def along(a, q):
        return lambda lane, inner: spread(back_ref, q * size + a * tile + lane * SUB + inner)

    def down(a, q):
        return lambda lane, inner: spread(back_ref, (a ^ turn) * size + q * tile + inner * SUB + lane)

    def chunk(ref, a, first, last):
        return ref[pl.ds(pl.multiple_of(a * size, size), size), first * channels : last * channels]

    def early_sums(a):
        sum_ref[:, 0:channels] += jnp.dot(flip_ref[0, a], chunk(d_ref, a, 4, 5), preferred_element_type=f32)
        sum_ref[:, channels : 2 * channels] += jnp.dot(flip_ref[1, a], chunk(hat_ref, a, 0, 1), preferred_element_type=f32)

    def left_sums(a):
        sum_ref[:, 2 * channels :] += jnp.dot(flip_ref[0, a], chunk(d_ref, a, 0, 2), preferred_element_type=f32)

    sum_ref[...] = jnp.zeros(sum_ref.shape, f32)
    triangle(n_row, n_col, n_col, by_right, along, zero, store(0), early_sums)
    triangle(n_row, n_col, n_row, by_left, down, zero, store(1), left_sums)

    scale = 1.0 / residues
    flipped = jnp.concatenate([flip_ref[0, col] for col in range(n_col)], axis=1)
    right_sums = jnp.dot(flipped, d_ref[:, 2 * channels : 4 * channels], preferred_element_type=f32)
    for s in range(2):
        part = slice(s * channels, (s + 1) * channels)
        weight_grad_ref[s] = sum_ref[:, (2 + s) * channels : (3 + s) * channels] * scale
        weight_grad_ref[2 + s] = right_sums[:, part] * scale
    weight_grad_ref[4] = sum_ref[:, 0:channels] * scale
    weight_grad_ref[5] = sum_ref[:, channels : 2 * channels].T * scale
    total = jnp.zeros((tile, channels), f32)
    for s in range(5):
        total = total + lax.dot_general(
            d_ref[0:tile, s * channels : (s + 1) * channels], weights_ref[s],
            (((1,), (1,)), ((), ())), preferred_element_type=f32,
        )
    grad = norm_back(total * gains_ref[0:1], own_ref[0], own_ref[1])
    pair_grad_ref[...] = grad.astype(bf16).reshape(pair_grad_ref.shape)


def flip(block, n_row, n_col, even, odd):
    pairs = []
    for row in range(n_row):
        for col in range(n_col):
            shift = odd if col % 2 else even
            pairs.append((row * n_col + col, (row ^ shift[0]) * n_col + (col ^ shift[1])))
    return lax.ppermute(block, ("row", "col"), pairs)


def gathered_body(n_row, n_col, pair_act, pair_mask, crop_length, weights, in_gain, out_gain, cotangent):
    tile_rows, tile_cols, channels = pair_act.shape
    tile = tile_rows * tile_cols
    size = n_row * tile
    pairs = size * n_col
    head = tile + 2 * SUB
    f32, bf16 = jnp.float32, jnp.bfloat16
    vmem = pl.BlockSpec(memory_space=pltpu.VMEM)
    smem = pl.BlockSpec(memory_space=pltpu.SMEM)
    hbm = pl.BlockSpec(memory_space=pltpu.HBM)
    in_gain, out_gain = in_gain.reshape(1, channels), out_gain.reshape(1, channels)

    def limit(mib):
        return pltpu.CompilerParams(vmem_limit_bytes=mib * 1024 * 1024)

    own = pl.pallas_call(
        pack_kernel,
        name="pack",
        out_shape=jax.ShapeDtypeStruct((head + tile, channels), bf16),
        in_specs=[hbm] * 4,
        out_specs=vmem,
        scratch_shapes=[
            pltpu.VMEM(pair_act.shape, pair_act.dtype),
            pltpu.VMEM(pair_mask.shape, jnp.int32),
            pltpu.VMEM((1, channels), f32),
            pltpu.SemaphoreType.DMA((4,)),
        ],
        compiler_params=limit(60),
    )(pair_act, pair_mask, cotangent.reshape(tile, channels), in_gain)
    crop_length, own = lax.optimization_barrier((crop_length, own))

    def move(block, even, odd):
        return flip(block, n_row, n_col, even, odd)

    def other(block):
        return move(block, (0, 1), (0, 1))

    held = pl.pallas_call(
        copy_kernel,
        name="hold",
        out_shape=jax.ShapeDtypeStruct(own.shape, bf16),
        in_specs=[vmem],
        out_specs=vmem,
        compiler_params=limit(2),
        cost_estimate=pl.CostEstimate(flops=100_000_000, bytes_accessed=1_000_000, transcendentals=0),
    )(own)
    both = pl.pallas_call(
        join_kernel,
        name="join",
        out_shape=jax.ShapeDtypeStruct((2 * own.shape[0] - 2 * SUB, channels), bf16),
        in_specs=[vmem] * 2,
        out_specs=vmem,
        compiler_params=limit(2),
    )(held, other(own))
    straight = move(own, (3, 0), (3, 0))
    first = move(both, (2, 0), (1, 0))
    second = move(both, (0, 2), (2, 2))
    third = move(both, (1, 2), (3, 2))
    straight, first, second, third = [(block, other(block)) for block in (straight, first, second, third)]
    chips = (((1, None), (2, 1), (2, 0), (2, None)), ((2, 0), (2, 0), (2, 1), (2, 1)))
    sources = ((both, *first, *first, *straight), (*second, *third, *second, *third))

    tri, parts, extra = [], [], []
    for side_x in range(n_col // 2):
        more = (pair_act, in_gain, out_gain) if side_x == 0 else (extra[1], *tri)
        more_shapes = () if side_x > 0 else (
            jax.ShapeDtypeStruct((3, tile, channels), f32),
            jax.ShapeDtypeStruct((SUB, channels), f32),
        )
        last = 3 + len(sources[side_x])
        results = pl.pallas_call(
            functools.partial(columns_kernel, n_row, n_col, side_x, chips[side_x]),
            name=f"columns_{side_x}",
            out_shape=(
                jax.ShapeDtypeStruct((pairs, channels), f32),
                jax.ShapeDtypeStruct((2, n_col, channels, size), bf16),
                jax.ShapeDtypeStruct((2 * size, channels), f32),
                jax.ShapeDtypeStruct((2 * size, channels), f32),
                jax.ShapeDtypeStruct((4, 2 * size, channels), f32),
                jax.ShapeDtypeStruct((2, 2 * size, channels), f32),
                *more_shapes,
            ),
            in_specs=[smem] + [vmem] * (1 + len(sources[side_x]) + len(more)),
            out_specs=(vmem,) * (6 + len(more_shapes)),
            input_output_aliases={last: 0, last + 1: 1} if side_x > 0 else {},
            compiler_params=limit(12),
            cost_estimate=pl.CostEstimate(flops=800_000_000, bytes_accessed=1_000_000, transcendentals=0),
        )(crop_length, weights, *sources[side_x], *more)
        tri = results[:2]
        parts += results[2:6]
        extra += results[6:]

    return pl.pallas_call(
        functools.partial(rest_kernel, n_row, n_col),
        name="rest",
        out_shape=(
            jax.ShapeDtypeStruct(pair_act.shape, bf16),
            jax.ShapeDtypeStruct(pair_act.shape, bf16),
            jax.ShapeDtypeStruct(weights.shape, f32),
        ),
        in_specs=[vmem] * (5 + len(parts)),
        out_specs=(vmem, vmem, vmem),
        scratch_shapes=[
            pltpu.VMEM((pairs, channels), f32),
            pltpu.VMEM((pairs, channels), bf16),
            pltpu.VMEM((pairs, 5 * channels), bf16),
            pltpu.VMEM((channels, 4 * channels), f32),
        ],
        compiler_params=limit(16),
    )(weights, *extra, *tri, *parts)


def body(n_row, n_col, pair_act, *others):
    tile_rows, tile_cols, channels = pair_act.shape
    pairs = tile_rows * n_row * tile_cols * n_col
    small = pairs * channels * 4 <= 1024 * 1024 and channels == 128
    square = n_row == 4 and n_col == 4 and tile_rows == SUB and tile_cols == SUB
    if small and square:
        return gathered_body(n_row, n_col, pair_act, *others)
    return spread_body(pair_act, *others)


def solution(mesh):
    return jax.shard_map(
        functools.partial(body, mesh.shape["row"], mesh.shape["col"]),
        mesh=mesh,
        in_specs=(
            P(("parts", "row"), "col", None),
            P(("parts", "row"), "col"),
            P("parts"),
            P(),
            P(),
            P(),
            P(("parts", "row"), "col", None),
        ),
        out_specs=(
            P(("parts", "row"), "col", None),
            P(("parts", "row"), "col", None),
            P("parts", None, None),
        ),
        check_vma=False,
    )
```

```python
import functools

import jax
import jax.numpy as jnp
from jax import lax
from jax.experimental import pallas as pl
from jax.experimental.pallas import tpu as pltpu
from jax.sharding import PartitionSpec as P

SUB = 8
EPS = 1e-05


def normalize(values):
    average = jnp.mean(values, axis=-1, keepdims=True)
    centered = values - average
    inverse = lax.rsqrt(jnp.mean(centered * centered, axis=-1, keepdims=True) + 1e-05)
    return (centered * inverse, inverse)


def norm_back(grad_hat, values_hat, inverse):
    first = jnp.mean(grad_hat, axis=-1, keepdims=True)
    second = jnp.mean(grad_hat * values_hat, axis=-1, keepdims=True)
    return (grad_hat - first - values_hat * second) * inverse


def gate_back(grad_act, proj_value, proj_gate, keep_mask):
    gate_sig = jax.nn.sigmoid(proj_gate)
    masked = grad_act * keep_mask
    grad_value = (masked * gate_sig).astype(jnp.bfloat16)
    grad_gate = (masked * proj_value * gate_sig * (1.0 - gate_sig)).astype(jnp.bfloat16)
    return (grad_value, grad_gate)


def spread_body(pair_act, pair_mask, crop_length, weights, in_gain, out_gain, cotangent):
    tile_rows, tile_cols, channels = pair_act.shape
    residues = tile_rows * lax.axis_size("row")
    row_pos = lax.axis_index("row") * tile_rows + jnp.arange(tile_rows, dtype=jnp.int32)
    col_pos = lax.axis_index("col") * tile_cols + jnp.arange(tile_cols, dtype=jnp.int32)
    row_in = (row_pos < crop_length[0]).astype(jnp.float32)
    col_in = (col_pos < crop_length[0]).astype(jnp.float32)
    keep_mask = (pair_mask.astype(jnp.float32) * row_in[:, None] * col_in[None, :])[:, :, None]
    z_hat, z_inverse = normalize(pair_act.astype(jnp.float32))
    normed = (z_hat * in_gain).astype(jnp.bfloat16)
    flat_norm = normed.reshape(tile_rows * tile_cols, channels)
    projections = jnp.einsum(
        "pc,scd->spd", flat_norm, weights[:5], preferred_element_type=jnp.float32
    )
    projections = projections.reshape(5, tile_rows, tile_cols, channels)
    left_act = (jax.nn.sigmoid(projections[1]) * projections[0] * keep_mask).astype(jnp.bfloat16)
    right_act = (jax.nn.sigmoid(projections[3]) * projections[2] * keep_mask).astype(jnp.bfloat16)
    partial_value = jnp.einsum(
        "ikh,jkh->ijh",
        left_act,
        lax.all_gather(right_act, "row", axis=0, tiled=True),
        preferred_element_type=jnp.float32,
    )
    tri_sum = lax.psum_scatter(
        partial_value.astype(jnp.bfloat16), "col", scatter_dimension=1, tiled=True
    ).astype(jnp.float32)
    x_hat, x_inverse = normalize(tri_sum)
    normed_out = (x_hat * out_gain).astype(jnp.bfloat16)
    flat_out = normed_out.reshape(tile_rows * tile_cols, channels)
    update_lin = jnp.dot(flat_out, weights[5], preferred_element_type=jnp.float32)
    update_lin = update_lin.reshape(tile_rows, tile_cols, channels)
    out_gate = jax.nn.sigmoid(projections[4])
    update = (out_gate * update_lin).astype(jnp.bfloat16)
    cot_value = cotangent.astype(jnp.float32)
    grad_lin = (cot_value * out_gate).astype(jnp.bfloat16)
    grad_gate_out = (cot_value * update_lin * out_gate * (1.0 - out_gate)).astype(jnp.bfloat16)
    flat_lin = grad_lin.reshape(tile_rows * tile_cols, channels)
    grad_norm_out = jnp.einsum(
        "pd,cd->pc", flat_lin, weights[5], preferred_element_type=jnp.float32
    )
    grad_norm_out = grad_norm_out.reshape(tile_rows, tile_cols, channels)
    grad_tri = norm_back(grad_norm_out * out_gain, x_hat, x_inverse).astype(jnp.bfloat16)
    grad_full = lax.all_gather(grad_tri, "col", axis=1, tiled=True)
    grad_slab = grad_full
    grad_left = jnp.einsum(
        "ijh,jkh->ikh",
        grad_slab,
        lax.all_gather(right_act, "row", axis=0, tiled=True),
        preferred_element_type=jnp.float32,
    )
    grad_slab = grad_full
    grad_right = lax.psum_scatter(
        jnp.einsum("ijh,ikh->jkh", grad_slab, left_act, preferred_element_type=jnp.float32).astype(
            jnp.bfloat16
        ),
        "row",
        scatter_dimension=0,
        tiled=True,
    ).astype(jnp.float32)
    grad_pa, grad_ga = gate_back(grad_left, projections[0], projections[1], keep_mask)
    grad_pb, grad_gb = gate_back(grad_right, projections[2], projections[3], keep_mask)
    grads = jnp.stack([grad_pa, grad_ga, grad_pb, grad_gb, grad_gate_out]).reshape(
        5, tile_rows * tile_cols, channels
    )
    grad_normed = jnp.einsum("spd,scd->pc", grads, weights[:5], preferred_element_type=jnp.float32)
    grad_normed = grad_normed.reshape(tile_rows, tile_cols, channels)
    pair_grad = norm_back(grad_normed * in_gain, z_hat, z_inverse).astype(jnp.bfloat16)
    local_in = jnp.einsum("pc,spd->scd", flat_norm, grads, preferred_element_type=jnp.float32)
    local_out = jnp.dot(flat_out.T, flat_lin, preferred_element_type=jnp.float32)
    local_grads = jnp.concatenate([local_in, local_out[None]], axis=0) / residues
    weight_grad = lax.psum(local_grads, ("row", "col"))
    return (update, pair_grad, weight_grad)


def pack_kernel(act_hbm, mask_hbm, cot_hbm, gain_hbm, out_ref, act_ref, mask_ref, gain_ref, sems):
    tile_rows, tile_cols, channels = act_ref.shape
    pairs = tile_rows * tile_cols
    head = out_ref.shape[0] - pairs
    pack_copies = [
        pltpu.make_async_copy(act_hbm, act_ref, sems.at[0]),
        pltpu.make_async_copy(gain_hbm, gain_ref, sems.at[1]),
        pltpu.make_async_copy(mask_hbm, mask_ref, sems.at[2]),
        pltpu.make_async_copy(cot_hbm, out_ref.at[head : head + pairs], sems.at[3]),
    ]
    for copy in pack_copies:
        copy.start()
    for copy in pack_copies:
        copy.wait()
    z_hat, _ = normalize(act_ref[...].astype(jnp.float32).reshape(pairs, channels))
    out_ref[0:pairs] = (z_hat * gain_ref[...]).astype(jnp.bfloat16)
    keep = mask_ref[...].astype(jnp.float32)
    wide = jnp.concatenate([keep, jnp.zeros((tile_rows, channels - tile_cols), jnp.float32)], axis=1)
    tall = jnp.concatenate([wide, jnp.zeros((channels - tile_rows, channels), jnp.float32)], axis=0)
    out_ref[pairs:head] = tall.T[0 : head - pairs].astype(jnp.bfloat16)


def copy_kernel(in_ref, out_ref):
    out_ref[...] = in_ref[...]


def join_kernel(own_ref, twin_ref, out_ref):
    tile = SUB * SUB
    refs = (own_ref, twin_ref)
    for at, ref in enumerate(refs):
        out_ref[at * tile : (at + 1) * tile] = ref[0:tile]
        spot = 2 * tile + 2 * SUB + at * tile
        out_ref[spot : spot + tile] = ref[tile + 2 * SUB :]
    masks = [ref[tile : tile + 2 * SUB].astype(jnp.float32)[0:SUB] for ref in refs]
    out_ref[2 * tile : 2 * tile + 2 * SUB] = jnp.concatenate(masks, axis=0).astype(jnp.bfloat16)


def normed_rows(ref, sub):
    return ref[sub * SUB * SUB : (sub + 1) * SUB * SUB]


def mask_rows(ref, sub):
    at = ref.shape[0] // 2 // (SUB * SUB) * SUB * SUB
    return ref[at : at + 2 * SUB].astype(jnp.float32)[sub * SUB : (sub + 1) * SUB]


def cot_rows(ref, sub):
    at = ref.shape[0] // 2 // (SUB * SUB) * SUB * SUB + 2 * SUB
    return ref[at + sub * SUB * SUB : at + (sub + 1) * SUB * SUB]


def chip_rows(rows_of, refs, core, direct_on):
    if direct_on is None:
        return rows_of(refs[min(core, len(refs) - 1)], core if len(refs) == 1 else 0)
    here = lax.axis_index("col") % 2 == direct_on
    return jnp.where(here, rows_of(refs[0], core), rows_of(refs[1], 1 - core))


def split_chips(refs, chips):
    split, at = [], 0
    for width, direct_on in chips:
        split.append((refs[at : at + width], direct_on))
        at += width
    return split


def doubled(top, bottom):
    return jnp.concatenate([top, bottom], axis=0).astype(jnp.bfloat16)


def triangle(blocks, groups, steps, vectors_at, factors_at, start_at, store_at, beside=None):
    def block(a, _):
        if beside is not None:
            beside(a)
        def step(q, totals):
            totals = list(totals)
            vectors = vectors_at(q)
            factors = factors_at(a, q)
            rows = [
                [doubled(vectors(g, inner), vectors(g + 1, inner)) for g in range(0, groups, 2)]
                for inner in range(SUB)
            ]
            for lane in range(SUB):
                chains = [[None, None] for _ in range(groups // 2)]
                for inner in range(SUB):
                    factor = factors(lane, inner)
                    factor = doubled(factor, factor)
                    for g in range(groups // 2):
                        term = factor * rows[inner][g]
                        chain = chains[g][inner % 2]
                        chains[g][inner % 2] = term if chain is None else chain + term
                for g in range(groups // 2):
                    wide = (chains[g][0] + chains[g][1]).astype(jnp.float32)
                    at = lane * groups + 2 * g
                    totals[at] = totals[at] + wide[0:SUB]
                    totals[at + 1] = totals[at + 1] + wide[SUB:]
            return tuple(totals)

        totals = tuple(start_at(a, g, lane) for lane in range(SUB) for g in range(groups))
        if steps > 4:
            totals = lax.fori_loop(0, steps, step, totals)
        else:
            for q in range(steps):
                totals = step(q, totals)
        for g in range(groups):
            store_at(a, g, [totals[lane * groups + g] for lane in range(SUB)])
        return 0

    lax.fori_loop(0, blocks, block, 0)


def spread(ref, row):
    return jnp.broadcast_to(ref[pl.ds(row, 1), :], (SUB, ref.shape[-1]))


def line(ref, row):
    return ref[pl.ds(pl.multiple_of(row, SUB), SUB), :]


def columns_kernel(n_row, n_col, side_x, chips, crop_ref, weights_ref, *refs):
    count = sum(width for width, _ in chips)
    chip_list, refs = split_chips(refs[:count], chips), refs[count:]
    own_ref = None
    if side_x == 0:
        act_ref, in_gain_ref, out_gain_ref, *refs, own_ref, gains_ref = refs
        z_hat, z_inverse = normalize(act_ref[...].astype(jnp.float32).reshape(own_ref.shape[1:]))
        own_ref[0] = z_hat
        own_ref[1] = jnp.broadcast_to(z_inverse, z_hat.shape)
        gains_ref[0:1] = in_gain_ref[...]
        gains_ref[1:2] = out_gain_ref[...]
    else:
        gains_ref, *refs = refs
    tri_in, (tri_ref, flip_ref, left_ref, right_ref, side_ref, back_ref) = refs[:-6], refs[-6:]
    channels = weights_ref.shape[-1]
    tile = SUB * SUB
    size = n_row * tile
    bf16, f32 = jnp.bfloat16, jnp.float32
    row_me, col_me = lax.axis_index("row"), lax.axis_index("col")
    chip_list = [(chip, on, core, b) for core in range(2) for b, (chip, on) in enumerate(chip_list)]
    normed = jnp.concatenate([chip_rows(normed_rows, chip, core, on) for chip, on, core, _ in chip_list], axis=0)
    same = lax.broadcasted_iota(jnp.int32, (channels, channels), 0) == lax.broadcasted_iota(jnp.int32, (channels, channels), 1)
    identity = jnp.where(same, 1.0, 0.0).astype(bf16)

    def turned(rows):
        return lax.dot_general(identity, rows, (((1,), (1,)), ((), ())), preferred_element_type=f32).astype(bf16)

    def put(kind, rows):
        both = turned(rows)
        for core in range(2):
            flip_ref[kind, 2 * side_x + core] = both[:, core * size : (core + 1) * size]

    put(0, normed)
    crop = crop_ref[0]
    col_offset = lax.broadcasted_iota(jnp.int32, (SUB, channels), 0)
    row_offset = lax.broadcasted_iota(jnp.int32, (SUB, channels), 1)
    kept = []
    for chip, on, core, b in chip_list:
        keep = chip_rows(mask_rows, chip, core, on)
        rows_in = row_offset < crop - (row_me ^ b) * SUB
        cols_in = col_offset < crop - (col_me ^ (2 * side_x + core)) * SUB
        keep = jnp.where(rows_in & cols_in, keep, 0.0)
        kept += [jnp.broadcast_to(keep[:, at : at + 1], (SUB, channels)) for at in range(SUB)]
    kept = jnp.concatenate(kept, axis=0)
    for side, act_ref in enumerate((left_ref, right_ref)):
        pair = jnp.concatenate([weights_ref[2 * side], weights_ref[2 * side + 1]], axis=1)
        proj = jnp.dot(normed, pair, preferred_element_type=f32)
        gate = jax.nn.sigmoid(proj[:, channels:])
        masked = gate * kept
        act = masked * proj[:, :channels]
        act_ref[...] = act.astype(bf16).astype(f32)
        side_ref[2 * side] = masked
        side_ref[2 * side + 1] = act * (1.0 - gate)
    out_gate = jax.nn.sigmoid(jnp.dot(normed, weights_ref[4], preferred_element_type=f32))
    if own_ref is not None:
        own_ref[2] = out_gate[0:tile]
    cot = jnp.concatenate([chip_rows(cot_rows, chip, core, on) for chip, on, core, _ in chip_list], axis=0)
    grad = cot.astype(f32) * out_gate
    grad_lin = grad.astype(bf16)
    put(1, grad_lin)
    back_ref[0] = grad * (1.0 - out_gate)
    back = lax.dot_general(grad_lin, weights_ref[5], (((1,), (1,)), ((), ())), preferred_element_type=f32)
    back = back * gains_ref[1:2]
    back_ref[1] = back - jnp.mean(back, axis=-1, keepdims=True)
    turn = row_me ^ col_me

    def flipped(q):
        firsts = [q * size + (turn ^ g) * tile for g in range(n_col)]
        return lambda g, inner: right_ref[pl.ds(firsts[g] + inner, SUB, stride=SUB), :]

    def along(a, q):
        return lambda lane, inner: spread(left_ref, q * size + a * tile + lane * SUB + inner)

    def start(a, g, lane):
        if len(tri_in) == 0:
            return jnp.zeros((SUB, channels), f32)
        return line(tri_in[0], g * size + a * tile + lane * SUB)

    def store(a, g, values):
        for lane in range(SUB):
            tri_ref[pl.ds(pl.multiple_of(g * size + a * tile + lane * SUB, SUB), SUB), :] = values[lane]

    triangle(n_row, n_col, 2, flipped, along, start, store)


def rest_kernel(n_row, n_col, weights_ref, own_ref, gains_ref, tri_ref, flip_ref, *refs):
    groups = [refs[at * 4 : at * 4 + 4] for at in range(n_col // 2)]
    update_ref, pair_grad_ref, weight_grad_ref, back_ref, hat_ref, d_ref, sum_ref = refs[4 * (n_col // 2) :]
    channels = tri_ref.shape[-1]
    tile = SUB * SUB
    size = n_row * tile
    columns = []
    for col in range(n_col):
        own = pl.ds(col % 2 * size, size)
        left, right, side, backs = groups[col // 2]
        columns.append((left.at[own], right.at[own], side.at[:, own], backs.at[:, own]))
    residues = n_row * SUB
    bf16, f32 = jnp.bfloat16, jnp.float32
    turn = lax.axis_index("row") ^ lax.axis_index("col")
    out_gain = gains_ref[1:2]
    for col, (_, _, _, backs_ref) in enumerate(columns):
        rows = slice(col * size, (col + 1) * size)
        x_hat, inverse = normalize(tri_ref[rows, :])
        normed_out = (x_hat * out_gain).astype(bf16)
        hat_ref[rows, :] = normed_out
        lin = jnp.dot(normed_out, weights_ref[5], preferred_element_type=f32)
        if col == 0:
            update_ref[...] = (own_ref[2] * lin[0:tile]).astype(bf16).reshape(update_ref.shape)
        d_ref[rows, 4 * channels : 5 * channels] = (backs_ref[0] * lin).astype(bf16)
        back = backs_ref[1]
        second = jnp.mean(back * x_hat, axis=-1, keepdims=True)
        back_ref[rows, :] = ((back - x_hat * second) * inverse).astype(bf16).astype(f32)

    lefts, rights, sides = [[column[at] for column in columns] for at in (0, 1, 2)]

    def zero(a, g, lane):
        return jnp.zeros((SUB, channels), f32)

    def store(side):
        def put(a, g, values):
            for lane in range(0, SUB, 2):
                at = pl.multiple_of(a * tile + lane * SUB, 2 * SUB)
                both = jnp.concatenate(values[lane : lane + 2], axis=0)
                rows = pl.ds(pl.multiple_of(g * size + at, 2 * SUB), 2 * SUB)
                for kind in range(2):
                    spot = (2 * side + kind) * channels
                    scaled = both * sides[g][2 * side + kind, pl.ds(at, 2 * SUB), :]
                    d_ref[rows, spot : spot + channels] = scaled.astype(bf16)
        return put

    def by_right(q):
        return lambda g, inner: line(rights[g], (q ^ turn) * tile + inner * SUB)

    def by_left(q):
        return lambda g, inner: line(lefts[g], q * tile + inner * SUB)

    def along(a, q):
        return lambda lane, inner: spread(back_ref, q * size + a * tile + lane * SUB + inner)

    def down(a, q):
        return lambda lane, inner: spread(back_ref, (a ^ turn) * size + q * tile + inner * SUB + lane)

    def chunk(ref, a, first, last):
        return ref[pl.ds(pl.multiple_of(a * size, size), size), first * channels : last * channels]

    def early_sums(a):
        sum_ref[:, 0:channels] += jnp.dot(flip_ref[0, a], chunk(d_ref, a, 4, 5), preferred_element_type=f32)
        sum_ref[:, channels : 2 * channels] += jnp.dot(flip_ref[1, a], chunk(hat_ref, a, 0, 1), preferred_element_type=f32)

    def left_sums(a):
        sum_ref[:, 2 * channels :] += jnp.dot(flip_ref[0, a], chunk(d_ref, a, 0, 2), preferred_element_type=f32)

    sum_ref[...] = jnp.zeros(sum_ref.shape, f32)
    triangle(n_row, n_col, n_col, by_right, along, zero, store(0), early_sums)
    triangle(n_row, n_col, n_row, by_left, down, zero, store(1), left_sums)

    scale = 1.0 / residues
    flipped = jnp.concatenate([flip_ref[0, col] for col in range(n_col)], axis=1)
    right_sums = jnp.dot(flipped, d_ref[:, 2 * channels : 4 * channels], preferred_element_type=f32)
    for s in range(2):
        part = slice(s * channels, (s + 1) * channels)
        weight_grad_ref[s] = sum_ref[:, (2 + s) * channels : (3 + s) * channels] * scale
        weight_grad_ref[2 + s] = right_sums[:, part] * scale
    weight_grad_ref[4] = sum_ref[:, 0:channels] * scale
    weight_grad_ref[5] = sum_ref[:, channels : 2 * channels].T * scale
    total = jnp.zeros((tile, channels), f32)
    for s in range(5):
        total = total + lax.dot_general(
            d_ref[0:tile, s * channels : (s + 1) * channels], weights_ref[s],
            (((1,), (1,)), ((), ())), preferred_element_type=f32,
        )
    grad = norm_back(total * gains_ref[0:1], own_ref[0], own_ref[1])
    pair_grad_ref[...] = grad.astype(bf16).reshape(pair_grad_ref.shape)


def flip(block, n_row, n_col, even, odd):
    pairs = []
    for row in range(n_row):
        for col in range(n_col):
            shift = odd if col % 2 else even
            pairs.append((row * n_col + col, (row ^ shift[0]) * n_col + (col ^ shift[1])))
    return lax.ppermute(block, ("row", "col"), pairs)


def gathered_body(n_row, n_col, pair_act, pair_mask, crop_length, weights, in_gain, out_gain, cotangent):
    tile_rows, tile_cols, channels = pair_act.shape
    tile = tile_rows * tile_cols
    size = n_row * tile
    pairs = size * n_col
    head = tile + 2 * SUB
    f32, bf16 = jnp.float32, jnp.bfloat16
    vmem = pl.BlockSpec(memory_space=pltpu.VMEM)
    smem = pl.BlockSpec(memory_space=pltpu.SMEM)
    hbm = pl.BlockSpec(memory_space=pltpu.HBM)
    in_gain, out_gain = in_gain.reshape(1, channels), out_gain.reshape(1, channels)

    def limit(mib):
        return pltpu.CompilerParams(vmem_limit_bytes=mib * 1024 * 1024)

    own = pl.pallas_call(
        pack_kernel,
        name="pack",
        out_shape=jax.ShapeDtypeStruct((head + tile, channels), bf16),
        in_specs=[hbm] * 4,
        out_specs=vmem,
        scratch_shapes=[
            pltpu.VMEM(pair_act.shape, pair_act.dtype),
            pltpu.VMEM(pair_mask.shape, jnp.int32),
            pltpu.VMEM((1, channels), f32),
            pltpu.SemaphoreType.DMA((4,)),
        ],
        compiler_params=limit(60),
    )(pair_act, pair_mask, cotangent.reshape(tile, channels), in_gain)
    crop_length, own = lax.optimization_barrier((crop_length, own))

    def move(block, even, odd):
        return flip(block, n_row, n_col, even, odd)

    def other(block):
        return move(block, (0, 1), (0, 1))

    held = pl.pallas_call(
        copy_kernel,
        name="hold",
        out_shape=jax.ShapeDtypeStruct(own.shape, bf16),
        in_specs=[vmem],
        out_specs=vmem,
        compiler_params=limit(2),
        cost_estimate=pl.CostEstimate(flops=100_000_000, bytes_accessed=1_000_000, transcendentals=0),
    )(own)
    both = pl.pallas_call(
        join_kernel,
        name="join",
        out_shape=jax.ShapeDtypeStruct((2 * own.shape[0] - 2 * SUB, channels), bf16),
        in_specs=[vmem] * 2,
        out_specs=vmem,
        compiler_params=limit(2),
    )(held, other(own))
    straight = move(own, (3, 0), (3, 0))
    first = move(both, (2, 0), (1, 0))
    second = move(both, (0, 2), (2, 2))
    third = move(both, (1, 2), (3, 2))
    straight, first, second, third = [(block, other(block)) for block in (straight, first, second, third)]
    chips = (((1, None), (2, 1), (2, 0), (2, None)), ((2, 0), (2, 0), (2, 1), (2, 1)))
    sources = ((both, *first, *first, *straight), (*second, *third, *second, *third))

    tri, parts, extra = [], [], []
    for side_x in range(n_col // 2):
        more = (pair_act, in_gain, out_gain) if side_x == 0 else (extra[1], *tri)
        more_shapes = () if side_x > 0 else (
            jax.ShapeDtypeStruct((3, tile, channels), f32),
            jax.ShapeDtypeStruct((SUB, channels), f32),
        )
        last = 3 + len(sources[side_x])
        results = pl.pallas_call(
            functools.partial(columns_kernel, n_row, n_col, side_x, chips[side_x]),
            name=f"columns_{side_x}",
            out_shape=(
                jax.ShapeDtypeStruct((pairs, channels), f32),
                jax.ShapeDtypeStruct((2, n_col, channels, size), bf16),
                jax.ShapeDtypeStruct((2 * size, channels), f32),
                jax.ShapeDtypeStruct((2 * size, channels), f32),
                jax.ShapeDtypeStruct((4, 2 * size, channels), f32),
                jax.ShapeDtypeStruct((2, 2 * size, channels), f32),
                *more_shapes,
            ),
            in_specs=[smem] + [vmem] * (1 + len(sources[side_x]) + len(more)),
            out_specs=(vmem,) * (6 + len(more_shapes)),
            input_output_aliases={last: 0, last + 1: 1} if side_x > 0 else {},
            compiler_params=limit(12),
            cost_estimate=pl.CostEstimate(flops=800_000_000, bytes_accessed=1_000_000, transcendentals=0),
        )(crop_length, weights, *sources[side_x], *more)
        tri = results[:2]
        parts += results[2:6]
        extra += results[6:]

    return pl.pallas_call(
        functools.partial(rest_kernel, n_row, n_col),
        name="rest",
        out_shape=(
            jax.ShapeDtypeStruct(pair_act.shape, bf16),
            jax.ShapeDtypeStruct(pair_act.shape, bf16),
            jax.ShapeDtypeStruct(weights.shape, f32),
        ),
        in_specs=[vmem] * (5 + len(parts)),
        out_specs=(vmem, vmem, vmem),
        scratch_shapes=[
            pltpu.VMEM((pairs, channels), f32),
            pltpu.VMEM((pairs, channels), bf16),
            pltpu.VMEM((pairs, 5 * channels), bf16),
            pltpu.VMEM((channels, 4 * channels), f32),
        ],
        compiler_params=limit(16),
    )(weights, *extra, *tri, *parts)


def body(n_row, n_col, pair_act, *others):
    tile_rows, tile_cols, channels = pair_act.shape
    pairs = tile_rows * n_row * tile_cols * n_col
    small = pairs * channels * 4 <= 1024 * 1024 and channels == 128
    square = n_row == 4 and n_col == 4 and tile_rows == SUB and tile_cols == SUB
    if small and square:
        return gathered_body(n_row, n_col, pair_act, *others)
    return spread_body(pair_act, *others)


def solution(mesh):
    return jax.shard_map(
        functools.partial(body, mesh.shape["row"], mesh.shape["col"]),
        mesh=mesh,
        in_specs=(
            P(("parts", "row"), "col", None),
            P(("parts", "row"), "col"),
            P("parts"),
            P(),
            P(),
            P(),
            P(("parts", "row"), "col", None),
        ),
        out_specs=(
            P(("parts", "row"), "col", None),
            P(("parts", "row"), "col", None),
            P("parts", None, None),
        ),
        check_vma=False,
    )
```

```python
import functools

import jax
import jax.numpy as jnp
from jax import lax
from jax.experimental import pallas as pl
from jax.experimental.pallas import tpu as pltpu
from jax.sharding import PartitionSpec as P

SUB = 8
EPS = 1e-05


def normalize(values):
    average = jnp.mean(values, axis=-1, keepdims=True)
    centered = values - average
    inverse = lax.rsqrt(jnp.mean(centered * centered, axis=-1, keepdims=True) + 1e-05)
    return (centered * inverse, inverse)


def norm_back(grad_hat, values_hat, inverse):
    first = jnp.mean(grad_hat, axis=-1, keepdims=True)
    second = jnp.mean(grad_hat * values_hat, axis=-1, keepdims=True)
    return (grad_hat - first - values_hat * second) * inverse


def gate_back(grad_act, proj_value, proj_gate, keep_mask):
    gate_sig = jax.nn.sigmoid(proj_gate)
    masked = grad_act * keep_mask
    grad_value = (masked * gate_sig).astype(jnp.bfloat16)
    grad_gate = (masked * proj_value * gate_sig * (1.0 - gate_sig)).astype(jnp.bfloat16)
    return (grad_value, grad_gate)


def spread_body(pair_act, pair_mask, crop_length, weights, in_gain, out_gain, cotangent):
    tile_rows, tile_cols, channels = pair_act.shape
    residues = tile_rows * lax.axis_size("row")
    row_pos = lax.axis_index("row") * tile_rows + jnp.arange(tile_rows, dtype=jnp.int32)
    col_pos = lax.axis_index("col") * tile_cols + jnp.arange(tile_cols, dtype=jnp.int32)
    row_in = (row_pos < crop_length[0]).astype(jnp.float32)
    col_in = (col_pos < crop_length[0]).astype(jnp.float32)
    keep_mask = (pair_mask.astype(jnp.float32) * row_in[:, None] * col_in[None, :])[:, :, None]
    z_hat, z_inverse = normalize(pair_act.astype(jnp.float32))
    normed = (z_hat * in_gain).astype(jnp.bfloat16)
    flat_norm = normed.reshape(tile_rows * tile_cols, channels)
    projections = jnp.einsum(
        "pc,scd->spd", flat_norm, weights[:5], preferred_element_type=jnp.float32
    )
    projections = projections.reshape(5, tile_rows, tile_cols, channels)
    left_act = (jax.nn.sigmoid(projections[1]) * projections[0] * keep_mask).astype(jnp.bfloat16)
    right_act = (jax.nn.sigmoid(projections[3]) * projections[2] * keep_mask).astype(jnp.bfloat16)
    partial_value = jnp.einsum(
        "ikh,jkh->ijh",
        left_act,
        lax.all_gather(right_act, "row", axis=0, tiled=True),
        preferred_element_type=jnp.float32,
    )
    tri_sum = lax.psum_scatter(
        partial_value.astype(jnp.bfloat16), "col", scatter_dimension=1, tiled=True
    ).astype(jnp.float32)
    x_hat, x_inverse = normalize(tri_sum)
    normed_out = (x_hat * out_gain).astype(jnp.bfloat16)
    flat_out = normed_out.reshape(tile_rows * tile_cols, channels)
    update_lin = jnp.dot(flat_out, weights[5], preferred_element_type=jnp.float32)
    update_lin = update_lin.reshape(tile_rows, tile_cols, channels)
    out_gate = jax.nn.sigmoid(projections[4])
    update = (out_gate * update_lin).astype(jnp.bfloat16)
    cot_value = cotangent.astype(jnp.float32)
    grad_lin = (cot_value * out_gate).astype(jnp.bfloat16)
    grad_gate_out = (cot_value * update_lin * out_gate * (1.0 - out_gate)).astype(jnp.bfloat16)
    flat_lin = grad_lin.reshape(tile_rows * tile_cols, channels)
    grad_norm_out = jnp.einsum(
        "pd,cd->pc", flat_lin, weights[5], preferred_element_type=jnp.float32
    )
    grad_norm_out = grad_norm_out.reshape(tile_rows, tile_cols, channels)
    grad_tri = norm_back(grad_norm_out * out_gain, x_hat, x_inverse).astype(jnp.bfloat16)
    grad_full = lax.all_gather(grad_tri, "col", axis=1, tiled=True)
    grad_slab = grad_full
    grad_left = jnp.einsum(
        "ijh,jkh->ikh",
        grad_slab,
        lax.all_gather(right_act, "row", axis=0, tiled=True),
        preferred_element_type=jnp.float32,
    )
    grad_slab = grad_full
    grad_right = lax.psum_scatter(
        jnp.einsum("ijh,ikh->jkh", grad_slab, left_act, preferred_element_type=jnp.float32).astype(
            jnp.bfloat16
        ),
        "row",
        scatter_dimension=0,
        tiled=True,
    ).astype(jnp.float32)
    grad_pa, grad_ga = gate_back(grad_left, projections[0], projections[1], keep_mask)
    grad_pb, grad_gb = gate_back(grad_right, projections[2], projections[3], keep_mask)
    grads = jnp.stack([grad_pa, grad_ga, grad_pb, grad_gb, grad_gate_out]).reshape(
        5, tile_rows * tile_cols, channels
    )
    grad_normed = jnp.einsum("spd,scd->pc", grads, weights[:5], preferred_element_type=jnp.float32)
    grad_normed = grad_normed.reshape(tile_rows, tile_cols, channels)
    pair_grad = norm_back(grad_normed * in_gain, z_hat, z_inverse).astype(jnp.bfloat16)
    local_in = jnp.einsum("pc,spd->scd", flat_norm, grads, preferred_element_type=jnp.float32)
    local_out = jnp.dot(flat_out.T, flat_lin, preferred_element_type=jnp.float32)
    local_grads = jnp.concatenate([local_in, local_out[None]], axis=0) / residues
    weight_grad = lax.psum(local_grads, ("row", "col"))
    return (update, pair_grad, weight_grad)


def pack_kernel(act_hbm, mask_hbm, cot_hbm, gain_hbm, out_ref, act_ref, mask_ref, gain_ref, sems):
    tile_rows, tile_cols, channels = act_ref.shape
    pairs = tile_rows * tile_cols
    head = out_ref.shape[0] - pairs
    pack_copies = [
        pltpu.make_async_copy(act_hbm, act_ref, sems.at[0]),
        pltpu.make_async_copy(gain_hbm, gain_ref, sems.at[1]),
        pltpu.make_async_copy(mask_hbm, mask_ref, sems.at[2]),
        pltpu.make_async_copy(cot_hbm, out_ref.at[head : head + pairs], sems.at[3]),
    ]
    for copy in pack_copies:
        copy.start()
    for copy in pack_copies:
        copy.wait()
    z_hat, _ = normalize(act_ref[...].astype(jnp.float32).reshape(pairs, channels))
    out_ref[0:pairs] = (z_hat * gain_ref[...]).astype(jnp.bfloat16)
    keep = mask_ref[...].astype(jnp.float32)
    wide = jnp.concatenate([keep, jnp.zeros((tile_rows, channels - tile_cols), jnp.float32)], axis=1)
    tall = jnp.concatenate([wide, jnp.zeros((channels - tile_rows, channels), jnp.float32)], axis=0)
    out_ref[pairs:head] = tall.T[0 : head - pairs].astype(jnp.bfloat16)


def copy_kernel(in_ref, out_ref):
    out_ref[...] = in_ref[...]


def join_kernel(own_ref, twin_ref, out_ref):
    tile = SUB * SUB
    refs = (own_ref, twin_ref)
    for at, ref in enumerate(refs):
        out_ref[at * tile : (at + 1) * tile] = ref[0:tile]
        spot = 2 * tile + 2 * SUB + at * tile
        out_ref[spot : spot + tile] = ref[tile + 2 * SUB :]
    masks = [ref[tile : tile + 2 * SUB].astype(jnp.float32)[0:SUB] for ref in refs]
    out_ref[2 * tile : 2 * tile + 2 * SUB] = jnp.concatenate(masks, axis=0).astype(jnp.bfloat16)


def normed_rows(ref, sub):
    return ref[sub * SUB * SUB : (sub + 1) * SUB * SUB]


def mask_rows(ref, sub):
    at = ref.shape[0] // 2 // (SUB * SUB) * SUB * SUB
    return ref[at : at + 2 * SUB].astype(jnp.float32)[sub * SUB : (sub + 1) * SUB]


def cot_rows(ref, sub):
    at = ref.shape[0] // 2 // (SUB * SUB) * SUB * SUB + 2 * SUB
    return ref[at + sub * SUB * SUB : at + (sub + 1) * SUB * SUB]


def chip_rows(rows_of, refs, core, direct_on):
    if direct_on is None:
        return rows_of(refs[min(core, len(refs) - 1)], core if len(refs) == 1 else 0)
    here = lax.axis_index("col") % 2 == direct_on
    return jnp.where(here, rows_of(refs[0], core), rows_of(refs[1], 1 - core))


def split_chips(refs, chips):
    split, at = [], 0
    for width, direct_on in chips:
        split.append((refs[at : at + width], direct_on))
        at += width
    return split


def doubled(top, bottom):
    return jnp.concatenate([top, bottom], axis=0).astype(jnp.bfloat16)


def triangle(blocks, groups, steps, vectors_at, factors_at, start_at, store_at, beside=None):
    def block(a, _):
        if beside is not None:
            beside(a)
        def step(q, totals):
            totals = list(totals)
            vectors = vectors_at(q)
            factors = factors_at(a, q)
            rows = [
                [doubled(vectors(g, inner), vectors(g + 1, inner)) for g in range(0, groups, 2)]
                for inner in range(SUB)
            ]
            for lane in range(SUB):
                chains = [[None, None] for _ in range(groups // 2)]
                for inner in range(SUB):
                    factor = factors(lane, inner)
                    factor = doubled(factor, factor)
                    for g in range(groups // 2):
                        term = factor * rows[inner][g]
                        chain = chains[g][inner % 2]
                        chains[g][inner % 2] = term if chain is None else chain + term
                for g in range(groups // 2):
                    wide = (chains[g][0] + chains[g][1]).astype(jnp.float32)
                    at = lane * groups + 2 * g
                    totals[at] = totals[at] + wide[0:SUB]
                    totals[at + 1] = totals[at + 1] + wide[SUB:]
            return tuple(totals)

        totals = tuple(start_at(a, g, lane) for lane in range(SUB) for g in range(groups))
        if steps > 4:
            totals = lax.fori_loop(0, steps, step, totals)
        else:
            for q in range(steps):
                totals = step(q, totals)
        for g in range(groups):
            store_at(a, g, [totals[lane * groups + g] for lane in range(SUB)])
        return 0

    lax.fori_loop(0, blocks, block, 0)


def spread(ref, row):
    return jnp.broadcast_to(ref[pl.ds(row, 1), :], (SUB, ref.shape[-1]))


def line(ref, row):
    return ref[pl.ds(pl.multiple_of(row, SUB), SUB), :]


def columns_kernel(n_row, n_col, side_x, chips, crop_ref, weights_ref, *refs):
    count = sum(width for width, _ in chips)
    chip_list, refs = split_chips(refs[:count], chips), refs[count:]
    own_ref = None
    if side_x == 0:
        act_ref, in_gain_ref, out_gain_ref, *refs, own_ref, gains_ref = refs
        z_hat, z_inverse = normalize(act_ref[...].astype(jnp.float32).reshape(own_ref.shape[1:]))
        own_ref[0] = z_hat
        own_ref[1] = jnp.broadcast_to(z_inverse, z_hat.shape)
        gains_ref[0:1] = in_gain_ref[...]
        gains_ref[1:2] = out_gain_ref[...]
    else:
        gains_ref, *refs = refs
    tri_in, (tri_ref, flip_ref, left_ref, right_ref, side_ref, back_ref) = refs[:-6], refs[-6:]
    channels = weights_ref.shape[-1]
    tile = SUB * SUB
    size = n_row * tile
    bf16, f32 = jnp.bfloat16, jnp.float32
    row_me, col_me = lax.axis_index("row"), lax.axis_index("col")
    chip_list = [(chip, on, core, b) for core in range(2) for b, (chip, on) in enumerate(chip_list)]
    normed = jnp.concatenate([chip_rows(normed_rows, chip, core, on) for chip, on, core, _ in chip_list], axis=0)
    same = lax.broadcasted_iota(jnp.int32, (channels, channels), 0) == lax.broadcasted_iota(jnp.int32, (channels, channels), 1)
    identity = jnp.where(same, 1.0, 0.0).astype(bf16)

    def turned(rows):
        return lax.dot_general(identity, rows, (((1,), (1,)), ((), ())), preferred_element_type=f32).astype(bf16)

    def put(kind, rows):
        both = turned(rows)
        for core in range(2):
            flip_ref[kind, 2 * side_x + core] = both[:, core * size : (core + 1) * size]

    put(0, normed)
    crop = crop_ref[0]
    col_offset = lax.broadcasted_iota(jnp.int32, (SUB, channels), 0)
    row_offset = lax.broadcasted_iota(jnp.int32, (SUB, channels), 1)
    kept = []
    for chip, on, core, b in chip_list:
        keep = chip_rows(mask_rows, chip, core, on)
        rows_in = row_offset < crop - (row_me ^ b) * SUB
        cols_in = col_offset < crop - (col_me ^ (2 * side_x + core)) * SUB
        keep = jnp.where(rows_in & cols_in, keep, 0.0)
        kept += [jnp.broadcast_to(keep[:, at : at + 1], (SUB, channels)) for at in range(SUB)]
    kept = jnp.concatenate(kept, axis=0)
    for side, act_ref in enumerate((left_ref, right_ref)):
        pair = jnp.concatenate([weights_ref[2 * side], weights_ref[2 * side + 1]], axis=1)
        proj = jnp.dot(normed, pair, preferred_element_type=f32)
        gate = jax.nn.sigmoid(proj[:, channels:])
        masked = gate * kept
        act = masked * proj[:, :channels]
        act_ref[...] = act.astype(bf16).astype(f32)
        side_ref[2 * side] = masked
        side_ref[2 * side + 1] = act * (1.0 - gate)
    out_gate = jax.nn.sigmoid(jnp.dot(normed, weights_ref[4], preferred_element_type=f32))
    if own_ref is not None:
        own_ref[2] = out_gate[0:tile]
    cot = jnp.concatenate([chip_rows(cot_rows, chip, core, on) for chip, on, core, _ in chip_list], axis=0)
    grad = cot.astype(f32) * out_gate
    grad_lin = grad.astype(bf16)
    put(1, grad_lin)
    back_ref[0] = grad * (1.0 - out_gate)
    back = lax.dot_general(grad_lin, weights_ref[5], (((1,), (1,)), ((), ())), preferred_element_type=f32)
    back = back * gains_ref[1:2]
    back_ref[1] = back - jnp.mean(back, axis=-1, keepdims=True)
    turn = row_me ^ col_me

    def flipped(q):
        firsts = [q * size + (turn ^ g) * tile for g in range(n_col)]
        return lambda g, inner: right_ref[pl.ds(firsts[g] + inner, SUB, stride=SUB), :]

    def along(a, q):
        return lambda lane, inner: spread(left_ref, q * size + a * tile + lane * SUB + inner)

    def start(a, g, lane):
        if len(tri_in) == 0:
            return jnp.zeros((SUB, channels), f32)
        return line(tri_in[0], g * size + a * tile + lane * SUB)

    def store(a, g, values):
        for lane in range(SUB):
            tri_ref[pl.ds(pl.multiple_of(g * size + a * tile + lane * SUB, SUB), SUB), :] = values[lane]

    triangle(n_row, n_col, 2, flipped, along, start, store)


def rest_kernel(n_row, n_col, weights_ref, own_ref, gains_ref, tri_ref, flip_ref, *refs):
    groups = [refs[at * 4 : at * 4 + 4] for at in range(n_col // 2)]
    outs, (back_ref, hat_ref, d_ref, sum_ref, update_ref, pair_grad_ref, weight_grad_ref, sems) = (
        refs[4 * (n_col // 2) : 4 * (n_col // 2) + 3],
        refs[4 * (n_col // 2) + 3 :],
    )
    copies = [
        pltpu.make_async_copy(update_ref, outs[0], sems.at[0]),
        pltpu.make_async_copy(pair_grad_ref, outs[1], sems.at[1]),
    ]
    copies += [
        pltpu.make_async_copy(weight_grad_ref.at[at : at + 2], outs[2].at[at : at + 2], sems.at[2 + at // 2])
        for at in range(0, 6, 2)
    ]
    channels = tri_ref.shape[-1]
    tile = SUB * SUB
    size = n_row * tile
    columns = []
    for col in range(n_col):
        own = pl.ds(col % 2 * size, size)
        left, right, side, backs = groups[col // 2]
        columns.append((left.at[own], right.at[own], side.at[:, own], backs.at[:, own]))
    residues = n_row * SUB
    bf16, f32 = jnp.bfloat16, jnp.float32
    turn = lax.axis_index("row") ^ lax.axis_index("col")
    out_gain = gains_ref[1:2]
    for col, (_, _, _, backs_ref) in enumerate(columns):
        rows = slice(col * size, (col + 1) * size)
        x_hat, inverse = normalize(tri_ref[rows, :])
        normed_out = (x_hat * out_gain).astype(bf16)
        hat_ref[rows, :] = normed_out
        lin = jnp.dot(normed_out, weights_ref[5], preferred_element_type=f32)
        if col == 0:
            update_ref[...] = (own_ref[2] * lin[0:tile]).astype(bf16).reshape(update_ref.shape)
            copies[0].start()
        d_ref[rows, 4 * channels : 5 * channels] = (backs_ref[0] * lin).astype(bf16)
        back = backs_ref[1]
        second = jnp.mean(back * x_hat, axis=-1, keepdims=True)
        back_ref[rows, :] = ((back - x_hat * second) * inverse).astype(bf16).astype(f32)

    lefts, rights, sides = [[column[at] for column in columns] for at in (0, 1, 2)]

    def zero(a, g, lane):
        return jnp.zeros((SUB, channels), f32)

    def store(side):
        def put(a, g, values):
            for lane in range(0, SUB, 2):
                at = pl.multiple_of(a * tile + lane * SUB, 2 * SUB)
                both = jnp.concatenate(values[lane : lane + 2], axis=0)
                rows = pl.ds(pl.multiple_of(g * size + at, 2 * SUB), 2 * SUB)
                for kind in range(2):
                    spot = (2 * side + kind) * channels
                    scaled = both * sides[g][2 * side + kind, pl.ds(at, 2 * SUB), :]
                    d_ref[rows, spot : spot + channels] = scaled.astype(bf16)
        return put

    def by_right(q):
        return lambda g, inner: line(rights[g], (q ^ turn) * tile + inner * SUB)

    def by_left(q):
        return lambda g, inner: line(lefts[g], q * tile + inner * SUB)

    def along(a, q):
        return lambda lane, inner: spread(back_ref, q * size + a * tile + lane * SUB + inner)

    def down(a, q):
        return lambda lane, inner: spread(back_ref, (a ^ turn) * size + q * tile + inner * SUB + lane)

    def chunk(ref, a, first, last):
        return ref[pl.ds(pl.multiple_of(a * size, size), size), first * channels : last * channels]

    def early_sums(a):
        sum_ref[:, 0:channels] += jnp.dot(flip_ref[0, a], chunk(d_ref, a, 4, 5), preferred_element_type=f32)
        sum_ref[:, channels : 2 * channels] += jnp.dot(flip_ref[1, a], chunk(hat_ref, a, 0, 1), preferred_element_type=f32)

    def left_sums(a):
        sum_ref[:, 2 * channels :] += jnp.dot(flip_ref[0, a], chunk(d_ref, a, 0, 2), preferred_element_type=f32)

    sum_ref[...] = jnp.zeros(sum_ref.shape, f32)
    scale = 1.0 / residues
    triangle(n_row, n_col, n_col, by_right, along, zero, store(0), early_sums)
    weight_grad_ref[4] = sum_ref[:, 0:channels] * scale
    weight_grad_ref[5] = sum_ref[:, channels : 2 * channels].T * scale
    copies[4].start()
    triangle(n_row, n_col, n_row, by_left, down, zero, store(1), left_sums)
    weight_grad_ref[0] = sum_ref[:, 2 * channels : 3 * channels] * scale
    weight_grad_ref[1] = sum_ref[:, 3 * channels :] * scale
    copies[2].start()
    wide = jnp.concatenate([weights_ref[s] for s in range(5)], axis=1)
    total = lax.dot_general(d_ref[0:tile], wide, (((1,), (1,)), ((), ())), preferred_element_type=f32)
    grad = norm_back(total * gains_ref[0:1], own_ref[0], own_ref[1])
    flipped = jnp.concatenate([flip_ref[0, col] for col in range(n_col)], axis=1)
    right_sums = jnp.dot(flipped, d_ref[:, 2 * channels : 4 * channels], preferred_element_type=f32) * scale
    pair_grad_ref[...] = grad.astype(bf16).reshape(pair_grad_ref.shape)
    weight_grad_ref[2] = right_sums[:, 0:channels]
    weight_grad_ref[3] = right_sums[:, channels:]
    copies[1].start()
    copies[3].start()
    for copy in copies:
        copy.wait()


def flip(block, n_row, n_col, even, odd):
    pairs = []
    for row in range(n_row):
        for col in range(n_col):
            shift = odd if col % 2 else even
            pairs.append((row * n_col + col, (row ^ shift[0]) * n_col + (col ^ shift[1])))
    return lax.ppermute(block, ("row", "col"), pairs)


def gathered_body(n_row, n_col, pair_act, pair_mask, crop_length, weights, in_gain, out_gain, cotangent):
    tile_rows, tile_cols, channels = pair_act.shape
    tile = tile_rows * tile_cols
    size = n_row * tile
    pairs = size * n_col
    head = tile + 2 * SUB
    f32, bf16 = jnp.float32, jnp.bfloat16
    vmem = pl.BlockSpec(memory_space=pltpu.VMEM)
    smem = pl.BlockSpec(memory_space=pltpu.SMEM)
    anywhere = pl.BlockSpec(memory_space=pl.ANY)
    hbm = pl.BlockSpec(memory_space=pltpu.HBM)
    in_gain, out_gain = in_gain.reshape(1, channels), out_gain.reshape(1, channels)

    def limit(mib):
        return pltpu.CompilerParams(vmem_limit_bytes=mib * 1024 * 1024)

    own = pl.pallas_call(
        pack_kernel,
        name="pack",
        out_shape=jax.ShapeDtypeStruct((head + tile, channels), bf16),
        in_specs=[hbm] * 4,
        out_specs=vmem,
        scratch_shapes=[
            pltpu.VMEM(pair_act.shape, pair_act.dtype),
            pltpu.VMEM(pair_mask.shape, jnp.int32),
            pltpu.VMEM((1, channels), f32),
            pltpu.SemaphoreType.DMA((4,)),
        ],
        compiler_params=limit(60),
    )(pair_act, pair_mask, cotangent.reshape(tile, channels), in_gain)
    crop_length, own = lax.optimization_barrier((crop_length, own))

    def move(block, even, odd):
        return flip(block, n_row, n_col, even, odd)

    def other(block):
        return move(block, (0, 1), (0, 1))

    held = pl.pallas_call(
        copy_kernel,
        name="hold",
        out_shape=jax.ShapeDtypeStruct(own.shape, bf16),
        in_specs=[vmem],
        out_specs=vmem,
        compiler_params=limit(2),
        cost_estimate=pl.CostEstimate(flops=100_000_000, bytes_accessed=1_000_000, transcendentals=0),
    )(own)
    both = pl.pallas_call(
        join_kernel,
        name="join",
        out_shape=jax.ShapeDtypeStruct((2 * own.shape[0] - 2 * SUB, channels), bf16),
        in_specs=[vmem] * 2,
        out_specs=vmem,
        compiler_params=limit(2),
    )(held, other(own))
    straight = move(own, (3, 0), (3, 0))
    first = move(both, (2, 0), (1, 0))
    second = move(both, (0, 2), (2, 2))
    third = move(both, (1, 2), (3, 2))
    straight, first, second, third = [(block, other(block)) for block in (straight, first, second, third)]
    chips = (((1, None), (2, 1), (2, 0), (2, None)), ((2, 0), (2, 0), (2, 1), (2, 1)))
    sources = ((both, *first, *first, *straight), (*second, *third, *second, *third))

    tri, parts, extra = [], [], []
    for side_x in range(n_col // 2):
        more = (pair_act, in_gain, out_gain) if side_x == 0 else (extra[1], *tri)
        more_shapes = () if side_x > 0 else (
            jax.ShapeDtypeStruct((3, tile, channels), f32),
            jax.ShapeDtypeStruct((SUB, channels), f32),
        )
        last = 3 + len(sources[side_x])
        results = pl.pallas_call(
            functools.partial(columns_kernel, n_row, n_col, side_x, chips[side_x]),
            name=f"columns_{side_x}",
            out_shape=(
                jax.ShapeDtypeStruct((pairs, channels), f32),
                jax.ShapeDtypeStruct((2, n_col, channels, size), bf16),
                jax.ShapeDtypeStruct((2 * size, channels), f32),
                jax.ShapeDtypeStruct((2 * size, channels), f32),
                jax.ShapeDtypeStruct((4, 2 * size, channels), f32),
                jax.ShapeDtypeStruct((2, 2 * size, channels), f32),
                *more_shapes,
            ),
            in_specs=[smem] + [vmem] * (1 + len(sources[side_x]) + len(more)),
            out_specs=(vmem,) * (6 + len(more_shapes)),
            input_output_aliases={last: 0, last + 1: 1} if side_x > 0 else {},
            compiler_params=limit(12),
            cost_estimate=pl.CostEstimate(flops=800_000_000, bytes_accessed=1_000_000, transcendentals=0),
        )(crop_length, weights, *sources[side_x], *more)
        tri = results[:2]
        parts += results[2:6]
        extra += results[6:]

    return pl.pallas_call(
        functools.partial(rest_kernel, n_row, n_col),
        name="rest",
        out_shape=(
            jax.ShapeDtypeStruct(pair_act.shape, bf16),
            jax.ShapeDtypeStruct(pair_act.shape, bf16),
            jax.ShapeDtypeStruct(weights.shape, f32),
        ),
        in_specs=[vmem] * (5 + len(parts)),
        out_specs=(anywhere,) * 3,
        scratch_shapes=[
            pltpu.VMEM((pairs, channels), f32),
            pltpu.VMEM((pairs, channels), bf16),
            pltpu.VMEM((pairs, 5 * channels), bf16),
            pltpu.VMEM((channels, 4 * channels), f32),
            pltpu.VMEM(pair_act.shape, bf16),
            pltpu.VMEM(pair_act.shape, bf16),
            pltpu.VMEM(weights.shape, f32),
            pltpu.SemaphoreType.DMA((5,)),
        ],
        compiler_params=limit(16),
    )(weights, *extra, *tri, *parts)


def body(n_row, n_col, pair_act, *others):
    tile_rows, tile_cols, channels = pair_act.shape
    pairs = tile_rows * n_row * tile_cols * n_col
    small = pairs * channels * 4 <= 1024 * 1024 and channels == 128
    square = n_row == 4 and n_col == 4 and tile_rows == SUB and tile_cols == SUB
    if small and square:
        return gathered_body(n_row, n_col, pair_act, *others)
    return spread_body(pair_act, *others)


def solution(mesh):
    return jax.shard_map(
        functools.partial(body, mesh.shape["row"], mesh.shape["col"]),
        mesh=mesh,
        in_specs=(
            P(("parts", "row"), "col", None),
            P(("parts", "row"), "col"),
            P("parts"),
            P(),
            P(),
            P(),
            P(("parts", "row"), "col", None),
        ),
        out_specs=(
            P(("parts", "row"), "col", None),
            P(("parts", "row"), "col", None),
            P("parts", None, None),
        ),
        check_vma=False,
    )
```

```python
import functools

import jax
import jax.numpy as jnp
from jax import lax
from jax.experimental import pallas as pl
from jax.experimental.pallas import tpu as pltpu
from jax.sharding import PartitionSpec as P

SUB = 8
EPS = 1e-05


def normalize(values):
    average = jnp.mean(values, axis=-1, keepdims=True)
    centered = values - average
    inverse = lax.rsqrt(jnp.mean(centered * centered, axis=-1, keepdims=True) + 1e-05)
    return (centered * inverse, inverse)


def norm_back(grad_hat, values_hat, inverse):
    first = jnp.mean(grad_hat, axis=-1, keepdims=True)
    second = jnp.mean(grad_hat * values_hat, axis=-1, keepdims=True)
    return (grad_hat - first - values_hat * second) * inverse


def gate_back(grad_act, proj_value, proj_gate, keep_mask):
    gate_sig = jax.nn.sigmoid(proj_gate)
    masked = grad_act * keep_mask
    grad_value = (masked * gate_sig).astype(jnp.bfloat16)
    grad_gate = (masked * proj_value * gate_sig * (1.0 - gate_sig)).astype(jnp.bfloat16)
    return (grad_value, grad_gate)


def spread_body(pair_act, pair_mask, crop_length, weights, in_gain, out_gain, cotangent):
    tile_rows, tile_cols, channels = pair_act.shape
    residues = tile_rows * lax.axis_size("row")
    row_pos = lax.axis_index("row") * tile_rows + jnp.arange(tile_rows, dtype=jnp.int32)
    col_pos = lax.axis_index("col") * tile_cols + jnp.arange(tile_cols, dtype=jnp.int32)
    row_in = (row_pos < crop_length[0]).astype(jnp.float32)
    col_in = (col_pos < crop_length[0]).astype(jnp.float32)
    keep_mask = (pair_mask.astype(jnp.float32) * row_in[:, None] * col_in[None, :])[:, :, None]
    z_hat, z_inverse = normalize(pair_act.astype(jnp.float32))
    normed = (z_hat * in_gain).astype(jnp.bfloat16)
    flat_norm = normed.reshape(tile_rows * tile_cols, channels)
    projections = jnp.einsum(
        "pc,scd->spd", flat_norm, weights[:5], preferred_element_type=jnp.float32
    )
    projections = projections.reshape(5, tile_rows, tile_cols, channels)
    left_act = (jax.nn.sigmoid(projections[1]) * projections[0] * keep_mask).astype(jnp.bfloat16)
    right_act = (jax.nn.sigmoid(projections[3]) * projections[2] * keep_mask).astype(jnp.bfloat16)
    partial_value = jnp.einsum(
        "ikh,jkh->ijh",
        left_act,
        lax.all_gather(right_act, "row", axis=0, tiled=True),
        preferred_element_type=jnp.float32,
    )
    tri_sum = lax.psum_scatter(
        partial_value.astype(jnp.bfloat16), "col", scatter_dimension=1, tiled=True
    ).astype(jnp.float32)
    x_hat, x_inverse = normalize(tri_sum)
    normed_out = (x_hat * out_gain).astype(jnp.bfloat16)
    flat_out = normed_out.reshape(tile_rows * tile_cols, channels)
    update_lin = jnp.dot(flat_out, weights[5], preferred_element_type=jnp.float32)
    update_lin = update_lin.reshape(tile_rows, tile_cols, channels)
    out_gate = jax.nn.sigmoid(projections[4])
    update = (out_gate * update_lin).astype(jnp.bfloat16)
    cot_value = cotangent.astype(jnp.float32)
    grad_lin = (cot_value * out_gate).astype(jnp.bfloat16)
    grad_gate_out = (cot_value * update_lin * out_gate * (1.0 - out_gate)).astype(jnp.bfloat16)
    flat_lin = grad_lin.reshape(tile_rows * tile_cols, channels)
    grad_norm_out = jnp.einsum(
        "pd,cd->pc", flat_lin, weights[5], preferred_element_type=jnp.float32
    )
    grad_norm_out = grad_norm_out.reshape(tile_rows, tile_cols, channels)
    grad_tri = norm_back(grad_norm_out * out_gain, x_hat, x_inverse).astype(jnp.bfloat16)
    grad_full = lax.all_gather(grad_tri, "col", axis=1, tiled=True)
    grad_slab = grad_full
    grad_left = jnp.einsum(
        "ijh,jkh->ikh",
        grad_slab,
        lax.all_gather(right_act, "row", axis=0, tiled=True),
        preferred_element_type=jnp.float32,
    )
    grad_slab = grad_full
    grad_right = lax.psum_scatter(
        jnp.einsum("ijh,ikh->jkh", grad_slab, left_act, preferred_element_type=jnp.float32).astype(
            jnp.bfloat16
        ),
        "row",
        scatter_dimension=0,
        tiled=True,
    ).astype(jnp.float32)
    grad_pa, grad_ga = gate_back(grad_left, projections[0], projections[1], keep_mask)
    grad_pb, grad_gb = gate_back(grad_right, projections[2], projections[3], keep_mask)
    grads = jnp.stack([grad_pa, grad_ga, grad_pb, grad_gb, grad_gate_out]).reshape(
        5, tile_rows * tile_cols, channels
    )
    grad_normed = jnp.einsum("spd,scd->pc", grads, weights[:5], preferred_element_type=jnp.float32)
    grad_normed = grad_normed.reshape(tile_rows, tile_cols, channels)
    pair_grad = norm_back(grad_normed * in_gain, z_hat, z_inverse).astype(jnp.bfloat16)
    local_in = jnp.einsum("pc,spd->scd", flat_norm, grads, preferred_element_type=jnp.float32)
    local_out = jnp.dot(flat_out.T, flat_lin, preferred_element_type=jnp.float32)
    local_grads = jnp.concatenate([local_in, local_out[None]], axis=0) / residues
    weight_grad = lax.psum(local_grads, ("row", "col"))
    return (update, pair_grad, weight_grad)


def pack_kernel(act_hbm, mask_hbm, cot_hbm, gain_hbm, out_ref, act_ref, mask_ref, gain_ref, sems):
    tile_rows, tile_cols, channels = act_ref.shape
    pairs = tile_rows * tile_cols
    head = out_ref.shape[0] - pairs
    pack_copies = [
        pltpu.make_async_copy(act_hbm, act_ref, sems.at[0]),
        pltpu.make_async_copy(gain_hbm, gain_ref, sems.at[1]),
        pltpu.make_async_copy(mask_hbm, mask_ref, sems.at[2]),
        pltpu.make_async_copy(cot_hbm, out_ref.at[head : head + pairs], sems.at[3]),
    ]
    for copy in pack_copies:
        copy.start()
    for copy in pack_copies:
        copy.wait()
    z_hat, _ = normalize(act_ref[...].astype(jnp.float32).reshape(pairs, channels))
    out_ref[0:pairs] = (z_hat * gain_ref[...]).astype(jnp.bfloat16)
    keep = mask_ref[...].astype(jnp.float32)
    wide = jnp.concatenate([keep, jnp.zeros((tile_rows, channels - tile_cols), jnp.float32)], axis=1)
    tall = jnp.concatenate([wide, jnp.zeros((channels - tile_rows, channels), jnp.float32)], axis=0)
    out_ref[pairs:head] = tall.T[0 : head - pairs].astype(jnp.bfloat16)


def copy_kernel(in_ref, out_ref):
    out_ref[...] = in_ref[...]


def join_kernel(own_ref, twin_ref, out_ref):
    tile = SUB * SUB
    refs = (own_ref, twin_ref)
    for at, ref in enumerate(refs):
        out_ref[at * tile : (at + 1) * tile] = ref[0:tile]
        spot = 2 * tile + 2 * SUB + at * tile
        out_ref[spot : spot + tile] = ref[tile + 2 * SUB :]
    masks = [ref[tile : tile + 2 * SUB].astype(jnp.float32)[0:SUB] for ref in refs]
    out_ref[2 * tile : 2 * tile + 2 * SUB] = jnp.concatenate(masks, axis=0).astype(jnp.bfloat16)


def normed_rows(ref, sub):
    return ref[sub * SUB * SUB : (sub + 1) * SUB * SUB]


def mask_rows(ref, sub):
    at = ref.shape[0] // 2 // (SUB * SUB) * SUB * SUB
    return ref[at : at + 2 * SUB].astype(jnp.float32)[sub * SUB : (sub + 1) * SUB]


def cot_rows(ref, sub):
    at = ref.shape[0] // 2 // (SUB * SUB) * SUB * SUB + 2 * SUB
    return ref[at + sub * SUB * SUB : at + (sub + 1) * SUB * SUB]


def chip_rows(rows_of, refs, core, direct_on):
    if direct_on is None:
        return rows_of(refs[min(core, len(refs) - 1)], core if len(refs) == 1 else 0)
    here = lax.axis_index("col") % 2 == direct_on
    return jnp.where(here, rows_of(refs[0], core), rows_of(refs[1], 1 - core))


def split_chips(refs, chips):
    split, at = [], 0
    for width, direct_on in chips:
        split.append((refs[at : at + width], direct_on))
        at += width
    return split


def doubled(top, bottom):
    return jnp.concatenate([top, bottom], axis=0).astype(jnp.bfloat16)


def triangle(blocks, groups, steps, vectors_at, factors_at, start_at, store_at, beside=None):
    def block(a):
        if beside is not None:
            beside(a)
        def step(q, totals):
            totals = list(totals)
            vectors = vectors_at(q)
            factors = factors_at(a, q)
            rows = [
                [doubled(vectors(g, inner), vectors(g + 1, inner)) for g in range(0, groups, 2)]
                for inner in range(SUB)
            ]
            for lane in range(SUB):
                chains = [[None, None] for _ in range(groups // 2)]
                for inner in range(SUB):
                    factor = factors(lane, inner)
                    factor = doubled(factor, factor)
                    for g in range(groups // 2):
                        term = factor * rows[inner][g]
                        chain = chains[g][inner % 2]
                        chains[g][inner % 2] = term if chain is None else chain + term
                for g in range(groups // 2):
                    wide = (chains[g][0] + chains[g][1]).astype(jnp.float32)
                    at = lane * groups + 2 * g
                    totals[at] = totals[at] + wide[0:SUB]
                    totals[at + 1] = totals[at + 1] + wide[SUB:]
            return tuple(totals)

        totals = tuple(start_at(a, g, lane) for lane in range(SUB) for g in range(groups))
        if steps > 4:
            totals = lax.fori_loop(0, steps, step, totals)
        else:
            for q in range(steps):
                totals = step(q, totals)
        for g in range(groups):
            store_at(a, g, [totals[lane * groups + g] for lane in range(SUB)])

    for a in range(blocks):
        block(a)


def spread(ref, row):
    return jnp.broadcast_to(ref[pl.ds(row, 1), :], (SUB, ref.shape[-1]))


def line(ref, row):
    return ref[pl.ds(pl.multiple_of(row, SUB), SUB), :]


def columns_kernel(n_row, n_col, side_x, chips, crop_ref, weights_ref, *refs):
    count = sum(width for width, _ in chips)
    chip_list, refs = split_chips(refs[:count], chips), refs[count:]
    own_ref = None
    if side_x == 0:
        act_ref, in_gain_ref, out_gain_ref, *refs, own_ref, gains_ref = refs
        z_hat, z_inverse = normalize(act_ref[...].astype(jnp.float32).reshape(own_ref.shape[1:]))
        own_ref[0] = z_hat
        own_ref[1] = jnp.broadcast_to(z_inverse, z_hat.shape)
        gains_ref[0:1] = in_gain_ref[...]
        gains_ref[1:2] = out_gain_ref[...]
    else:
        gains_ref, *refs = refs
    tri_in, (tri_ref, flip_ref, left_ref, right_ref, side_ref, back_ref) = refs[:-6], refs[-6:]
    channels = weights_ref.shape[-1]
    tile = SUB * SUB
    size = n_row * tile
    bf16, f32 = jnp.bfloat16, jnp.float32
    row_me, col_me = lax.axis_index("row"), lax.axis_index("col")
    chip_list = [(chip, on, core, b) for core in range(2) for b, (chip, on) in enumerate(chip_list)]
    normed = jnp.concatenate([chip_rows(normed_rows, chip, core, on) for chip, on, core, _ in chip_list], axis=0)
    same = lax.broadcasted_iota(jnp.int32, (channels, channels), 0) == lax.broadcasted_iota(jnp.int32, (channels, channels), 1)
    identity = jnp.where(same, 1.0, 0.0).astype(bf16)

    def turned(rows):
        return lax.dot_general(identity, rows, (((1,), (1,)), ((), ())), preferred_element_type=f32).astype(bf16)

    def put(kind, rows):
        both = turned(rows)
        for core in range(2):
            flip_ref[kind, 2 * side_x + core] = both[:, core * size : (core + 1) * size]

    put(0, normed)
    crop = crop_ref[0]
    col_offset = lax.broadcasted_iota(jnp.int32, (SUB, channels), 0)
    row_offset = lax.broadcasted_iota(jnp.int32, (SUB, channels), 1)
    kept = []
    for chip, on, core, b in chip_list:
        keep = chip_rows(mask_rows, chip, core, on)
        rows_in = row_offset < crop - (row_me ^ b) * SUB
        cols_in = col_offset < crop - (col_me ^ (2 * side_x + core)) * SUB
        keep = jnp.where(rows_in & cols_in, keep, 0.0)
        kept += [jnp.broadcast_to(keep[:, at : at + 1], (SUB, channels)) for at in range(SUB)]
    kept = jnp.concatenate(kept, axis=0)
    for side, act_ref in enumerate((left_ref, right_ref)):
        pair = jnp.concatenate([weights_ref[2 * side], weights_ref[2 * side + 1]], axis=1)
        proj = jnp.dot(normed, pair, preferred_element_type=f32)
        gate = jax.nn.sigmoid(proj[:, channels:])
        masked = gate * kept
        act = masked * proj[:, :channels]
        act_ref[...] = act.astype(bf16).astype(f32)
        side_ref[2 * side] = masked
        side_ref[2 * side + 1] = act * (1.0 - gate)
    out_gate = jax.nn.sigmoid(jnp.dot(normed, weights_ref[4], preferred_element_type=f32))
    if own_ref is not None:
        own_ref[2] = out_gate[0:tile]
    cot = jnp.concatenate([chip_rows(cot_rows, chip, core, on) for chip, on, core, _ in chip_list], axis=0)
    grad = cot.astype(f32) * out_gate
    grad_lin = grad.astype(bf16)
    put(1, grad_lin)
    back_ref[0] = grad * (1.0 - out_gate)
    back = lax.dot_general(grad_lin, weights_ref[5], (((1,), (1,)), ((), ())), preferred_element_type=f32)
    back = back * gains_ref[1:2]
    back_ref[1] = back - jnp.mean(back, axis=-1, keepdims=True)
    turn = row_me ^ col_me

    def flipped(q):
        firsts = [q * size + (turn ^ g) * tile for g in range(n_col)]
        return lambda g, inner: right_ref[pl.ds(firsts[g] + inner, SUB, stride=SUB), :]

    def along(a, q):
        return lambda lane, inner: spread(left_ref, q * size + a * tile + lane * SUB + inner)

    def start(a, g, lane):
        if len(tri_in) == 0:
            return jnp.zeros((SUB, channels), f32)
        return line(tri_in[0], g * size + a * tile + lane * SUB)

    def store(a, g, values):
        for lane in range(SUB):
            tri_ref[pl.ds(pl.multiple_of(g * size + a * tile + lane * SUB, SUB), SUB), :] = values[lane]

    triangle(n_row, n_col, 2, flipped, along, start, store)


def rest_kernel(n_row, n_col, weights_ref, own_ref, gains_ref, tri_ref, flip_ref, *refs):
    groups = [refs[at * 4 : at * 4 + 4] for at in range(n_col // 2)]
    update_ref, pair_grad_ref, weight_grad_ref, back_ref, hat_ref, d_ref, sum_ref = refs[4 * (n_col // 2) :]
    channels = tri_ref.shape[-1]
    tile = SUB * SUB
    size = n_row * tile
    columns = []
    for col in range(n_col):
        own = pl.ds(col % 2 * size, size)
        left, right, side, backs = groups[col // 2]
        columns.append((left.at[own], right.at[own], side.at[:, own], backs.at[:, own]))
    residues = n_row * SUB
    bf16, f32 = jnp.bfloat16, jnp.float32
    turn = lax.axis_index("row") ^ lax.axis_index("col")
    out_gain = gains_ref[1:2]
    for col, (_, _, _, backs_ref) in enumerate(columns):
        rows = slice(col * size, (col + 1) * size)
        x_hat, inverse = normalize(tri_ref[rows, :])
        normed_out = (x_hat * out_gain).astype(bf16)
        hat_ref[rows, :] = normed_out
        lin = jnp.dot(normed_out, weights_ref[5], preferred_element_type=f32)
        if col == 0:
            update_ref[...] = (own_ref[2] * lin[0:tile]).astype(bf16).reshape(update_ref.shape)
        d_ref[rows, 4 * channels : 5 * channels] = (backs_ref[0] * lin).astype(bf16)
        back = backs_ref[1]
        second = jnp.mean(back * x_hat, axis=-1, keepdims=True)
        back_ref[rows, :] = ((back - x_hat * second) * inverse).astype(bf16).astype(f32)

    lefts, rights, sides = [[column[at] for column in columns] for at in (0, 1, 2)]

    def zero(a, g, lane):
        return jnp.zeros((SUB, channels), f32)

    def store(side):
        def put(a, g, values):
            for lane in range(0, SUB, 2):
                at = pl.multiple_of(a * tile + lane * SUB, 2 * SUB)
                both = jnp.concatenate(values[lane : lane + 2], axis=0)
                rows = pl.ds(pl.multiple_of(g * size + at, 2 * SUB), 2 * SUB)
                for kind in range(2):
                    spot = (2 * side + kind) * channels
                    scaled = both * sides[g][2 * side + kind, pl.ds(at, 2 * SUB), :]
                    d_ref[rows, spot : spot + channels] = scaled.astype(bf16)
        return put

    def by_right(q):
        return lambda g, inner: line(rights[g], (q ^ turn) * tile + inner * SUB)

    def by_left(q):
        return lambda g, inner: line(lefts[g], q * tile + inner * SUB)

    def along(a, q):
        return lambda lane, inner: spread(back_ref, q * size + a * tile + lane * SUB + inner)

    def down(a, q):
        return lambda lane, inner: spread(back_ref, (a ^ turn) * size + q * tile + inner * SUB + lane)

    def chunk(ref, a, first, last):
        return ref[pl.ds(pl.multiple_of(a * size, size), size), first * channels : last * channels]

    def early_sums(a):
        sum_ref[:, 0:channels] += jnp.dot(flip_ref[0, a], chunk(d_ref, a, 4, 5), preferred_element_type=f32)
        sum_ref[:, channels : 2 * channels] += jnp.dot(flip_ref[1, a], chunk(hat_ref, a, 0, 1), preferred_element_type=f32)

    def left_sums(a):
        sum_ref[:, 2 * channels :] += jnp.dot(flip_ref[0, a], chunk(d_ref, a, 0, 2), preferred_element_type=f32)

    sum_ref[...] = jnp.zeros(sum_ref.shape, f32)
    triangle(n_row, n_col, n_col, by_right, along, zero, store(0), early_sums)
    triangle(n_row, n_col, n_row, by_left, down, zero, store(1), left_sums)

    scale = 1.0 / residues
    flipped = jnp.concatenate([flip_ref[0, col] for col in range(n_col)], axis=1)
    right_sums = jnp.dot(flipped, d_ref[:, 2 * channels : 4 * channels], preferred_element_type=f32)
    for s in range(2):
        part = slice(s * channels, (s + 1) * channels)
        weight_grad_ref[s] = sum_ref[:, (2 + s) * channels : (3 + s) * channels] * scale
        weight_grad_ref[2 + s] = right_sums[:, part] * scale
    weight_grad_ref[4] = sum_ref[:, 0:channels] * scale
    weight_grad_ref[5] = sum_ref[:, channels : 2 * channels].T * scale
    wide = jnp.concatenate([weights_ref[s] for s in range(5)], axis=1)
    total = lax.dot_general(d_ref[0:tile], wide, (((1,), (1,)), ((), ())), preferred_element_type=f32)
    grad = norm_back(total * gains_ref[0:1], own_ref[0], own_ref[1])
    pair_grad_ref[...] = grad.astype(bf16).reshape(pair_grad_ref.shape)


def flip(block, n_row, n_col, even, odd):
    pairs = []
    for row in range(n_row):
        for col in range(n_col):
            shift = odd if col % 2 else even
            pairs.append((row * n_col + col, (row ^ shift[0]) * n_col + (col ^ shift[1])))
    return lax.ppermute(block, ("row", "col"), pairs)


def gathered_body(n_row, n_col, pair_act, pair_mask, crop_length, weights, in_gain, out_gain, cotangent):
    tile_rows, tile_cols, channels = pair_act.shape
    tile = tile_rows * tile_cols
    size = n_row * tile
    pairs = size * n_col
    head = tile + 2 * SUB
    f32, bf16 = jnp.float32, jnp.bfloat16
    vmem = pl.BlockSpec(memory_space=pltpu.VMEM)
    smem = pl.BlockSpec(memory_space=pltpu.SMEM)
    hbm = pl.BlockSpec(memory_space=pltpu.HBM)
    in_gain, out_gain = in_gain.reshape(1, channels), out_gain.reshape(1, channels)

    def limit(mib):
        return pltpu.CompilerParams(vmem_limit_bytes=mib * 1024 * 1024)

    own = pl.pallas_call(
        pack_kernel,
        name="pack",
        out_shape=jax.ShapeDtypeStruct((head + tile, channels), bf16),
        in_specs=[hbm] * 4,
        out_specs=vmem,
        scratch_shapes=[
            pltpu.VMEM(pair_act.shape, pair_act.dtype),
            pltpu.VMEM(pair_mask.shape, jnp.int32),
            pltpu.VMEM((1, channels), f32),
            pltpu.SemaphoreType.DMA((4,)),
        ],
        compiler_params=limit(60),
    )(pair_act, pair_mask, cotangent.reshape(tile, channels), in_gain)
    crop_length, own = lax.optimization_barrier((crop_length, own))

    def move(block, even, odd):
        return flip(block, n_row, n_col, even, odd)

    def other(block):
        return move(block, (0, 1), (0, 1))

    held = pl.pallas_call(
        copy_kernel,
        name="hold",
        out_shape=jax.ShapeDtypeStruct(own.shape, bf16),
        in_specs=[vmem],
        out_specs=vmem,
        compiler_params=limit(2),
        cost_estimate=pl.CostEstimate(flops=100_000_000, bytes_accessed=1_000_000, transcendentals=0),
    )(own)
    both = pl.pallas_call(
        join_kernel,
        name="join",
        out_shape=jax.ShapeDtypeStruct((2 * own.shape[0] - 2 * SUB, channels), bf16),
        in_specs=[vmem] * 2,
        out_specs=vmem,
        compiler_params=limit(2),
    )(held, other(own))
    straight = move(own, (3, 0), (3, 0))
    first = move(both, (2, 0), (1, 0))
    second = move(both, (0, 2), (2, 2))
    third = move(both, (1, 2), (3, 2))
    straight, first, second, third = [(block, other(block)) for block in (straight, first, second, third)]
    chips = (((1, None), (2, 1), (2, 0), (2, None)), ((2, 0), (2, 0), (2, 1), (2, 1)))
    sources = ((both, *first, *first, *straight), (*second, *third, *second, *third))

    tri, parts, extra = [], [], []
    for side_x in range(n_col // 2):
        more = (pair_act, in_gain, out_gain) if side_x == 0 else (extra[1], *tri)
        more_shapes = () if side_x > 0 else (
            jax.ShapeDtypeStruct((3, tile, channels), f32),
            jax.ShapeDtypeStruct((SUB, channels), f32),
        )
        last = 3 + len(sources[side_x])
        results = pl.pallas_call(
            functools.partial(columns_kernel, n_row, n_col, side_x, chips[side_x]),
            name=f"columns_{side_x}",
            out_shape=(
                jax.ShapeDtypeStruct((pairs, channels), f32),
                jax.ShapeDtypeStruct((2, n_col, channels, size), bf16),
                jax.ShapeDtypeStruct((2 * size, channels), f32),
                jax.ShapeDtypeStruct((2 * size, channels), f32),
                jax.ShapeDtypeStruct((4, 2 * size, channels), f32),
                jax.ShapeDtypeStruct((2, 2 * size, channels), f32),
                *more_shapes,
            ),
            in_specs=[smem] + [vmem] * (1 + len(sources[side_x]) + len(more)),
            out_specs=(vmem,) * (6 + len(more_shapes)),
            input_output_aliases={last: 0, last + 1: 1} if side_x > 0 else {},
            compiler_params=limit(12),
            cost_estimate=pl.CostEstimate(flops=800_000_000, bytes_accessed=1_000_000, transcendentals=0),
        )(crop_length, weights, *sources[side_x], *more)
        tri = results[:2]
        parts += results[2:6]
        extra += results[6:]

    return pl.pallas_call(
        functools.partial(rest_kernel, n_row, n_col),
        name="rest",
        out_shape=(
            jax.ShapeDtypeStruct(pair_act.shape, bf16),
            jax.ShapeDtypeStruct(pair_act.shape, bf16),
            jax.ShapeDtypeStruct(weights.shape, f32),
        ),
        in_specs=[vmem] * (5 + len(parts)),
        out_specs=(vmem, vmem, vmem),
        scratch_shapes=[
            pltpu.VMEM((pairs, channels), f32),
            pltpu.VMEM((pairs, channels), bf16),
            pltpu.VMEM((pairs, 5 * channels), bf16),
            pltpu.VMEM((channels, 4 * channels), f32),
        ],
        compiler_params=limit(16),
    )(weights, *extra, *tri, *parts)


def body(n_row, n_col, pair_act, *others):
    tile_rows, tile_cols, channels = pair_act.shape
    pairs = tile_rows * n_row * tile_cols * n_col
    small = pairs * channels * 4 <= 1024 * 1024 and channels == 128
    square = n_row == 4 and n_col == 4 and tile_rows == SUB and tile_cols == SUB
    if small and square:
        return gathered_body(n_row, n_col, pair_act, *others)
    return spread_body(pair_act, *others)


def solution(mesh):
    return jax.shard_map(
        functools.partial(body, mesh.shape["row"], mesh.shape["col"]),
        mesh=mesh,
        in_specs=(
            P(("parts", "row"), "col", None),
            P(("parts", "row"), "col"),
            P("parts"),
            P(),
            P(),
            P(),
            P(("parts", "row"), "col", None),
        ),
        out_specs=(
            P(("parts", "row"), "col", None),
            P(("parts", "row"), "col", None),
            P("parts", None, None),
        ),
        check_vma=False,
    )
```

```python
import functools

import jax
import jax.numpy as jnp
from jax import lax
from jax.experimental import pallas as pl
from jax.experimental.pallas import tpu as pltpu
from jax.sharding import PartitionSpec as P

SUB = 8
EPS = 1e-05


def normalize(values):
    average = jnp.mean(values, axis=-1, keepdims=True)
    centered = values - average
    inverse = lax.rsqrt(jnp.mean(centered * centered, axis=-1, keepdims=True) + 1e-05)
    return (centered * inverse, inverse)


def norm_back(grad_hat, values_hat, inverse):
    first = jnp.mean(grad_hat, axis=-1, keepdims=True)
    second = jnp.mean(grad_hat * values_hat, axis=-1, keepdims=True)
    return (grad_hat - first - values_hat * second) * inverse


def gate_back(grad_act, proj_value, proj_gate, keep_mask):
    gate_sig = jax.nn.sigmoid(proj_gate)
    masked = grad_act * keep_mask
    grad_value = (masked * gate_sig).astype(jnp.bfloat16)
    grad_gate = (masked * proj_value * gate_sig * (1.0 - gate_sig)).astype(jnp.bfloat16)
    return (grad_value, grad_gate)


def spread_body(pair_act, pair_mask, crop_length, weights, in_gain, out_gain, cotangent):
    tile_rows, tile_cols, channels = pair_act.shape
    residues = tile_rows * lax.axis_size("row")
    row_pos = lax.axis_index("row") * tile_rows + jnp.arange(tile_rows, dtype=jnp.int32)
    col_pos = lax.axis_index("col") * tile_cols + jnp.arange(tile_cols, dtype=jnp.int32)
    row_in = (row_pos < crop_length[0]).astype(jnp.float32)
    col_in = (col_pos < crop_length[0]).astype(jnp.float32)
    keep_mask = (pair_mask.astype(jnp.float32) * row_in[:, None] * col_in[None, :])[:, :, None]
    z_hat, z_inverse = normalize(pair_act.astype(jnp.float32))
    normed = (z_hat * in_gain).astype(jnp.bfloat16)
    flat_norm = normed.reshape(tile_rows * tile_cols, channels)
    projections = jnp.einsum(
        "pc,scd->spd", flat_norm, weights[:5], preferred_element_type=jnp.float32
    )
    projections = projections.reshape(5, tile_rows, tile_cols, channels)
    left_act = (jax.nn.sigmoid(projections[1]) * projections[0] * keep_mask).astype(jnp.bfloat16)
    right_act = (jax.nn.sigmoid(projections[3]) * projections[2] * keep_mask).astype(jnp.bfloat16)
    partial_value = jnp.einsum(
        "ikh,jkh->ijh",
        left_act,
        lax.all_gather(right_act, "row", axis=0, tiled=True),
        preferred_element_type=jnp.float32,
    )
    tri_sum = lax.psum_scatter(
        partial_value.astype(jnp.bfloat16), "col", scatter_dimension=1, tiled=True
    ).astype(jnp.float32)
    x_hat, x_inverse = normalize(tri_sum)
    normed_out = (x_hat * out_gain).astype(jnp.bfloat16)
    flat_out = normed_out.reshape(tile_rows * tile_cols, channels)
    update_lin = jnp.dot(flat_out, weights[5], preferred_element_type=jnp.float32)
    update_lin = update_lin.reshape(tile_rows, tile_cols, channels)
    out_gate = jax.nn.sigmoid(projections[4])
    update = (out_gate * update_lin).astype(jnp.bfloat16)
    cot_value = cotangent.astype(jnp.float32)
    grad_lin = (cot_value * out_gate).astype(jnp.bfloat16)
    grad_gate_out = (cot_value * update_lin * out_gate * (1.0 - out_gate)).astype(jnp.bfloat16)
    flat_lin = grad_lin.reshape(tile_rows * tile_cols, channels)
    grad_norm_out = jnp.einsum(
        "pd,cd->pc", flat_lin, weights[5], preferred_element_type=jnp.float32
    )
    grad_norm_out = grad_norm_out.reshape(tile_rows, tile_cols, channels)
    grad_tri = norm_back(grad_norm_out * out_gain, x_hat, x_inverse).astype(jnp.bfloat16)
    grad_full = lax.all_gather(grad_tri, "col", axis=1, tiled=True)
    grad_slab = grad_full
    grad_left = jnp.einsum(
        "ijh,jkh->ikh",
        grad_slab,
        lax.all_gather(right_act, "row", axis=0, tiled=True),
        preferred_element_type=jnp.float32,
    )
    grad_slab = grad_full
    grad_right = lax.psum_scatter(
        jnp.einsum("ijh,ikh->jkh", grad_slab, left_act, preferred_element_type=jnp.float32).astype(
            jnp.bfloat16
        ),
        "row",
        scatter_dimension=0,
        tiled=True,
    ).astype(jnp.float32)
    grad_pa, grad_ga = gate_back(grad_left, projections[0], projections[1], keep_mask)
    grad_pb, grad_gb = gate_back(grad_right, projections[2], projections[3], keep_mask)
    grads = jnp.stack([grad_pa, grad_ga, grad_pb, grad_gb, grad_gate_out]).reshape(
        5, tile_rows * tile_cols, channels
    )
    grad_normed = jnp.einsum("spd,scd->pc", grads, weights[:5], preferred_element_type=jnp.float32)
    grad_normed = grad_normed.reshape(tile_rows, tile_cols, channels)
    pair_grad = norm_back(grad_normed * in_gain, z_hat, z_inverse).astype(jnp.bfloat16)
    local_in = jnp.einsum("pc,spd->scd", flat_norm, grads, preferred_element_type=jnp.float32)
    local_out = jnp.dot(flat_out.T, flat_lin, preferred_element_type=jnp.float32)
    local_grads = jnp.concatenate([local_in, local_out[None]], axis=0) / residues
    weight_grad = lax.psum(local_grads, ("row", "col"))
    return (update, pair_grad, weight_grad)


def pack_kernel(act_hbm, mask_hbm, cot_hbm, gain_hbm, out_ref, act_ref, mask_ref, gain_ref, sems):
    tile_rows, tile_cols, channels = act_ref.shape
    pairs = tile_rows * tile_cols
    head = out_ref.shape[0] - pairs
    pack_copies = [
        pltpu.make_async_copy(act_hbm, act_ref, sems.at[0]),
        pltpu.make_async_copy(gain_hbm, gain_ref, sems.at[1]),
        pltpu.make_async_copy(mask_hbm, mask_ref, sems.at[2]),
        pltpu.make_async_copy(cot_hbm, out_ref.at[head : head + pairs], sems.at[3]),
    ]
    for copy in pack_copies:
        copy.start()
    for copy in pack_copies:
        copy.wait()
    z_hat, _ = normalize(act_ref[...].astype(jnp.float32).reshape(pairs, channels))
    out_ref[0:pairs] = (z_hat * gain_ref[...]).astype(jnp.bfloat16)
    keep = mask_ref[...].astype(jnp.float32)
    wide = jnp.concatenate([keep, jnp.zeros((tile_rows, channels - tile_cols), jnp.float32)], axis=1)
    tall = jnp.concatenate([wide, jnp.zeros((channels - tile_rows, channels), jnp.float32)], axis=0)
    out_ref[pairs:head] = tall.T[0 : head - pairs].astype(jnp.bfloat16)


def copy_kernel(in_ref, out_ref):
    out_ref[...] = in_ref[...]


def join_kernel(own_ref, twin_ref, out_ref):
    tile = SUB * SUB
    refs = (own_ref, twin_ref)
    for at, ref in enumerate(refs):
        out_ref[at * tile : (at + 1) * tile] = ref[0:tile]
        spot = 2 * tile + 2 * SUB + at * tile
        out_ref[spot : spot + tile] = ref[tile + 2 * SUB :]
    masks = [ref[tile : tile + 2 * SUB].astype(jnp.float32)[0:SUB] for ref in refs]
    out_ref[2 * tile : 2 * tile + 2 * SUB] = jnp.concatenate(masks, axis=0).astype(jnp.bfloat16)


def normed_rows(ref, sub):
    return ref[sub * SUB * SUB : (sub + 1) * SUB * SUB]


def mask_rows(ref, sub):
    at = ref.shape[0] // 2 // (SUB * SUB) * SUB * SUB
    return ref[at : at + 2 * SUB].astype(jnp.float32)[sub * SUB : (sub + 1) * SUB]


def cot_rows(ref, sub):
    at = ref.shape[0] // 2 // (SUB * SUB) * SUB * SUB + 2 * SUB
    return ref[at + sub * SUB * SUB : at + (sub + 1) * SUB * SUB]


def chip_rows(rows_of, refs, core, direct_on):
    if direct_on is None:
        return rows_of(refs[min(core, len(refs) - 1)], core if len(refs) == 1 else 0)
    here = lax.axis_index("col") % 2 == direct_on
    return jnp.where(here, rows_of(refs[0], core), rows_of(refs[1], 1 - core))


def split_chips(refs, chips):
    split, at = [], 0
    for width, direct_on in chips:
        split.append((refs[at : at + width], direct_on))
        at += width
    return split


def doubled(top, bottom):
    return jnp.concatenate([top, bottom], axis=0).astype(jnp.bfloat16)


def triangle(blocks, groups, steps, vectors_at, factors_at, start_at, store_at, beside=None, unrolled=False):
    def block(a):
        if beside is not None:
            beside(a)
        def step(q, totals):
            totals = list(totals)
            vectors = vectors_at(q)
            factors = factors_at(a, q)
            rows = [
                [doubled(vectors(g, inner), vectors(g + 1, inner)) for g in range(0, groups, 2)]
                for inner in range(SUB)
            ]
            for lane in range(SUB):
                chains = [[None, None] for _ in range(groups // 2)]
                for inner in range(SUB):
                    factor = factors(lane, inner)
                    factor = doubled(factor, factor)
                    for g in range(groups // 2):
                        term = factor * rows[inner][g]
                        chain = chains[g][inner % 2]
                        chains[g][inner % 2] = term if chain is None else chain + term
                for g in range(groups // 2):
                    wide = (chains[g][0] + chains[g][1]).astype(jnp.float32)
                    at = lane * groups + 2 * g
                    totals[at] = totals[at] + wide[0:SUB]
                    totals[at + 1] = totals[at + 1] + wide[SUB:]
            return tuple(totals)

        totals = tuple(start_at(a, g, lane) for lane in range(SUB) for g in range(groups))
        if steps > 4:
            totals = lax.fori_loop(0, steps, step, totals)
        else:
            for q in range(steps):
                totals = step(q, totals)
        for g in range(groups):
            store_at(a, g, [totals[lane * groups + g] for lane in range(SUB)])

    if unrolled:
        for a in range(blocks):
            block(a)
    else:
        pl.loop(0, blocks)(block)


def spread(ref, row):
    return jnp.broadcast_to(ref[pl.ds(row, 1), :], (SUB, ref.shape[-1]))


def line(ref, row):
    return ref[pl.ds(pl.multiple_of(row, SUB), SUB), :]


def columns_kernel(n_row, n_col, side_x, chips, crop_ref, weights_ref, *refs):
    count = sum(width for width, _ in chips)
    chip_list, refs = split_chips(refs[:count], chips), refs[count:]
    own_ref = None
    if side_x == 0:
        act_ref, in_gain_ref, out_gain_ref, *refs, own_ref, gains_ref = refs
        z_hat, z_inverse = normalize(act_ref[...].astype(jnp.float32).reshape(own_ref.shape[1:]))
        own_ref[0] = z_hat
        own_ref[1] = jnp.broadcast_to(z_inverse, z_hat.shape)
        gains_ref[0:1] = in_gain_ref[...]
        gains_ref[1:2] = out_gain_ref[...]
    else:
        gains_ref, *refs = refs
    tri_in, (tri_ref, flip_ref, left_ref, right_ref, side_ref, back_ref) = refs[:-6], refs[-6:]
    channels = weights_ref.shape[-1]
    tile = SUB * SUB
    size = n_row * tile
    bf16, f32 = jnp.bfloat16, jnp.float32
    row_me, col_me = lax.axis_index("row"), lax.axis_index("col")
    chip_list = [(chip, on, core, b) for core in range(2) for b, (chip, on) in enumerate(chip_list)]
    normed = jnp.concatenate([chip_rows(normed_rows, chip, core, on) for chip, on, core, _ in chip_list], axis=0)
    same = lax.broadcasted_iota(jnp.int32, (channels, channels), 0) == lax.broadcasted_iota(jnp.int32, (channels, channels), 1)
    identity = jnp.where(same, 1.0, 0.0).astype(bf16)

    def turned(rows):
        return lax.dot_general(identity, rows, (((1,), (1,)), ((), ())), preferred_element_type=f32).astype(bf16)

    def put(kind, rows):
        both = turned(rows)
        for core in range(2):
            flip_ref[kind, 2 * side_x + core] = both[:, core * size : (core + 1) * size]

    put(0, normed)
    crop = crop_ref[0]
    col_offset = lax.broadcasted_iota(jnp.int32, (SUB, channels), 0)
    row_offset = lax.broadcasted_iota(jnp.int32, (SUB, channels), 1)
    kept = []
    for chip, on, core, b in chip_list:
        keep = chip_rows(mask_rows, chip, core, on)
        rows_in = row_offset < crop - (row_me ^ b) * SUB
        cols_in = col_offset < crop - (col_me ^ (2 * side_x + core)) * SUB
        keep = jnp.where(rows_in & cols_in, keep, 0.0)
        kept += [jnp.broadcast_to(keep[:, at : at + 1], (SUB, channels)) for at in range(SUB)]
    kept = jnp.concatenate(kept, axis=0)
    for side, act_ref in enumerate((left_ref, right_ref)):
        pair = jnp.concatenate([weights_ref[2 * side], weights_ref[2 * side + 1]], axis=1)
        proj = jnp.dot(normed, pair, preferred_element_type=f32)
        gate = jax.nn.sigmoid(proj[:, channels:])
        masked = gate * kept
        act = masked * proj[:, :channels]
        act_ref[...] = act.astype(bf16).astype(f32)
        side_ref[2 * side] = masked
        side_ref[2 * side + 1] = act * (1.0 - gate)
    out_gate = jax.nn.sigmoid(jnp.dot(normed, weights_ref[4], preferred_element_type=f32))
    if own_ref is not None:
        own_ref[2] = out_gate[0:tile]
    cot = jnp.concatenate([chip_rows(cot_rows, chip, core, on) for chip, on, core, _ in chip_list], axis=0)
    grad = cot.astype(f32) * out_gate
    grad_lin = grad.astype(bf16)
    put(1, grad_lin)
    back_ref[0] = grad * (1.0 - out_gate)
    back = lax.dot_general(grad_lin, weights_ref[5], (((1,), (1,)), ((), ())), preferred_element_type=f32)
    back = back * gains_ref[1:2]
    back_ref[1] = back - jnp.mean(back, axis=-1, keepdims=True)
    turn = row_me ^ col_me

    def flipped(q):
        firsts = [q * size + (turn ^ g) * tile for g in range(n_col)]
        return lambda g, inner: right_ref[pl.ds(firsts[g] + inner, SUB, stride=SUB), :]

    def along(a, q):
        return lambda lane, inner: spread(left_ref, q * size + a * tile + lane * SUB + inner)

    def start(a, g, lane):
        if len(tri_in) == 0:
            return jnp.zeros((SUB, channels), f32)
        return line(tri_in[0], g * size + a * tile + lane * SUB)

    def store(a, g, values):
        for lane in range(SUB):
            tri_ref[pl.ds(pl.multiple_of(g * size + a * tile + lane * SUB, SUB), SUB), :] = values[lane]

    triangle(n_row, n_col, 2, flipped, along, start, store)


def rest_kernel(n_row, n_col, weights_ref, own_ref, gains_ref, tri_ref, flip_ref, *refs):
    groups = [refs[at * 4 : at * 4 + 4] for at in range(n_col // 2)]
    update_ref, pair_grad_ref, weight_grad_ref, back_ref, hat_ref, d_ref, sum_ref = refs[4 * (n_col // 2) :]
    channels = tri_ref.shape[-1]
    tile = SUB * SUB
    size = n_row * tile
    columns = []
    for col in range(n_col):
        own = pl.ds(col % 2 * size, size)
        left, right, side, backs = groups[col // 2]
        columns.append((left.at[own], right.at[own], side.at[:, own], backs.at[:, own]))
    residues = n_row * SUB
    bf16, f32 = jnp.bfloat16, jnp.float32
    turn = lax.axis_index("row") ^ lax.axis_index("col")
    out_gain = gains_ref[1:2]
    for col, (_, _, _, backs_ref) in enumerate(columns):
        rows = slice(col * size, (col + 1) * size)
        x_hat, inverse = normalize(tri_ref[rows, :])
        normed_out = (x_hat * out_gain).astype(bf16)
        hat_ref[rows, :] = normed_out
        lin = jnp.dot(normed_out, weights_ref[5], preferred_element_type=f32)
        if col == 0:
            update_ref[...] = (own_ref[2] * lin[0:tile]).astype(bf16).reshape(update_ref.shape)
        d_ref[rows, 4 * channels : 5 * channels] = (backs_ref[0] * lin).astype(bf16)
        back = backs_ref[1]
        second = jnp.mean(back * x_hat, axis=-1, keepdims=True)
        back_ref[rows, :] = ((back - x_hat * second) * inverse).astype(bf16).astype(f32)

    lefts, rights, sides = [[column[at] for column in columns] for at in (0, 1, 2)]

    def zero(a, g, lane):
        return jnp.zeros((SUB, channels), f32)

    def store(side):
        def put(a, g, values):
            for lane in range(0, SUB, 2):
                at = pl.multiple_of(a * tile + lane * SUB, 2 * SUB)
                both = jnp.concatenate(values[lane : lane + 2], axis=0)
                rows = pl.ds(pl.multiple_of(g * size + at, 2 * SUB), 2 * SUB)
                for kind in range(2):
                    spot = (2 * side + kind) * channels
                    scaled = both * sides[g][2 * side + kind, pl.ds(at, 2 * SUB), :]
                    d_ref[rows, spot : spot + channels] = scaled.astype(bf16)
        return put

    def by_right(q):
        return lambda g, inner: line(rights[g], (q ^ turn) * tile + inner * SUB)

    def by_left(q):
        return lambda g, inner: line(lefts[g], q * tile + inner * SUB)

    def along(a, q):
        return lambda lane, inner: spread(back_ref, q * size + a * tile + lane * SUB + inner)

    def down(a, q):
        return lambda lane, inner: spread(back_ref, (a ^ turn) * size + q * tile + inner * SUB + lane)

    def chunk(ref, a, first, last):
        return ref[pl.ds(pl.multiple_of(a * size, size), size), first * channels : last * channels]

    def early_sums(a):
        sum_ref[:, 0:channels] += jnp.dot(flip_ref[0, a], chunk(d_ref, a, 4, 5), preferred_element_type=f32)
        sum_ref[:, channels : 2 * channels] += jnp.dot(flip_ref[1, a], chunk(hat_ref, a, 0, 1), preferred_element_type=f32)

    def left_sums(a):
        sum_ref[:, 2 * channels :] += jnp.dot(flip_ref[0, a], chunk(d_ref, a, 0, 2), preferred_element_type=f32)

    sum_ref[...] = jnp.zeros(sum_ref.shape, f32)
    triangle(n_row, n_col, n_col, by_right, along, zero, store(0), early_sums, True)
    triangle(n_row, n_col, n_row, by_left, down, zero, store(1), left_sums, True)

    scale = 1.0 / residues
    flipped = jnp.concatenate([flip_ref[0, col] for col in range(n_col)], axis=1)
    right_sums = jnp.dot(flipped, d_ref[:, 2 * channels : 4 * channels], preferred_element_type=f32)
    for s in range(2):
        part = slice(s * channels, (s + 1) * channels)
        weight_grad_ref[s] = sum_ref[:, (2 + s) * channels : (3 + s) * channels] * scale
        weight_grad_ref[2 + s] = right_sums[:, part] * scale
    weight_grad_ref[4] = sum_ref[:, 0:channels] * scale
    weight_grad_ref[5] = sum_ref[:, channels : 2 * channels].T * scale
    wide = jnp.concatenate([weights_ref[s] for s in range(5)], axis=1)
    total = lax.dot_general(d_ref[0:tile], wide, (((1,), (1,)), ((), ())), preferred_element_type=f32)
    grad = norm_back(total * gains_ref[0:1], own_ref[0], own_ref[1])
    pair_grad_ref[...] = grad.astype(bf16).reshape(pair_grad_ref.shape)


def flip(block, n_row, n_col, even, odd):
    pairs = []
    for row in range(n_row):
        for col in range(n_col):
            shift = odd if col % 2 else even
            pairs.append((row * n_col + col, (row ^ shift[0]) * n_col + (col ^ shift[1])))
    return lax.ppermute(block, ("row", "col"), pairs)


def gathered_body(n_row, n_col, pair_act, pair_mask, crop_length, weights, in_gain, out_gain, cotangent):
    tile_rows, tile_cols, channels = pair_act.shape
    tile = tile_rows * tile_cols
    size = n_row * tile
    pairs = size * n_col
    head = tile + 2 * SUB
    f32, bf16 = jnp.float32, jnp.bfloat16
    vmem = pl.BlockSpec(memory_space=pltpu.VMEM)
    smem = pl.BlockSpec(memory_space=pltpu.SMEM)
    hbm = pl.BlockSpec(memory_space=pltpu.HBM)
    in_gain, out_gain = in_gain.reshape(1, channels), out_gain.reshape(1, channels)

    def limit(mib):
        return pltpu.CompilerParams(vmem_limit_bytes=mib * 1024 * 1024)

    own = pl.pallas_call(
        pack_kernel,
        name="pack",
        out_shape=jax.ShapeDtypeStruct((head + tile, channels), bf16),
        in_specs=[hbm] * 4,
        out_specs=vmem,
        scratch_shapes=[
            pltpu.VMEM(pair_act.shape, pair_act.dtype),
            pltpu.VMEM(pair_mask.shape, jnp.int32),
            pltpu.VMEM((1, channels), f32),
            pltpu.SemaphoreType.DMA((4,)),
        ],
        compiler_params=limit(60),
    )(pair_act, pair_mask, cotangent.reshape(tile, channels), in_gain)
    crop_length, own = lax.optimization_barrier((crop_length, own))

    def move(block, even, odd):
        return flip(block, n_row, n_col, even, odd)

    def other(block):
        return move(block, (0, 1), (0, 1))

    held = pl.pallas_call(
        copy_kernel,
        name="hold",
        out_shape=jax.ShapeDtypeStruct(own.shape, bf16),
        in_specs=[vmem],
        out_specs=vmem,
        compiler_params=limit(2),
        cost_estimate=pl.CostEstimate(flops=100_000_000, bytes_accessed=1_000_000, transcendentals=0),
    )(own)
    both = pl.pallas_call(
        join_kernel,
        name="join",
        out_shape=jax.ShapeDtypeStruct((2 * own.shape[0] - 2 * SUB, channels), bf16),
        in_specs=[vmem] * 2,
        out_specs=vmem,
        compiler_params=limit(2),
    )(held, other(own))
    straight = move(own, (3, 0), (3, 0))
    first = move(both, (2, 0), (1, 0))
    second = move(both, (0, 2), (2, 2))
    third = move(both, (1, 2), (3, 2))
    straight, first, second, third = [(block, other(block)) for block in (straight, first, second, third)]
    chips = (((1, None), (2, 1), (2, 0), (2, None)), ((2, 0), (2, 0), (2, 1), (2, 1)))
    sources = ((both, *first, *first, *straight), (*second, *third, *second, *third))

    tri, parts, extra = [], [], []
    for side_x in range(n_col // 2):
        more = (pair_act, in_gain, out_gain) if side_x == 0 else (extra[1], *tri)
        more_shapes = () if side_x > 0 else (
            jax.ShapeDtypeStruct((3, tile, channels), f32),
            jax.ShapeDtypeStruct((SUB, channels), f32),
        )
        last = 3 + len(sources[side_x])
        results = pl.pallas_call(
            functools.partial(columns_kernel, n_row, n_col, side_x, chips[side_x]),
            name=f"columns_{side_x}",
            out_shape=(
                jax.ShapeDtypeStruct((pairs, channels), f32),
                jax.ShapeDtypeStruct((2, n_col, channels, size), bf16),
                jax.ShapeDtypeStruct((2 * size, channels), f32),
                jax.ShapeDtypeStruct((2 * size, channels), f32),
                jax.ShapeDtypeStruct((4, 2 * size, channels), f32),
                jax.ShapeDtypeStruct((2, 2 * size, channels), f32),
                *more_shapes,
            ),
            in_specs=[smem] + [vmem] * (1 + len(sources[side_x]) + len(more)),
            out_specs=(vmem,) * (6 + len(more_shapes)),
            input_output_aliases={last: 0, last + 1: 1} if side_x > 0 else {},
            compiler_params=limit(12),
            cost_estimate=pl.CostEstimate(flops=800_000_000, bytes_accessed=1_000_000, transcendentals=0),
        )(crop_length, weights, *sources[side_x], *more)
        tri = results[:2]
        parts += results[2:6]
        extra += results[6:]

    return pl.pallas_call(
        functools.partial(rest_kernel, n_row, n_col),
        name="rest",
        out_shape=(
            jax.ShapeDtypeStruct(pair_act.shape, bf16),
            jax.ShapeDtypeStruct(pair_act.shape, bf16),
            jax.ShapeDtypeStruct(weights.shape, f32),
        ),
        in_specs=[vmem] * (5 + len(parts)),
        out_specs=(vmem, vmem, vmem),
        scratch_shapes=[
            pltpu.VMEM((pairs, channels), f32),
            pltpu.VMEM((pairs, channels), bf16),
            pltpu.VMEM((pairs, 5 * channels), bf16),
            pltpu.VMEM((channels, 4 * channels), f32),
        ],
        compiler_params=limit(16),
    )(weights, *extra, *tri, *parts)


def body(n_row, n_col, pair_act, *others):
    tile_rows, tile_cols, channels = pair_act.shape
    pairs = tile_rows * n_row * tile_cols * n_col
    small = pairs * channels * 4 <= 1024 * 1024 and channels == 128
    square = n_row == 4 and n_col == 4 and tile_rows == SUB and tile_cols == SUB
    if small and square:
        return gathered_body(n_row, n_col, pair_act, *others)
    return spread_body(pair_act, *others)


def solution(mesh):
    return jax.shard_map(
        functools.partial(body, mesh.shape["row"], mesh.shape["col"]),
        mesh=mesh,
        in_specs=(
            P(("parts", "row"), "col", None),
            P(("parts", "row"), "col"),
            P("parts"),
            P(),
            P(),
            P(),
            P(("parts", "row"), "col", None),
        ),
        out_specs=(
            P(("parts", "row"), "col", None),
            P(("parts", "row"), "col", None),
            P("parts", None, None),
        ),
        check_vma=False,
    )
```

```python
import functools

import jax
import jax.numpy as jnp
from jax import lax
from jax.experimental import pallas as pl
from jax.experimental.pallas import tpu as pltpu
from jax.sharding import PartitionSpec as P

SUB = 8
EPS = 1e-05


def normalize(values):
    average = jnp.mean(values, axis=-1, keepdims=True)
    centered = values - average
    inverse = lax.rsqrt(jnp.mean(centered * centered, axis=-1, keepdims=True) + 1e-05)
    return (centered * inverse, inverse)


def norm_back(grad_hat, values_hat, inverse):
    first = jnp.mean(grad_hat, axis=-1, keepdims=True)
    second = jnp.mean(grad_hat * values_hat, axis=-1, keepdims=True)
    return (grad_hat - first - values_hat * second) * inverse


def gate_back(grad_act, proj_value, proj_gate, keep_mask):
    gate_sig = jax.nn.sigmoid(proj_gate)
    masked = grad_act * keep_mask
    grad_value = (masked * gate_sig).astype(jnp.bfloat16)
    grad_gate = (masked * proj_value * gate_sig * (1.0 - gate_sig)).astype(jnp.bfloat16)
    return (grad_value, grad_gate)


def spread_body(pair_act, pair_mask, crop_length, weights, in_gain, out_gain, cotangent):
    tile_rows, tile_cols, channels = pair_act.shape
    residues = tile_rows * lax.axis_size("row")
    row_pos = lax.axis_index("row") * tile_rows + jnp.arange(tile_rows, dtype=jnp.int32)
    col_pos = lax.axis_index("col") * tile_cols + jnp.arange(tile_cols, dtype=jnp.int32)
    row_in = (row_pos < crop_length[0]).astype(jnp.float32)
    col_in = (col_pos < crop_length[0]).astype(jnp.float32)
    keep_mask = (pair_mask.astype(jnp.float32) * row_in[:, None] * col_in[None, :])[:, :, None]
    z_hat, z_inverse = normalize(pair_act.astype(jnp.float32))
    normed = (z_hat * in_gain).astype(jnp.bfloat16)
    flat_norm = normed.reshape(tile_rows * tile_cols, channels)
    projections = jnp.einsum(
        "pc,scd->spd", flat_norm, weights[:5], preferred_element_type=jnp.float32
    )
    projections = projections.reshape(5, tile_rows, tile_cols, channels)
    left_act = (jax.nn.sigmoid(projections[1]) * projections[0] * keep_mask).astype(jnp.bfloat16)
    right_act = (jax.nn.sigmoid(projections[3]) * projections[2] * keep_mask).astype(jnp.bfloat16)
    partial_value = jnp.einsum(
        "ikh,jkh->ijh",
        left_act,
        lax.all_gather(right_act, "row", axis=0, tiled=True),
        preferred_element_type=jnp.float32,
    )
    tri_sum = lax.psum_scatter(
        partial_value.astype(jnp.bfloat16), "col", scatter_dimension=1, tiled=True
    ).astype(jnp.float32)
    x_hat, x_inverse = normalize(tri_sum)
    normed_out = (x_hat * out_gain).astype(jnp.bfloat16)
    flat_out = normed_out.reshape(tile_rows * tile_cols, channels)
    update_lin = jnp.dot(flat_out, weights[5], preferred_element_type=jnp.float32)
    update_lin = update_lin.reshape(tile_rows, tile_cols, channels)
    out_gate = jax.nn.sigmoid(projections[4])
    update = (out_gate * update_lin).astype(jnp.bfloat16)
    cot_value = cotangent.astype(jnp.float32)
    grad_lin = (cot_value * out_gate).astype(jnp.bfloat16)
    grad_gate_out = (cot_value * update_lin * out_gate * (1.0 - out_gate)).astype(jnp.bfloat16)
    flat_lin = grad_lin.reshape(tile_rows * tile_cols, channels)
    grad_norm_out = jnp.einsum(
        "pd,cd->pc", flat_lin, weights[5], preferred_element_type=jnp.float32
    )
    grad_norm_out = grad_norm_out.reshape(tile_rows, tile_cols, channels)
    grad_tri = norm_back(grad_norm_out * out_gain, x_hat, x_inverse).astype(jnp.bfloat16)
    grad_full = lax.all_gather(grad_tri, "col", axis=1, tiled=True)
    grad_slab = grad_full
    grad_left = jnp.einsum(
        "ijh,jkh->ikh",
        grad_slab,
        lax.all_gather(right_act, "row", axis=0, tiled=True),
        preferred_element_type=jnp.float32,
    )
    grad_slab = grad_full
    grad_right = lax.psum_scatter(
        jnp.einsum("ijh,ikh->jkh", grad_slab, left_act, preferred_element_type=jnp.float32).astype(
            jnp.bfloat16
        ),
        "row",
        scatter_dimension=0,
        tiled=True,
    ).astype(jnp.float32)
    grad_pa, grad_ga = gate_back(grad_left, projections[0], projections[1], keep_mask)
    grad_pb, grad_gb = gate_back(grad_right, projections[2], projections[3], keep_mask)
    grads = jnp.stack([grad_pa, grad_ga, grad_pb, grad_gb, grad_gate_out]).reshape(
        5, tile_rows * tile_cols, channels
    )
    grad_normed = jnp.einsum("spd,scd->pc", grads, weights[:5], preferred_element_type=jnp.float32)
    grad_normed = grad_normed.reshape(tile_rows, tile_cols, channels)
    pair_grad = norm_back(grad_normed * in_gain, z_hat, z_inverse).astype(jnp.bfloat16)
    local_in = jnp.einsum("pc,spd->scd", flat_norm, grads, preferred_element_type=jnp.float32)
    local_out = jnp.dot(flat_out.T, flat_lin, preferred_element_type=jnp.float32)
    local_grads = jnp.concatenate([local_in, local_out[None]], axis=0) / residues
    weight_grad = lax.psum(local_grads, ("row", "col"))
    return (update, pair_grad, weight_grad)


def pack_kernel(act_hbm, mask_hbm, cot_hbm, gain_hbm, out_ref, act_ref, mask_ref, gain_ref, sems):
    tile_rows, tile_cols = mask_ref.shape
    pairs, channels = act_ref.shape
    head = out_ref.shape[0] - pairs
    pack_copies = [
        pltpu.make_async_copy(act_hbm, act_ref, sems.at[0]),
        pltpu.make_async_copy(gain_hbm, gain_ref, sems.at[1]),
        pltpu.make_async_copy(mask_hbm, mask_ref, sems.at[2]),
        pltpu.make_async_copy(cot_hbm, out_ref.at[head : head + pairs], sems.at[3]),
    ]
    for copy in pack_copies:
        copy.start()
    for copy in pack_copies:
        copy.wait()
    z_hat, _ = normalize(act_ref[...].astype(jnp.float32))
    out_ref[0:pairs] = (z_hat * gain_ref[...]).astype(jnp.bfloat16)
    keep = mask_ref[...].astype(jnp.float32)
    wide = jnp.concatenate([keep, jnp.zeros((tile_rows, channels - tile_cols), jnp.float32)], axis=1)
    tall = jnp.concatenate([wide, jnp.zeros((channels - tile_rows, channels), jnp.float32)], axis=0)
    out_ref[pairs:head] = tall.T[0 : head - pairs].astype(jnp.bfloat16)


def copy_kernel(in_ref, out_ref):
    out_ref[...] = in_ref[...]


def join_kernel(own_ref, twin_ref, out_ref):
    tile = SUB * SUB
    refs = (own_ref, twin_ref)
    for at, ref in enumerate(refs):
        out_ref[at * tile : (at + 1) * tile] = ref[0:tile]
        spot = 2 * tile + 2 * SUB + at * tile
        out_ref[spot : spot + tile] = ref[tile + 2 * SUB :]
    masks = [ref[tile : tile + 2 * SUB].astype(jnp.float32)[0:SUB] for ref in refs]
    out_ref[2 * tile : 2 * tile + 2 * SUB] = jnp.concatenate(masks, axis=0).astype(jnp.bfloat16)


def normed_rows(ref, sub):
    return ref[sub * SUB * SUB : (sub + 1) * SUB * SUB]


def mask_rows(ref, sub):
    at = ref.shape[0] // 2 // (SUB * SUB) * SUB * SUB
    return ref[at : at + 2 * SUB].astype(jnp.float32)[sub * SUB : (sub + 1) * SUB]


def cot_rows(ref, sub):
    at = ref.shape[0] // 2 // (SUB * SUB) * SUB * SUB + 2 * SUB
    return ref[at + sub * SUB * SUB : at + (sub + 1) * SUB * SUB]


def chip_rows(rows_of, refs, core, direct_on):
    if direct_on is None:
        return rows_of(refs[min(core, len(refs) - 1)], core if len(refs) == 1 else 0)
    here = lax.axis_index("col") % 2 == direct_on
    return jnp.where(here, rows_of(refs[0], core), rows_of(refs[1], 1 - core))


def split_chips(refs, chips):
    split, at = [], 0
    for width, direct_on in chips:
        split.append((refs[at : at + width], direct_on))
        at += width
    return split


def doubled(top, bottom):
    return jnp.concatenate([top, bottom], axis=0).astype(jnp.bfloat16)


def triangle(blocks, groups, steps, vectors_at, factors_at, start_at, store_at, beside=None, unrolled=False):
    def block(a):
        if beside is not None:
            beside(a)
        def step(q, totals):
            totals = list(totals)
            vectors = vectors_at(q)
            factors = factors_at(a, q)
            rows = [
                [doubled(vectors(g, inner), vectors(g + 1, inner)) for g in range(0, groups, 2)]
                for inner in range(SUB)
            ]
            for lane in range(SUB):
                chains = [[None, None] for _ in range(groups // 2)]
                for inner in range(SUB):
                    factor = factors(lane, inner)
                    factor = doubled(factor, factor)
                    for g in range(groups // 2):
                        term = factor * rows[inner][g]
                        chain = chains[g][inner % 2]
                        chains[g][inner % 2] = term if chain is None else chain + term
                for g in range(groups // 2):
                    wide = (chains[g][0] + chains[g][1]).astype(jnp.float32)
                    at = lane * groups + 2 * g
                    totals[at] = totals[at] + wide[0:SUB]
                    totals[at + 1] = totals[at + 1] + wide[SUB:]
            return tuple(totals)

        totals = tuple(start_at(a, g, lane) for lane in range(SUB) for g in range(groups))
        if steps > 4:
            totals = lax.fori_loop(0, steps, step, totals)
        else:
            for q in range(steps):
                totals = step(q, totals)
        for g in range(groups):
            store_at(a, g, [totals[lane * groups + g] for lane in range(SUB)])

    if unrolled:
        for a in range(blocks):
            block(a)
    else:
        pl.loop(0, blocks)(block)


def spread(ref, row):
    return jnp.broadcast_to(ref[pl.ds(row, 1), :], (SUB, ref.shape[-1]))


def line(ref, row):
    return ref[pl.ds(pl.multiple_of(row, SUB), SUB), :]


def columns_kernel(n_row, n_col, side_x, chips, crop_ref, weights_ref, *refs):
    count = sum(width for width, _ in chips)
    chip_list, refs = split_chips(refs[:count], chips), refs[count:]
    own_ref = None
    if side_x == 0:
        act_ref, in_gain_ref, out_gain_ref, *refs, own_ref, gains_ref = refs
        z_hat, z_inverse = normalize(act_ref[...].astype(jnp.float32).reshape(own_ref.shape[1:]))
        own_ref[0] = z_hat
        own_ref[1] = jnp.broadcast_to(z_inverse, z_hat.shape)
        gains_ref[0:1] = in_gain_ref[...]
        gains_ref[1:2] = out_gain_ref[...]
    else:
        gains_ref, *refs = refs
    tri_in, (tri_ref, flip_ref, left_ref, right_ref, side_ref, back_ref) = refs[:-6], refs[-6:]
    channels = weights_ref.shape[-1]
    tile = SUB * SUB
    size = n_row * tile
    bf16, f32 = jnp.bfloat16, jnp.float32
    row_me, col_me = lax.axis_index("row"), lax.axis_index("col")
    chip_list = [(chip, on, core, b) for core in range(2) for b, (chip, on) in enumerate(chip_list)]
    normed = jnp.concatenate([chip_rows(normed_rows, chip, core, on) for chip, on, core, _ in chip_list], axis=0)
    same = lax.broadcasted_iota(jnp.int32, (channels, channels), 0) == lax.broadcasted_iota(jnp.int32, (channels, channels), 1)
    identity = jnp.where(same, 1.0, 0.0).astype(bf16)

    def turned(rows):
        return lax.dot_general(identity, rows, (((1,), (1,)), ((), ())), preferred_element_type=f32).astype(bf16)

    def put(kind, rows):
        both = turned(rows)
        for core in range(2):
            flip_ref[kind, 2 * side_x + core] = both[:, core * size : (core + 1) * size]

    put(0, normed)
    crop = crop_ref[0]
    col_offset = lax.broadcasted_iota(jnp.int32, (SUB, channels), 0)
    row_offset = lax.broadcasted_iota(jnp.int32, (SUB, channels), 1)
    kept = []
    for chip, on, core, b in chip_list:
        keep = chip_rows(mask_rows, chip, core, on)
        rows_in = row_offset < crop - (row_me ^ b) * SUB
        cols_in = col_offset < crop - (col_me ^ (2 * side_x + core)) * SUB
        keep = jnp.where(rows_in & cols_in, keep, 0.0)
        kept += [jnp.broadcast_to(keep[:, at : at + 1], (SUB, channels)) for at in range(SUB)]
    kept = jnp.concatenate(kept, axis=0)
    for side, act_ref in enumerate((left_ref, right_ref)):
        pair = jnp.concatenate([weights_ref[2 * side], weights_ref[2 * side + 1]], axis=1)
        proj = jnp.dot(normed, pair, preferred_element_type=f32)
        gate = jax.nn.sigmoid(proj[:, channels:])
        masked = gate * kept
        act = masked * proj[:, :channels]
        act_ref[...] = act.astype(bf16).astype(f32)
        side_ref[2 * side] = masked
        side_ref[2 * side + 1] = act * (1.0 - gate)
    out_gate = jax.nn.sigmoid(jnp.dot(normed, weights_ref[4], preferred_element_type=f32))
    if own_ref is not None:
        own_ref[2] = out_gate[0:tile]
    cot = jnp.concatenate([chip_rows(cot_rows, chip, core, on) for chip, on, core, _ in chip_list], axis=0)
    grad = cot.astype(f32) * out_gate
    grad_lin = grad.astype(bf16)
    put(1, grad_lin)
    back_ref[0] = grad * (1.0 - out_gate)
    back = lax.dot_general(grad_lin, weights_ref[5], (((1,), (1,)), ((), ())), preferred_element_type=f32)
    back = back * gains_ref[1:2]
    back_ref[1] = back - jnp.mean(back, axis=-1, keepdims=True)
    turn = row_me ^ col_me

    def flipped(q):
        firsts = [q * size + (turn ^ g) * tile for g in range(n_col)]
        return lambda g, inner: right_ref[pl.ds(firsts[g] + inner, SUB, stride=SUB), :]

    def along(a, q):
        return lambda lane, inner: spread(left_ref, q * size + a * tile + lane * SUB + inner)

    def start(a, g, lane):
        if len(tri_in) == 0:
            return jnp.zeros((SUB, channels), f32)
        return line(tri_in[0], g * size + a * tile + lane * SUB)

    def store(a, g, values):
        for lane in range(SUB):
            tri_ref[pl.ds(pl.multiple_of(g * size + a * tile + lane * SUB, SUB), SUB), :] = values[lane]

    triangle(n_row, n_col, 2, flipped, along, start, store)


def rest_kernel(n_row, n_col, weights_ref, own_ref, gains_ref, tri_ref, flip_ref, *refs):
    groups = [refs[at * 4 : at * 4 + 4] for at in range(n_col // 2)]
    update_ref, pair_grad_ref, weight_grad_ref, back_ref, hat_ref, d_ref, sum_ref = refs[4 * (n_col // 2) :]
    channels = tri_ref.shape[-1]
    tile = SUB * SUB
    size = n_row * tile
    columns = []
    for col in range(n_col):
        own = pl.ds(col % 2 * size, size)
        left, right, side, backs = groups[col // 2]
        columns.append((left.at[own], right.at[own], side.at[:, own], backs.at[:, own]))
    residues = n_row * SUB
    bf16, f32 = jnp.bfloat16, jnp.float32
    turn = lax.axis_index("row") ^ lax.axis_index("col")
    out_gain = gains_ref[1:2]
    for col, (_, _, _, backs_ref) in enumerate(columns):
        rows = slice(col * size, (col + 1) * size)
        x_hat, inverse = normalize(tri_ref[rows, :])
        normed_out = (x_hat * out_gain).astype(bf16)
        hat_ref[rows, :] = normed_out
        lin = jnp.dot(normed_out, weights_ref[5], preferred_element_type=f32)
        if col == 0:
            update_ref[...] = (own_ref[2] * lin[0:tile]).astype(bf16).reshape(update_ref.shape)
        d_ref[rows, 4 * channels : 5 * channels] = (backs_ref[0] * lin).astype(bf16)
        back = backs_ref[1]
        second = jnp.mean(back * x_hat, axis=-1, keepdims=True)
        back_ref[rows, :] = ((back - x_hat * second) * inverse).astype(bf16).astype(f32)

    lefts, rights, sides = [[column[at] for column in columns] for at in (0, 1, 2)]

    def zero(a, g, lane):
        return jnp.zeros((SUB, channels), f32)

    def store(side):
        def put(a, g, values):
            for lane in range(0, SUB, 2):
                at = pl.multiple_of(a * tile + lane * SUB, 2 * SUB)
                both = jnp.concatenate(values[lane : lane + 2], axis=0)
                rows = pl.ds(pl.multiple_of(g * size + at, 2 * SUB), 2 * SUB)
                for kind in range(2):
                    spot = (2 * side + kind) * channels
                    scaled = both * sides[g][2 * side + kind, pl.ds(at, 2 * SUB), :]
                    d_ref[rows, spot : spot + channels] = scaled.astype(bf16)
        return put

    def by_right(q):
        return lambda g, inner: line(rights[g], (q ^ turn) * tile + inner * SUB)

    def by_left(q):
        return lambda g, inner: line(lefts[g], q * tile + inner * SUB)

    def along(a, q):
        return lambda lane, inner: spread(back_ref, q * size + a * tile + lane * SUB + inner)

    def down(a, q):
        return lambda lane, inner: spread(back_ref, (a ^ turn) * size + q * tile + inner * SUB + lane)

    def chunk(ref, a, first, last):
        return ref[pl.ds(pl.multiple_of(a * size, size), size), first * channels : last * channels]

    def early_sums(a):
        sum_ref[:, 0:channels] += jnp.dot(flip_ref[0, a], chunk(d_ref, a, 4, 5), preferred_element_type=f32)
        sum_ref[:, channels : 2 * channels] += jnp.dot(flip_ref[1, a], chunk(hat_ref, a, 0, 1), preferred_element_type=f32)

    def left_sums(a):
        sum_ref[:, 2 * channels :] += jnp.dot(flip_ref[0, a], chunk(d_ref, a, 0, 2), preferred_element_type=f32)

    sum_ref[...] = jnp.zeros(sum_ref.shape, f32)
    triangle(n_row, n_col, n_col, by_right, along, zero, store(0), early_sums, True)
    triangle(n_row, n_col, n_row, by_left, down, zero, store(1), left_sums, True)

    scale = 1.0 / residues
    flipped = jnp.concatenate([flip_ref[0, col] for col in range(n_col)], axis=1)
    right_sums = jnp.dot(flipped, d_ref[:, 2 * channels : 4 * channels], preferred_element_type=f32)
    for s in range(2):
        part = slice(s * channels, (s + 1) * channels)
        weight_grad_ref[s] = sum_ref[:, (2 + s) * channels : (3 + s) * channels] * scale
        weight_grad_ref[2 + s] = right_sums[:, part] * scale
    weight_grad_ref[4] = sum_ref[:, 0:channels] * scale
    weight_grad_ref[5] = sum_ref[:, channels : 2 * channels].T * scale
    wide = jnp.concatenate([weights_ref[s] for s in range(5)], axis=1)
    total = lax.dot_general(d_ref[0:tile], wide, (((1,), (1,)), ((), ())), preferred_element_type=f32)
    grad = norm_back(total * gains_ref[0:1], own_ref[0], own_ref[1])
    pair_grad_ref[...] = grad.astype(bf16).reshape(pair_grad_ref.shape)


def flip(block, n_row, n_col, even, odd):
    pairs = []
    for row in range(n_row):
        for col in range(n_col):
            shift = odd if col % 2 else even
            pairs.append((row * n_col + col, (row ^ shift[0]) * n_col + (col ^ shift[1])))
    return lax.ppermute(block, ("row", "col"), pairs)


def gathered_body(n_row, n_col, pair_act, pair_mask, crop_length, weights, in_gain, out_gain, cotangent):
    tile_rows, tile_cols, channels = pair_act.shape
    tile = tile_rows * tile_cols
    size = n_row * tile
    pairs = size * n_col
    head = tile + 2 * SUB
    f32, bf16 = jnp.float32, jnp.bfloat16
    vmem = pl.BlockSpec(memory_space=pltpu.VMEM)
    smem = pl.BlockSpec(memory_space=pltpu.SMEM)
    hbm = pl.BlockSpec(memory_space=pltpu.HBM)
    in_gain, out_gain = in_gain.reshape(1, channels), out_gain.reshape(1, channels)

    def limit(mib):
        return pltpu.CompilerParams(vmem_limit_bytes=mib * 1024 * 1024)

    own = pl.pallas_call(
        pack_kernel,
        name="pack",
        out_shape=jax.ShapeDtypeStruct((head + tile, channels), bf16),
        in_specs=[hbm] * 4,
        out_specs=vmem,
        scratch_shapes=[
            pltpu.VMEM((tile, channels), bf16),
            pltpu.VMEM(pair_mask.shape, jnp.int32),
            pltpu.VMEM((1, channels), f32),
            pltpu.SemaphoreType.DMA((4,)),
        ],
        compiler_params=limit(60),
    )(pair_act.reshape(tile, channels), pair_mask, cotangent.reshape(tile, channels), in_gain)
    crop_length, own = lax.optimization_barrier((crop_length, own))

    def move(block, even, odd):
        return flip(block, n_row, n_col, even, odd)

    def other(block):
        return move(block, (0, 1), (0, 1))

    held = pl.pallas_call(
        copy_kernel,
        name="hold",
        out_shape=jax.ShapeDtypeStruct(own.shape, bf16),
        in_specs=[vmem],
        out_specs=vmem,
        compiler_params=limit(2),
        cost_estimate=pl.CostEstimate(flops=100_000_000, bytes_accessed=1_000_000, transcendentals=0),
    )(own)
    both = pl.pallas_call(
        join_kernel,
        name="join",
        out_shape=jax.ShapeDtypeStruct((2 * own.shape[0] - 2 * SUB, channels), bf16),
        in_specs=[vmem] * 2,
        out_specs=vmem,
        compiler_params=limit(2),
    )(held, other(own))
    straight = move(own, (3, 0), (3, 0))
    first = move(both, (2, 0), (1, 0))
    second = move(both, (0, 2), (2, 2))
    third = move(both, (1, 2), (3, 2))
    straight, first, second, third = [(block, other(block)) for block in (straight, first, second, third)]
    chips = (((1, None), (2, 1), (2, 0), (2, None)), ((2, 0), (2, 0), (2, 1), (2, 1)))
    sources = ((both, *first, *first, *straight), (*second, *third, *second, *third))

    tri, parts, extra = [], [], []
    for side_x in range(n_col // 2):
        more = (pair_act, in_gain, out_gain) if side_x == 0 else (extra[1], *tri)
        more_shapes = () if side_x > 0 else (
            jax.ShapeDtypeStruct((3, tile, channels), f32),
            jax.ShapeDtypeStruct((SUB, channels), f32),
        )
        last = 3 + len(sources[side_x])
        results = pl.pallas_call(
            functools.partial(columns_kernel, n_row, n_col, side_x, chips[side_x]),
            name=f"columns_{side_x}",
            out_shape=(
                jax.ShapeDtypeStruct((pairs, channels), f32),
                jax.ShapeDtypeStruct((2, n_col, channels, size), bf16),
                jax.ShapeDtypeStruct((2 * size, channels), f32),
                jax.ShapeDtypeStruct((2 * size, channels), f32),
                jax.ShapeDtypeStruct((4, 2 * size, channels), f32),
                jax.ShapeDtypeStruct((2, 2 * size, channels), f32),
                *more_shapes,
            ),
            in_specs=[smem] + [vmem] * (1 + len(sources[side_x]) + len(more)),
            out_specs=(vmem,) * (6 + len(more_shapes)),
            input_output_aliases={last: 0, last + 1: 1} if side_x > 0 else {},
            compiler_params=limit(12),
            cost_estimate=pl.CostEstimate(flops=800_000_000, bytes_accessed=1_000_000, transcendentals=0),
        )(crop_length, weights, *sources[side_x], *more)
        tri = results[:2]
        parts += results[2:6]
        extra += results[6:]

    return pl.pallas_call(
        functools.partial(rest_kernel, n_row, n_col),
        name="rest",
        out_shape=(
            jax.ShapeDtypeStruct(pair_act.shape, bf16),
            jax.ShapeDtypeStruct(pair_act.shape, bf16),
            jax.ShapeDtypeStruct(weights.shape, f32),
        ),
        in_specs=[vmem] * (5 + len(parts)),
        out_specs=(vmem, vmem, vmem),
        scratch_shapes=[
            pltpu.VMEM((pairs, channels), f32),
            pltpu.VMEM((pairs, channels), bf16),
            pltpu.VMEM((pairs, 5 * channels), bf16),
            pltpu.VMEM((channels, 4 * channels), f32),
        ],
        compiler_params=limit(16),
    )(weights, *extra, *tri, *parts)


def body(n_row, n_col, pair_act, *others):
    tile_rows, tile_cols, channels = pair_act.shape
    pairs = tile_rows * n_row * tile_cols * n_col
    small = pairs * channels * 4 <= 1024 * 1024 and channels == 128
    square = n_row == 4 and n_col == 4 and tile_rows == SUB and tile_cols == SUB
    if small and square:
        return gathered_body(n_row, n_col, pair_act, *others)
    return spread_body(pair_act, *others)


def solution(mesh):
    return jax.shard_map(
        functools.partial(body, mesh.shape["row"], mesh.shape["col"]),
        mesh=mesh,
        in_specs=(
            P(("parts", "row"), "col", None),
            P(("parts", "row"), "col"),
            P("parts"),
            P(),
            P(),
            P(),
            P(("parts", "row"), "col", None),
        ),
        out_specs=(
            P(("parts", "row"), "col", None),
            P(("parts", "row"), "col", None),
            P("parts", None, None),
        ),
        check_vma=False,
    )
```
